32 devices in a mesh: gx: 4 (over y, core), gy: 8 (over z, x).
Axes of the slice: x: 2, y: 2, z: 4, core: 2. Of those that a mesh axis runs over, the one named last changes fastest.
Arguments:
- tiles: float32 [2, 3, 16384, 128], P(None, None, ('gx', 'gy')), may hold values from -6 to 6
- tile_owner: int32 [16384, 1], P(('gx', 'gy')), may hold values from 0 to 31; in each aligned block of 512 rows (0 to 511, 512 to 1023, ...) at most 32 rows name the same one
- tile_slot: int32 [16384], P(('gx', 'gy')), may hold values from 0 to 1023
- tile_count: int32 [32], P(('gx', 'gy')), may hold values from 384 to 512, as said below
- green: float32 [2, 6, 1, 2048, 2048], P(None, None, None, ('gx', 'gy')), may hold values from -6 to 6
Outputs:
- field_hat: float32 [2, 3, 1, 2048, 2048], P(None, None, None, ('gx', 'gy'))
The draws below stay inside these ranges and needn't reach their ends.
Inputs may be any that keep to these rules, and one draw needn't show every extreme that they name: `tile_owner`: within the 512 entries of one device, live or not, no owner is named by more than 32; that many is reached. `tile_count`: some device has all 512 entries live.
All inputs are finite; a program needn't handle non-finite values.
Results may differ from the reference program's by a relative error of at most 0.00007.
Values sent between devices are 32-bit elements; how exact they have to be, the bound alone decides.
No kernel may reach another device: no remote copies, remote signals or barrier semaphores. Data moves between devices by JAX's collectives and lax.ppermute only.
A program may use at most 128 MiB of HBM per device.

```python
import math
import jax
import jax.numpy as jnp
import numpy as np

NX = 2048
NY = 2048
PLANES = 1
TILE = 128
TILES_DEV = 512
CAP = 32
TILES = 16384
SLOTS = 1024
N_GX = 4
N_GY = 8
DEVICES = 32


def draw_tile_count(key, part):
    count_key = jax.random.fold_in(key, 11)
    full_key = jax.random.fold_in(key, 23)
    counts = jax.random.randint(count_key, (DEVICES,), 3 * TILES_DEV // 4, TILES_DEV + 1)
    full_device = jax.random.randint(full_key, (), 0, DEVICES)
    return jnp.where(jnp.arange(DEVICES) == full_device, TILES_DEV, counts).astype(jnp.int32)


def set_ends(result, own_key, smallest, largest):
    longest = result.shape.index(max(result.shape))
    spots = []
    for shift in (0, 1):
        where = [jax.random.randint(jax.random.fold_in(own_key, axis), (), 0, length) for axis, length in enumerate(result.shape)]
        where[longest] = (where[longest] + shift) % result.shape[longest]
        spots.append(tuple(where))
    return result.at[spots[0]].set(smallest).at[spots[1]].set(largest)


def block_scale(stream_key, dims, pieces, low, top_value):
    def one(axis_at, blocks):
        draws = jax.random.uniform(jax.random.fold_in(jax.random.fold_in(stream_key, 6), axis_at), (blocks,), jnp.float32, low / len(pieces), top_value / len(pieces))
        return jnp.repeat(jnp.exp(draws), dims[axis_at] // blocks).reshape((-1,) + (1,) * (len(dims) - axis_at - 1))

    loudness = one(*pieces[0])
    for cut in pieces[1:]:
        loudness = loudness * one(*cut)
    return loudness


def shared_out(key, own, number, rows, count, top, reach, lean):
    sequence = jax.random.permutation(key, count)
    heavy_load, ordinary = shares(count, rows * top, reach, lean, True), shares(count, rows * top, reach, lean, False)
    places = jnp.arange(count)

    def named(tallies, turn):
        used = int((tallies > 0).sum())
        fixed = max(1, used // 4)
        moved = fixed + (places - fixed + turn * (used - fixed)) % max(1, count - fixed)
        return jnp.zeros((count,), jnp.int32).at[sequence[jnp.where(places < fixed, places, moved)]].set(jnp.asarray(tallies, jnp.int32))

    tallies = jnp.where(number % 4 == 0, named(heavy_load, number // 4), named(ordinary, number - number // 4 - 1))
    mixed = jax.random.permutation(jax.random.fold_in(own, 3), count)
    giver, sink = mixed[0:count // 2 * 2:2], mixed[1:count // 2 * 2:2]
    margin = jnp.minimum(tallies[giver] - 1, reach - tallies[sink]) // 2
    margin = jnp.where((giver == sequence[0]) | (sink == sequence[0]) | (tallies[sink] == 0), 0, jnp.maximum(margin, 0))
    moved = jax.random.randint(jax.random.fold_in(own, 4), (count // 2,), 0, 1 << 20) % (margin + 1)
    tallies = tallies.at[giver].add(-moved).at[sink].add(moved)
    labels = jnp.searchsorted(jnp.cumsum(tallies), jnp.arange(rows * top), side="right").astype(jnp.int32)
    grid = labels.reshape(top, rows).T
    grid = grid[jax.random.permutation(jax.random.fold_in(own, 1), rows)]
    turn = jax.random.randint(jax.random.fold_in(own, 2), (rows, 1), 0, top)
    return jnp.take_along_axis(grid, (jnp.arange(top)[None, :] + turn) % top, axis=1)


def shares(count, total, limit, slope, full):
    loads = [(1 << 20) // math.isqrt(standing ** slope) + 1 for standing in range(1, count + 1)]
    largest = limit if full else min(limit, max(-(-total // count), total * loads[0] // sum(loads)))
    least = 1 if total - largest >= count - 1 else 0
    given, rest = [largest] + [least] * (count - 1), total - largest - least * (count - 1)
    while rest > 0:
        candidates = [i for i in range(1, count) if given[i] < largest] or [i for i in range(1, count) if given[i] < limit]
        mass, left = sum([loads[i] for i in candidates]), rest
        for i in candidates:
            more = min(limit - given[i], max(1, left * loads[i] // mass), rest)
            given[i] = given[i] + more
            rest = rest - more
    return np.array(given)


def bell_draw(own_key, extent, deviation, reach, split=(), held_as=jnp.bfloat16):
    entries = jax.random.normal(own_key, extent, jnp.float32) * deviation
    if len(split) > 0:
        entries = block_scale(own_key, extent, split, -0.22, 0.18) * entries
    return jnp.clip(entries, min=-reach, max=reach).astype(held_as)


def setup_inputs(seed: int = 0) -> dict:
    streams_of = jax.random.split(jax.random.key(seed), 6)
    tiles = bell_draw(streams_of[0], (2, 3, TILES, TILE), 1.0, 6.0, ((2, 32),), jnp.float32)
    tile_owner_keys = jax.random.split(jax.random.fold_in(streams_of[1], 1), TILES // TILES_DEV)
    tile_owner_turns = jax.random.permutation(jax.random.fold_in(streams_of[1], 3), TILES // TILES_DEV)
    tile_owner = jax.vmap(lambda own, number: shared_out(jax.random.fold_in(streams_of[1], 2), own, number, TILES_DEV, DEVICES, 1, CAP, 2))(tile_owner_keys, tile_owner_turns).reshape((TILES, 1))
    tile_slot = set_ends(jax.random.randint(streams_of[2], (TILES,), 0, SLOTS), jax.random.fold_in(streams_of[2], 1), 0, SLOTS - 1).astype(jnp.int32)
    tile_count = draw_tile_count(jax.random.fold_in(streams_of[5], 71), 0)
    green = bell_draw(streams_of[4], (2, 6, PLANES, NY, NX), 1.0, 6.0, ((3, 32),), jnp.float32)
    return dict(tiles=tiles, tile_owner=tile_owner, tile_slot=tile_slot, tile_count=tile_count, green=green)


pair_index = ((0, 3, 4), (3, 1, 5), (4, 5, 2))


def reference(tiles, tile_owner, tile_slot, tile_count, green):
    devices = N_GX * N_GY
    tile_index = jnp.arange(TILES, dtype=jnp.int32)
    is_live = (tile_index % TILES_DEV) < tile_count[tile_index // TILES_DEV]
    weight = jnp.where(is_live, 1.0, 0.0).astype(tiles.dtype)
    target = tile_owner[:, 0] * SLOTS + tile_slot
    dipole_grid = jnp.zeros((2, 3, devices * SLOTS, TILE), tiles.dtype)
    dipole_grid = dipole_grid.at[:, :, target, :].add(tiles * weight[None, None, :, None])
    x_local = NX // devices
    dipole_grid = dipole_grid.reshape(2, 3, devices, PLANES, x_local, NY)
    dipole_grid = dipole_grid.transpose(0, 1, 3, 2, 4, 5).reshape(2, 3, PLANES, NX, NY)
    complex_field = dipole_grid[0] + 1j * dipole_grid[1]
    spectrum = jnp.fft.fft2(complex_field, axes=(2, 3), norm="ortho")
    spectrum = jnp.swapaxes(spectrum, 2, 3)
    tensor = green[0] + 1j * green[1]
    mixed_rows = []
    for row_comp in range(3):
        total = tensor[pair_index[row_comp][0]] * spectrum[0]
        for col_comp in range(1, 3):
            total = total + tensor[pair_index[row_comp][col_comp]] * spectrum[col_comp]
        mixed_rows.append(total)
    mixed = jnp.stack(mixed_rows)
    return jnp.stack([jnp.real(mixed), jnp.imag(mixed)]).astype(tiles.dtype)
```

```python
import functools
import math

import jax
import jax.numpy as jnp
import ml_dtypes
import numpy as np
from jax import lax
from jax.experimental import pallas as pl
from jax.experimental.pallas import tpu as pltpu
from jax.sharding import PartitionSpec as P

pair_index = ((0, 3, 4), (3, 1, 5), (4, 5, 2))
vmem_bytes = 56 * 1024 * 1024
by_rows = (((1,), (1,)), ((), ()))


def params():
    return pltpu.CompilerParams(vmem_limit_bytes=vmem_bytes)


def cost(flops, moved):
    return pl.CostEstimate(flops=flops, bytes_accessed=moved, transcendentals=0)


def angles(rows, columns, length):
    products = np.outer(np.arange(rows), np.arange(columns)) % length
    return 2.0 * math.pi / length * products


def halves(table):
    wide = np.asarray(table, np.float32)
    high = wide.astype(ml_dtypes.bfloat16)
    low = (wide - high.astype(np.float32)).astype(ml_dtypes.bfloat16)
    return jnp.asarray(high), jnp.asarray(low)


def split_two(data):
    high = data.astype(jnp.bfloat16)
    return high, (data - high.astype(jnp.float32)).astype(jnp.bfloat16)


def split_three(data):
    high = data.astype(jnp.bfloat16)
    rest = data - high.astype(jnp.float32)
    middle = rest.astype(jnp.bfloat16)
    return high, middle, (rest - middle.astype(jnp.float32)).astype(jnp.bfloat16)


def dot_rows(left, right):
    return lax.dot_general(left, right, by_rows, preferred_element_type=jnp.float32)


def dot_rows_split(table_high, table_low, data):
    high, low = split_two(data)
    return (
        dot_rows(table_high, high) + dot_rows(table_high, low) + dot_rows(table_low, high)
    )


def flat_fft(values, times):
    length = len(values)
    if length == 1:
        return values
    even = flat_fft(values[0::2], times)
    odd = flat_fft(values[1::2], times)
    lower, upper = [], []
    for k in range(length // 2):
        turned = times(odd[k], k, length)
        lower.append(jax.tree.map(lambda a, b: a + b, even[k], turned))
        upper.append(jax.tree.map(lambda a, b: a - b, even[k], turned))
    return lower + upper


def times_pair(value, k, length):
    real, imag = value
    if k == 0:
        return value
    if 4 * k == length:
        return (imag, -real)
    cos_k = math.cos(2.0 * math.pi * k / length)
    sin_k = math.sin(2.0 * math.pi * k / length)
    return (real * cos_k + imag * sin_k, imag * cos_k - real * sin_k)


def pack_kernel(devices, per_owner, with_slots, count, owner_col, owner_row, slot_row, tiles, out):
    listed = owner_row.shape[1]
    live_count = count[0]
    owners = owner_row[...]
    sender = lax.broadcasted_iota(jnp.int32, (listed, listed), 0)
    reader = lax.broadcasted_iota(jnp.int32, (listed, listed), 1)
    earlier = (owner_col[...] == owners) & (sender < reader) & (sender < live_count)
    rank = jnp.sum(jnp.where(earlier, 1.0, 0.0), axis=0, keepdims=True).astype(jnp.int32)
    live = lax.broadcasted_iota(jnp.int32, (1, listed), 1) < live_count
    target = jnp.where(live, owners * per_owner + rank, -1)
    places = lax.broadcasted_iota(jnp.int32, (devices * per_owner, listed), 0)
    chosen = jnp.where(places == target, 1.0, 0.0).astype(jnp.bfloat16)
    for comp in range(tiles.shape[1]):
        parts = [part for r in range(2) for part in split_three(tiles[r, comp])]
        got = jnp.dot(
            chosen, jnp.concatenate(parts, axis=1), preferred_element_type=jnp.float32
        )
        for r in range(2):
            one = got[:, 384 * r : 384 * r + 384]
            whole = (one[:, :128] + one[:, 128:256]) + one[:, 256:]
            out[comp, :, r * per_owner : (r + 1) * per_owner, :] = whole.reshape(
                devices, per_owner, 128
            )
    if with_slots:
        named = slot_row[...] + 1
        owner_at = lax.broadcasted_iota(jnp.int32, (devices, listed), 0)
        mine = (owner_at == owners) & live
        rank_at = lax.broadcasted_iota(jnp.int32, (128, listed), 0)
        ranked = jnp.where(rank_at == rank, 1.0, 0.0).astype(jnp.bfloat16)
        coarse = jnp.where(mine, (named >> 5).astype(jnp.float32), 0.0).astype(jnp.bfloat16)
        fine = jnp.where(mine, (named & 31).astype(jnp.float32), 0.0).astype(jnp.bfloat16)
        slots = 32.0 * dot_rows(coarse, ranked) + dot_rows(fine, ranked) - 1.0
        out[0, :, 2 * per_owner : 2 * per_owner + 8, :] = jnp.broadcast_to(
            slots[:, None, :], (devices, 8, 128)
        )


def pack(tiles, owner_col, owner_row, slot_row, count, devices, per_owner, with_slots):
    comps, listed = tiles.shape[1], tiles.shape[2]
    rows = 2 * per_owner + (8 if with_slots else 0)
    return pl.pallas_call(
        functools.partial(pack_kernel, devices, per_owner, with_slots),
        out_shape=jax.ShapeDtypeStruct((comps, devices, rows, 128), jnp.float32),
        in_specs=[pl.BlockSpec(memory_space=pltpu.SMEM)]
        + [pl.BlockSpec(memory_space=pltpu.VMEM)] * 4,
        out_specs=pl.BlockSpec(memory_space=pltpu.VMEM),
        compiler_params=params(),
        cost_estimate=cost(
            comps * devices * per_owner * listed * 768 * 2, comps * devices * rows * 1024
        ),
    )(count, owner_col, owner_row, slot_row, tiles)


def slab_kernel(
    x_local, blocks, per_owner, slots, data, table_high, table_low, twist, out, slab, turned
):
    devices = data.shape[0]
    entries = devices * per_owner
    wide = 2 * x_local
    slot = slots[...]
    shift = blocks.bit_length() - 1
    landing = jnp.where(slot >= 0, (slot & (blocks - 1)) * x_local + (slot >> shift), -1)
    parts = []
    for r in range(2):
        arrived = data[:, r * per_owner : (r + 1) * per_owner, :].reshape(entries, 128)
        parts.extend(split_two(arrived))
    parts = jnp.concatenate(parts, axis=1)
    for start in range(0, blocks * x_local, 256):
        place = start + lax.broadcasted_iota(jnp.int32, (256, entries), 0)
        chosen = jnp.where(place == landing, 1.0, 0.0).astype(jnp.bfloat16)
        got = jnp.dot(chosen, parts, preferred_element_type=jnp.float32)
        for r in range(2):
            slab[r, start : start + 256, :] = (
                got[:, 256 * r : 256 * r + 128] + got[:, 256 * r + 128 : 256 * r + 256]
            )

    @pl.loop(0, x_local // 8)
    def _(step):
        at = pl.multiple_of(step * 8, 8)
        values = [
            tuple(slab[r, pl.ds(t * x_local + at, 8), :] for r in range(2))
            for t in range(blocks)
        ]
        waves = flat_fft(values, times_pair)
        for k in range(blocks):
            real, imag = waves[k]
            cos_k, sin_k = twist[0, k : k + 1, :], twist[1, k : k + 1, :]
            new_real = real * cos_k + imag * sin_k
            new_imag = imag * cos_k - real * sin_k
            first = pl.ds(k * wide + at, 8)
            second = pl.ds(k * wide + x_local + at, 8)
            turned[first, :128] = new_real
            turned[first, 128:] = new_imag
            turned[second, :128] = new_imag
            turned[second, 128:] = -new_real

    for k in range(blocks):
        moved = dot_rows_split(
            table_high[...], table_low[...], turned[k * wide : (k + 1) * wide, :]
        )
        out[pl.ds(k, 128, stride=blocks), :] = moved


def slab_waves(slots, data, x_local, blocks, per_owner):
    y_cells = blocks * 128
    fine = angles(128, 128, 128)
    table = np.concatenate([np.cos(fine), np.sin(fine)], axis=1)
    twist_angle = angles(blocks, 128, y_cells)
    twist = np.stack([np.cos(twist_angle), np.sin(twist_angle)]).astype(np.float32)
    entries = data.shape[0] * per_owner
    return pl.pallas_call(
        functools.partial(slab_kernel, x_local, blocks, per_owner),
        out_shape=jax.ShapeDtypeStruct((y_cells, 2 * x_local), jnp.float32),
        in_specs=[pl.BlockSpec(memory_space=pltpu.VMEM)] * 5,
        out_specs=pl.BlockSpec(memory_space=pltpu.VMEM),
        scratch_shapes=[
            pltpu.VMEM((2, blocks * x_local, 128), jnp.float32),
            pltpu.VMEM((blocks * 2 * x_local, 256), jnp.float32),
        ],
        compiler_params=params(),
        cost_estimate=cost(
            blocks * x_local * entries * 512 * 2 + y_cells * x_local * 256 * 12,
            data.size * 4 + y_cells * x_local * 8,
        ),
    )(slots, data, *halves(table), jnp.asarray(twist))


def swap_parts(value, x_local):
    if 2 * x_local == 128:
        return pltpu.roll(value, x_local, 1)
    return jnp.concatenate([value[:, x_local:], value[:, :x_local]], axis=1)


def x_kernel(
    devices, x_local, y_local, data, twist, table_high, table_low, out, turned, columns
):
    wide = 2 * x_local
    lane = lax.broadcasted_iota(jnp.int32, (1, wide), 1)
    sign = jnp.where(lane < x_local, 1.0, -1.0)

    def times(value, k, length):
        if k == 0:
            return value
        swapped = swap_parts(value, x_local) * sign
        if 4 * k == length:
            return swapped
        cos_k = math.cos(2.0 * math.pi * k / length)
        sin_k = math.sin(2.0 * math.pi * k / length)
        return value * cos_k + swapped * sin_k

    @pl.loop(0, y_local // 8)
    def _(step):
        at = pl.multiple_of(step * 8, 8)
        values = [data[pl.ds(o * y_local + at, 8), :] for o in range(devices)]
        waves = flat_fft(values, times)
        for k in range(devices):
            swapped = swap_parts(waves[k], x_local)
            new = waves[k] * twist[0, k : k + 1, :] + swapped * twist[1, k : k + 1, :]
            turned[k, pl.ds(at, 8), :] = new
            turned[k, pl.ds(y_local + at, 8), :] = swap_parts(new, x_local) * sign

    for k in range(devices):
        columns[pl.ds(k, x_local, stride=devices), :] = dot_rows_split(
            table_high[...], table_low[...], turned[k]
        )
    for start in range(0, devices * x_local, 128):
        block = columns[start : start + 128, :].T
        out[0, :, start : start + 128] = block[:y_local]
        out[1, :, start : start + 128] = block[y_local:]


def x_waves(data, devices, x_local, y_local, y_cells):
    x_cells = devices * x_local
    fine = angles(x_local, x_local, x_local)
    scale = 1.0 / math.sqrt(x_cells * y_cells)
    table = np.concatenate([np.cos(fine), np.sin(fine)], axis=1) * scale
    angle = angles(devices, x_local, x_cells)
    cos_a, sin_a = np.cos(angle), np.sin(angle)
    twist = np.stack(
        [np.concatenate([cos_a, cos_a], axis=1), np.concatenate([sin_a, -sin_a], axis=1)]
    ).astype(np.float32)
    return pl.pallas_call(
        functools.partial(x_kernel, devices, x_local, y_local),
        out_shape=jax.ShapeDtypeStruct((2, y_local, x_cells), jnp.float32),
        in_specs=[pl.BlockSpec(memory_space=pltpu.VMEM)] * 4,
        out_specs=pl.BlockSpec(memory_space=pltpu.VMEM),
        scratch_shapes=[
            pltpu.VMEM((devices, 2 * y_local, 2 * x_local), jnp.float32),
            pltpu.VMEM((x_cells, 2 * y_local), jnp.float32),
        ],
        compiler_params=params(),
        cost_estimate=cost(x_cells * y_local * x_local * 24, x_cells * y_local * 16),
    )(data, jnp.asarray(twist), *halves(table))


def mix_kernel(green, first, second, third, out):
    waves = [(one[0], one[1]) for one in (first, second, third)]
    for row in range(3):
        real_sum = imag_sum = None
        for col in range(3):
            entry = pair_index[row][col]
            green_real, green_imag = green[0, entry], green[1, entry]
            real, imag = waves[col]
            real_term = green_real * real - green_imag * imag
            imag_term = green_real * imag + green_imag * real
            real_sum = real_term if real_sum is None else real_sum + real_term
            imag_sum = imag_term if imag_sum is None else imag_sum + imag_term
        out[0, row] = real_sum
        out[1, row] = imag_sum


def mix(green, waves):
    y_local, x_cells = green.shape[2], green.shape[3]
    step = 256
    wave_spec = pl.BlockSpec((2, y_local, step), lambda i: (0, 0, i))
    return pl.pallas_call(
        mix_kernel,
        grid=(x_cells // step,),
        out_shape=jax.ShapeDtypeStruct((2, 3, y_local, x_cells), jnp.float32),
        in_specs=[pl.BlockSpec((2, 6, y_local, step), lambda i: (0, 0, 0, i))] + [wave_spec] * 3,
        out_specs=pl.BlockSpec((2, 3, y_local, step), lambda i: (0, 0, 0, i)),
        compiler_params=params(),
        cost_estimate=cost(72 * y_local * x_cells, 96 * y_local * x_cells),
    )(green, *waves)


def exchange(data):
    return lax.all_to_all(data, ("gx", "gy"), split_axis=0, concat_axis=0, tiled=True)


def per_device(tiles, tile_owner, tile_slot, tile_count, green):
    devices = lax.axis_size("gx") * lax.axis_size("gy")
    tile_total, tile_len = tiles.shape[2], tiles.shape[3]
    planes, y_local, x_cells = green.shape[2:]
    y_cells = y_local * devices
    x_local = x_cells // devices
    blocks = y_cells // tile_len
    per_owner = max(2, 2 * tile_total // devices)
    assert planes == 1 and tile_len == 128
    lists = (tile_owner, tile_owner.reshape(1, tile_total), tile_slot.reshape(1, tile_total))
    lists = lists + (tile_count,)
    head = pack(tiles[:, :1], *lists, devices, per_owner, True)
    tail = pack(tiles[:, 1:], *lists, devices, per_owner, False)
    arrived = [exchange(head[0]), exchange(tail[0]), exchange(tail[1])]
    slots = arrived[0][:, 2 * per_owner, :per_owner].reshape(1, devices * per_owner)
    slots = slots.astype(jnp.int32)
    waves = []
    for comp in range(3):
        ready = slab_waves(slots, arrived[comp], x_local, blocks, per_owner)
        moved = exchange(ready.reshape(devices, y_local, 2 * x_local))
        moved = moved.reshape(devices * y_local, 2 * x_local)
        waves.append(x_waves(moved, devices, x_local, y_local, y_cells))
    mixed = mix(green.reshape(2, 6, y_local, x_cells), waves)
    return mixed.reshape(2, 3, planes, y_local, x_cells)


def solution(mesh):
    in_specs = (
        P(None, None, ("gx", "gy"), None),
        P(("gx", "gy"), None),
        P(("gx", "gy")),
        P(("gx", "gy")),
        P(None, None, None, ("gx", "gy"), None),
    )
    out_specs = P(None, None, None, ("gx", "gy"), None)
    return jax.shard_map(
        per_device, mesh=mesh, in_specs=in_specs, out_specs=out_specs, check_vma=False
    )
```

```python
import functools
import math

import jax
import jax.numpy as jnp
import ml_dtypes
import numpy as np
from jax import lax
from jax.experimental import pallas as pl
from jax.experimental.pallas import tpu as pltpu
from jax.sharding import PartitionSpec as P

pair_index = ((0, 3, 4), (3, 1, 5), (4, 5, 2))
vmem_bytes = 56 * 1024 * 1024
by_rows = (((1,), (1,)), ((), ()))


def params():
    return pltpu.CompilerParams(vmem_limit_bytes=vmem_bytes)


def cost(flops, moved):
    return pl.CostEstimate(flops=flops, bytes_accessed=moved, transcendentals=0)


def angles(rows, columns, length):
    products = np.outer(np.arange(rows), np.arange(columns)) % length
    return 2.0 * math.pi / length * products


def halves(table):
    wide = np.asarray(table, np.float32)
    high = wide.astype(ml_dtypes.bfloat16)
    low = (wide - high.astype(np.float32)).astype(ml_dtypes.bfloat16)
    return jnp.asarray(high), jnp.asarray(low)


def split_two(data):
    high = data.astype(jnp.bfloat16)
    return high, (data - high.astype(jnp.float32)).astype(jnp.bfloat16)


def split_three(data):
    high = data.astype(jnp.bfloat16)
    rest = data - high.astype(jnp.float32)
    middle = rest.astype(jnp.bfloat16)
    return high, middle, (rest - middle.astype(jnp.float32)).astype(jnp.bfloat16)


def dot_rows(left, right):
    return lax.dot_general(left, right, by_rows, preferred_element_type=jnp.float32)


def dot_rows_split(table_high, table_low, data):
    high, low = split_two(data)
    return (
        dot_rows(table_high, high) + dot_rows(table_high, low) + dot_rows(table_low, high)
    )


def flat_fft(values, times):
    length = len(values)
    if length == 1:
        return values
    even = flat_fft(values[0::2], times)
    odd = flat_fft(values[1::2], times)
    lower, upper = [], []
    for k in range(length // 2):
        turned = times(odd[k], k, length)
        lower.append(jax.tree.map(lambda a, b: a + b, even[k], turned))
        upper.append(jax.tree.map(lambda a, b: a - b, even[k], turned))
    return lower + upper


def times_pair(value, k, length):
    real, imag = value
    if k == 0:
        return value
    if 4 * k == length:
        return (imag, -real)
    cos_k = math.cos(2.0 * math.pi * k / length)
    sin_k = math.sin(2.0 * math.pi * k / length)
    return (real * cos_k + imag * sin_k, imag * cos_k - real * sin_k)


def block_mask(place, devices):
    rest = place % (devices // 4)
    return (place // (devices // 4)) * 2 + (rest & 1) + (rest >> 1) * 8


def pack_kernel(devices, per_owner, with_slots, count, me, owner_row, slot_row, tiles, *out):
    listed = owner_row.shape[1]
    rest = devices // 4
    live_count = count[0]
    owners = owner_row[...]
    live = lax.broadcasted_iota(jnp.int32, (1, listed), 1) < live_count
    apart = owners ^ me[0]
    place = ((apart >> 1) & 3) * rest + (apart & 1) + ((apart >> 3) << 1)
    place = jnp.where(live, place, -1)
    named = jnp.where(
        lax.broadcasted_iota(jnp.int32, (devices, listed), 0) == place, 1.0, 0.0
    )
    sender = lax.broadcasted_iota(jnp.int32, (listed, listed), 0)
    reader = lax.broadcasted_iota(jnp.int32, (listed, listed), 1)
    before = jnp.where(sender < reader, 1.0, 0.0).astype(jnp.bfloat16)
    counted = jnp.dot(named.astype(jnp.bfloat16), before, preferred_element_type=jnp.float32)
    rank = jnp.sum(counted * named, axis=0, keepdims=True).astype(jnp.int32)
    target = jnp.where(live, place * per_owner + rank, -1)
    places = lax.broadcasted_iota(jnp.int32, (devices * per_owner, listed), 0)
    chosen = jnp.where(places == target, 1.0, 0.0).astype(jnp.bfloat16)
    parts = [part for r in range(2) for part in split_three(tiles[r, 0])]
    got = jnp.dot(chosen, jnp.concatenate(parts, axis=1), preferred_element_type=jnp.float32)
    for r in range(2):
        one = got[:, 384 * r : 384 * r + 384]
        whole = (one[:, :128] + one[:, 128:256]) + one[:, 256:]
        whole = whole.reshape(4, rest, per_owner, 128)
        for part in range(4):
            out[part][:, r * per_owner : (r + 1) * per_owner, :] = whole[part]
    if with_slots:
        stated = slot_row[...] + 1
        rank_at = lax.broadcasted_iota(jnp.int32, (128, listed), 0)
        ranked = jnp.where(rank_at == rank, 1.0, 0.0).astype(jnp.bfloat16)
        coarse = (named * (stated >> 5).astype(jnp.float32)).astype(jnp.bfloat16)
        fine = (named * (stated & 31).astype(jnp.float32)).astype(jnp.bfloat16)
        slots = 32.0 * dot_rows(coarse, ranked) + dot_rows(fine, ranked) - 1.0
        slots = jnp.broadcast_to(slots[:, None, :], (devices, 8, 128)).reshape(4, rest, 8, 128)
        for part in range(4):
            out[part][:, 2 * per_owner : 2 * per_owner + 8, :] = slots[part]


def pack(tiles, comp, owner_row, slot_row, count, me, devices, per_owner):
    listed = tiles.shape[2]
    rows = 2 * per_owner + (8 if comp == 0 else 0)
    rest = devices // 4
    whole = pl.BlockSpec((1, listed), lambda i: (0, 0))
    return pl.pallas_call(
        functools.partial(pack_kernel, devices, per_owner, comp == 0),
        grid=(1,),
        out_shape=[jax.ShapeDtypeStruct((rest, rows, 128), jnp.float32)] * 4,
        in_specs=[pl.BlockSpec(memory_space=pltpu.SMEM)] * 2
        + [whole, whole, pl.BlockSpec((2, 1, listed, 128), lambda i: (0, comp, 0, 0))],
        out_specs=[pl.BlockSpec((rest, rows, 128), lambda i: (0, 0, 0))] * 4,
        compiler_params=params(),
        cost_estimate=cost(
            devices * per_owner * listed * 768 * 2, devices * rows * 1024
        ),
    )(count, me, owner_row, slot_row, tiles)


def regroup_kernel(outer, *refs):
    given, made = refs[:outer], refs[outer:]
    for i, source in enumerate(given):
        for j, target in enumerate(made):
            target[i] = source[j]


def regroup(arrays):
    outer, inner = len(arrays), arrays[0].shape[0]
    shape = (outer,) + arrays[0].shape[1:]
    return pl.pallas_call(
        functools.partial(regroup_kernel, outer),
        out_shape=[jax.ShapeDtypeStruct(shape, jnp.float32)] * inner,
        in_specs=[pl.BlockSpec(memory_space=pltpu.VMEM)] * outer,
        out_specs=[pl.BlockSpec(memory_space=pltpu.VMEM)] * inner,
        compiler_params=params(),
        cost_estimate=cost(0, arrays[0].size * 8 * outer),
    )(*arrays)


def slab_kernel(x_local, blocks, per_owner, groups, me, slots, table, twist, *refs):
    data, out = refs[:groups], refs[groups : 2 * groups]
    slab, turned, ordered = refs[2 * groups :]
    entries = groups * data[0].shape[0] * per_owner
    devices = table.shape[0]
    kept = table.shape[1]
    wide = 2 * x_local
    slot = slots[...]
    shift = blocks.bit_length() - 1
    landing = jnp.where(slot >= 0, (slot & (blocks - 1)) * x_local + (slot >> shift), -1)
    parts = []
    for r in range(2):
        arrived = jnp.concatenate(
            [
                one[:, r * per_owner : (r + 1) * per_owner, :].reshape(entries // groups, 128)
                for one in data
            ]
        )
        parts.extend(split_two(arrived))
    parts = jnp.concatenate(parts, axis=1)
    for start in range(0, blocks * x_local, 256):
        place = start + lax.broadcasted_iota(jnp.int32, (256, entries), 0)
        chosen = jnp.where(place == landing, 1.0, 0.0).astype(jnp.bfloat16)
        got = jnp.dot(chosen, parts, preferred_element_type=jnp.float32)
        for r in range(2):
            slab[r, start : start + 256, :] = (
                got[:, 256 * r : 256 * r + 128] + got[:, 256 * r + 128 : 256 * r + 256]
            )
    for place in range(devices):
        part, rest = place % 4, place // 4
        mask = block_mask(part * (devices // 4) + rest, devices)
        ordered[place * kept : (place + 1) * kept, :] = table[me[0] ^ mask]

    @pl.loop(0, x_local // 8)
    def _(step):
        at = pl.multiple_of(step * 8, 8)
        values = [
            tuple(slab[r, pl.ds(t * x_local + at, 8), :] for r in range(2))
            for t in range(blocks)
        ]
        waves = flat_fft(values, times_pair)
        for k in range(blocks):
            real, imag = waves[k]
            cos_k, sin_k = twist[0, k : k + 1, :], twist[1, k : k + 1, :]
            new_real = real * cos_k + imag * sin_k
            new_imag = imag * cos_k - real * sin_k
            first = pl.ds(k * wide + at, 8)
            second = pl.ds(k * wide + x_local + at, 8)
            turned[first, :128] = new_real
            turned[first, 128:] = new_imag
            turned[second, :128] = new_imag
            turned[second, 128:] = -new_real

    table_high, table_low = split_two(ordered[...])
    together = 4
    for start in range(0, blocks, together):
        moved = dot_rows_split(
            table_high, table_low, turned[start * wide : (start + together) * wide, :]
        )
        for k in range(start, start + together):
            one = moved[:, (k - start) * wide : (k - start + 1) * wide]
            for group in range(groups):
                rows = 128 // groups
                out[group][pl.ds(k, rows, stride=blocks), :] = one[group * rows :][:rows]


def slab_waves(me, slots, data, x_local, blocks, per_owner):
    y_cells = blocks * 128
    groups = len(data)
    devices = groups * data[0].shape[0]
    fine = angles(128, 128, 128)
    table = np.concatenate([np.cos(fine), np.sin(fine)], axis=1).astype(np.float32)
    table = table.reshape(devices, 128 // devices, 256)
    twist_angle = angles(blocks, 128, y_cells)
    twist = np.stack([np.cos(twist_angle), np.sin(twist_angle)]).astype(np.float32)
    entries = devices * per_owner
    made = jax.ShapeDtypeStruct((y_cells // groups, 2 * x_local), jnp.float32)
    return pl.pallas_call(
        functools.partial(slab_kernel, x_local, blocks, per_owner, groups),
        out_shape=[made] * groups,
        in_specs=[pl.BlockSpec(memory_space=pltpu.SMEM)]
        + [pl.BlockSpec(memory_space=pltpu.VMEM)] * (3 + groups),
        out_specs=[pl.BlockSpec(memory_space=pltpu.VMEM)] * groups,
        scratch_shapes=[
            pltpu.VMEM((2, blocks * x_local, 128), jnp.float32),
            pltpu.VMEM((blocks * 2 * x_local, 256), jnp.float32),
            pltpu.VMEM((128, 256), jnp.float32),
        ],
        compiler_params=params(),
        cost_estimate=cost(
            blocks * x_local * entries * 512 * 2 + y_cells * x_local * 256 * 12,
            entries * 1024 + y_cells * x_local * 8,
        ),
    )(me, slots, jnp.asarray(table), jnp.asarray(twist), *data)


def swap_parts(value, x_local):
    if 2 * x_local == 128:
        return pltpu.roll(value, x_local, 1)
    return jnp.concatenate([value[:, x_local:], value[:, :x_local]], axis=1)


def x_steps(devices, x_local, y_local, me, twist, table, data, placed, turned, columns, store):
    wide = 2 * x_local
    lane = lax.broadcasted_iota(jnp.int32, (1, wide), 1)
    sign = jnp.where(lane < x_local, 1.0, -1.0)
    for place in range(devices):
        part, rest = place // (devices // 4), place % (devices // 4)
        placed[me[0] ^ block_mask(place, devices)] = data[part][rest]

    def times(value, k, length):
        if k == 0:
            return value
        swapped = swap_parts(value, x_local) * sign
        if 4 * k == length:
            return swapped
        cos_k = math.cos(2.0 * math.pi * k / length)
        sin_k = math.sin(2.0 * math.pi * k / length)
        return value * cos_k + swapped * sin_k

    @pl.loop(0, y_local // 8)
    def _(step):
        at = pl.multiple_of(step * 8, 8)
        values = [placed[o, pl.ds(at, 8), :] for o in range(devices)]
        waves = flat_fft(values, times)
        for k in range(devices):
            swapped = swap_parts(waves[k], x_local)
            new = waves[k] * twist[0, k : k + 1, :] + swapped * twist[1, k : k + 1, :]
            turned[k, pl.ds(at, 8), :] = new
            turned[k, pl.ds(y_local + at, 8), :] = swap_parts(new, x_local) * sign

    table_high, table_low = split_two(table[...])
    together = 4
    for start in range(0, devices, together):
        stacked = turned[start : start + together].reshape(together * 2 * y_local, wide)
        moved = dot_rows_split(table_high, table_low, stacked)
        for k in range(start, start + together):
            columns[pl.ds(k, x_local, stride=devices), :] = moved[
                :, (k - start) * 2 * y_local : (k - start + 1) * 2 * y_local
            ]
    for start in range(0, devices * x_local, 128):
        store(start, columns[start : start + 128, :].T)


def x_kernel(devices, x_local, y_local, me, twist, table, *refs):
    data, out, scratch = refs[:4], refs[4], refs[5:]

    def store(start, block):
        out[0, :, start : start + 128] = block[:y_local]
        out[1, :, start : start + 128] = block[y_local:]

    x_steps(devices, x_local, y_local, me, twist, table, data, *scratch, store)


def last_kernel(devices, x_local, y_local, me, twist, table, *refs):
    data, (green, first, second, out) = refs[:4], refs[4:8]
    scratch, (tensor, kept, made, in_sems, out_sems) = refs[8:11], refs[11:]
    x_cells = devices * x_local
    pieces = made.shape[0]
    width = x_cells // pieces
    fetches = [
        pltpu.make_async_copy(first, kept.at[0], in_sems.at[0]),
        pltpu.make_async_copy(second, kept.at[1], in_sems.at[1]),
        pltpu.make_async_copy(green, tensor, in_sems.at[2]),
    ]
    for fetch in fetches:
        fetch.start()

    def store(start, block):
        kept[2, 0, :, start : start + 128] = block[:y_local]
        kept[2, 1, :, start : start + 128] = block[y_local:]

    x_steps(devices, x_local, y_local, me, twist, table, data, *scratch, store)
    for fetch in fetches:
        fetch.wait()
    sends = []
    for piece in range(pieces):

        @pl.loop(0, y_local // 8)
        def _(step):
            rows = pl.ds(pl.multiple_of(step * 8, 8), 8)
            columns = pl.ds(piece * width, width)
            waves = [(kept[c, 0, rows, columns], kept[c, 1, rows, columns]) for c in range(3)]
            sums = [[None, None] for _ in range(3)]
            for entry in range(6):
                green_real = tensor[0, entry, rows, columns]
                green_imag = tensor[1, entry, rows, columns]
                for row in range(3):
                    for col in range(3):
                        if pair_index[row][col] != entry:
                            continue
                        real, imag = waves[col]
                        real_term = green_real * real - green_imag * imag
                        imag_term = green_real * imag + green_imag * real
                        old = sums[row]
                        sums[row] = [
                            real_term if old[0] is None else old[0] + real_term,
                            imag_term if old[1] is None else old[1] + imag_term,
                        ]
            for row in range(3):
                made[piece, 0, row, rows, :] = sums[row][0]
                made[piece, 1, row, rows, :] = sums[row][1]

        send = pltpu.make_async_copy(
            made.at[piece],
            out.at[:, :, :, pl.ds(piece * width, width)],
            out_sems.at[piece],
        )
        send.start()
        sends.append(send)
    for send in sends:
        send.wait()


def x_tables(devices, x_local, y_cells):
    x_cells = devices * x_local
    fine = angles(x_local, x_local, x_local)
    scale = 1.0 / math.sqrt(x_cells * y_cells)
    table = np.concatenate([np.cos(fine), np.sin(fine)], axis=1) * scale
    angle = angles(devices, x_local, x_cells)
    cos_a, sin_a = np.cos(angle), np.sin(angle)
    twist = np.stack(
        [np.concatenate([cos_a, cos_a], axis=1), np.concatenate([sin_a, -sin_a], axis=1)]
    )
    return jnp.asarray(twist.astype(np.float32)), jnp.asarray(table.astype(np.float32))


def x_scratch(devices, x_local, y_local):
    return [
        pltpu.VMEM((devices, y_local, 2 * x_local), jnp.float32),
        pltpu.VMEM((devices, 2 * y_local, 2 * x_local), jnp.float32),
        pltpu.VMEM((devices * x_local, 2 * y_local), jnp.float32),
    ]


def x_waves(me, data, devices, x_local, y_local, y_cells):
    x_cells = devices * x_local
    return pl.pallas_call(
        functools.partial(x_kernel, devices, x_local, y_local),
        out_shape=jax.ShapeDtypeStruct((2, y_local, x_cells), jnp.float32),
        in_specs=[pl.BlockSpec(memory_space=pltpu.SMEM)]
        + [pl.BlockSpec(memory_space=pltpu.VMEM)] * 6,
        out_specs=pl.BlockSpec(memory_space=pltpu.VMEM),
        scratch_shapes=x_scratch(devices, x_local, y_local),
        compiler_params=params(),
        cost_estimate=cost(x_cells * y_local * x_local * 24, x_cells * y_local * 16),
    )(me, *x_tables(devices, x_local, y_cells), *data)


def last_waves(me, data, green, first, second, devices, x_local, y_local, y_cells):
    x_cells = devices * x_local
    pieces = 8
    return pl.pallas_call(
        functools.partial(last_kernel, devices, x_local, y_local),
        out_shape=jax.ShapeDtypeStruct((2, 3, y_local, x_cells), jnp.float32),
        in_specs=[pl.BlockSpec(memory_space=pltpu.SMEM)]
        + [pl.BlockSpec(memory_space=pltpu.VMEM)] * 6
        + [pl.BlockSpec(memory_space=pl.ANY)] * 3,
        out_specs=pl.BlockSpec(memory_space=pl.ANY),
        scratch_shapes=x_scratch(devices, x_local, y_local)
        + [
            pltpu.VMEM((2, 6, y_local, x_cells), jnp.float32),
            pltpu.VMEM((3, 2, y_local, x_cells), jnp.float32),
            pltpu.VMEM((pieces, 2, 3, y_local, x_cells // pieces), jnp.float32),
            pltpu.SemaphoreType.DMA((3,)),
            pltpu.SemaphoreType.DMA((pieces,)),
        ],
        compiler_params=params(),
        cost_estimate=cost(x_cells * y_local * (x_local * 24 + 72), x_cells * y_local * 96),
    )(me, *x_tables(devices, x_local, y_cells), *data, green, first, second)


def permute(data, mask, devices):
    if mask == 0:
        return data
    return lax.ppermute(data, ("gx", "gy"), [(d, d ^ mask) for d in range(devices)])


def exchange_first(arrays, devices):
    return [permute(a, block_mask(i * (devices // 4), devices), devices) for i, a in enumerate(arrays)]


def exchange_rest(arrays, devices):
    return [permute(a, block_mask(i, devices), devices) for i, a in enumerate(arrays)]


def per_device(tiles, tile_owner, tile_slot, tile_count, green):
    devices = lax.axis_size("gx") * lax.axis_size("gy")
    tile_total, tile_len = tiles.shape[2], tiles.shape[3]
    planes, y_local, x_cells = green.shape[2:]
    y_cells = y_local * devices
    x_local = x_cells // devices
    blocks = y_cells // tile_len
    per_owner = max(2, 2 * tile_total // devices)
    assert planes == 1 and tile_len == 128
    me = (lax.axis_index("gx") * lax.axis_size("gy") + lax.axis_index("gy")).reshape(1)
    me = me.astype(jnp.int32)
    owner_row, slot_row = tile_owner.reshape(1, tile_total), tile_slot.reshape(1, tile_total)
    green = green.reshape(2, 6, y_local, x_cells)
    waves, slots = [], None
    arrived = []
    for comp in range(3):
        packed = pack(tiles, comp, owner_row, slot_row, tile_count, me, devices, per_owner)
        arrived.append(exchange_rest(regroup(exchange_first(packed, devices)), devices))
    slots = [one[:, 2 * per_owner, :per_owner] for one in arrived[0]]
    slots = jnp.concatenate(slots, axis=0).reshape(1, devices * per_owner).astype(jnp.int32)
    for comp in range(3):
        ready = slab_waves(me, slots, arrived[comp], x_local, blocks, per_owner)
        ready = [one.reshape(4, y_local, 2 * x_local) for one in ready]
        moved = exchange_first(regroup(exchange_rest(ready, devices)), devices)
        if comp < 2:
            waves.append(x_waves(me, moved, devices, x_local, y_local, y_cells))
    mixed = last_waves(me, moved, green, *waves, devices, x_local, y_local, y_cells)
    return mixed.reshape(2, 3, planes, y_local, x_cells)


def solution(mesh):
    in_specs = (
        P(None, None, ("gx", "gy"), None),
        P(("gx", "gy"), None),
        P(("gx", "gy")),
        P(("gx", "gy")),
        P(None, None, None, ("gx", "gy"), None),
    )
    out_specs = P(None, None, None, ("gx", "gy"), None)
    return jax.shard_map(
        per_device, mesh=mesh, in_specs=in_specs, out_specs=out_specs, check_vma=False
    )
```

```python
import functools
import math

import jax
import jax.numpy as jnp
import ml_dtypes
import numpy as np
from jax import lax
from jax.experimental import pallas as pl
from jax.experimental.pallas import tpu as pltpu
from jax.sharding import PartitionSpec as P

pair_index = ((0, 3, 4), (3, 1, 5), (4, 5, 2))
by_rows = (((1,), (1,)), ((), ()))


def params(mebibytes):
    return pltpu.CompilerParams(vmem_limit_bytes=mebibytes * 1024 * 1024)


def cost(flops, moved):
    return pl.CostEstimate(flops=flops, bytes_accessed=moved, transcendentals=0)


def angles(rows, columns, length):
    products = np.outer(np.arange(rows), np.arange(columns)) % length
    return 2.0 * math.pi / length * products


def halves(table):
    wide = np.asarray(table, np.float32)
    high = wide.astype(ml_dtypes.bfloat16)
    low = (wide - high.astype(np.float32)).astype(ml_dtypes.bfloat16)
    return jnp.asarray(high), jnp.asarray(low)


def split_two(data):
    high = data.astype(jnp.bfloat16)
    return high, (data - high.astype(jnp.float32)).astype(jnp.bfloat16)


def split_three(data):
    high = data.astype(jnp.bfloat16)
    rest = data - high.astype(jnp.float32)
    middle = rest.astype(jnp.bfloat16)
    return high, middle, (rest - middle.astype(jnp.float32)).astype(jnp.bfloat16)


def dot_rows(left, right):
    return lax.dot_general(left, right, by_rows, preferred_element_type=jnp.float32)


def dot_rows_split(table, data):
    rows, depth = table.shape
    table_high, table_low = split_two(table)
    high, low = split_two(data)
    if depth > 128:
        both = dot_rows(jnp.concatenate([table_high, table_low]), high)
        return both[:rows] + both[rows:] + dot_rows(table_high, low)
    left = jnp.concatenate(
        [
            jnp.concatenate([table_high, table_high], axis=1),
            jnp.concatenate([table_low, jnp.zeros_like(table_low)], axis=1),
        ]
    )
    both = dot_rows(left, jnp.concatenate([high, low], axis=1))
    return both[:rows] + both[rows:]


def flat_fft(values, times):
    length = len(values)
    if length == 1:
        return values
    even = flat_fft(values[0::2], times)
    odd = flat_fft(values[1::2], times)
    lower, upper = [], []
    for k in range(length // 2):
        turned = times(odd[k], k, length)
        lower.append(jax.tree.map(lambda a, b: a + b, even[k], turned))
        upper.append(jax.tree.map(lambda a, b: a - b, even[k], turned))
    return lower + upper


def times_pair(value, k, length):
    real, imag = value
    if k == 0:
        return value
    if 4 * k == length:
        return (imag, -real)
    cos_k = math.cos(2.0 * math.pi * k / length)
    sin_k = math.sin(2.0 * math.pi * k / length)
    return (real * cos_k + imag * sin_k, imag * cos_k - real * sin_k)


def device_at(gx, z, gl, count_gl):
    return (gx * 4 + z) * count_gl + gl


def pack_kernel(
    devices, count_gl, per_owner, with_slots, count, my_z, owner_row, slot_row, tiles, _, *out
):
    listed = owner_row.shape[1]
    rest = devices // 4
    shift = count_gl.bit_length() - 1
    live_count = count[0]
    owners = owner_row[...]
    live = lax.broadcasted_iota(jnp.int32, (1, listed), 1) < live_count
    across = ((owners >> shift) & 3) ^ my_z[0]
    place = across * rest + ((owners >> (shift + 2)) << shift) + (owners & (count_gl - 1))
    place = jnp.where(live, place, -1)
    named = jnp.where(
        lax.broadcasted_iota(jnp.int32, (devices, listed), 0) == place, 1.0, 0.0
    )
    sender = lax.broadcasted_iota(jnp.int32, (listed, listed), 0)
    reader = lax.broadcasted_iota(jnp.int32, (listed, listed), 1)
    before = jnp.where(sender < reader, 1.0, 0.0).astype(jnp.bfloat16)
    counted = jnp.dot(named.astype(jnp.bfloat16), before, preferred_element_type=jnp.float32)
    rank = jnp.sum(counted * named, axis=0, keepdims=True).astype(jnp.int32)
    target = jnp.where(live, place * per_owner + rank, -1)
    places = lax.broadcasted_iota(jnp.int32, (devices * per_owner, listed), 0)
    chosen = jnp.where(places == target, 1.0, 0.0).astype(jnp.bfloat16)
    parts = [part for r in range(2) for part in split_three(tiles[r, 0])]
    got = jnp.dot(chosen, jnp.concatenate(parts, axis=1), preferred_element_type=jnp.float32)
    for r in range(2):
        one = got[:, 384 * r : 384 * r + 384]
        whole = (one[:, :128] + one[:, 128:256]) + one[:, 256:]
        whole = whole.reshape(4, rest, per_owner, 128)
        for part in range(4):
            out[part][:, r * per_owner : (r + 1) * per_owner, :] = whole[part]
    if with_slots:
        stated = slot_row[...] + 1
        rank_at = lax.broadcasted_iota(jnp.int32, (128, listed), 0)
        ranked = jnp.where(rank_at == rank, 1.0, 0.0).astype(jnp.bfloat16)
        coarse = (named * (stated >> 5).astype(jnp.float32)).astype(jnp.bfloat16)
        fine = (named * (stated & 31).astype(jnp.float32)).astype(jnp.bfloat16)
        slots = 32.0 * dot_rows(coarse, ranked) + dot_rows(fine, ranked) - 1.0
        slots = jnp.broadcast_to(slots[:, None, :], (devices, 8, 128)).reshape(4, rest, 8, 128)
        for part in range(4):
            out[part][:, 2 * per_owner : 2 * per_owner + 8, :] = slots[part]


def pack(tiles, comp, owner_row, slot_row, count, my_z, after, devices, count_gl, per_owner):
    listed = tiles.shape[2]
    rows = 2 * per_owner + (8 if comp == 0 else 0)
    rest = devices // 4
    whole = pl.BlockSpec((1, listed), lambda i: (0, 0))
    return pl.pallas_call(
        functools.partial(pack_kernel, devices, count_gl, per_owner, comp == 0),
        grid=(1,),
        out_shape=[jax.ShapeDtypeStruct((rest, rows, 128), jnp.float32)] * 4,
        in_specs=[pl.BlockSpec(memory_space=pltpu.SMEM)] * 2
        + [whole, whole, pl.BlockSpec((2, 1, listed, 128), lambda i: (0, comp, 0, 0))]
        + [pl.BlockSpec(memory_space=pl.ANY)],
        out_specs=[pl.BlockSpec((rest, rows, 128), lambda i: (0, 0, 0))] * 4,
        compiler_params=params(24),
        cost_estimate=cost(
            devices * per_owner * listed * 768 * 2, devices * rows * 1024
        ),
    )(count, my_z, owner_row, slot_row, tiles, after)


def stack_kernel(first, second, third, fourth, _, out):
    for i, one in enumerate((first, second, third, fourth)):
        out[:, i] = one[...]


def stack(arrays, after):
    inside, rows, lanes = arrays[0].shape
    return pl.pallas_call(
        stack_kernel,
        out_shape=jax.ShapeDtypeStruct((inside, 4, rows, lanes), jnp.float32),
        in_specs=[pl.BlockSpec(memory_space=pltpu.VMEM)] * 4
        + [pl.BlockSpec(memory_space=pl.ANY)],
        out_specs=pl.BlockSpec(memory_space=pltpu.VMEM),
        compiler_params=params(8),
        cost_estimate=cost(0, arrays[0].size * 32),
    )(*arrays, after)


def slab_kernel(
    x_local, blocks, per_owner, count_gl, my_z, slots, table, twist, data, out, slab, turned, ordered
):
    devices = table.shape[0]
    rest = devices // 4
    entries = devices * per_owner
    kept = table.shape[1]
    wide = 2 * x_local
    slot = slots[...]
    shift = blocks.bit_length() - 1
    landing = jnp.where(slot >= 0, (slot & (blocks - 1)) * x_local + (slot >> shift), -1)
    parts = []
    for r in range(2):
        arrived = data[:, :, r * per_owner : (r + 1) * per_owner, :].reshape(entries, 128)
        parts.extend(split_two(arrived))
    parts = jnp.concatenate(parts, axis=1)
    for start in range(0, blocks * x_local, 256):
        place = start + lax.broadcasted_iota(jnp.int32, (256, entries), 0)
        chosen = jnp.where(place == landing, 1.0, 0.0).astype(jnp.bfloat16)
        got = jnp.dot(chosen, parts, preferred_element_type=jnp.float32)
        for r in range(2):
            slab[r, start : start + 256, :] = (
                got[:, 256 * r : 256 * r + 128] + got[:, 256 * r + 128 : 256 * r + 256]
            )
    for place in range(devices):
        across, inside = place % 4, place // 4
        source = device_at(inside // count_gl, my_z[0] ^ across, inside % count_gl, count_gl)
        ordered[place * kept : (place + 1) * kept, :] = table[source]

    @pl.loop(0, x_local // 8)
    def _(step):
        at = pl.multiple_of(step * 8, 8)
        values = [
            tuple(slab[r, pl.ds(t * x_local + at, 8), :] for r in range(2))
            for t in range(blocks)
        ]
        waves = flat_fft(values, times_pair)
        for k in range(blocks):
            real, imag = waves[k]
            cos_k, sin_k = twist[0, k : k + 1, :], twist[1, k : k + 1, :]
            new_real = real * cos_k + imag * sin_k
            new_imag = imag * cos_k - real * sin_k
            first = pl.ds(k * wide + at, 8)
            second = pl.ds(k * wide + x_local + at, 8)
            turned[first, :128] = new_real
            turned[first, 128:] = new_imag
            turned[second, :128] = new_imag
            turned[second, 128:] = -new_real

    together = 4
    for start in range(0, blocks, together):
        moved = dot_rows_split(
            ordered[...], turned[start * wide : (start + together) * wide, :]
        )
        for k in range(start, start + together):
            one = moved[:, (k - start) * wide : (k - start + 1) * wide]
            out[pl.ds(k, 128, stride=blocks), :] = one


def slab_waves(my_z, slots, data, devices, x_local, blocks, count_gl, per_owner):
    y_cells = blocks * 128
    fine = angles(128, 128, 128)
    table = np.concatenate([np.cos(fine), np.sin(fine)], axis=1).astype(np.float32)
    table = table.reshape(devices, 128 // devices, 256)
    twist_angle = angles(blocks, 128, y_cells)
    twist = np.stack([np.cos(twist_angle), np.sin(twist_angle)]).astype(np.float32)
    entries = devices * per_owner
    return pl.pallas_call(
        functools.partial(slab_kernel, x_local, blocks, per_owner, count_gl),
        out_shape=jax.ShapeDtypeStruct((y_cells, 2 * x_local), jnp.float32),
        in_specs=[pl.BlockSpec(memory_space=pltpu.SMEM)]
        + [pl.BlockSpec(memory_space=pltpu.VMEM)] * 4,
        out_specs=pl.BlockSpec(memory_space=pltpu.VMEM),
        scratch_shapes=[
            pltpu.VMEM((2, blocks * x_local, 128), jnp.float32),
            pltpu.VMEM((blocks * 2 * x_local, 256), jnp.float32),
            pltpu.VMEM((128, 256), jnp.float32),
        ],
        compiler_params=params(24),
        cost_estimate=cost(
            blocks * x_local * entries * 512 * 2 + y_cells * x_local * 256 * 12,
            entries * 1024 + y_cells * x_local * 8,
        ),
    )(my_z, slots, jnp.asarray(table), jnp.asarray(twist), data)


def swap_parts(value, x_local):
    if 2 * x_local == 128:
        return pltpu.roll(value, x_local, 1)
    return jnp.concatenate([value[:, x_local:], value[:, :x_local]], axis=1)


def x_steps(
    devices, x_local, y_local, count_gl, my_z, twist, table, data, placed, turned, columns, store
):
    wide = 2 * x_local
    lane = lax.broadcasted_iota(jnp.int32, (1, wide), 1)
    sign = jnp.where(lane < x_local, 1.0, -1.0)
    for across in range(4):
        for inside in range(devices // 4):
            source = device_at(inside // count_gl, my_z[0] ^ across, inside % count_gl, count_gl)
            placed[source] = data[0][inside, 0] if across == 0 else data[across][inside]

    def times(value, k, length):
        if k == 0:
            return value
        swapped = swap_parts(value, x_local) * sign
        if 4 * k == length:
            return swapped
        cos_k = math.cos(2.0 * math.pi * k / length)
        sin_k = math.sin(2.0 * math.pi * k / length)
        return value * cos_k + swapped * sin_k

    @pl.loop(0, y_local // 8)
    def _(step):
        at = pl.multiple_of(step * 8, 8)
        values = [placed[o, pl.ds(at, 8), :] for o in range(devices)]
        waves = flat_fft(values, times)
        for k in range(devices):
            swapped = swap_parts(waves[k], x_local)
            new = waves[k] * twist[0, k : k + 1, :] + swapped * twist[1, k : k + 1, :]
            turned[k, pl.ds(at, 8), :] = new
            turned[k, pl.ds(y_local + at, 8), :] = swap_parts(new, x_local) * sign

    together = 4
    for start in range(0, devices, together):
        stacked = turned[start : start + together].reshape(together * 2 * y_local, wide)
        moved = dot_rows_split(table[...], stacked)
        for k in range(start, start + together):
            columns[pl.ds(k, x_local, stride=devices), :] = moved[
                :, (k - start) * 2 * y_local : (k - start + 1) * 2 * y_local
            ]
    for start in range(0, devices * x_local, 128):
        store(start, columns[start : start + 128, :].T)


def x_kernel(devices, x_local, y_local, count_gl, my_z, twist, table, *refs):
    data, out, scratch = refs[:4], refs[4], refs[5:]

    def store(start, block):
        out[0, :, start : start + 128] = block[:y_local]
        out[1, :, start : start + 128] = block[y_local:]

    x_steps(devices, x_local, y_local, count_gl, my_z, twist, table, data, *scratch, store)


def last_kernel(devices, x_local, y_local, count_gl, my_z, twist, table, *refs):
    data, (green, first, second, out) = refs[:4], refs[4:8]
    scratch, (tensor, kept, made, in_sems, out_sems) = refs[8:11], refs[11:]
    x_cells = devices * x_local
    pieces = made.shape[0]
    width = x_cells // pieces
    fetches = [
        pltpu.make_async_copy(first, kept.at[0], in_sems.at[0]),
        pltpu.make_async_copy(second, kept.at[1], in_sems.at[1]),
        pltpu.make_async_copy(green, tensor, in_sems.at[2]),
    ]
    for fetch in fetches:
        fetch.start()

    def store(start, block):
        kept[2, 0, :, start : start + 128] = block[:y_local]
        kept[2, 1, :, start : start + 128] = block[y_local:]

    x_steps(devices, x_local, y_local, count_gl, my_z, twist, table, data, *scratch, store)
    for fetch in fetches:
        fetch.wait()
    sends = []
    for piece in range(pieces):

        @pl.loop(0, y_local // 8)
        def _(step):
            rows = pl.ds(pl.multiple_of(step * 8, 8), 8)
            columns = pl.ds(piece * width, width)
            waves = [(kept[c, 0, rows, columns], kept[c, 1, rows, columns]) for c in range(3)]
            sums = [[None, None] for _ in range(3)]
            for entry in range(6):
                green_real = tensor[0, entry, rows, columns]
                green_imag = tensor[1, entry, rows, columns]
                for row in range(3):
                    for col in range(3):
                        if pair_index[row][col] != entry:
                            continue
                        real, imag = waves[col]
                        real_term = green_real * real - green_imag * imag
                        imag_term = green_real * imag + green_imag * real
                        old = sums[row]
                        sums[row] = [
                            real_term if old[0] is None else old[0] + real_term,
                            imag_term if old[1] is None else old[1] + imag_term,
                        ]
            for row in range(3):
                made[piece, 0, row, rows, :] = sums[row][0]
                made[piece, 1, row, rows, :] = sums[row][1]

        send = pltpu.make_async_copy(
            made.at[piece],
            out.at[:, :, :, pl.ds(piece * width, width)],
            out_sems.at[piece],
        )
        send.start()
        sends.append(send)
    for send in sends:
        send.wait()


def x_tables(devices, x_local, y_cells):
    x_cells = devices * x_local
    fine = angles(x_local, x_local, x_local)
    scale = 1.0 / math.sqrt(x_cells * y_cells)
    table = np.concatenate([np.cos(fine), np.sin(fine)], axis=1) * scale
    angle = angles(devices, x_local, x_cells)
    cos_a, sin_a = np.cos(angle), np.sin(angle)
    twist = np.stack(
        [np.concatenate([cos_a, cos_a], axis=1), np.concatenate([sin_a, -sin_a], axis=1)]
    )
    return jnp.asarray(twist.astype(np.float32)), jnp.asarray(table.astype(np.float32))


def x_scratch(devices, x_local, y_local):
    return [
        pltpu.VMEM((devices, y_local, 2 * x_local), jnp.float32),
        pltpu.VMEM((devices, 2 * y_local, 2 * x_local), jnp.float32),
        pltpu.VMEM((devices * x_local, 2 * y_local), jnp.float32),
    ]


def x_waves(my_z, data, devices, x_local, y_local, y_cells, count_gl):
    x_cells = devices * x_local
    return pl.pallas_call(
        functools.partial(x_kernel, devices, x_local, y_local, count_gl),
        out_shape=jax.ShapeDtypeStruct((2, y_local, x_cells), jnp.float32),
        in_specs=[pl.BlockSpec(memory_space=pltpu.SMEM)]
        + [pl.BlockSpec(memory_space=pltpu.VMEM)] * 6,
        out_specs=pl.BlockSpec(memory_space=pltpu.VMEM),
        scratch_shapes=x_scratch(devices, x_local, y_local),
        compiler_params=params(24),
        cost_estimate=cost(x_cells * y_local * x_local * 24, x_cells * y_local * 16),
    )(my_z, *x_tables(devices, x_local, y_cells), *data)


def last_waves(my_z, data, green, first, second, devices, x_local, y_local, y_cells, count_gl):
    x_cells = devices * x_local
    pieces = 8
    return pl.pallas_call(
        functools.partial(last_kernel, devices, x_local, y_local, count_gl),
        out_shape=jax.ShapeDtypeStruct((2, 3, y_local, x_cells), jnp.float32),
        in_specs=[pl.BlockSpec(memory_space=pltpu.SMEM)]
        + [pl.BlockSpec(memory_space=pltpu.VMEM)] * 6
        + [pl.BlockSpec(memory_space=pl.ANY)] * 3,
        out_specs=pl.BlockSpec(memory_space=pl.ANY),
        scratch_shapes=x_scratch(devices, x_local, y_local)
        + [
            pltpu.VMEM((2, 6, y_local, x_cells), jnp.float32),
            pltpu.VMEM((3, 2, y_local, x_cells), jnp.float32),
            pltpu.VMEM((pieces, 2, 3, y_local, x_cells // pieces), jnp.float32),
            pltpu.SemaphoreType.DMA((3,)),
            pltpu.SemaphoreType.DMA((pieces,)),
        ],
        compiler_params=params(40),
        cost_estimate=cost(x_cells * y_local * (x_local * 24 + 72), x_cells * y_local * 96),
    )(my_z, *x_tables(devices, x_local, y_cells), *data, green, first, second)


def along_z(arrays):
    made = [arrays[0]]
    for across in range(1, 4):
        pairs = [(z, z ^ across) for z in range(4)]
        made.append(lax.ppermute(arrays[across], "gz", pairs))
    return made


def in_plane(data):
    return lax.all_to_all(data, ("gx", "gl"), split_axis=0, concat_axis=0, tiled=True)


def per_device(tiles, tile_owner, tile_slot, tile_count, green):
    count_gl = lax.axis_size("gl")
    devices = lax.axis_size("gx") * 4 * count_gl
    tile_total, tile_len = tiles.shape[2], tiles.shape[3]
    planes, y_local, x_cells = green.shape[2:]
    y_cells = y_local * devices
    x_local = x_cells // devices
    blocks = y_cells // tile_len
    per_owner = max(2, 2 * tile_total // devices)
    assert planes == 1 and tile_len == 128
    my_z = lax.axis_index("gz").reshape(1).astype(jnp.int32)
    owner_row, slot_row = tile_owner.reshape(1, tile_total), tile_slot.reshape(1, tile_total)
    green = green.reshape(2, 6, y_local, x_cells)
    sizes = (devices, x_local, y_local, y_cells, count_gl)
    lists = (owner_row, slot_row, tile_count, my_z)
    after, fetched = my_z, []
    for comp in range(3):
        packed = pack(tiles, comp, *lists, after, devices, count_gl, per_owner)
        after = packed[0]
        fetched.append(along_z(packed))

    def place(comp):
        ready = slab_waves(
            my_z, slots, arrived[comp], devices, x_local, blocks, count_gl, per_owner
        )
        return in_plane(ready.reshape(devices // 4, 4, y_local, 2 * x_local))

    def spread(data):
        return along_z([data] + [data[:, across] for across in range(1, 4)])

    arrived = [in_plane(stack(fetched[0], after))]
    arrived.append(in_plane(stack(fetched[1], arrived[0])))
    slots = arrived[0][:, :, 2 * per_owner, :per_owner]
    slots = slots.reshape(1, devices * per_owner).astype(jnp.int32)
    halfway = [place(0)]
    arrived.append(in_plane(stack(fetched[2], halfway[0])))
    halfway.append(place(1))
    halfway.append(place(2))
    moved = [spread(one) for one in halfway]
    waves = [x_waves(my_z, one, *sizes) for one in moved[:2]]
    mixed = last_waves(my_z, moved[2], green, *waves, *sizes)
    return mixed.reshape(2, 3, planes, y_local, x_cells)


def solution(mesh):
    count_gx, count_gy = mesh.devices.shape
    fine_mesh = jax.sharding.Mesh(
        mesh.devices.reshape(count_gx, 4, count_gy // 4), ("gx", "gz", "gl")
    )
    every = ("gx", "gz", "gl")
    in_specs = (
        P(None, None, every, None),
        P(every, None),
        P(every),
        P(every),
        P(None, None, None, every, None),
    )
    out_specs = P(None, None, None, every, None)
    return jax.shard_map(
        per_device, mesh=fine_mesh, in_specs=in_specs, out_specs=out_specs, check_vma=False
    )
```

```python
import functools
import math

import jax
import jax.numpy as jnp
import ml_dtypes
import numpy as np
from jax import lax
from jax.experimental import pallas as pl
from jax.experimental.pallas import tpu as pltpu
from jax.sharding import PartitionSpec as P

pair_index = ((0, 3, 4), (3, 1, 5), (4, 5, 2))
by_rows = (((1,), (1,)), ((), ()))


def params(mebibytes):
    return pltpu.CompilerParams(vmem_limit_bytes=mebibytes * 1024 * 1024)


def cost(flops, moved):
    return pl.CostEstimate(flops=flops, bytes_accessed=moved, transcendentals=0)


def angles(rows, columns, length):
    products = np.outer(np.arange(rows), np.arange(columns)) % length
    return 2.0 * math.pi / length * products


def halves(table):
    wide = np.asarray(table, np.float32)
    high = wide.astype(ml_dtypes.bfloat16)
    low = (wide - high.astype(np.float32)).astype(ml_dtypes.bfloat16)
    return jnp.asarray(high), jnp.asarray(low)


def split_two(data):
    high = data.astype(jnp.bfloat16)
    return high, (data - high.astype(jnp.float32)).astype(jnp.bfloat16)


def split_three(data):
    high = data.astype(jnp.bfloat16)
    rest = data - high.astype(jnp.float32)
    middle = rest.astype(jnp.bfloat16)
    return high, middle, (rest - middle.astype(jnp.float32)).astype(jnp.bfloat16)


def dot_rows(left, right):
    return lax.dot_general(left, right, by_rows, preferred_element_type=jnp.float32)


def dot_rows_split(table, data):
    rows, depth = table.shape
    table_high, table_low = split_two(table)
    high, low = split_two(data)
    if depth > 128:
        both = dot_rows(jnp.concatenate([table_high, table_low]), high)
        return both[:rows] + both[rows:] + dot_rows(table_high, low)
    left = jnp.concatenate(
        [
            jnp.concatenate([table_high, table_high], axis=1),
            jnp.concatenate([table_low, jnp.zeros_like(table_low)], axis=1),
        ]
    )
    both = dot_rows(left, jnp.concatenate([high, low], axis=1))
    return both[:rows] + both[rows:]


def flat_fft(values, times):
    length = len(values)
    if length == 1:
        return values
    even = flat_fft(values[0::2], times)
    odd = flat_fft(values[1::2], times)
    lower, upper = [], []
    for k in range(length // 2):
        turned = times(odd[k], k, length)
        lower.append(jax.tree.map(lambda a, b: a + b, even[k], turned))
        upper.append(jax.tree.map(lambda a, b: a - b, even[k], turned))
    return lower + upper


def times_pair(value, k, length):
    real, imag = value
    if k == 0:
        return value
    if 4 * k == length:
        return (imag, -real)
    cos_k = math.cos(2.0 * math.pi * k / length)
    sin_k = math.sin(2.0 * math.pi * k / length)
    return (real * cos_k + imag * sin_k, imag * cos_k - real * sin_k)


def pack_kernel(devices, per_owner, count, me, owner_row, slot_row, tiles, *out):
    listed = owner_row.shape[1]
    comps = tiles.shape[1]
    live_count = count[0]
    owners = owner_row[...]
    live = lax.broadcasted_iota(jnp.int32, (1, listed), 1) < live_count
    place = jnp.where(live, owners ^ me[0], -1)
    named = jnp.where(
        lax.broadcasted_iota(jnp.int32, (devices, listed), 0) == place, 1.0, 0.0
    )
    sender = lax.broadcasted_iota(jnp.int32, (listed, listed), 0)
    reader = lax.broadcasted_iota(jnp.int32, (listed, listed), 1)
    before = jnp.where(sender < reader, 1.0, 0.0).astype(jnp.bfloat16)
    counted = jnp.dot(named.astype(jnp.bfloat16), before, preferred_element_type=jnp.float32)
    rank = jnp.sum(counted * named, axis=0, keepdims=True).astype(jnp.int32)
    target = jnp.where(live, place * per_owner + rank, -1)
    places = lax.broadcasted_iota(jnp.int32, (devices * per_owner, listed), 0)
    chosen = jnp.where(places == target, 1.0, 0.0).astype(jnp.bfloat16)
    for comp in range(comps):
        parts = [part for r in range(2) for part in split_three(tiles[r, comp])]
        got = jnp.dot(
            chosen, jnp.concatenate(parts, axis=1), preferred_element_type=jnp.float32
        )
        for r in range(2):
            one = got[:, 384 * r : 384 * r + 384]
            whole = (one[:, :128] + one[:, 128:256]) + one[:, 256:]
            start = (2 * comp + r) * per_owner
            for part in range(devices):
                out[part][start : start + per_owner, :] = whole[part * per_owner :][:per_owner]
    stated = slot_row[...] + 1
    lane = rank + (place & (128 // per_owner - 1)) * per_owner
    lane_at = lax.broadcasted_iota(jnp.int32, (128, listed), 0)
    ranked = jnp.where(lane_at == lane, 1.0, 0.0).astype(jnp.bfloat16)
    coarse = (named * (stated >> 5).astype(jnp.float32)).astype(jnp.bfloat16)
    fine = (named * (stated & 31).astype(jnp.float32)).astype(jnp.bfloat16)
    slots = 32.0 * dot_rows(coarse, ranked) + dot_rows(fine, ranked)
    for part in range(devices):
        out[part][2 * comps * per_owner :, :] = jnp.broadcast_to(slots[part : part + 1], (8, 128))


def pack(tiles, owner_row, slot_row, count, me, devices, per_owner):
    comps, listed = tiles.shape[1:3]
    rows = 2 * comps * per_owner + 8
    return pl.pallas_call(
        functools.partial(pack_kernel, devices, per_owner),
        out_shape=[jax.ShapeDtypeStruct((rows, 128), jnp.float32)] * devices,
        in_specs=[pl.BlockSpec(memory_space=pltpu.SMEM)] * 2
        + [pl.BlockSpec(memory_space=pltpu.VMEM)] * 3,
        out_specs=[pl.BlockSpec(memory_space=pltpu.VMEM)] * devices,
        compiler_params=params(24),
        cost_estimate=cost(
            devices * per_owner * listed * 768 * 2 * comps, devices * rows * 1024
        ),
    )(count, me, owner_row, slot_row, tiles)


def slab_kernel(comps, x_local, blocks, per_owner, me, table, twist, *refs):
    devices, kept = table.shape[:2]
    data, out = refs[:devices], refs[devices : 2 * devices]
    slab, turned, ordered = refs[2 * devices :]
    entries = devices * per_owner
    y_local = kept * blocks
    wide = 2 * x_local
    shift = blocks.bit_length() - 1
    every = 128 // per_owner
    slots = []
    for start in range(0, devices, every):
        slots.append(sum([one[one.shape[0] - 8 :, :][:1] for one in data[start : start + every]]))
    slot = jnp.concatenate(slots, axis=1).astype(jnp.int32) - 1
    landing = jnp.where(slot >= 0, (slot & (blocks - 1)) * x_local + (slot >> shift), -1)
    for place in range(devices):
        ordered[place * kept : (place + 1) * kept, :] = table[me[0] ^ place]
    for index, comp in enumerate(comps):
        parts = []
        for r in range(2):
            start = (2 * comp + r) * per_owner
            arrived = jnp.concatenate([one[start : start + per_owner, :] for one in data])
            parts.extend(split_two(arrived))
        parts = jnp.concatenate(parts, axis=1)
        for start in range(0, blocks * x_local, 256):
            place = start + lax.broadcasted_iota(jnp.int32, (256, entries), 0)
            chosen = jnp.where(place == landing, 1.0, 0.0).astype(jnp.bfloat16)
            got = jnp.dot(chosen, parts, preferred_element_type=jnp.float32)
            for r in range(2):
                slab[r, start : start + 256, :] = (
                    got[:, 256 * r : 256 * r + 128] + got[:, 256 * r + 128 : 256 * r + 256]
                )

        @pl.loop(0, x_local // 8)
        def _(step):
            at = pl.multiple_of(step * 8, 8)
            values = [
                tuple(slab[r, pl.ds(t * x_local + at, 8), :] for r in range(2))
                for t in range(blocks)
            ]
            waves = flat_fft(values, times_pair)
            for k in range(blocks):
                real, imag = waves[k]
                cos_k, sin_k = twist[0, k : k + 1, :], twist[1, k : k + 1, :]
                new_real = real * cos_k + imag * sin_k
                new_imag = imag * cos_k - real * sin_k
                first = pl.ds(k * wide + at, 8)
                second = pl.ds(k * wide + x_local + at, 8)
                turned[first, :128] = new_real
                turned[first, 128:] = new_imag
                turned[second, :128] = new_imag
                turned[second, 128:] = -new_real

        together = 4
        for start in range(0, blocks, together):
            moved = dot_rows_split(
                ordered[...], turned[start * wide : (start + together) * wide, :]
            )
            for k in range(start, start + together):
                one = moved[:, (k - start) * wide : (k - start + 1) * wide]
                for part in range(devices):
                    rows = pl.ds(index * y_local + k, kept, stride=blocks)
                    out[part][rows, :] = one[part * kept : (part + 1) * kept]


def slab_waves(me, comps, data, x_local, blocks, per_owner):
    devices = len(data)
    y_cells = blocks * 128
    fine = angles(128, 128, 128)
    table = np.concatenate([np.cos(fine), np.sin(fine)], axis=1).astype(np.float32)
    table = table.reshape(devices, 128 // devices, 256)
    twist_angle = angles(blocks, 128, y_cells)
    twist = np.stack([np.cos(twist_angle), np.sin(twist_angle)]).astype(np.float32)
    entries = devices * per_owner
    made = jax.ShapeDtypeStruct((len(comps) * y_cells // devices, 2 * x_local), jnp.float32)
    return pl.pallas_call(
        functools.partial(slab_kernel, comps, x_local, blocks, per_owner),
        out_shape=[made] * devices,
        in_specs=[pl.BlockSpec(memory_space=pltpu.SMEM)]
        + [pl.BlockSpec(memory_space=pltpu.VMEM)] * (2 + devices),
        out_specs=[pl.BlockSpec(memory_space=pltpu.VMEM)] * devices,
        scratch_shapes=[
            pltpu.VMEM((2, blocks * x_local, 128), jnp.float32),
            pltpu.VMEM((blocks * 2 * x_local, 256), jnp.float32),
            pltpu.VMEM((128, 256), jnp.float32),
        ],
        compiler_params=params(24),
        cost_estimate=cost(
            len(comps) * (blocks * x_local * entries * 1024 + y_cells * x_local * 3072),
            len(comps) * (entries * 1024 + y_cells * x_local * 8),
        ),
    )(me, jnp.asarray(table), jnp.asarray(twist), *data)


def swap_parts(value, x_local):
    if 2 * x_local == 128:
        return pltpu.roll(value, x_local, 1)
    return jnp.concatenate([value[:, x_local:], value[:, :x_local]], axis=1)


def x_steps(
    devices, x_local, y_local, index, me, twist, table, data, placed, turned, columns, store
):
    wide = 2 * x_local
    lane = lax.broadcasted_iota(jnp.int32, (1, wide), 1)
    sign = jnp.where(lane < x_local, 1.0, -1.0)
    for place in range(devices):
        placed[me[0] ^ place] = data[place][index * y_local : (index + 1) * y_local, :]

    def times(value, k, length):
        if k == 0:
            return value
        swapped = swap_parts(value, x_local) * sign
        if 4 * k == length:
            return swapped
        cos_k = math.cos(2.0 * math.pi * k / length)
        sin_k = math.sin(2.0 * math.pi * k / length)
        return value * cos_k + swapped * sin_k

    @pl.loop(0, y_local // 8)
    def _(step):
        at = pl.multiple_of(step * 8, 8)
        values = [placed[o, pl.ds(at, 8), :] for o in range(devices)]
        waves = flat_fft(values, times)
        for k in range(devices):
            swapped = swap_parts(waves[k], x_local)
            new = waves[k] * twist[0, k : k + 1, :] + swapped * twist[1, k : k + 1, :]
            turned[k, pl.ds(at, 8), :] = new
            turned[k, pl.ds(y_local + at, 8), :] = swap_parts(new, x_local) * sign

    together = 4
    for start in range(0, devices, together):
        stacked = turned[start : start + together].reshape(together * 2 * y_local, wide)
        moved = dot_rows_split(table[...], stacked)
        for k in range(start, start + together):
            columns[pl.ds(k, x_local, stride=devices), :] = moved[
                :, (k - start) * 2 * y_local : (k - start + 1) * 2 * y_local
            ]
    for start in range(0, devices * x_local, 128):
        store(start, columns[start : start + 128, :].T)


def x_kernel(devices, x_local, y_local, index, me, twist, table, *refs):
    data, out, scratch = refs[:devices], refs[devices], refs[devices + 1 :]

    def store(start, block):
        out[0, :, start : start + 128] = block[:y_local]
        out[1, :, start : start + 128] = block[y_local:]

    x_steps(devices, x_local, y_local, index, me, twist, table, data, *scratch, store)


def last_kernel(devices, x_local, y_local, index, me, twist, table, *refs):
    data, (green, first, second, out) = refs[:devices], refs[devices : devices + 4]
    scratch, (tensor, kept, made, in_sems, out_sems) = refs[devices + 4 :][:3], refs[devices + 7 :]
    x_cells = devices * x_local
    pieces = made.shape[0]
    width = x_cells // pieces
    fetches = [
        pltpu.make_async_copy(first, kept.at[0], in_sems.at[0]),
        pltpu.make_async_copy(second, kept.at[1], in_sems.at[1]),
        pltpu.make_async_copy(green, tensor, in_sems.at[2]),
    ]
    for fetch in fetches:
        fetch.start()

    def store(start, block):
        kept[2, 0, :, start : start + 128] = block[:y_local]
        kept[2, 1, :, start : start + 128] = block[y_local:]

    x_steps(devices, x_local, y_local, index, me, twist, table, data, *scratch, store)
    for fetch in fetches:
        fetch.wait()
    sends = []
    for piece in range(pieces):

        @pl.loop(0, y_local // 8)
        def _(step):
            rows = pl.ds(pl.multiple_of(step * 8, 8), 8)
            columns = pl.ds(piece * width, width)
            waves = [(kept[c, 0, rows, columns], kept[c, 1, rows, columns]) for c in range(3)]
            sums = [[None, None] for _ in range(3)]
            for entry in range(6):
                green_real = tensor[0, entry, rows, columns]
                green_imag = tensor[1, entry, rows, columns]
                for row in range(3):
                    for col in range(3):
                        if pair_index[row][col] != entry:
                            continue
                        real, imag = waves[col]
                        real_term = green_real * real - green_imag * imag
                        imag_term = green_real * imag + green_imag * real
                        old = sums[row]
                        sums[row] = [
                            real_term if old[0] is None else old[0] + real_term,
                            imag_term if old[1] is None else old[1] + imag_term,
                        ]
            for row in range(3):
                made[piece, 0, row, rows, :] = sums[row][0]
                made[piece, 1, row, rows, :] = sums[row][1]

        send = pltpu.make_async_copy(
            made.at[piece],
            out.at[:, :, :, pl.ds(piece * width, width)],
            out_sems.at[piece],
        )
        send.start()
        sends.append(send)
    for send in sends:
        send.wait()


def x_tables(devices, x_local, y_cells):
    x_cells = devices * x_local
    fine = angles(x_local, x_local, x_local)
    scale = 1.0 / math.sqrt(x_cells * y_cells)
    table = np.concatenate([np.cos(fine), np.sin(fine)], axis=1) * scale
    angle = angles(devices, x_local, x_cells)
    cos_a, sin_a = np.cos(angle), np.sin(angle)
    twist = np.stack(
        [np.concatenate([cos_a, cos_a], axis=1), np.concatenate([sin_a, -sin_a], axis=1)]
    )
    return jnp.asarray(twist.astype(np.float32)), jnp.asarray(table.astype(np.float32))


def x_scratch(devices, x_local, y_local):
    return [
        pltpu.VMEM((devices, y_local, 2 * x_local), jnp.float32),
        pltpu.VMEM((devices, 2 * y_local, 2 * x_local), jnp.float32),
        pltpu.VMEM((devices * x_local, 2 * y_local), jnp.float32),
    ]


def x_waves(me, index, data, devices, x_local, y_local, y_cells):
    x_cells = devices * x_local
    return pl.pallas_call(
        functools.partial(x_kernel, devices, x_local, y_local, index),
        out_shape=jax.ShapeDtypeStruct((2, y_local, x_cells), jnp.float32),
        in_specs=[pl.BlockSpec(memory_space=pltpu.SMEM)]
        + [pl.BlockSpec(memory_space=pltpu.VMEM)] * (2 + devices),
        out_specs=pl.BlockSpec(memory_space=pltpu.VMEM),
        scratch_shapes=x_scratch(devices, x_local, y_local),
        compiler_params=params(24),
        cost_estimate=cost(x_cells * y_local * x_local * 24, x_cells * y_local * 16),
    )(me, *x_tables(devices, x_local, y_cells), *data)


def last_waves(me, index, data, green, first, second, devices, x_local, y_local, y_cells):
    x_cells = devices * x_local
    pieces = 8
    return pl.pallas_call(
        functools.partial(last_kernel, devices, x_local, y_local, index),
        out_shape=jax.ShapeDtypeStruct((2, 3, y_local, x_cells), jnp.float32),
        in_specs=[pl.BlockSpec(memory_space=pltpu.SMEM)]
        + [pl.BlockSpec(memory_space=pltpu.VMEM)] * (2 + devices)
        + [pl.BlockSpec(memory_space=pl.ANY)] * 3,
        out_specs=pl.BlockSpec(memory_space=pl.ANY),
        scratch_shapes=x_scratch(devices, x_local, y_local)
        + [
            pltpu.VMEM((2, 6, y_local, x_cells), jnp.float32),
            pltpu.VMEM((3, 2, y_local, x_cells), jnp.float32),
            pltpu.VMEM((pieces, 2, 3, y_local, x_cells // pieces), jnp.float32),
            pltpu.SemaphoreType.DMA((3,)),
            pltpu.SemaphoreType.DMA((pieces,)),
        ],
        compiler_params=params(40),
        cost_estimate=cost(x_cells * y_local * (x_local * 24 + 72), x_cells * y_local * 96),
    )(me, *x_tables(devices, x_local, y_cells), *data, green, first, second)


def exchange(blocks):
    devices = len(blocks)
    far = [m for m in range(devices) if m & 4]
    near = [m for m in range(1, devices) if not m & 4]
    arrived = [blocks[0]] + [None] * (devices - 1)
    for pair in zip(far, near + [None]):
        for m in pair:
            if m is not None:
                moves = [(d, d ^ m) for d in range(devices)]
                arrived[m] = lax.ppermute(blocks[m], ("gx", "gy"), moves)
    return arrived


def per_device(tiles, tile_owner, tile_slot, tile_count, green):
    devices = lax.axis_size("gx") * lax.axis_size("gy")
    tile_total, tile_len = tiles.shape[2], tiles.shape[3]
    planes, y_local, x_cells = green.shape[2:]
    y_cells = y_local * devices
    x_local = x_cells // devices
    blocks = y_cells // tile_len
    per_owner = max(2, 2 * tile_total // devices)
    assert planes == 1 and tile_len == 128
    me = (lax.axis_index("gx") * lax.axis_size("gy") + lax.axis_index("gy")).reshape(1)
    me = me.astype(jnp.int32)
    owner_row, slot_row = tile_owner.reshape(1, tile_total), tile_slot.reshape(1, tile_total)
    green = green.reshape(2, 6, y_local, x_cells)
    arrived = exchange(pack(tiles, owner_row, slot_row, tile_count, me, devices, per_owner))
    moved = {}
    for comps in ((0,), (1, 2)):
        got = exchange(slab_waves(me, comps, arrived, x_local, blocks, per_owner))
        moved.update({comp: (me, i, got) for i, comp in enumerate(comps)})
    sizes = (devices, x_local, y_local, y_cells)
    waves = [x_waves(*moved[comp], *sizes) for comp in range(2)]
    mixed = last_waves(*moved[2], green, *waves, *sizes)
    return mixed.reshape(2, 3, planes, y_local, x_cells)


def solution(mesh):
    in_specs = (
        P(None, None, ("gx", "gy"), None),
        P(("gx", "gy"), None),
        P(("gx", "gy")),
        P(("gx", "gy")),
        P(None, None, None, ("gx", "gy"), None),
    )
    out_specs = P(None, None, None, ("gx", "gy"), None)
    return jax.shard_map(
        per_device, mesh=mesh, in_specs=in_specs, out_specs=out_specs, check_vma=False
    )
```

```python
import functools
import math

import jax
import jax.numpy as jnp
import ml_dtypes
import numpy as np
from jax import lax
from jax.experimental import pallas as pl
from jax.experimental.pallas import tpu as pltpu
from jax.sharding import PartitionSpec as P

pair_index = ((0, 3, 4), (3, 1, 5), (4, 5, 2))
by_rows = (((1,), (1,)), ((), ()))


def params(mebibytes):
    return pltpu.CompilerParams(vmem_limit_bytes=mebibytes * 1024 * 1024)


def cost(flops, moved):
    return pl.CostEstimate(flops=flops, bytes_accessed=moved, transcendentals=0)


def angles(rows, columns, length):
    products = np.outer(np.arange(rows), np.arange(columns)) % length
    return 2.0 * math.pi / length * products


def halves(table):
    wide = np.asarray(table, np.float32)
    high = wide.astype(ml_dtypes.bfloat16)
    low = (wide - high.astype(np.float32)).astype(ml_dtypes.bfloat16)
    return jnp.asarray(high), jnp.asarray(low)


def split_two(data):
    high = data.astype(jnp.bfloat16)
    return high, (data - high.astype(jnp.float32)).astype(jnp.bfloat16)


def split_three(data):
    high = data.astype(jnp.bfloat16)
    rest = data - high.astype(jnp.float32)
    middle = rest.astype(jnp.bfloat16)
    return high, middle, (rest - middle.astype(jnp.float32)).astype(jnp.bfloat16)


def dot_rows(left, right):
    return lax.dot_general(left, right, by_rows, preferred_element_type=jnp.float32)


def dot_rows_split(table, data):
    rows, depth = table.shape
    table_high, table_low = split_two(table)
    high, low = split_two(data)
    if depth > 128:
        both = dot_rows(jnp.concatenate([table_high, table_low]), high)
        return both[:rows] + both[rows:] + dot_rows(table_high, low)
    left = jnp.concatenate(
        [
            jnp.concatenate([table_high, table_high], axis=1),
            jnp.concatenate([table_low, jnp.zeros_like(table_low)], axis=1),
        ]
    )
    both = dot_rows(left, jnp.concatenate([high, low], axis=1))
    return both[:rows] + both[rows:]


def flat_fft(values, times):
    length = len(values)
    if length == 1:
        return values
    even = flat_fft(values[0::2], times)
    odd = flat_fft(values[1::2], times)
    lower, upper = [], []
    for k in range(length // 2):
        turned = times(odd[k], k, length)
        lower.append(jax.tree.map(lambda a, b: a + b, even[k], turned))
        upper.append(jax.tree.map(lambda a, b: a - b, even[k], turned))
    return lower + upper


def times_pair(value, k, length):
    real, imag = value
    if k == 0:
        return value
    if 4 * k == length:
        return (imag, -real)
    cos_k = math.cos(2.0 * math.pi * k / length)
    sin_k = math.sin(2.0 * math.pi * k / length)
    return (real * cos_k + imag * sin_k, imag * cos_k - real * sin_k)


def pack_kernel(
    devices, per_owner, comps, with_slots, count, me, owner_row, slot_row, tiles, *refs
):
    out, held, sems = refs[-3:]
    listed = owner_row.shape[1]
    fetches = [
        pltpu.make_async_copy(tiles.at[:, comp], held.at[i], sems.at[i])
        for i, comp in enumerate(comps)
    ]
    for fetch in fetches:
        fetch.start()
    live_count = count[0]
    owners = owner_row[...]
    live = lax.broadcasted_iota(jnp.int32, (1, listed), 1) < live_count
    owner_at = lax.broadcasted_iota(jnp.int32, (devices, listed), 0)
    named = jnp.where((owner_at == owners) & live, 1.0, 0.0)
    sender = lax.broadcasted_iota(jnp.int32, (listed, listed), 0)
    reader = lax.broadcasted_iota(jnp.int32, (listed, listed), 1)
    before = jnp.where(sender < reader, 1.0, 0.0).astype(jnp.bfloat16)
    counted = jnp.dot(named.astype(jnp.bfloat16), before, preferred_element_type=jnp.float32)
    rank = jnp.sum(counted * named, axis=0, keepdims=True).astype(jnp.int32)
    target = jnp.where(live, owners * per_owner + rank, -1)
    places = lax.broadcasted_iota(jnp.int32, (devices * per_owner, listed), 0)
    chosen = jnp.where(places == target, 1.0, 0.0).astype(jnp.bfloat16)
    if with_slots:
        stated = slot_row[...] + 1
        lane = rank + (me[0] & (128 // per_owner - 1)) * per_owner
        lane_at = lax.broadcasted_iota(jnp.int32, (128, listed), 0)
        ranked = jnp.where(lane_at == lane, 1.0, 0.0).astype(jnp.bfloat16)
        coarse = (named * (stated >> 5).astype(jnp.float32)).astype(jnp.bfloat16)
        fine = (named * (stated & 31).astype(jnp.float32)).astype(jnp.bfloat16)
        slots = 32.0 * dot_rows(coarse, ranked) + dot_rows(fine, ranked)
        out[:, 2 * len(comps) * per_owner :, :] = jnp.broadcast_to(
            slots[:, None, :], (devices, 8, 128)
        )
    for i, fetch in enumerate(fetches):
        fetch.wait()
        parts = [part for r in range(2) for part in split_three(held[i, r])]
        got = jnp.dot(
            chosen, jnp.concatenate(parts, axis=1), preferred_element_type=jnp.float32
        )
        for r in range(2):
            one = got[:, 384 * r : 384 * r + 384]
            whole = (one[:, :128] + one[:, 128:256]) + one[:, 256:]
            start = (2 * i + r) * per_owner
            out[:, start : start + per_owner, :] = whole.reshape(devices, per_owner, 128)


def pack(tiles, comps, owner_row, slot_row, count, me, after, devices, per_owner):
    listed = tiles.shape[2]
    with_slots = after is None
    rows = 2 * len(comps) * per_owner + (8 if with_slots else 0)
    extra = () if with_slots else (after,)
    return pl.pallas_call(
        functools.partial(pack_kernel, devices, per_owner, comps, with_slots),
        out_shape=jax.ShapeDtypeStruct((devices, rows, 128), jnp.float32),
        in_specs=[pl.BlockSpec(memory_space=pltpu.SMEM)] * 2
        + [pl.BlockSpec(memory_space=pltpu.VMEM)] * 2
        + [pl.BlockSpec(memory_space=pl.ANY)] * (1 + len(extra)),
        out_specs=pl.BlockSpec(memory_space=pltpu.VMEM),
        scratch_shapes=[
            pltpu.VMEM((len(comps), 2, listed, 128), jnp.float32),
            pltpu.SemaphoreType.DMA((len(comps),)),
        ],
        compiler_params=params(24),
        cost_estimate=cost(
            devices * per_owner * listed * 768 * 2 * len(comps), devices * rows * 1024
        ),
    )(count, me, owner_row, slot_row, tiles, *extra)


def slab_kernel(
    comps, places, x_local, blocks, per_owner, slots, table, twist, data, out, slab, turned
):
    devices = data.shape[0]
    entries = devices * per_owner
    y_local = blocks * 128 // devices
    wide = 2 * x_local
    shift = blocks.bit_length() - 1
    every = 128 // per_owner
    stated = [
        sum([slots[o, :1] for o in range(start, start + every)])
        for start in range(0, devices, every)
    ]
    slot = jnp.concatenate(stated, axis=1).astype(jnp.int32) - 1
    landing = jnp.where(slot >= 0, (slot & (blocks - 1)) * x_local + (slot >> shift), -1)
    for index, comp in enumerate(comps):
        parts = []
        for r in range(2):
            start = (2 * places[index] + r) * per_owner
            parts.extend(split_two(data[:, start : start + per_owner, :].reshape(entries, 128)))
        parts = jnp.concatenate(parts, axis=1)
        for start in range(0, blocks * x_local, 256):
            place = start + lax.broadcasted_iota(jnp.int32, (256, entries), 0)
            chosen = jnp.where(place == landing, 1.0, 0.0).astype(jnp.bfloat16)
            got = jnp.dot(chosen, parts, preferred_element_type=jnp.float32)
            for r in range(2):
                slab[r, start : start + 256, :] = (
                    got[:, 256 * r : 256 * r + 128] + got[:, 256 * r + 128 : 256 * r + 256]
                )

        @pl.loop(0, x_local // 8)
        def _(step):
            at = pl.multiple_of(step * 8, 8)
            values = [
                tuple(slab[r, pl.ds(t * x_local + at, 8), :] for r in range(2))
                for t in range(blocks)
            ]
            waves = flat_fft(values, times_pair)
            for k in range(blocks):
                real, imag = waves[k]
                cos_k, sin_k = twist[0, k : k + 1, :], twist[1, k : k + 1, :]
                new_real = real * cos_k + imag * sin_k
                new_imag = imag * cos_k - real * sin_k
                first = pl.ds(k * wide + at, 8)
                second = pl.ds(k * wide + x_local + at, 8)
                turned[first, :128] = new_real
                turned[first, 128:] = new_imag
                turned[second, :128] = new_imag
                turned[second, 128:] = -new_real

        together = 4
        for start in range(0, blocks, together):
            moved = dot_rows_split(
                table[...], turned[start * wide : (start + together) * wide, :]
            )
            for k in range(start, start + together):
                one = moved[:, (k - start) * wide : (k - start + 1) * wide]
                if len(comps) == 1:
                    out[pl.ds(k, 128, stride=blocks), :] = one
                else:
                    kept = 128 // devices
                    for o in range(devices):
                        rows = pl.ds((o * len(comps) + index) * y_local + k, kept, stride=blocks)
                        out[rows, :] = one[o * kept : (o + 1) * kept]


def slab_waves(slots, comps, places, data, x_local, blocks, per_owner):
    devices = data.shape[0]
    y_cells = blocks * 128
    fine = angles(128, 128, 128)
    table = np.concatenate([np.cos(fine), np.sin(fine)], axis=1).astype(np.float32)
    twist_angle = angles(blocks, 128, y_cells)
    twist = np.stack([np.cos(twist_angle), np.sin(twist_angle)]).astype(np.float32)
    entries = devices * per_owner
    rows = len(comps) * y_cells
    made = pl.pallas_call(
        functools.partial(slab_kernel, comps, places, x_local, blocks, per_owner),
        out_shape=jax.ShapeDtypeStruct((rows, 2 * x_local), jnp.float32),
        in_specs=[pl.BlockSpec(memory_space=pltpu.VMEM)] * 4,
        out_specs=pl.BlockSpec(memory_space=pltpu.VMEM),
        scratch_shapes=[
            pltpu.VMEM((2, blocks * x_local, 128), jnp.float32),
            pltpu.VMEM((blocks * 2 * x_local, 256), jnp.float32),
        ],
        compiler_params=params(24),
        cost_estimate=cost(
            len(comps) * (blocks * x_local * entries * 1024 + y_cells * x_local * 3072),
            len(comps) * (entries * 1024 + y_cells * x_local * 8),
        ),
    )(slots, jnp.asarray(table), jnp.asarray(twist), data)
    return made.reshape(devices, rows // devices, 2 * x_local)


def swap_parts(value, x_local):
    if 2 * x_local == 128:
        return pltpu.roll(value, x_local, 1)
    return jnp.concatenate([value[:, x_local:], value[:, :x_local]], axis=1)


def x_steps(
    devices, x_local, y_local, index, twist, table, data, turned, columns, store
):
    wide = 2 * x_local
    lane = lax.broadcasted_iota(jnp.int32, (1, wide), 1)
    sign = jnp.where(lane < x_local, 1.0, -1.0)

    def times(value, k, length):
        if k == 0:
            return value
        swapped = swap_parts(value, x_local) * sign
        if 4 * k == length:
            return swapped
        cos_k = math.cos(2.0 * math.pi * k / length)
        sin_k = math.sin(2.0 * math.pi * k / length)
        return value * cos_k + swapped * sin_k

    @pl.loop(0, y_local // 8)
    def _(step):
        at = pl.multiple_of(step * 8, 8)
        values = [data[o, pl.ds(index * y_local + at, 8), :] for o in range(devices)]
        waves = flat_fft(values, times)
        for k in range(devices):
            swapped = swap_parts(waves[k], x_local)
            new = waves[k] * twist[0, k : k + 1, :] + swapped * twist[1, k : k + 1, :]
            turned[k, pl.ds(at, 8), :] = new
            turned[k, pl.ds(y_local + at, 8), :] = swap_parts(new, x_local) * sign

    together = 4
    for start in range(0, devices, together):
        stacked = turned[start : start + together].reshape(together * 2 * y_local, wide)
        moved = dot_rows_split(table[...], stacked)
        for k in range(start, start + together):
            columns[pl.ds(k, x_local, stride=devices), :] = moved[
                :, (k - start) * 2 * y_local : (k - start + 1) * 2 * y_local
            ]
    for start in range(0, devices * x_local, 128):
        store(start, columns[start : start + 128, :].T)


def x_kernel(devices, x_local, y_local, index, twist, table, data, *refs):
    out, scratch = refs[0], refs[1:]

    def store(start, block):
        out[0, :, start : start + 128] = block[:y_local]
        out[1, :, start : start + 128] = block[y_local:]

    x_steps(devices, x_local, y_local, index, twist, table, data, *scratch, store)


def last_kernel(devices, x_local, y_local, index, twist, table, data, *refs):
    green, first, second, out = refs[:4]
    scratch, (tensor, kept, made, in_sems, out_sems) = refs[4:6], refs[6:]
    x_cells = devices * x_local
    pieces = made.shape[0]
    width = x_cells // pieces
    fetches = [
        pltpu.make_async_copy(first, kept.at[0], in_sems.at[0]),
        pltpu.make_async_copy(second, kept.at[1], in_sems.at[1]),
        pltpu.make_async_copy(green, tensor, in_sems.at[2]),
    ]
    for fetch in fetches:
        fetch.start()

    def store(start, block):
        kept[2, 0, :, start : start + 128] = block[:y_local]
        kept[2, 1, :, start : start + 128] = block[y_local:]

    x_steps(devices, x_local, y_local, index, twist, table, data, *scratch, store)
    for fetch in fetches:
        fetch.wait()
    sends = []
    for piece in range(pieces):

        @pl.loop(0, y_local // 8)
        def _(step):
            rows = pl.ds(pl.multiple_of(step * 8, 8), 8)
            columns = pl.ds(piece * width, width)
            waves = [(kept[c, 0, rows, columns], kept[c, 1, rows, columns]) for c in range(3)]
            sums = [[None, None] for _ in range(3)]
            for entry in range(6):
                green_real = tensor[0, entry, rows, columns]
                green_imag = tensor[1, entry, rows, columns]
                for row in range(3):
                    for col in range(3):
                        if pair_index[row][col] != entry:
                            continue
                        real, imag = waves[col]
                        real_term = green_real * real - green_imag * imag
                        imag_term = green_real * imag + green_imag * real
                        old = sums[row]
                        sums[row] = [
                            real_term if old[0] is None else old[0] + real_term,
                            imag_term if old[1] is None else old[1] + imag_term,
                        ]
            for row in range(3):
                made[piece, 0, row, rows, :] = sums[row][0]
                made[piece, 1, row, rows, :] = sums[row][1]

        send = pltpu.make_async_copy(
            made.at[piece],
            out.at[:, :, :, pl.ds(piece * width, width)],
            out_sems.at[piece],
        )
        send.start()
        sends.append(send)
    for send in sends:
        send.wait()


def x_tables(devices, x_local, y_cells):
    x_cells = devices * x_local
    fine = angles(x_local, x_local, x_local)
    scale = 1.0 / math.sqrt(x_cells * y_cells)
    table = np.concatenate([np.cos(fine), np.sin(fine)], axis=1) * scale
    angle = angles(devices, x_local, x_cells)
    cos_a, sin_a = np.cos(angle), np.sin(angle)
    twist = np.stack(
        [np.concatenate([cos_a, cos_a], axis=1), np.concatenate([sin_a, -sin_a], axis=1)]
    )
    return jnp.asarray(twist.astype(np.float32)), jnp.asarray(table.astype(np.float32))


def x_scratch(devices, x_local, y_local):
    return [
        pltpu.VMEM((devices, 2 * y_local, 2 * x_local), jnp.float32),
        pltpu.VMEM((devices * x_local, 2 * y_local), jnp.float32),
    ]


def x_waves(index, data, devices, x_local, y_local, y_cells):
    x_cells = devices * x_local
    return pl.pallas_call(
        functools.partial(x_kernel, devices, x_local, y_local, index),
        out_shape=jax.ShapeDtypeStruct((2, y_local, x_cells), jnp.float32),
        in_specs=[pl.BlockSpec(memory_space=pltpu.VMEM)] * 3,
        out_specs=pl.BlockSpec(memory_space=pltpu.VMEM),
        scratch_shapes=x_scratch(devices, x_local, y_local),
        compiler_params=params(24),
        cost_estimate=cost(x_cells * y_local * x_local * 24, x_cells * y_local * 16),
    )(*x_tables(devices, x_local, y_cells), data)


def last_waves(index, data, green, first, second, devices, x_local, y_local, y_cells):
    x_cells = devices * x_local
    pieces = 8
    return pl.pallas_call(
        functools.partial(last_kernel, devices, x_local, y_local, index),
        out_shape=jax.ShapeDtypeStruct((2, 3, y_local, x_cells), jnp.float32),
        in_specs=[pl.BlockSpec(memory_space=pltpu.VMEM)] * 3
        + [pl.BlockSpec(memory_space=pl.ANY)] * 3,
        out_specs=pl.BlockSpec(memory_space=pl.ANY),
        scratch_shapes=x_scratch(devices, x_local, y_local)
        + [
            pltpu.VMEM((2, 6, y_local, x_cells), jnp.float32),
            pltpu.VMEM((3, 2, y_local, x_cells), jnp.float32),
            pltpu.VMEM((pieces, 2, 3, y_local, x_cells // pieces), jnp.float32),
            pltpu.SemaphoreType.DMA((3,)),
            pltpu.SemaphoreType.DMA((pieces,)),
        ],
        compiler_params=params(40),
        cost_estimate=cost(x_cells * y_local * (x_local * 24 + 72), x_cells * y_local * 96),
    )(*x_tables(devices, x_local, y_cells), data, green, first, second)


def gate_kernel(data, after, out):
    del data, after, out


def once_after(data, after):
    return pl.pallas_call(
        gate_kernel,
        out_shape=jax.ShapeDtypeStruct(data.shape, data.dtype),
        in_specs=[pl.BlockSpec(memory_space=pl.ANY)] * 2,
        out_specs=pl.BlockSpec(memory_space=pl.ANY),
        input_output_aliases={0: 0},
        compiler_params=params(1),
        cost_estimate=cost(0, 0),
    )(data, after)


def exchange(data):
    return lax.all_to_all(data, ("gx", "gy"), split_axis=0, concat_axis=0, tiled=True)


def per_device(tiles, tile_owner, tile_slot, tile_count, green):
    devices = lax.axis_size("gx") * lax.axis_size("gy")
    tile_total, tile_len = tiles.shape[2], tiles.shape[3]
    planes, y_local, x_cells = green.shape[2:]
    y_cells = y_local * devices
    x_local = x_cells // devices
    blocks = y_cells // tile_len
    per_owner = max(2, 2 * tile_total // devices)
    assert planes == 1 and tile_len == 128
    owner_row, slot_row = tile_owner.reshape(1, tile_total), tile_slot.reshape(1, tile_total)
    green = green.reshape(2, 6, y_local, x_cells)
    me = (lax.axis_index("gx") * lax.axis_size("gy") + lax.axis_index("gy")).reshape(1)
    lists = (owner_row, slot_row, tile_count, me.astype(jnp.int32))
    early = pack(tiles, (0, 1), *lists, None, devices, per_owner)
    late = pack(tiles, (2,), *lists, early, devices, per_owner)
    early, late = exchange(early), exchange(late)
    slots = early[:, 4 * per_owner :, :]
    grid = (x_local, blocks, per_owner)
    early = slab_waves(slots, (0, 1), (0, 1), early, *grid)
    early = exchange(once_after(early, late))
    late = slab_waves(slots, (2,), (0,), late, *grid)
    late = exchange(once_after(late, early))
    sizes = (devices, x_local, y_local, y_cells)
    waves = [x_waves(comp, early, *sizes) for comp in range(2)]
    mixed = last_waves(0, late, green, *waves, *sizes)
    return mixed.reshape(2, 3, planes, y_local, x_cells)


def solution(mesh):
    in_specs = (
        P(None, None, ("gx", "gy"), None),
        P(("gx", "gy"), None),
        P(("gx", "gy")),
        P(("gx", "gy")),
        P(None, None, None, ("gx", "gy"), None),
    )
    out_specs = P(None, None, None, ("gx", "gy"), None)
    return jax.shard_map(
        per_device, mesh=mesh, in_specs=in_specs, out_specs=out_specs, check_vma=False
    )
```

```python
import functools
import math

import jax
import jax.numpy as jnp
import ml_dtypes
import numpy as np
from jax import lax
from jax.experimental import pallas as pl
from jax.experimental.pallas import tpu as pltpu
from jax.sharding import PartitionSpec as P

pair_index = ((0, 3, 4), (3, 1, 5), (4, 5, 2))
by_rows = (((1,), (1,)), ((), ()))


def params(mebibytes):
    return pltpu.CompilerParams(vmem_limit_bytes=mebibytes * 1024 * 1024)


def in_hbm(array):
    return pltpu.with_memory_space_constraint(array, pltpu.HBM)


def cost(flops, moved):
    return pl.CostEstimate(flops=flops, bytes_accessed=moved, transcendentals=0)


def angles(rows, columns, length):
    products = np.outer(np.arange(rows), np.arange(columns)) % length
    return 2.0 * math.pi / length * products


def halves(table):
    wide = np.asarray(table, np.float32)
    high = wide.astype(ml_dtypes.bfloat16)
    low = (wide - high.astype(np.float32)).astype(ml_dtypes.bfloat16)
    return jnp.asarray(high), jnp.asarray(low)


def split_two(data):
    high = data.astype(jnp.bfloat16)
    return high, (data - high.astype(jnp.float32)).astype(jnp.bfloat16)


def split_three(data):
    high = data.astype(jnp.bfloat16)
    rest = data - high.astype(jnp.float32)
    middle = rest.astype(jnp.bfloat16)
    return high, middle, (rest - middle.astype(jnp.float32)).astype(jnp.bfloat16)


def dot_rows(left, right):
    return lax.dot_general(left, right, by_rows, preferred_element_type=jnp.float32)


def dot_rows_split(table, data):
    rows, depth = table.shape
    table_high, table_low = split_two(table)
    high, low = split_two(data)
    if depth > 128:
        both = dot_rows(jnp.concatenate([table_high, table_low]), high)
        return both[:rows] + both[rows:] + dot_rows(table_high, low)
    left = jnp.concatenate(
        [
            jnp.concatenate([table_high, table_high], axis=1),
            jnp.concatenate([table_low, jnp.zeros_like(table_low)], axis=1),
        ]
    )
    both = dot_rows(left, jnp.concatenate([high, low], axis=1))
    return both[:rows] + both[rows:]


def flat_fft(values, times):
    length = len(values)
    if length == 1:
        return values
    even = flat_fft(values[0::2], times)
    odd = flat_fft(values[1::2], times)
    lower, upper = [], []
    for k in range(length // 2):
        turned = times(odd[k], k, length)
        lower.append(jax.tree.map(lambda a, b: a + b, even[k], turned))
        upper.append(jax.tree.map(lambda a, b: a - b, even[k], turned))
    return lower + upper


def times_pair(value, k, length):
    real, imag = value
    if k == 0:
        return value
    if 4 * k == length:
        return (imag, -real)
    cos_k = math.cos(2.0 * math.pi * k / length)
    sin_k = math.sin(2.0 * math.pi * k / length)
    return (real * cos_k + imag * sin_k, imag * cos_k - real * sin_k)


def place_of(owner, count_gl):
    shift = count_gl.bit_length() - 1
    z = (owner >> shift) & 3
    return (((owner >> (shift + 2)) << shift) + (owner & (count_gl - 1))) * 4 + z


def owner_order(devices, count_gl):
    order = [0] * devices
    for owner in range(devices):
        order[place_of(owner, count_gl)] = owner
    return order


def pack_kernel(
    devices, count_gl, per_owner, comps, with_slots, count, me, owner_row, slot_row, tiles, *refs
):
    out, held, made, lists, sems, out_sems = refs[-6:]
    listed = owner_row.shape[1]
    fetches = [
        pltpu.make_async_copy(owner_row, lists.at[0], sems.at[0]),
        pltpu.make_async_copy(slot_row, lists.at[1], sems.at[1]),
    ]
    fetches += [
        pltpu.make_async_copy(tiles.at[:, comp], held.at[i], sems.at[2 + i])
        for i, comp in enumerate(comps)
    ]
    for fetch in fetches:
        fetch.start()
    fetches[0].wait()
    live_count = count[0]
    live = lax.broadcasted_iota(jnp.int32, (1, listed), 1) < live_count
    place = jnp.where(live, place_of(lists[0], count_gl), -1)
    place_at = lax.broadcasted_iota(jnp.int32, (devices, listed), 0)
    named = jnp.where(place_at == place, 1.0, 0.0)
    sender = lax.broadcasted_iota(jnp.int32, (listed, listed), 0)
    reader = lax.broadcasted_iota(jnp.int32, (listed, listed), 1)
    before = jnp.where(sender < reader, 1.0, 0.0).astype(jnp.bfloat16)
    counted = jnp.dot(named.astype(jnp.bfloat16), before, preferred_element_type=jnp.float32)
    rank = jnp.sum(counted * named, axis=0, keepdims=True).astype(jnp.int32)
    target = jnp.where(live, place * per_owner + rank, -1)
    target_at = lax.broadcasted_iota(jnp.int32, (devices * per_owner, listed), 0)
    chosen = jnp.where(target_at == target, 1.0, 0.0).astype(jnp.bfloat16)
    fetches[1].wait()
    sends = []

    def send(start, rows):
        part = pl.ds(start, rows)
        copy = pltpu.make_async_copy(
            made.at[:, part], out.at[:, part], out_sems.at[len(sends)]
        )
        copy.start()
        sends.append(copy)

    for i, fetch in enumerate(fetches[2:]):
        fetch.wait()
        parts = [part for r in range(2) for part in split_three(held[i, r])]
        got = jnp.dot(
            chosen, jnp.concatenate(parts, axis=1), preferred_element_type=jnp.float32
        )
        for r in range(2):
            one = got[:, 384 * r : 384 * r + 384]
            whole = (one[:, :128] + one[:, 128:256]) + one[:, 256:]
            start = (2 * i + r) * per_owner
            made[:, start : start + per_owner, :] = whole.reshape(devices, per_owner, 128)
        send(2 * i * per_owner, 2 * per_owner)
    if with_slots:
        stated = lists[1] + 1
        lane = rank + (place_of(me[0], count_gl) & (128 // per_owner - 1)) * per_owner
        lane_at = lax.broadcasted_iota(jnp.int32, (128, listed), 0)
        ranked = jnp.where(lane_at == lane, 1.0, 0.0).astype(jnp.bfloat16)
        coarse = (named * (stated >> 5).astype(jnp.float32)).astype(jnp.bfloat16)
        fine = (named * (stated & 31).astype(jnp.float32)).astype(jnp.bfloat16)
        slots = 32.0 * dot_rows(coarse, ranked) + dot_rows(fine, ranked)
        start = 2 * len(comps) * per_owner
        made[:, start:, :] = jnp.broadcast_to(slots[:, None, :], (devices, 8, 128))
        send(start, 8)
    for copy in sends:
        copy.wait()


def pack(tiles, comps, owner_row, slot_row, count, me, after, devices, count_gl, per_owner):
    listed = tiles.shape[2]
    with_slots = after is None
    rows = 2 * len(comps) * per_owner + (8 if with_slots else 0)
    extra = () if with_slots else (after,)
    return pl.pallas_call(
        functools.partial(pack_kernel, devices, count_gl, per_owner, comps, with_slots),
        out_shape=pltpu.HBM((devices, rows, 128), jnp.float32),
        in_specs=[pl.BlockSpec(memory_space=pltpu.SMEM)] * 2
        + [pl.BlockSpec(memory_space=pltpu.HBM)] * (3 + len(extra)),
        out_specs=pl.BlockSpec(memory_space=pltpu.HBM),
        scratch_shapes=[
            pltpu.VMEM((len(comps), 2, listed, 128), jnp.float32),
            pltpu.VMEM((devices, rows, 128), jnp.float32),
            pltpu.VMEM((2, 1, listed), jnp.int32),
            pltpu.SemaphoreType.DMA((2 + len(comps),)),
            pltpu.SemaphoreType.DMA((1 + len(comps),)),
        ],
        compiler_params=params(24),
        cost_estimate=cost(
            devices * per_owner * listed * 768 * 2 * len(comps), devices * rows * 1024
        ),
    )(count, me, *[in_hbm(a) for a in (owner_row, slot_row, tiles, *extra)])


def slab_kernel(
    comps, places, x_local, blocks, per_owner, table, twist, packed, data, out, *scratch
):
    slots, held, made, slab, turned, sems, out_sems = scratch
    devices = data.shape[0]
    fetches = [
        pltpu.make_async_copy(
            data.at[:, pl.ds(2 * place * per_owner, 2 * per_owner)], held.at[i], sems.at[i]
        )
        for i, place in enumerate(places)
    ]
    fetches.append(
        pltpu.make_async_copy(
            packed.at[:, pl.ds(packed.shape[1] - 8, 8)], slots, sems.at[len(comps)]
        )
    )
    for fetch in fetches:
        fetch.start()
    fetches[-1].wait()
    entries = devices * per_owner
    y_local = blocks * 128 // devices
    wide = 2 * x_local
    shift = blocks.bit_length() - 1
    every = 128 // per_owner
    stated = [
        sum([slots[o, :1] for o in range(start, start + every)])
        for start in range(0, devices, every)
    ]
    slot = jnp.concatenate(stated, axis=1).astype(jnp.int32) - 1
    landing = jnp.where(slot >= 0, (slot & (blocks - 1)) * x_local + (slot >> shift), -1)
    sends = []
    for index, comp in enumerate(comps):
        fetches[index].wait()
        parts = []
        for r in range(2):
            start = r * per_owner
            one = held[index, :, start : start + per_owner, :]
            parts.extend(split_two(one.reshape(entries, 128)))
        parts = jnp.concatenate(parts, axis=1)
        for start in range(0, blocks * x_local, 256):
            place = start + lax.broadcasted_iota(jnp.int32, (256, entries), 0)
            chosen = jnp.where(place == landing, 1.0, 0.0).astype(jnp.bfloat16)
            got = jnp.dot(chosen, parts, preferred_element_type=jnp.float32)
            for r in range(2):
                slab[r, start : start + 256, :] = (
                    got[:, 256 * r : 256 * r + 128] + got[:, 256 * r + 128 : 256 * r + 256]
                )

        @pl.loop(0, x_local // 8)
        def _(step):
            at = pl.multiple_of(step * 8, 8)
            values = [
                tuple(slab[r, pl.ds(t * x_local + at, 8), :] for r in range(2))
                for t in range(blocks)
            ]
            waves = flat_fft(values, times_pair)
            for k in range(blocks):
                real, imag = waves[k]
                cos_k, sin_k = twist[0, k : k + 1, :], twist[1, k : k + 1, :]
                new_real = real * cos_k + imag * sin_k
                new_imag = imag * cos_k - real * sin_k
                first = pl.ds(k * wide + at, 8)
                second = pl.ds(k * wide + x_local + at, 8)
                turned[first, :128] = new_real
                turned[first, 128:] = new_imag
                turned[second, :128] = new_imag
                turned[second, 128:] = -new_real

        together = 4
        for start in range(0, blocks, together):
            moved = dot_rows_split(
                table[...], turned[start * wide : (start + together) * wide, :]
            )
            for k in range(start, start + together):
                one = moved[:, (k - start) * wide : (k - start + 1) * wide]
                made[index, pl.ds(k, 128, stride=blocks), :] = one
        send = pltpu.make_async_copy(
            made.at[index].reshape(devices, y_local, wide),
            out.at[:, pl.ds(index * y_local, y_local)],
            out_sems.at[index],
        )
        send.start()
        sends.append(send)
    for send in sends:
        send.wait()


def slab_waves(packed, comps, places, data, x_local, blocks, count_gl, per_owner):
    devices = data.shape[0]
    y_cells = blocks * 128
    y_local = y_cells // devices
    fine = angles(128, 128, 128)
    table = np.concatenate([np.cos(fine), np.sin(fine)], axis=1).astype(np.float32)
    order = owner_order(devices, count_gl)
    table = table.reshape(devices, 128 // devices, 256)[order].reshape(128, 256)
    twist_angle = angles(blocks, 128, y_cells)
    twist = np.stack([np.cos(twist_angle), np.sin(twist_angle)]).astype(np.float32)
    entries = devices * per_owner
    count = len(comps)
    return pl.pallas_call(
        functools.partial(slab_kernel, comps, places, x_local, blocks, per_owner),
        out_shape=pltpu.HBM((devices, count * y_local, 2 * x_local), jnp.float32),
        in_specs=[pl.BlockSpec(memory_space=pltpu.VMEM)] * 2
        + [pl.BlockSpec(memory_space=pltpu.HBM)] * 2,
        out_specs=pl.BlockSpec(memory_space=pltpu.HBM),
        scratch_shapes=[
            pltpu.VMEM((devices, 8, 128), jnp.float32),
            pltpu.VMEM((count, devices, 2 * per_owner, 128), jnp.float32),
            pltpu.VMEM((count, y_cells, 2 * x_local), jnp.float32),
            pltpu.VMEM((2, blocks * x_local, 128), jnp.float32),
            pltpu.VMEM((blocks * 2 * x_local, 256), jnp.float32),
            pltpu.SemaphoreType.DMA((count + 1,)),
            pltpu.SemaphoreType.DMA((count,)),
        ],
        compiler_params=params(24),
        cost_estimate=cost(
            count * (blocks * x_local * entries * 1024 + y_cells * x_local * 3072),
            count * (entries * 1024 + y_cells * x_local * 8),
        ),
    )(jnp.asarray(table), jnp.asarray(twist), in_hbm(packed), in_hbm(data))


def swap_parts(value, x_local):
    if 2 * x_local == 128:
        return pltpu.roll(value, x_local, 1)
    return jnp.concatenate([value[:, x_local:], value[:, :x_local]], axis=1)


def x_steps(
    devices, x_local, y_local, order, index, twist, table, data, held, turned, columns, sems, store
):
    wide = 2 * x_local
    lane = lax.broadcasted_iota(jnp.int32, (1, wide), 1)
    sign = jnp.where(lane < x_local, 1.0, -1.0)

    def times(value, k, length):
        if k == 0:
            return value
        swapped = swap_parts(value, x_local) * sign
        if 4 * k == length:
            return swapped
        cos_k = math.cos(2.0 * math.pi * k / length)
        sin_k = math.sin(2.0 * math.pi * k / length)
        return value * cos_k + swapped * sin_k

    def fetch(step):
        at = pl.multiple_of(step * 8, 8)
        return pltpu.make_async_copy(
            data.at[:, pl.ds(index * y_local + at, 8)], held.at[step], sems.at[step]
        )

    for step in range(y_local // 8):
        fetch(step).start()

    @pl.loop(0, y_local // 8)
    def _(step):
        fetch(step).wait()
        at = pl.multiple_of(step * 8, 8)
        values = [held[step, order.index(o)] for o in range(devices)]
        waves = flat_fft(values, times)
        for k in range(devices):
            swapped = swap_parts(waves[k], x_local)
            new = waves[k] * twist[0, k : k + 1, :] + swapped * twist[1, k : k + 1, :]
            turned[k, pl.ds(at, 8), :] = new
            turned[k, pl.ds(y_local + at, 8), :] = swap_parts(new, x_local) * sign

    together = 4
    for start in range(0, devices, together):
        stacked = turned[start : start + together].reshape(together * 2 * y_local, wide)
        moved = dot_rows_split(table[...], stacked)
        for k in range(start, start + together):
            columns[pl.ds(k, x_local, stride=devices), :] = moved[
                :, (k - start) * 2 * y_local : (k - start + 1) * 2 * y_local
            ]
    for start in range(0, devices * x_local, 128):
        store(start, columns[start : start + 128, :].T)


def x_kernel(devices, x_local, y_local, order, index, twist, table, data, out, *scratch):
    made, out_sem = scratch[:2]

    def store(start, block):
        made[0, :, start : start + 128] = block[:y_local]
        made[1, :, start : start + 128] = block[y_local:]

    x_steps(
        devices, x_local, y_local, order, index, twist, table, data, *scratch[2:], store
    )
    send = pltpu.make_async_copy(made, out, out_sem)
    send.start()
    send.wait()


def last_kernel(devices, x_local, y_local, order, index, twist, table, data, *refs):
    green, first, second, out = refs[:4]
    scratch, (tensor, kept, made, in_sems, out_sems) = refs[4:8], refs[8:]
    x_cells = devices * x_local
    pieces = made.shape[0]
    width = x_cells // pieces
    fetches = [
        pltpu.make_async_copy(first, kept.at[0], in_sems.at[0]),
        pltpu.make_async_copy(second, kept.at[1], in_sems.at[1]),
        pltpu.make_async_copy(green, tensor, in_sems.at[2]),
    ]
    for fetch in fetches:
        fetch.start()

    def store(start, block):
        kept[2, 0, :, start : start + 128] = block[:y_local]
        kept[2, 1, :, start : start + 128] = block[y_local:]

    x_steps(devices, x_local, y_local, order, index, twist, table, data, *scratch, store)
    for fetch in fetches:
        fetch.wait()
    sends = []
    for piece in range(pieces):

        @pl.loop(0, y_local // 8)
        def _(step):
            rows = pl.ds(pl.multiple_of(step * 8, 8), 8)
            columns = pl.ds(piece * width, width)
            waves = [(kept[c, 0, rows, columns], kept[c, 1, rows, columns]) for c in range(3)]
            sums = [[None, None] for _ in range(3)]
            for entry in range(6):
                green_real = tensor[0, entry, rows, columns]
                green_imag = tensor[1, entry, rows, columns]
                for row in range(3):
                    for col in range(3):
                        if pair_index[row][col] != entry:
                            continue
                        real, imag = waves[col]
                        real_term = green_real * real - green_imag * imag
                        imag_term = green_real * imag + green_imag * real
                        old = sums[row]
                        sums[row] = [
                            real_term if old[0] is None else old[0] + real_term,
                            imag_term if old[1] is None else old[1] + imag_term,
                        ]
            for row in range(3):
                made[piece, 0, row, rows, :] = sums[row][0]
                made[piece, 1, row, rows, :] = sums[row][1]

        send = pltpu.make_async_copy(
            made.at[piece],
            out.at[:, :, :, pl.ds(piece * width, width)],
            out_sems.at[piece],
        )
        send.start()
        sends.append(send)
    for send in sends:
        send.wait()


def x_tables(devices, x_local, y_cells):
    x_cells = devices * x_local
    fine = angles(x_local, x_local, x_local)
    scale = 1.0 / math.sqrt(x_cells * y_cells)
    table = np.concatenate([np.cos(fine), np.sin(fine)], axis=1) * scale
    angle = angles(devices, x_local, x_cells)
    cos_a, sin_a = np.cos(angle), np.sin(angle)
    twist = np.stack(
        [np.concatenate([cos_a, cos_a], axis=1), np.concatenate([sin_a, -sin_a], axis=1)]
    )
    return jnp.asarray(twist.astype(np.float32)), jnp.asarray(table.astype(np.float32))


def x_scratch(devices, x_local, y_local):
    return [
        pltpu.VMEM((y_local // 8, devices, 8, 2 * x_local), jnp.float32),
        pltpu.VMEM((devices, 2 * y_local, 2 * x_local), jnp.float32),
        pltpu.VMEM((devices * x_local, 2 * y_local), jnp.float32),
        pltpu.SemaphoreType.DMA((y_local // 8,)),
    ]


def x_waves(index, data, devices, x_local, y_local, y_cells, count_gl):
    x_cells = devices * x_local
    order = owner_order(devices, count_gl)
    return pl.pallas_call(
        functools.partial(x_kernel, devices, x_local, y_local, order, index),
        out_shape=pltpu.HBM((2, y_local, x_cells), jnp.float32),
        in_specs=[pl.BlockSpec(memory_space=pltpu.VMEM)] * 2
        + [pl.BlockSpec(memory_space=pltpu.HBM)],
        out_specs=pl.BlockSpec(memory_space=pltpu.HBM),
        scratch_shapes=[
            pltpu.VMEM((2, y_local, x_cells), jnp.float32),
            pltpu.SemaphoreType.DMA(()),
        ]
        + x_scratch(devices, x_local, y_local),
        compiler_params=params(24),
        cost_estimate=cost(x_cells * y_local * x_local * 24, x_cells * y_local * 16),
    )(*x_tables(devices, x_local, y_cells), in_hbm(data))


def last_waves(index, data, green, first, second, devices, x_local, y_local, y_cells, count_gl):
    x_cells = devices * x_local
    order = owner_order(devices, count_gl)
    pieces = 8
    return pl.pallas_call(
        functools.partial(last_kernel, devices, x_local, y_local, order, index),
        out_shape=pltpu.HBM((2, 3, y_local, x_cells), jnp.float32),
        in_specs=[pl.BlockSpec(memory_space=pltpu.VMEM)] * 2
        + [pl.BlockSpec(memory_space=pltpu.HBM)] * 4,
        out_specs=pl.BlockSpec(memory_space=pltpu.HBM),
        scratch_shapes=x_scratch(devices, x_local, y_local)
        + [
            pltpu.VMEM((2, 6, y_local, x_cells), jnp.float32),
            pltpu.VMEM((3, 2, y_local, x_cells), jnp.float32),
            pltpu.VMEM((pieces, 2, 3, y_local, x_cells // pieces), jnp.float32),
            pltpu.SemaphoreType.DMA((3,)),
            pltpu.SemaphoreType.DMA((pieces,)),
        ],
        compiler_params=params(40),
        cost_estimate=cost(x_cells * y_local * (x_local * 24 + 72), x_cells * y_local * 96),
    )(
        *x_tables(devices, x_local, y_cells),
        *[in_hbm(a) for a in (data, green, first, second)],
    )


def gate_kernel(data, after, out):
    del data, after, out


def once_after(data, after):
    return pl.pallas_call(
        gate_kernel,
        out_shape=pltpu.HBM(data.shape, data.dtype),
        in_specs=[pl.BlockSpec(memory_space=pltpu.HBM)] * 2,
        out_specs=pl.BlockSpec(memory_space=pltpu.HBM),
        input_output_aliases={0: 0},
        compiler_params=params(1),
        cost_estimate=cost(0, 0),
    )(in_hbm(data), in_hbm(after))


def exchange(data):
    return lax.all_to_all(data, ("gx", "gl", "gz"), split_axis=0, concat_axis=0, tiled=True)


def per_device(tiles, tile_owner, tile_slot, tile_count, green):
    count_gl = lax.axis_size("gl")
    devices = lax.axis_size("gx") * 4 * count_gl
    tile_total, tile_len = tiles.shape[2], tiles.shape[3]
    planes, y_local, x_cells = green.shape[2:]
    y_cells = y_local * devices
    x_local = x_cells // devices
    blocks = y_cells // tile_len
    per_owner = max(2, 2 * tile_total // devices)
    assert planes == 1 and tile_len == 128
    owner_row, slot_row = tile_owner.reshape(1, tile_total), tile_slot.reshape(1, tile_total)
    green = green.reshape(2, 6, y_local, x_cells)
    me = (lax.axis_index("gx") * 4 + lax.axis_index("gz")) * count_gl + lax.axis_index("gl")
    lists = (owner_row, slot_row, tile_count, me.reshape(1).astype(jnp.int32))
    early = pack(tiles, (0, 1), *lists, None, devices, count_gl, per_owner)
    late = pack(tiles, (2,), *lists, early, devices, count_gl, per_owner)
    early, late = exchange(early), exchange(late)
    packed = early
    grid = (x_local, blocks, count_gl, per_owner)
    early = slab_waves(packed, (0, 1), (0, 1), early, *grid)
    early = exchange(once_after(early, late))
    late = slab_waves(packed, (2,), (0,), late, *grid)
    late = exchange(once_after(late, early))
    sizes = (devices, x_local, y_local, y_cells, count_gl)
    waves = [x_waves(comp, early, *sizes) for comp in range(2)]
    mixed = last_waves(0, late, green, *waves, *sizes)
    return mixed.reshape(2, 3, planes, y_local, x_cells)


def solution(mesh):
    count_gx, count_gy = mesh.devices.shape
    fine_mesh = jax.sharding.Mesh(
        mesh.devices.reshape(count_gx, 4, count_gy // 4), ("gx", "gz", "gl")
    )
    every = ("gx", "gz", "gl")
    in_specs = (
        P(None, None, every, None),
        P(every, None),
        P(every),
        P(every),
        P(None, None, None, every, None),
    )
    out_specs = P(None, None, None, every, None)
    return jax.shard_map(
        per_device, mesh=fine_mesh, in_specs=in_specs, out_specs=out_specs, check_vma=False
    )
```

```python
import functools
import math

import jax
import jax.numpy as jnp
import ml_dtypes
import numpy as np
from jax import lax
from jax.experimental import pallas as pl
from jax.experimental.pallas import tpu as pltpu
from jax.sharding import PartitionSpec as P

pair_index = ((0, 3, 4), (3, 1, 5), (4, 5, 2))
by_rows = (((1,), (1,)), ((), ()))


def params(mebibytes):
    return pltpu.CompilerParams(vmem_limit_bytes=mebibytes * 1024 * 1024)


def in_hbm(array):
    return pltpu.with_memory_space_constraint(array, pltpu.HBM)


def in_vmem(array):
    return pltpu.with_memory_space_constraint(array, pltpu.VMEM)


def cost(flops, moved):
    return pl.CostEstimate(flops=flops, bytes_accessed=moved, transcendentals=0)


def angles(rows, columns, length):
    products = np.outer(np.arange(rows), np.arange(columns)) % length
    return 2.0 * math.pi / length * products


def halves(table):
    wide = np.asarray(table, np.float32)
    high = wide.astype(ml_dtypes.bfloat16)
    low = (wide - high.astype(np.float32)).astype(ml_dtypes.bfloat16)
    return jnp.asarray(high), jnp.asarray(low)


def split_two(data):
    high = data.astype(jnp.bfloat16)
    return high, (data - high.astype(jnp.float32)).astype(jnp.bfloat16)


def split_three(data):
    high = data.astype(jnp.bfloat16)
    rest = data - high.astype(jnp.float32)
    middle = rest.astype(jnp.bfloat16)
    return high, middle, (rest - middle.astype(jnp.float32)).astype(jnp.bfloat16)


def dot_rows(left, right):
    return lax.dot_general(left, right, by_rows, preferred_element_type=jnp.float32)


def dot_rows_split(table, data):
    rows, depth = table.shape
    table_high, table_low = split_two(table)
    high, low = split_two(data)
    if depth > 128:
        both = dot_rows(jnp.concatenate([table_high, table_low]), high)
        return both[:rows] + both[rows:] + dot_rows(table_high, low)
    left = jnp.concatenate(
        [
            jnp.concatenate([table_high, table_high], axis=1),
            jnp.concatenate([table_low, jnp.zeros_like(table_low)], axis=1),
        ]
    )
    both = dot_rows(left, jnp.concatenate([high, low], axis=1))
    return both[:rows] + both[rows:]


def flat_fft(values, times):
    length = len(values)
    if length == 1:
        return values
    even = flat_fft(values[0::2], times)
    odd = flat_fft(values[1::2], times)
    lower, upper = [], []
    for k in range(length // 2):
        turned = times(odd[k], k, length)
        lower.append(jax.tree.map(lambda a, b: a + b, even[k], turned))
        upper.append(jax.tree.map(lambda a, b: a - b, even[k], turned))
    return lower + upper


def times_pair(value, k, length):
    real, imag = value
    if k == 0:
        return value
    if 4 * k == length:
        return (imag, -real)
    cos_k = math.cos(2.0 * math.pi * k / length)
    sin_k = math.sin(2.0 * math.pi * k / length)
    return (real * cos_k + imag * sin_k, imag * cos_k - real * sin_k)


def place_of(owner, count_gl):
    shift = count_gl.bit_length() - 1
    z = (owner >> shift) & 3
    return (((owner >> (shift + 2)) << shift) + (owner & (count_gl - 1))) * 4 + z


def owner_order(devices, count_gl):
    order = [0] * devices
    for owner in range(devices):
        order[place_of(owner, count_gl)] = owner
    return order


def pack_kernel(
    devices, count_gl, per_owner, count, me, owner_row, slot_row, tiles, out, *scratch
):
    held, made, lists, sems, out_sems = scratch
    comps = tiles.shape[1]
    listed = owner_row.shape[1]
    fetches = [
        pltpu.make_async_copy(owner_row, lists.at[0], sems.at[0]),
        pltpu.make_async_copy(slot_row, lists.at[1], sems.at[1]),
    ]
    fetches += [
        pltpu.make_async_copy(tiles.at[:, comp], held.at[i], sems.at[2 + i])
        for i, comp in enumerate(range(comps))
    ]
    for fetch in fetches:
        fetch.start()
    fetches[0].wait()
    live_count = count[0]
    live = lax.broadcasted_iota(jnp.int32, (1, listed), 1) < live_count
    place = jnp.where(live, place_of(lists[0], count_gl), -1)
    place_at = lax.broadcasted_iota(jnp.int32, (devices, listed), 0)
    named = jnp.where(place_at == place, 1.0, 0.0)
    sender = lax.broadcasted_iota(jnp.int32, (listed, listed), 0)
    reader = lax.broadcasted_iota(jnp.int32, (listed, listed), 1)
    before = jnp.where(sender < reader, 1.0, 0.0).astype(jnp.bfloat16)
    counted = jnp.dot(named.astype(jnp.bfloat16), before, preferred_element_type=jnp.float32)
    rank = jnp.sum(counted * named, axis=0, keepdims=True).astype(jnp.int32)
    target = jnp.where(live, place * per_owner + rank, -1)
    target_at = lax.broadcasted_iota(jnp.int32, (devices * per_owner, listed), 0)
    chosen = jnp.where(target_at == target, 1.0, 0.0).astype(jnp.bfloat16)
    fetches[1].wait()
    sends = []

    def send(start, rows):
        part = pl.ds(start, rows)
        copy = pltpu.make_async_copy(
            made.at[:, part], out.at[:, part], out_sems.at[len(sends)]
        )
        copy.start()
        sends.append(copy)

    stated = lists[1] + 1
    lane = rank + (place_of(me[0], count_gl) & (128 // per_owner - 1)) * per_owner
    lane_at = lax.broadcasted_iota(jnp.int32, (128, listed), 0)
    ranked = jnp.where(lane_at == lane, 1.0, 0.0).astype(jnp.bfloat16)
    coarse = (named * (stated >> 5).astype(jnp.float32)).astype(jnp.bfloat16)
    fine = (named * (stated & 31).astype(jnp.float32)).astype(jnp.bfloat16)
    slots = 32.0 * dot_rows(coarse, ranked) + dot_rows(fine, ranked)
    start = 2 * comps * per_owner
    made[:, start:, :] = jnp.broadcast_to(slots[:, None, :], (devices, 8, 128))
    send(start, 8)
    for comp in range(comps):
        fetches[2 + comp].wait()
        for r in range(2):
            parts = jnp.concatenate(split_three(held[comp, r]), axis=1)
            got = jnp.dot(chosen, parts, preferred_element_type=jnp.float32)
            whole = (got[:, :128] + got[:, 128:256]) + got[:, 256:]
            start = (2 * comp + r) * per_owner
            made[:, start : start + per_owner, :] = whole.reshape(devices, per_owner, 128)
            send(start, per_owner)
    for copy in sends:
        copy.wait()


def pack(tiles, owner_row, slot_row, count, me, devices, count_gl, per_owner):
    comps, listed = tiles.shape[1:3]
    rows = 2 * comps * per_owner + 8
    return pl.pallas_call(
        functools.partial(pack_kernel, devices, count_gl, per_owner),
        out_shape=pltpu.HBM((devices, rows, 128), jnp.float32),
        in_specs=[pl.BlockSpec(memory_space=pltpu.SMEM)] * 2
        + [pl.BlockSpec(memory_space=pltpu.HBM)] * 3,
        out_specs=pl.BlockSpec(memory_space=pltpu.HBM),
        scratch_shapes=[
            pltpu.VMEM((comps, 2, listed, 128), jnp.float32),
            pltpu.VMEM((devices, rows, 128), jnp.float32),
            pltpu.VMEM((2, 1, listed), jnp.int32),
            pltpu.SemaphoreType.DMA((2 + comps,)),
            pltpu.SemaphoreType.DMA((1 + 2 * comps,)),
        ],
        compiler_params=params(24),
        cost_estimate=cost(
            devices * per_owner * listed * 768 * 2 * comps, devices * rows * 1024
        ),
    )(count, me, *[in_hbm(a) for a in (owner_row, slot_row, tiles)])


def slab_kernel(comps, x_local, blocks, per_owner, table, twist, data, out, *scratch):
    made, slab, turned, out_sems = scratch
    devices = data.shape[0]
    entries = devices * per_owner
    y_local = blocks * 128 // devices
    wide = 2 * x_local
    shift = blocks.bit_length() - 1
    every = 128 // per_owner
    stated = [
        sum([data[o, data.shape[1] - 8 :][:1] for o in range(start, start + every)])
        for start in range(0, devices, every)
    ]
    slot = jnp.concatenate(stated, axis=1).astype(jnp.int32) - 1
    landing = jnp.where(slot >= 0, (slot & (blocks - 1)) * x_local + (slot >> shift), -1)
    parts = []
    for comp in comps:
        for r in range(2):
            start = (2 * comp + r) * per_owner
            one = data[:, start : start + per_owner, :]
            parts.extend(split_two(one.reshape(entries, 128)))
    parts = jnp.concatenate(parts, axis=1)
    for start in range(0, blocks * x_local, 256):
        place = start + lax.broadcasted_iota(jnp.int32, (256, entries), 0)
        chosen = jnp.where(place == landing, 1.0, 0.0).astype(jnp.bfloat16)
        got = jnp.dot(chosen, parts, preferred_element_type=jnp.float32)
        for i in range(2 * len(comps)):
            slab[i // 2, i % 2, start : start + 256, :] = (
                got[:, 256 * i : 256 * i + 128] + got[:, 256 * i + 128 : 256 * i + 256]
            )
    sends = []
    for index in range(len(comps)):

        @pl.loop(0, x_local // 8)
        def _(step):
            at = pl.multiple_of(step * 8, 8)
            values = [
                tuple(slab[index, r, pl.ds(t * x_local + at, 8), :] for r in range(2))
                for t in range(blocks)
            ]
            waves = flat_fft(values, times_pair)
            for k in range(blocks):
                real, imag = waves[k]
                cos_k, sin_k = twist[0, k : k + 1, :], twist[1, k : k + 1, :]
                new_real = real * cos_k + imag * sin_k
                new_imag = imag * cos_k - real * sin_k
                first = pl.ds(k * wide + at, 8)
                second = pl.ds(k * wide + x_local + at, 8)
                turned[first, :128] = new_real
                turned[first, 128:] = new_imag
                turned[second, :128] = new_imag
                turned[second, 128:] = -new_real

        together = 4
        for start in range(0, blocks, together):
            moved = dot_rows_split(
                table[...], turned[start * wide : (start + together) * wide, :]
            )
            for k in range(start, start + together):
                one = moved[:, (k - start) * wide : (k - start + 1) * wide]
                made[index, pl.ds(k, 128, stride=blocks), :] = one
        send = pltpu.make_async_copy(
            made.at[index].reshape(devices, y_local, wide),
            out.at[:, pl.ds(index * y_local, y_local)],
            out_sems.at[index],
        )
        send.start()
        sends.append(send)
    for send in sends:
        send.wait()


def slab_waves(comps, data, x_local, blocks, count_gl, per_owner):
    devices = data.shape[0]
    y_cells = blocks * 128
    y_local = y_cells // devices
    fine = angles(128, 128, 128)
    table = np.concatenate([np.cos(fine), np.sin(fine)], axis=1).astype(np.float32)
    order = owner_order(devices, count_gl)
    table = table.reshape(devices, 128 // devices, 256)[order].reshape(128, 256)
    twist_angle = angles(blocks, 128, y_cells)
    twist = np.stack([np.cos(twist_angle), np.sin(twist_angle)]).astype(np.float32)
    entries = devices * per_owner
    count = len(comps)
    return pl.pallas_call(
        functools.partial(slab_kernel, comps, x_local, blocks, per_owner),
        out_shape=pltpu.HBM((devices, count * y_local, 2 * x_local), jnp.float32),
        in_specs=[pl.BlockSpec(memory_space=pltpu.VMEM)] * 3,
        out_specs=pl.BlockSpec(memory_space=pltpu.HBM),
        scratch_shapes=[
            pltpu.VMEM((count, y_cells, 2 * x_local), jnp.float32),
            pltpu.VMEM((count, 2, blocks * x_local, 128), jnp.float32),
            pltpu.VMEM((blocks * 2 * x_local, 256), jnp.float32),
            pltpu.SemaphoreType.DMA((count,)),
        ],
        compiler_params=params(24),
        cost_estimate=cost(
            count * (blocks * x_local * entries * 1024 + y_cells * x_local * 3072),
            count * (entries * 1024 + y_cells * x_local * 8),
        ),
    )(jnp.asarray(table), jnp.asarray(twist), in_vmem(data))


def swap_parts(value, x_local):
    if 2 * x_local == 128:
        return pltpu.roll(value, x_local, 1)
    return jnp.concatenate([value[:, x_local:], value[:, :x_local]], axis=1)


def x_steps(
    devices, x_local, y_local, order, index, twist, table, data, turned, columns, store
):
    wide = 2 * x_local
    lane = lax.broadcasted_iota(jnp.int32, (1, wide), 1)
    sign = jnp.where(lane < x_local, 1.0, -1.0)

    def times(value, k, length):
        if k == 0:
            return value
        swapped = swap_parts(value, x_local) * sign
        if 4 * k == length:
            return swapped
        cos_k = math.cos(2.0 * math.pi * k / length)
        sin_k = math.sin(2.0 * math.pi * k / length)
        return value * cos_k + swapped * sin_k

    @pl.loop(0, y_local // 8)
    def _(step):
        at = pl.multiple_of(step * 8, 8)
        rows = pl.ds(index * y_local + at, 8)
        values = [data[order.index(o), rows, :] for o in range(devices)]
        waves = flat_fft(values, times)
        for k in range(devices):
            swapped = swap_parts(waves[k], x_local)
            new = waves[k] * twist[0, k : k + 1, :] + swapped * twist[1, k : k + 1, :]
            turned[k, pl.ds(at, 8), :] = new
            turned[k, pl.ds(y_local + at, 8), :] = swap_parts(new, x_local) * sign

    together = 4
    for start in range(0, devices, together):
        stacked = turned[start : start + together].reshape(together * 2 * y_local, wide)
        moved = dot_rows_split(table[...], stacked)
        for k in range(start, start + together):
            columns[pl.ds(k, x_local, stride=devices), :] = moved[
                :, (k - start) * 2 * y_local : (k - start + 1) * 2 * y_local
            ]
    for start in range(0, devices * x_local, 128):
        store(start, columns[start : start + 128, :].T)


def x_kernel(devices, x_local, y_local, order, index, twist, table, data, out, *scratch):
    made, out_sem = scratch[:2]

    def store(start, block):
        made[0, :, start : start + 128] = block[:y_local]
        made[1, :, start : start + 128] = block[y_local:]

    x_steps(
        devices, x_local, y_local, order, index, twist, table, data, *scratch[2:], store
    )
    send = pltpu.make_async_copy(made, out, out_sem)
    send.start()
    send.wait()


def last_kernel(devices, x_local, y_local, order, index, twist, table, data, *refs):
    green, first, second, out = refs[:4]
    scratch, (tensor, kept, made, in_sems, out_sems) = refs[4:6], refs[6:]
    x_cells = devices * x_local
    pieces = made.shape[0]
    width = x_cells // pieces
    fetches = [
        pltpu.make_async_copy(first, kept.at[0], in_sems.at[0]),
        pltpu.make_async_copy(second, kept.at[1], in_sems.at[1]),
        pltpu.make_async_copy(green, tensor, in_sems.at[2]),
    ]
    for fetch in fetches:
        fetch.start()

    def store(start, block):
        kept[2, 0, :, start : start + 128] = block[:y_local]
        kept[2, 1, :, start : start + 128] = block[y_local:]

    x_steps(devices, x_local, y_local, order, index, twist, table, data, *scratch, store)
    for fetch in fetches:
        fetch.wait()
    sends = []
    for piece in range(pieces):

        @pl.loop(0, y_local // 8)
        def _(step):
            rows = pl.ds(pl.multiple_of(step * 8, 8), 8)
            columns = pl.ds(piece * width, width)
            waves = [(kept[c, 0, rows, columns], kept[c, 1, rows, columns]) for c in range(3)]
            sums = [[None, None] for _ in range(3)]
            for entry in range(6):
                green_real = tensor[0, entry, rows, columns]
                green_imag = tensor[1, entry, rows, columns]
                for row in range(3):
                    for col in range(3):
                        if pair_index[row][col] != entry:
                            continue
                        real, imag = waves[col]
                        real_term = green_real * real - green_imag * imag
                        imag_term = green_real * imag + green_imag * real
                        old = sums[row]
                        sums[row] = [
                            real_term if old[0] is None else old[0] + real_term,
                            imag_term if old[1] is None else old[1] + imag_term,
                        ]
            for row in range(3):
                made[piece, 0, row, rows, :] = sums[row][0]
                made[piece, 1, row, rows, :] = sums[row][1]

        send = pltpu.make_async_copy(
            made.at[piece],
            out.at[:, :, :, pl.ds(piece * width, width)],
            out_sems.at[piece],
        )
        send.start()
        sends.append(send)
    for send in sends:
        send.wait()


def x_tables(devices, x_local, y_cells):
    x_cells = devices * x_local
    fine = angles(x_local, x_local, x_local)
    scale = 1.0 / math.sqrt(x_cells * y_cells)
    table = np.concatenate([np.cos(fine), np.sin(fine)], axis=1) * scale
    angle = angles(devices, x_local, x_cells)
    cos_a, sin_a = np.cos(angle), np.sin(angle)
    twist = np.stack(
        [np.concatenate([cos_a, cos_a], axis=1), np.concatenate([sin_a, -sin_a], axis=1)]
    )
    return jnp.asarray(twist.astype(np.float32)), jnp.asarray(table.astype(np.float32))


def x_scratch(devices, x_local, y_local):
    return [
        pltpu.VMEM((devices, 2 * y_local, 2 * x_local), jnp.float32),
        pltpu.VMEM((devices * x_local, 2 * y_local), jnp.float32),
    ]


def x_waves(index, data, devices, x_local, y_local, y_cells, count_gl):
    x_cells = devices * x_local
    order = owner_order(devices, count_gl)
    return pl.pallas_call(
        functools.partial(x_kernel, devices, x_local, y_local, order, index),
        out_shape=pltpu.HBM((2, y_local, x_cells), jnp.float32),
        in_specs=[pl.BlockSpec(memory_space=pltpu.VMEM)] * 3,
        out_specs=pl.BlockSpec(memory_space=pltpu.HBM),
        scratch_shapes=[
            pltpu.VMEM((2, y_local, x_cells), jnp.float32),
            pltpu.SemaphoreType.DMA(()),
        ]
        + x_scratch(devices, x_local, y_local),
        compiler_params=params(24),
        cost_estimate=cost(x_cells * y_local * x_local * 24, x_cells * y_local * 16),
    )(*x_tables(devices, x_local, y_cells), in_vmem(data))


def last_waves(index, data, green, first, second, devices, x_local, y_local, y_cells, count_gl):
    x_cells = devices * x_local
    order = owner_order(devices, count_gl)
    pieces = 8
    return pl.pallas_call(
        functools.partial(last_kernel, devices, x_local, y_local, order, index),
        out_shape=pltpu.HBM((2, 3, y_local, x_cells), jnp.float32),
        in_specs=[pl.BlockSpec(memory_space=pltpu.VMEM)] * 3
        + [pl.BlockSpec(memory_space=pltpu.HBM)] * 3,
        out_specs=pl.BlockSpec(memory_space=pltpu.HBM),
        scratch_shapes=x_scratch(devices, x_local, y_local)
        + [
            pltpu.VMEM((2, 6, y_local, x_cells), jnp.float32),
            pltpu.VMEM((3, 2, y_local, x_cells), jnp.float32),
            pltpu.VMEM((pieces, 2, 3, y_local, x_cells // pieces), jnp.float32),
            pltpu.SemaphoreType.DMA((3,)),
            pltpu.SemaphoreType.DMA((pieces,)),
        ],
        compiler_params=params(40),
        cost_estimate=cost(x_cells * y_local * (x_local * 24 + 72), x_cells * y_local * 96),
    )(
        *x_tables(devices, x_local, y_cells),
        in_vmem(data),
        *[in_hbm(a) for a in (green, first, second)],
    )


def gate_kernel(data, after, out):
    del data, after, out


def once_after(data, after):
    return pl.pallas_call(
        gate_kernel,
        out_shape=pltpu.HBM(data.shape, data.dtype),
        in_specs=[pl.BlockSpec(memory_space=pltpu.HBM), pl.BlockSpec(memory_space=pl.ANY)],
        out_specs=pl.BlockSpec(memory_space=pltpu.HBM),
        input_output_aliases={0: 0},
        compiler_params=params(1),
        cost_estimate=cost(0, 0),
    )(in_hbm(data), after)


def exchange(data):
    return lax.all_to_all(data, ("gx", "gl", "gz"), split_axis=0, concat_axis=0, tiled=True)


def per_device(tiles, tile_owner, tile_slot, tile_count, green):
    count_gl = lax.axis_size("gl")
    devices = lax.axis_size("gx") * 4 * count_gl
    tile_total, tile_len = tiles.shape[2], tiles.shape[3]
    planes, y_local, x_cells = green.shape[2:]
    y_cells = y_local * devices
    x_local = x_cells // devices
    blocks = y_cells // tile_len
    per_owner = max(2, 2 * tile_total // devices)
    assert planes == 1 and tile_len == 128
    owner_row, slot_row = tile_owner.reshape(1, tile_total), tile_slot.reshape(1, tile_total)
    green = green.reshape(2, 6, y_local, x_cells)
    me = (lax.axis_index("gx") * 4 + lax.axis_index("gz")) * count_gl + lax.axis_index("gl")
    lists = (owner_row, slot_row, tile_count, me.reshape(1).astype(jnp.int32))
    arrived = exchange(pack(tiles, *lists, devices, count_gl, per_owner))
    grid = (x_local, blocks, count_gl, per_owner)
    early = exchange(slab_waves((0, 1), arrived, *grid))
    late = slab_waves((2,), arrived, *grid)
    late = exchange(once_after(late, early))
    sizes = (devices, x_local, y_local, y_cells, count_gl)
    waves = [x_waves(comp, early, *sizes) for comp in range(2)]
    mixed = last_waves(0, late, green, *waves, *sizes)
    return mixed.reshape(2, 3, planes, y_local, x_cells)


def solution(mesh):
    count_gx, count_gy = mesh.devices.shape
    fine_mesh = jax.sharding.Mesh(
        mesh.devices.reshape(count_gx, 4, count_gy // 4), ("gx", "gz", "gl")
    )
    every = ("gx", "gz", "gl")
    in_specs = (
        P(None, None, every, None),
        P(every, None),
        P(every),
        P(every),
        P(None, None, None, every, None),
    )
    out_specs = P(None, None, None, every, None)
    return jax.shard_map(
        per_device, mesh=fine_mesh, in_specs=in_specs, out_specs=out_specs, check_vma=False
    )
```

```python
import functools
import math

import jax
import jax.numpy as jnp
import ml_dtypes
import numpy as np
from jax import lax
from jax.experimental import pallas as pl
from jax.experimental.pallas import tpu as pltpu
from jax.sharding import PartitionSpec as P

pair_index = ((0, 3, 4), (3, 1, 5), (4, 5, 2))
by_rows = (((1,), (1,)), ((), ()))


def params(mebibytes):
    return pltpu.CompilerParams(vmem_limit_bytes=mebibytes * 1024 * 1024)


def in_hbm(array):
    return pltpu.with_memory_space_constraint(array, pltpu.HBM)


def in_vmem(array):
    return pltpu.with_memory_space_constraint(array, pltpu.VMEM)


def cost(flops, moved):
    return pl.CostEstimate(flops=flops, bytes_accessed=moved, transcendentals=0)


def angles(rows, columns, length):
    products = np.outer(np.arange(rows), np.arange(columns)) % length
    return 2.0 * math.pi / length * products


def halves(table):
    wide = np.asarray(table, np.float32)
    high = wide.astype(ml_dtypes.bfloat16)
    low = (wide - high.astype(np.float32)).astype(ml_dtypes.bfloat16)
    return jnp.asarray(high), jnp.asarray(low)


def split_two(data):
    high = data.astype(jnp.bfloat16)
    return high, (data - high.astype(jnp.float32)).astype(jnp.bfloat16)


def split_three(data):
    high = data.astype(jnp.bfloat16)
    rest = data - high.astype(jnp.float32)
    middle = rest.astype(jnp.bfloat16)
    return high, middle, (rest - middle.astype(jnp.float32)).astype(jnp.bfloat16)


def dot_rows(left, right):
    return lax.dot_general(left, right, by_rows, preferred_element_type=jnp.float32)


def dot_rows_split(table, data):
    rows, depth = table.shape
    table_high, table_low = split_two(table)
    high, low = split_two(data)
    if depth > 128:
        both = dot_rows(jnp.concatenate([table_high, table_low]), high)
        return both[:rows] + both[rows:] + dot_rows(table_high, low)
    left = jnp.concatenate(
        [
            jnp.concatenate([table_high, table_high], axis=1),
            jnp.concatenate([table_low, jnp.zeros_like(table_low)], axis=1),
        ]
    )
    both = dot_rows(left, jnp.concatenate([high, low], axis=1))
    return both[:rows] + both[rows:]


def flat_fft(values, times):
    length = len(values)
    if length == 1:
        return values
    even = flat_fft(values[0::2], times)
    odd = flat_fft(values[1::2], times)
    lower, upper = [], []
    for k in range(length // 2):
        turned = times(odd[k], k, length)
        lower.append(jax.tree.map(lambda a, b: a + b, even[k], turned))
        upper.append(jax.tree.map(lambda a, b: a - b, even[k], turned))
    return lower + upper


def times_pair(value, k, length):
    real, imag = value
    if k == 0:
        return value
    if 4 * k == length:
        return (imag, -real)
    cos_k = math.cos(2.0 * math.pi * k / length)
    sin_k = math.sin(2.0 * math.pi * k / length)
    return (real * cos_k + imag * sin_k, imag * cos_k - real * sin_k)


def place_of(owner, count_gl):
    shift = count_gl.bit_length() - 1
    z = (owner >> shift) & 3
    return (((owner >> (shift + 2)) << shift) + (owner & (count_gl - 1))) * 4 + z


def owner_order(devices, count_gl):
    order = [0] * devices
    for owner in range(devices):
        order[place_of(owner, count_gl)] = owner
    return order


def pack_kernel(
    devices, count_gl, per_owner, comps, with_slots, count, me, owner_row, slot_row, tiles, *refs
):
    out, held, made, lists, sems, out_sems = refs[-6:]
    listed = owner_row.shape[1]
    fetches = [
        pltpu.make_async_copy(owner_row, lists.at[0], sems.at[0]),
        pltpu.make_async_copy(slot_row, lists.at[1], sems.at[1]),
    ]
    fetches += [
        pltpu.make_async_copy(tiles.at[:, comp], held.at[i], sems.at[2 + i])
        for i, comp in enumerate(comps)
    ]
    for fetch in fetches:
        fetch.start()
    fetches[0].wait()
    live_count = count[0]
    live = lax.broadcasted_iota(jnp.int32, (1, listed), 1) < live_count
    place = jnp.where(live, place_of(lists[0], count_gl), -1)
    place_at = lax.broadcasted_iota(jnp.int32, (devices, listed), 0)
    named = jnp.where(place_at == place, 1.0, 0.0)
    sender = lax.broadcasted_iota(jnp.int32, (listed, listed), 0)
    reader = lax.broadcasted_iota(jnp.int32, (listed, listed), 1)
    before = jnp.where(sender < reader, 1.0, 0.0).astype(jnp.bfloat16)
    counted = jnp.dot(named.astype(jnp.bfloat16), before, preferred_element_type=jnp.float32)
    rank = jnp.sum(counted * named, axis=0, keepdims=True).astype(jnp.int32)
    target = jnp.where(live, place * per_owner + rank, -1)
    target_at = lax.broadcasted_iota(jnp.int32, (devices * per_owner, listed), 0)
    chosen = jnp.where(target_at == target, 1.0, 0.0).astype(jnp.bfloat16)
    fetches[1].wait()
    sends = []

    def send(start, rows):
        part = pl.ds(start, rows)
        copy = pltpu.make_async_copy(
            made.at[:, part], out.at[:, part], out_sems.at[len(sends)]
        )
        copy.start()
        sends.append(copy)

    if with_slots:
        stated = lists[1] + 1
        lane = rank + (place_of(me[0], count_gl) & (128 // per_owner - 1)) * per_owner
        lane_at = lax.broadcasted_iota(jnp.int32, (128, listed), 0)
        ranked = jnp.where(lane_at == lane, 1.0, 0.0).astype(jnp.bfloat16)
        coarse = (named * (stated >> 5).astype(jnp.float32)).astype(jnp.bfloat16)
        fine = (named * (stated & 31).astype(jnp.float32)).astype(jnp.bfloat16)
        slots = 32.0 * dot_rows(coarse, ranked) + dot_rows(fine, ranked)
        start = 2 * len(comps) * per_owner
        made[:, start:, :] = jnp.broadcast_to(slots[:, None, :], (devices, 8, 128))
        send(start, 8)
    for i in range(len(comps)):
        fetches[2 + i].wait()
        for r in range(2):
            parts = jnp.concatenate(split_three(held[i, r]), axis=1)
            got = jnp.dot(chosen, parts, preferred_element_type=jnp.float32)
            whole = (got[:, :128] + got[:, 128:256]) + got[:, 256:]
            start = (2 * i + r) * per_owner
            made[:, start : start + per_owner, :] = whole.reshape(devices, per_owner, 128)
            send(start, per_owner)
    for copy in sends:
        copy.wait()


def pack(tiles, comps, owner_row, slot_row, count, me, after, devices, count_gl, per_owner):
    listed = tiles.shape[2]
    with_slots = after is None
    rows = 2 * len(comps) * per_owner + (8 if with_slots else 0)
    extra = () if with_slots else (after,)
    return pl.pallas_call(
        functools.partial(pack_kernel, devices, count_gl, per_owner, comps, with_slots),
        out_shape=pltpu.HBM((devices, rows, 128), jnp.float32),
        in_specs=[pl.BlockSpec(memory_space=pltpu.SMEM)] * 2
        + [pl.BlockSpec(memory_space=pltpu.HBM)] * (3 + len(extra)),
        out_specs=pl.BlockSpec(memory_space=pltpu.HBM),
        scratch_shapes=[
            pltpu.VMEM((len(comps), 2, listed, 128), jnp.float32),
            pltpu.VMEM((devices, rows, 128), jnp.float32),
            pltpu.VMEM((2, 1, listed), jnp.int32),
            pltpu.SemaphoreType.DMA((2 + len(comps),)),
            pltpu.SemaphoreType.DMA((1 + 2 * len(comps),)),
        ],
        compiler_params=params(24),
        cost_estimate=cost(
            devices * per_owner * listed * 768 * 2 * len(comps), devices * rows * 1024
        ),
    )(count, me, *[in_hbm(a) for a in (owner_row, slot_row, tiles, *extra)])


def complex_table(cos_part, sin_part):
    return np.concatenate(
        [
            np.concatenate([cos_part, sin_part], axis=1),
            np.concatenate([-sin_part, cos_part], axis=1),
        ]
    ).astype(np.float32)


def slab_kernel(count, x_local, blocks, per_owner, first, table, twist, data, *refs):
    if first:
        out, landings, made, slab, turned, out_sems = refs
    else:
        landings, out, made, slab, turned, out_sems = refs
    devices = data.shape[0]
    entries = devices * per_owner
    group = 128 // x_local
    pairs = blocks // group
    shift = blocks.bit_length() - 1
    if first:
        every = 128 // per_owner
        stated = [
            sum([data[o, data.shape[1] - 8 :][:1] for o in range(start, start + every)])
            for start in range(0, devices, every)
        ]
        slot = jnp.concatenate(stated, axis=1).astype(jnp.int32) - 1
        landing = jnp.where(slot >= 0, (slot & (blocks - 1)) * x_local + (slot >> shift), -1)
        landings[...] = landing
    else:
        landing = landings[...]
    parts = []
    for i in range(2 * count):
        one = data[:, i * per_owner : (i + 1) * per_owner, :]
        parts.extend(split_two(one.reshape(entries, 128)))
    parts = jnp.concatenate(parts, axis=1)
    for start in range(0, blocks * x_local, 256):
        place = start + lax.broadcasted_iota(jnp.int32, (256, entries), 0)
        chosen = jnp.where(place == landing, 1.0, 0.0).astype(jnp.bfloat16)
        got = jnp.dot(chosen, parts, preferred_element_type=jnp.float32)
        for i in range(2 * count):
            slab[i // 2, i % 2, start : start + 256, :] = (
                got[:, 256 * i : 256 * i + 128] + got[:, 256 * i + 128 : 256 * i + 256]
            )
    sends = []
    for index in range(count):

        @pl.loop(0, x_local // 8)
        def _(step):
            at = pl.multiple_of(step * 8, 8)
            values = [
                tuple(slab[index, r, pl.ds(t * x_local + at, 8), :] for r in range(2))
                for t in range(blocks)
            ]
            waves = flat_fft(values, times_pair)
            for k in range(blocks):
                real, imag = waves[k]
                cos_k, sin_k = twist[0, k : k + 1, :], twist[1, k : k + 1, :]
                rows = pl.ds(((k % pairs) * group + k // pairs) * x_local + at, 8)
                turned[rows, :128] = real * cos_k + imag * sin_k
                turned[rows, 128:] = imag * cos_k - real * sin_k

        for start in range(0, pairs, 2):
            moved = dot_rows_split(table[...], turned[start * 128 : (start + 2) * 128, :])
            for k in range(2):
                for r in range(2):
                    rows = pl.ds(r * pairs + start + k, 128, stride=2 * pairs)
                    made[index, rows, :] = moved[
                        r * 128 : (r + 1) * 128, k * 128 : (k + 1) * 128
                    ]
        send = pltpu.make_async_copy(
            made.at[index].reshape(devices, made.shape[1] // devices, 128),
            out.at[:, index],
            out_sems.at[index],
        )
        send.start()
        sends.append(send)
    for send in sends:
        send.wait()


def slab_waves(data, landings, x_local, blocks, count_gl, per_owner):
    devices = data.shape[0]
    count = data.shape[1] // (2 * per_owner)
    first = landings is None
    fine = angles(128, 128, 128)
    order = owner_order(devices, count_gl)
    fine = fine.reshape(devices, 128 // devices, 128)[order].reshape(128, 128)
    table = complex_table(np.cos(fine), np.sin(fine))
    twist_angle = angles(blocks, 128, blocks * 128)
    twist = np.stack([np.cos(twist_angle), np.sin(twist_angle)]).astype(np.float32)
    entries = devices * per_owner
    rows = blocks * x_local * 2
    out = pltpu.HBM((devices, count, rows // devices, 128), jnp.float32)
    landing = jax.ShapeDtypeStruct((1, entries), jnp.int32)
    in_place = pl.BlockSpec(memory_space=pltpu.VMEM)
    return pl.pallas_call(
        functools.partial(slab_kernel, count, x_local, blocks, per_owner, first),
        out_shape=(out, landing) if first else out,
        in_specs=[in_place] * (3 if first else 4),
        out_specs=(
            (pl.BlockSpec(memory_space=pltpu.HBM), in_place)
            if first
            else pl.BlockSpec(memory_space=pltpu.HBM)
        ),
        scratch_shapes=[
            pltpu.VMEM((count, rows, 128), jnp.float32),
            pltpu.VMEM((count, 2, blocks * x_local, 128), jnp.float32),
            pltpu.VMEM((blocks * x_local, 256), jnp.float32),
            pltpu.SemaphoreType.DMA((count,)),
        ],
        compiler_params=params(24),
        cost_estimate=cost(
            count * blocks * x_local * (entries * 1024 + 512 * 1024),
            count * (entries * 1024 + rows * 512),
        ),
    )(jnp.asarray(table), jnp.asarray(twist), in_vmem(data), *(() if first else (landings,)))


def choose(options, mask_of):
    made = options[0]
    for i in range(1, len(options)):
        made = jnp.where(mask_of(i), options[i], made)
    return made


def x_steps(
    devices, x_local, y_local, blocks, order, index, twist, table, data, turned, columns, store
):
    group = 128 // x_local
    pairs = blocks // group
    kept = y_local // blocks
    narrow = kept * pairs
    banks = 2 * group

    @pl.loop(0, kept)
    def _(step):
        at = pl.multiple_of(step * 2 * pairs, 2 * pairs)
        values = [
            tuple(
                data[order.index(o), index, pl.ds(at + r * pairs, pairs), :] for r in range(2)
            )
            for o in range(devices)
        ]
        waves = flat_fft(values, times_pair)
        rows = pl.ds(pl.multiple_of(step * pairs, pairs), pairs)
        for k in range(devices):
            real, imag = waves[k]
            cos_k, sin_k = twist[0, k : k + 1, :], twist[1, k : k + 1, :]
            turned[k, rows, :128] = real * cos_k + imag * sin_k
            turned[k, rows, 128:] = imag * cos_k - real * sin_k

    lane = lax.broadcasted_iota(jnp.int32, (1, 128), 1)
    square = banks * narrow == 128 and 128 // narrow == banks
    together = min(devices, 256 // narrow)
    for start in range(0, devices, together):
        stacked = turned[start : start + together].reshape(together * narrow, 256)
        moved = dot_rows_split(table[...], stacked)
        if square:
            for base in range(0, together, banks):
                rolled = []
                for bank in range(banks):
                    one = moved[bank * x_local : (bank + 1) * x_local, base * narrow :][:, :128]
                    rolled.append(pltpu.roll(one, bank * narrow, 1) if bank else one)
                for k in range(banks):
                    options = [rolled[(place - k) % banks] for place in range(banks)]
                    rows = pl.ds(start + base + k, x_local, stride=devices)
                    columns[rows, :] = choose(options, lambda i: lane // narrow == i)
        else:
            for k in range(together):
                one = jnp.concatenate(
                    [
                        moved[bank * x_local : (bank + 1) * x_local, k * narrow : (k + 1) * narrow]
                        for bank in range(banks)
                    ],
                    axis=1,
                )
                columns[pl.ds(start + k, x_local, stride=devices), :] = one
    for start in range(0, devices * x_local, 128):
        block = columns[start : start + 128, :].T
        pieces = [block[bank * narrow : (bank + 1) * narrow] for bank in range(banks)]
        for bank in range(banks):
            one = pieces[bank]
            if square:
                options = [pieces[(bank + k) % banks] for k in range(banks)]
                one = choose(options, lambda i: lane % banks == i)
            for step in range(kept):
                row = step * blocks + (bank % group) * pairs
                store(bank // group, row, start, one[step * pairs : (step + 1) * pairs])


def x_kernel(devices, x_local, y_local, blocks, order, index, twist, table, data, out, *scratch):
    made, out_sem = scratch[:2]

    def store(r, row, start, block):
        made[r, row : row + block.shape[0], start : start + 128] = block

    x_steps(
        devices, x_local, y_local, blocks, order, index, twist, table, data, *scratch[2:], store
    )
    send = pltpu.make_async_copy(made, out, out_sem)
    send.start()
    send.wait()


def last_kernel(devices, x_local, y_local, blocks, order, index, twist, table, data, *refs):
    green, first, second, out = refs[:4]
    scratch, (tensor, kept, made, in_sems, out_sems) = refs[4:6], refs[6:]
    x_cells = devices * x_local
    pieces = made.shape[0]
    width = x_cells // pieces
    fetches = [
        pltpu.make_async_copy(first, kept.at[0], in_sems.at[0]),
        pltpu.make_async_copy(second, kept.at[1], in_sems.at[1]),
        pltpu.make_async_copy(green, tensor, in_sems.at[2]),
    ]
    for fetch in fetches:
        fetch.start()

    def store(r, row, start, block):
        kept[2, r, row : row + block.shape[0], start : start + 128] = block

    x_steps(
        devices, x_local, y_local, blocks, order, index, twist, table, data, *scratch, store
    )
    for fetch in fetches:
        fetch.wait()
    sends = []
    for piece in range(pieces):

        @pl.loop(0, y_local // 8)
        def _(step):
            rows = pl.ds(pl.multiple_of(step * 8, 8), 8)
            columns = pl.ds(piece * width, width)
            waves = [(kept[c, 0, rows, columns], kept[c, 1, rows, columns]) for c in range(3)]
            sums = [[None, None] for _ in range(3)]
            for entry in range(6):
                green_real = tensor[0, entry, rows, columns]
                green_imag = tensor[1, entry, rows, columns]
                for row in range(3):
                    for col in range(3):
                        if pair_index[row][col] != entry:
                            continue
                        real, imag = waves[col]
                        real_term = green_real * real - green_imag * imag
                        imag_term = green_real * imag + green_imag * real
                        old = sums[row]
                        sums[row] = [
                            real_term if old[0] is None else old[0] + real_term,
                            imag_term if old[1] is None else old[1] + imag_term,
                        ]
            for row in range(3):
                made[piece, 0, row, rows, :] = sums[row][0]
                made[piece, 1, row, rows, :] = sums[row][1]

        send = pltpu.make_async_copy(
            made.at[piece],
            out.at[:, :, :, pl.ds(piece * width, width)],
            out_sems.at[piece],
        )
        send.start()
        sends.append(send)
    for send in sends:
        send.wait()


def x_tables(devices, x_local, y_cells):
    x_cells = devices * x_local
    group = 128 // x_local
    fine = angles(x_local, x_local, x_local)
    scale = 1.0 / math.sqrt(x_cells * y_cells)
    apart = np.eye(group) * scale
    table = complex_table(np.kron(apart, np.cos(fine)), np.kron(apart, np.sin(fine)))
    angle = np.tile(angles(devices, x_local, x_cells), (1, group))
    twist = np.stack([np.cos(angle), np.sin(angle)]).astype(np.float32)
    return jnp.asarray(twist), jnp.asarray(table)


def x_scratch(devices, x_local, y_local):
    return [
        pltpu.VMEM((devices, y_local * x_local // 128, 256), jnp.float32),
        pltpu.VMEM((devices * x_local, 2 * y_local), jnp.float32),
    ]


def x_waves(index, data, devices, x_local, y_local, y_cells, count_gl):
    x_cells = devices * x_local
    order = owner_order(devices, count_gl)
    return pl.pallas_call(
        functools.partial(x_kernel, devices, x_local, y_local, y_cells // 128, order, index),
        out_shape=pltpu.HBM((2, y_local, x_cells), jnp.float32),
        in_specs=[pl.BlockSpec(memory_space=pltpu.VMEM)] * 3,
        out_specs=pl.BlockSpec(memory_space=pltpu.HBM),
        scratch_shapes=[
            pltpu.VMEM((2, y_local, x_cells), jnp.float32),
            pltpu.SemaphoreType.DMA(()),
        ]
        + x_scratch(devices, x_local, y_local),
        compiler_params=params(24),
        cost_estimate=cost(x_cells * y_local * x_local * 24, x_cells * y_local * 16),
    )(*x_tables(devices, x_local, y_cells), in_vmem(data))


def last_waves(index, data, green, first, second, devices, x_local, y_local, y_cells, count_gl):
    x_cells = devices * x_local
    order = owner_order(devices, count_gl)
    pieces = 8
    return pl.pallas_call(
        functools.partial(last_kernel, devices, x_local, y_local, y_cells // 128, order, index),
        out_shape=pltpu.HBM((2, 3, y_local, x_cells), jnp.float32),
        in_specs=[pl.BlockSpec(memory_space=pltpu.VMEM)] * 3
        + [pl.BlockSpec(memory_space=pltpu.HBM)] * 3,
        out_specs=pl.BlockSpec(memory_space=pltpu.HBM),
        scratch_shapes=x_scratch(devices, x_local, y_local)
        + [
            pltpu.VMEM((2, 6, y_local, x_cells), jnp.float32),
            pltpu.VMEM((3, 2, y_local, x_cells), jnp.float32),
            pltpu.VMEM((pieces, 2, 3, y_local, x_cells // pieces), jnp.float32),
            pltpu.SemaphoreType.DMA((3,)),
            pltpu.SemaphoreType.DMA((pieces,)),
        ],
        compiler_params=params(40),
        cost_estimate=cost(x_cells * y_local * (x_local * 24 + 72), x_cells * y_local * 96),
    )(
        *x_tables(devices, x_local, y_cells),
        in_vmem(data),
        *[in_hbm(a) for a in (green, first, second)],
    )


def gate_kernel(data, after, out):
    del data, after, out


def once_after(data, after):
    return pl.pallas_call(
        gate_kernel,
        out_shape=pltpu.HBM(data.shape, data.dtype),
        in_specs=[pl.BlockSpec(memory_space=pltpu.HBM), pl.BlockSpec(memory_space=pl.ANY)],
        out_specs=pl.BlockSpec(memory_space=pltpu.HBM),
        input_output_aliases={0: 0},
        compiler_params=params(1),
        cost_estimate=cost(0, 0),
    )(in_hbm(data), after)


def exchange(data):
    return lax.all_to_all(data, ("gx", "gl", "gz"), split_axis=0, concat_axis=0, tiled=True)


def per_device(tiles, tile_owner, tile_slot, tile_count, green):
    count_gl = lax.axis_size("gl")
    devices = lax.axis_size("gx") * 4 * count_gl
    tile_total, tile_len = tiles.shape[2], tiles.shape[3]
    planes, y_local, x_cells = green.shape[2:]
    y_cells = y_local * devices
    x_local = x_cells // devices
    blocks = y_cells // tile_len
    per_owner = max(2, 2 * tile_total // devices)
    assert planes == 1 and tile_len == 128
    owner_row, slot_row = tile_owner.reshape(1, tile_total), tile_slot.reshape(1, tile_total)
    green = green.reshape(2, 6, y_local, x_cells)
    me = (lax.axis_index("gx") * 4 + lax.axis_index("gz")) * count_gl + lax.axis_index("gl")
    lists = (owner_row, slot_row, tile_count, me.reshape(1).astype(jnp.int32))
    early = pack(tiles, (0, 1), *lists, None, devices, count_gl, per_owner)
    late = pack(tiles, (2,), *lists, early, devices, count_gl, per_owner)
    early = exchange(early)
    late = exchange(once_after(late, early))
    grid = (x_local, blocks, count_gl, per_owner)
    early, landings = slab_waves(early, None, *grid)
    early = exchange(once_after(early, late))
    late = slab_waves(late, landings, *grid)
    late = exchange(once_after(late, early))
    sizes = (devices, x_local, y_local, y_cells, count_gl)
    waves = [x_waves(comp, early, *sizes) for comp in range(2)]
    mixed = last_waves(0, late, green, *waves, *sizes)
    return mixed.reshape(2, 3, planes, y_local, x_cells)


def solution(mesh):
    count_gx, count_gy = mesh.devices.shape
    fine_mesh = jax.sharding.Mesh(
        mesh.devices.reshape(count_gx, 4, count_gy // 4), ("gx", "gz", "gl")
    )
    every = ("gx", "gz", "gl")
    in_specs = (
        P(None, None, every, None),
        P(every, None),
        P(every),
        P(every),
        P(None, None, None, every, None),
    )
    out_specs = P(None, None, None, every, None)
    return jax.shard_map(
        per_device, mesh=fine_mesh, in_specs=in_specs, out_specs=out_specs, check_vma=False
    )
```

```python
import functools
import math

import jax
import jax.numpy as jnp
import ml_dtypes
import numpy as np
from jax import lax
from jax.experimental import pallas as pl
from jax.experimental.pallas import tpu as pltpu
from jax.sharding import PartitionSpec as P

pair_index = ((0, 3, 4), (3, 1, 5), (4, 5, 2))
by_rows = (((1,), (1,)), ((), ()))


def params(mebibytes):
    return pltpu.CompilerParams(vmem_limit_bytes=mebibytes * 1024 * 1024)


def in_hbm(array):
    return pltpu.with_memory_space_constraint(array, pltpu.HBM)


def in_vmem(array):
    return pltpu.with_memory_space_constraint(array, pltpu.VMEM)


def cost(flops, moved):
    return pl.CostEstimate(flops=flops, bytes_accessed=moved, transcendentals=0)


def angles(rows, columns, length):
    products = np.outer(np.arange(rows), np.arange(columns)) % length
    return 2.0 * math.pi / length * products


def halves(table):
    wide = np.asarray(table, np.float32)
    high = wide.astype(ml_dtypes.bfloat16)
    low = (wide - high.astype(np.float32)).astype(ml_dtypes.bfloat16)
    return jnp.asarray(high), jnp.asarray(low)


def split_two(data):
    high = data.astype(jnp.bfloat16)
    return high, (data - high.astype(jnp.float32)).astype(jnp.bfloat16)


def split_three(data):
    high = data.astype(jnp.bfloat16)
    rest = data - high.astype(jnp.float32)
    middle = rest.astype(jnp.bfloat16)
    return high, middle, (rest - middle.astype(jnp.float32)).astype(jnp.bfloat16)


def dot_rows(left, right):
    return lax.dot_general(left, right, by_rows, preferred_element_type=jnp.float32)


def dot_rows_split(table, data):
    rows, depth = table.shape
    table_high, table_low = split_two(table)
    high, low = split_two(data)
    if depth > 128:
        both = dot_rows(jnp.concatenate([table_high, table_low]), high)
        return both[:rows] + both[rows:] + dot_rows(table_high, low)
    left = jnp.concatenate(
        [
            jnp.concatenate([table_high, table_high], axis=1),
            jnp.concatenate([table_low, jnp.zeros_like(table_low)], axis=1),
        ]
    )
    both = dot_rows(left, jnp.concatenate([high, low], axis=1))
    return both[:rows] + both[rows:]


def flat_fft(values, times):
    length = len(values)
    if length == 1:
        return values
    even = flat_fft(values[0::2], times)
    odd = flat_fft(values[1::2], times)
    lower, upper = [], []
    for k in range(length // 2):
        turned = times(odd[k], k, length)
        lower.append(jax.tree.map(lambda a, b: a + b, even[k], turned))
        upper.append(jax.tree.map(lambda a, b: a - b, even[k], turned))
    return lower + upper


def times_pair(value, k, length):
    real, imag = value
    if k == 0:
        return value
    if 4 * k == length:
        return (imag, -real)
    cos_k = math.cos(2.0 * math.pi * k / length)
    sin_k = math.sin(2.0 * math.pi * k / length)
    return (real * cos_k + imag * sin_k, imag * cos_k - real * sin_k)


def place_of(owner, count_gl):
    shift = count_gl.bit_length() - 1
    z = (owner >> shift) & 3
    return (((owner >> (shift + 2)) << shift) + (owner & (count_gl - 1))) * 4 + z


def owner_order(devices, count_gl):
    order = [0] * devices
    for owner in range(devices):
        order[place_of(owner, count_gl)] = owner
    return order


def pack_kernel(
    devices, count_gl, per_owner, comps, with_slots, count, owner_row, slot_row, tiles, *refs
):
    held, made, lists, sems, out_sems = refs[-5:]
    out = refs[0] if with_slots else refs[1]
    listed = owner_row.shape[1]
    fetches = [
        pltpu.make_async_copy(owner_row, lists.at[0], sems.at[0]),
        pltpu.make_async_copy(slot_row, lists.at[1], sems.at[1]),
    ]
    fetches += [
        pltpu.make_async_copy(tiles.at[:, comp], held.at[i], sems.at[2 + i])
        for i, comp in enumerate(comps)
    ]
    for fetch in fetches:
        fetch.start()
    sender = lax.broadcasted_iota(jnp.int32, (listed, listed), 0)
    reader = lax.broadcasted_iota(jnp.int32, (listed, listed), 1)
    before = jnp.where(sender < reader, 1.0, 0.0).astype(jnp.bfloat16)
    live = lax.broadcasted_iota(jnp.int32, (1, listed), 1) < count[0]
    fetches[0].wait()
    place = jnp.where(live, place_of(lists[0], count_gl), -1)
    place_at = lax.broadcasted_iota(jnp.int32, (devices, listed), 0)
    named = jnp.where(place_at == place, 1.0, 0.0)
    counted = jnp.dot(named.astype(jnp.bfloat16), before, preferred_element_type=jnp.float32)
    rank = jnp.sum(counted * named, axis=0, keepdims=True).astype(jnp.int32)
    target = jnp.where(live, place * per_owner + rank, -1)
    target_at = lax.broadcasted_iota(jnp.int32, (devices * per_owner, listed), 0)
    chosen = jnp.where(target_at == target, 1.0, 0.0).astype(jnp.bfloat16)
    fetches[1].wait()
    sends = []

    def send(start, rows):
        part = pl.ds(start, rows)
        copy = pltpu.make_async_copy(
            made.at[:, part], out.at[:, part], out_sems.at[len(sends)]
        )
        copy.start()
        sends.append(copy)

    for i in range(len(comps)):
        fetches[2 + i].wait()
        parts = [part for r in range(2) for part in split_two(held[i, r])]
        got = jnp.dot(
            chosen, jnp.concatenate(parts, axis=1), preferred_element_type=jnp.float32
        )
        for r in range(2):
            whole = got[:, 256 * r : 256 * r + 128] + got[:, 256 * r + 128 : 256 * r + 256]
            start = (2 * i + r) * per_owner
            made[:, start : start + per_owner, :] = whole.reshape(devices, per_owner, 128)
            send(start, per_owner)
    if with_slots:
        stated = lists[1] + 1
        every = 128 // per_owner
        lane = jnp.where(live, rank + (place & (every - 1)) * per_owner, -1)
        lane_at = lax.broadcasted_iota(jnp.int32, (128, listed), 0)
        laned = jnp.where(lane_at == lane, 1.0, 0.0).astype(jnp.bfloat16)
        row_at = lax.broadcasted_iota(jnp.int32, (8, listed), 0)
        rowed = jnp.where(row_at == place >> (every.bit_length() - 1), 1.0, 0.0)
        coarse = (rowed * (stated >> 5).astype(jnp.float32)).astype(jnp.bfloat16)
        fine = (rowed * (stated & 31).astype(jnp.float32)).astype(jnp.bfloat16)
        refs[1][...] = 32.0 * dot_rows(coarse, laned) + dot_rows(fine, laned)
    for copy in sends:
        copy.wait()


def pack(tiles, comps, owner_row, slot_row, count, after, devices, count_gl, per_owner):
    listed = tiles.shape[2]
    with_slots = after is None
    rows = 2 * len(comps) * per_owner
    extra = () if with_slots else (after,)
    assert devices * per_owner == 1024
    blocks = pltpu.HBM((devices, rows, 128), jnp.float32)
    blocks_spec = pl.BlockSpec(memory_space=pltpu.HBM)
    slots = jax.ShapeDtypeStruct((8, 128), jnp.float32)
    return pl.pallas_call(
        functools.partial(pack_kernel, devices, count_gl, per_owner, comps, with_slots),
        out_shape=(blocks, slots) if with_slots else blocks,
        in_specs=[pl.BlockSpec(memory_space=pltpu.SMEM)]
        + [pl.BlockSpec(memory_space=pltpu.HBM)] * (3 + len(extra)),
        out_specs=(
            (blocks_spec, pl.BlockSpec(memory_space=pltpu.VMEM)) if with_slots else blocks_spec
        ),
        scratch_shapes=[
            pltpu.VMEM((len(comps), 2, listed, 128), jnp.float32),
            pltpu.VMEM((devices, rows, 128), jnp.float32),
            pltpu.VMEM((2, 1, listed), jnp.int32),
            pltpu.SemaphoreType.DMA((2 + len(comps),)),
            pltpu.SemaphoreType.DMA((2 * len(comps),)),
        ],
        compiler_params=params(24),
        cost_estimate=cost(
            devices * per_owner * listed * 512 * 2 * len(comps), devices * rows * 1024
        ),
    )(count, *[in_hbm(a) for a in (owner_row, slot_row, tiles, *extra)])


def complex_table(cos_part, sin_part):
    return np.concatenate(
        [
            np.concatenate([cos_part, sin_part], axis=1),
            np.concatenate([-sin_part, cos_part], axis=1),
        ]
    ).astype(np.float32)


def slab_kernel(count, x_local, blocks, per_owner, first, table, twist, data, *refs):
    if first:
        me, slots, out, landings, made, slab, turned, out_sems = refs
    else:
        landings, out, made, slab, turned, out_sems = refs
    devices = data.shape[0]
    entries = devices * per_owner
    group = 128 // x_local
    pairs = blocks // group
    shift = blocks.bit_length() - 1
    if first:
        every = 128 // per_owner
        lane = lax.broadcasted_iota(jnp.int32, (1, 128), 1)
        mine = me[0] & (every - 1)
        row = me[0] >> (every.bit_length() - 1)
        stated = []
        for start in range(0, devices, every):
            whole = None
            for i in range(every):
                one = slots[start + i, pl.ds(row, 1), :]
                one = pltpu.roll(one, ((i + every - mine) & (every - 1)) * per_owner, 1)
                whole = one if i == 0 else jnp.where(lane // per_owner == i, one, whole)
            stated.append(whole)
        slot = jnp.concatenate(stated, axis=1).astype(jnp.int32) - 1
        landing = jnp.where(slot >= 0, (slot & (blocks - 1)) * x_local + (slot >> shift), -1)
        landings[...] = landing
    else:
        landing = landings[...]
    parts = []
    for i in range(2 * count):
        one = data[:, i * per_owner : (i + 1) * per_owner, :]
        parts.extend(split_two(one.reshape(entries, 128)))
    parts = jnp.concatenate(parts, axis=1)
    for start in range(0, blocks * x_local, 256):
        place = start + lax.broadcasted_iota(jnp.int32, (256, entries), 0)
        chosen = jnp.where(place == landing, 1.0, 0.0).astype(jnp.bfloat16)
        got = jnp.dot(chosen, parts, preferred_element_type=jnp.float32)
        for i in range(2 * count):
            slab[i // 2, i % 2, start : start + 256, :] = (
                got[:, 256 * i : 256 * i + 128] + got[:, 256 * i + 128 : 256 * i + 256]
            )
    sends = []
    for index in range(count):

        @pl.loop(0, x_local // 8)
        def _(step):
            at = pl.multiple_of(step * 8, 8)
            values = [
                tuple(slab[index, r, pl.ds(t * x_local + at, 8), :] for r in range(2))
                for t in range(blocks)
            ]
            waves = flat_fft(values, times_pair)
            for k in range(blocks):
                real, imag = waves[k]
                cos_k, sin_k = twist[0, k : k + 1, :], twist[1, k : k + 1, :]
                rows = pl.ds(((k % pairs) * group + k // pairs) * x_local + at, 8)
                turned[rows, :128] = real * cos_k + imag * sin_k
                turned[rows, 128:] = imag * cos_k - real * sin_k

        for start in range(0, pairs, 2):
            moved = dot_rows_split(table[...], turned[start * 128 : (start + 2) * 128, :])
            for k in range(2):
                for r in range(2):
                    rows = pl.ds(r * pairs + start + k, 128, stride=2 * pairs)
                    made[index, rows, :] = moved[
                        r * 128 : (r + 1) * 128, k * 128 : (k + 1) * 128
                    ]
        send = pltpu.make_async_copy(
            made.at[index].reshape(devices, made.shape[1] // devices, 128),
            out.at[:, index],
            out_sems.at[index],
        )
        send.start()
        sends.append(send)
    for send in sends:
        send.wait()


def slab_waves(data, extra, x_local, blocks, count_gl, per_owner):
    devices = data.shape[0]
    count = data.shape[1] // (2 * per_owner)
    first = len(extra) == 2
    fine = angles(128, 128, 128)
    order = owner_order(devices, count_gl)
    fine = fine.reshape(devices, 128 // devices, 128)[order].reshape(128, 128)
    table = complex_table(np.cos(fine), np.sin(fine))
    twist_angle = angles(blocks, 128, blocks * 128)
    twist = np.stack([np.cos(twist_angle), np.sin(twist_angle)]).astype(np.float32)
    entries = devices * per_owner
    rows = blocks * x_local * 2
    out = pltpu.HBM((devices, count, rows // devices, 128), jnp.float32)
    landing = jax.ShapeDtypeStruct((1, entries), jnp.int32)
    in_place = pl.BlockSpec(memory_space=pltpu.VMEM)
    return pl.pallas_call(
        functools.partial(slab_kernel, count, x_local, blocks, per_owner, first),
        out_shape=(out, landing) if first else out,
        in_specs=[in_place] * 3
        + ([pl.BlockSpec(memory_space=pltpu.SMEM), in_place] if first else [in_place]),
        out_specs=(
            (pl.BlockSpec(memory_space=pltpu.HBM), in_place)
            if first
            else pl.BlockSpec(memory_space=pltpu.HBM)
        ),
        scratch_shapes=[
            pltpu.VMEM((count, rows, 128), jnp.float32),
            pltpu.VMEM((count, 2, blocks * x_local, 128), jnp.float32),
            pltpu.VMEM((blocks * x_local, 256), jnp.float32),
            pltpu.SemaphoreType.DMA((count,)),
        ],
        compiler_params=params(24),
        cost_estimate=cost(
            count * blocks * x_local * (entries * 1024 + 512 * 1024),
            count * (entries * 1024 + rows * 512),
        ),
    )(jnp.asarray(table), jnp.asarray(twist), in_vmem(data), *extra)


def choose(options, mask_of):
    made = options[0]
    for i in range(1, len(options)):
        made = jnp.where(mask_of(i), options[i], made)
    return made


def x_steps(
    devices, x_local, y_local, blocks, order, index, twist, table, data, turned, columns, store
):
    group = 128 // x_local
    pairs = blocks // group
    kept = y_local // blocks
    narrow = kept * pairs
    banks = 2 * group

    @pl.loop(0, kept)
    def _(step):
        at = pl.multiple_of(step * 2 * pairs, 2 * pairs)
        values = [
            tuple(
                data[order.index(o), index, pl.ds(at + r * pairs, pairs), :] for r in range(2)
            )
            for o in range(devices)
        ]
        waves = flat_fft(values, times_pair)
        rows = pl.ds(pl.multiple_of(step * pairs, pairs), pairs)
        for k in range(devices):
            real, imag = waves[k]
            cos_k, sin_k = twist[0, k : k + 1, :], twist[1, k : k + 1, :]
            turned[k, rows, :128] = real * cos_k + imag * sin_k
            turned[k, rows, 128:] = imag * cos_k - real * sin_k

    lane = lax.broadcasted_iota(jnp.int32, (1, 128), 1)
    square = banks * narrow == 128 and 128 // narrow == banks
    together = min(devices, 256 // narrow)
    for start in range(0, devices, together):
        stacked = turned[start : start + together].reshape(together * narrow, 256)
        moved = dot_rows_split(table[...], stacked)
        if square:
            for base in range(0, together, banks):
                rolled = []
                for bank in range(banks):
                    one = moved[bank * x_local : (bank + 1) * x_local, base * narrow :][:, :128]
                    rolled.append(pltpu.roll(one, bank * narrow, 1) if bank else one)
                for k in range(banks):
                    options = [rolled[(place - k) % banks] for place in range(banks)]
                    rows = pl.ds(start + base + k, x_local, stride=devices)
                    columns[rows, :] = choose(options, lambda i: lane // narrow == i)
        else:
            for k in range(together):
                one = jnp.concatenate(
                    [
                        moved[bank * x_local : (bank + 1) * x_local, k * narrow : (k + 1) * narrow]
                        for bank in range(banks)
                    ],
                    axis=1,
                )
                columns[pl.ds(start + k, x_local, stride=devices), :] = one
    for start in range(0, devices * x_local, 128):
        block = columns[start : start + 128, :].T
        pieces = [block[bank * narrow : (bank + 1) * narrow] for bank in range(banks)]
        for bank in range(banks):
            one = pieces[bank]
            if square:
                options = [pieces[(bank + k) % banks] for k in range(banks)]
                one = choose(options, lambda i: lane % banks == i)
            for step in range(kept):
                row = step * blocks + (bank % group) * pairs
                store(bank // group, row, start, one[step * pairs : (step + 1) * pairs])


def mix_rows(rows, columns, tensor, waves, sums, terms):
    for row, entry, wave in terms:
        green_real, green_imag = tensor[entry, 0, rows, columns], tensor[entry, 1, rows, columns]
        real, imag = waves[wave][0, rows, columns], waves[wave][1, rows, columns]
        real_term = green_real * real - green_imag * imag
        imag_term = green_real * imag + green_imag * real
        old = sums[row]
        sums[row] = (
            (real_term, imag_term) if old is None else (old[0] + real_term, old[1] + imag_term)
        )
    return sums


def mix_pieces(y_local, width, made, out, out_sems, sums_of):
    sends = []
    for piece in range(made.shape[0]):
        columns = pl.ds(piece * width, width)

        @pl.loop(0, y_local // 8)
        def _(step):
            rows = pl.ds(pl.multiple_of(step * 8, 8), 8)
            for row, pair in enumerate(sums_of(rows, columns)):
                for r in range(2):
                    made[piece, r, row, rows, :] = pair[r]

        send = pltpu.make_async_copy(
            made.at[piece], out.at[:, :, :, columns], out_sems.at[piece]
        )
        send.start()
        sends.append(send)
    for send in sends:
        send.wait()


def fetch_entries(green, tensor, entries, sems):
    fetches = [
        pltpu.make_async_copy(green.at[:, entry], tensor.at[i], sems.at[i])
        for i, entry in enumerate(entries)
    ]
    for fetch in fetches:
        fetch.start()
    return fetches


early_entries, late_entries = (0, 1, 3, 4, 5), (4, 5, 2)


def early_kernel(sizes, twist, table, data, green, out, *scratch):
    y_local, x_cells = green.shape[2:]
    turned, columns, tensor, kept, made, in_sems, out_sems = scratch
    fetches = fetch_entries(green, tensor, early_entries, in_sems)
    for comp in range(2):

        def store(r, row, start, block):
            kept[comp, r, row : row + block.shape[0], start : start + 128] = block

        x_steps(*sizes, comp, twist, table, data, turned, columns, store)
    for fetch in fetches:
        fetch.wait()
    terms = [
        (row, early_entries.index(pair_index[row][comp]), comp)
        for row in range(3)
        for comp in range(2)
    ]
    waves = [kept.at[0], kept.at[1]]

    def sums_of(rows, columns):
        return mix_rows(rows, columns, tensor, waves, [None] * 3, terms)

    mix_pieces(y_local, x_cells // made.shape[0], made, out, out_sems, sums_of)


def last_kernel(sizes, twist, table, data, green, partial, out, *scratch):
    y_local, x_cells = green.shape[2:]
    turned, columns, tensor, kept, held, made, in_sems, out_sems = scratch
    fetches = fetch_entries(green, tensor, late_entries, in_sems)
    fetches.append(pltpu.make_async_copy(partial, held, in_sems.at[len(late_entries)]))
    fetches[-1].start()

    def store(r, row, start, block):
        kept[r, row : row + block.shape[0], start : start + 128] = block

    x_steps(*sizes, 0, twist, table, data, turned, columns, store)
    for fetch in fetches:
        fetch.wait()

    def sums_of(rows, columns):
        sums = [(held[0, row, rows, columns], held[1, row, rows, columns]) for row in range(3)]
        return mix_rows(rows, columns, tensor, [kept], sums, [(row, row, 0) for row in range(3)])

    mix_pieces(y_local, x_cells // made.shape[0], made, out, out_sems, sums_of)


def x_tables(devices, x_local, y_cells):
    x_cells = devices * x_local
    group = 128 // x_local
    fine = angles(x_local, x_local, x_local)
    scale = 1.0 / math.sqrt(x_cells * y_cells)
    apart = np.eye(group) * scale
    table = complex_table(np.kron(apart, np.cos(fine)), np.kron(apart, np.sin(fine)))
    angle = np.tile(angles(devices, x_local, x_cells), (1, group))
    twist = np.stack([np.cos(angle), np.sin(angle)]).astype(np.float32)
    return jnp.asarray(twist), jnp.asarray(table)


def x_scratch(devices, x_local, y_local):
    return [
        pltpu.VMEM((devices, y_local * x_local // 128, 256), jnp.float32),
        pltpu.VMEM((devices * x_local, 2 * y_local), jnp.float32),
    ]


def mixed_waves(data, green, partial, devices, x_local, y_local, y_cells, count_gl):
    x_cells = devices * x_local
    pieces = 8
    sizes = (devices, x_local, y_local, y_cells // 128, owner_order(devices, count_gl))
    first = partial is None
    comps, entries = (2, 5) if first else (1, 3)
    plane = (y_local, x_cells)
    held = [pltpu.VMEM((entries, 2) + plane, jnp.float32)]
    if first:
        held += [pltpu.VMEM((2, 2) + plane, jnp.float32)]
    else:
        held += [
            pltpu.VMEM((2,) + plane, jnp.float32),
            pltpu.VMEM((2, 3) + plane, jnp.float32),
        ]
    operands = (green,) if first else (green, partial)
    return pl.pallas_call(
        functools.partial(early_kernel if first else last_kernel, sizes),
        out_shape=pltpu.HBM((2, 3) + plane, jnp.float32),
        in_specs=[pl.BlockSpec(memory_space=pltpu.VMEM)] * 3
        + [pl.BlockSpec(memory_space=pltpu.HBM)] * len(operands),
        out_specs=pl.BlockSpec(memory_space=pltpu.HBM),
        scratch_shapes=x_scratch(devices, x_local, y_local)
        + held
        + [
            pltpu.VMEM((pieces, 2, 3, y_local, x_cells // pieces), jnp.float32),
            pltpu.SemaphoreType.DMA((5,)),
            pltpu.SemaphoreType.DMA((pieces,)),
        ],
        compiler_params=params(40),
        cost_estimate=cost(
            comps * x_cells * y_local * (x_local * 24 + 24), x_cells * y_local * 64
        ),
    )(
        *x_tables(devices, x_local, y_cells),
        in_vmem(data),
        *[in_hbm(a) for a in operands],
    )


def gate_kernel(data, after, out):
    del data, after, out


def once_after(data, after):
    return pl.pallas_call(
        gate_kernel,
        out_shape=pltpu.HBM(data.shape, data.dtype),
        in_specs=[pl.BlockSpec(memory_space=pltpu.HBM), pl.BlockSpec(memory_space=pl.ANY)],
        out_specs=pl.BlockSpec(memory_space=pltpu.HBM),
        input_output_aliases={0: 0},
        compiler_params=params(1),
        cost_estimate=cost(0, 0),
    )(in_hbm(data), after)


places = ("gx", "gl", "gz")


def exchange(data):
    return lax.all_to_all(data, places, split_axis=0, concat_axis=0, tiled=True)


def per_device(tiles, tile_owner, tile_slot, tile_count, green):
    count_gl = lax.axis_size("gl")
    devices = lax.axis_size("gx") * 4 * count_gl
    tile_total, tile_len = tiles.shape[2], tiles.shape[3]
    planes, y_local, x_cells = green.shape[2:]
    y_cells = y_local * devices
    x_local = x_cells // devices
    blocks = y_cells // tile_len
    per_owner = max(2, 2 * tile_total // devices)
    assert planes == 1 and tile_len == 128
    owner_row, slot_row = tile_owner.reshape(1, tile_total), tile_slot.reshape(1, tile_total)
    green = green.reshape(2, 6, y_local, x_cells)
    me = (lax.axis_index("gx") * count_gl + lax.axis_index("gl")) * 4 + lax.axis_index("gz")
    me = me.reshape(1).astype(jnp.int32)
    lists = (owner_row, slot_row, tile_count)
    early, slots = pack(tiles, (0, 1), *lists, None, devices, count_gl, per_owner)
    late = pack(tiles, (2,), *lists, early, devices, count_gl, per_owner)
    slots = lax.all_gather(slots, places)
    early = exchange(early)
    late = exchange(once_after(late, early))
    grid = (x_local, blocks, count_gl, per_owner)
    early, landings = slab_waves(early, (me, slots), *grid)
    early = exchange(once_after(early, late))
    late = slab_waves(late, (landings,), *grid)
    late = exchange(once_after(late, early))
    sizes = (devices, x_local, y_local, y_cells, count_gl)
    mixed = mixed_waves(early, green, None, *sizes)
    mixed = mixed_waves(late, green, mixed, *sizes)
    return mixed.reshape(2, 3, planes, y_local, x_cells)


def solution(mesh):
    count_gx, count_gy = mesh.devices.shape
    fine_mesh = jax.sharding.Mesh(
        mesh.devices.reshape(count_gx, 4, count_gy // 4), ("gx", "gz", "gl")
    )
    every = ("gx", "gz", "gl")
    in_specs = (
        P(None, None, every, None),
        P(every, None),
        P(every),
        P(every),
        P(None, None, None, every, None),
    )
    out_specs = P(None, None, None, every, None)
    return jax.shard_map(
        per_device, mesh=fine_mesh, in_specs=in_specs, out_specs=out_specs, check_vma=False
    )
```

```python
import functools
import math

import jax
import jax.numpy as jnp
import ml_dtypes
import numpy as np
from jax import lax
from jax.experimental import pallas as pl
from jax.experimental.pallas import tpu as pltpu
from jax.sharding import PartitionSpec as P

pair_index = ((0, 3, 4), (3, 1, 5), (4, 5, 2))
by_rows = (((1,), (1,)), ((), ()))


def params(mebibytes):
    return pltpu.CompilerParams(vmem_limit_bytes=mebibytes * 1024 * 1024)


def in_hbm(array):
    return pltpu.with_memory_space_constraint(array, pltpu.HBM)


def in_vmem(array):
    return pltpu.with_memory_space_constraint(array, pltpu.VMEM)


def cost(flops, moved):
    return pl.CostEstimate(flops=flops, bytes_accessed=moved, transcendentals=0)


def angles(rows, columns, length):
    products = np.outer(np.arange(rows), np.arange(columns)) % length
    return 2.0 * math.pi / length * products


def halves(table):
    wide = np.asarray(table, np.float32)
    high = wide.astype(ml_dtypes.bfloat16)
    low = (wide - high.astype(np.float32)).astype(ml_dtypes.bfloat16)
    return jnp.asarray(high), jnp.asarray(low)


def split_two(data):
    high = data.astype(jnp.bfloat16)
    return high, (data - high.astype(jnp.float32)).astype(jnp.bfloat16)


def split_three(data):
    high = data.astype(jnp.bfloat16)
    rest = data - high.astype(jnp.float32)
    middle = rest.astype(jnp.bfloat16)
    return high, middle, (rest - middle.astype(jnp.float32)).astype(jnp.bfloat16)


def dot_rows(left, right):
    return lax.dot_general(left, right, by_rows, preferred_element_type=jnp.float32)


def dot_rows_split(table, data):
    rows, depth = table.shape
    table_high, table_low = split_two(table)
    high, low = split_two(data)
    if depth > 128:
        both = dot_rows(jnp.concatenate([table_high, table_low]), high)
        return both[:rows] + both[rows:] + dot_rows(table_high, low)
    left = jnp.concatenate(
        [
            jnp.concatenate([table_high, table_high], axis=1),
            jnp.concatenate([table_low, jnp.zeros_like(table_low)], axis=1),
        ]
    )
    both = dot_rows(left, jnp.concatenate([high, low], axis=1))
    return both[:rows] + both[rows:]


def flat_fft(values, times):
    length = len(values)
    if length == 1:
        return values
    even = flat_fft(values[0::2], times)
    odd = flat_fft(values[1::2], times)
    lower, upper = [], []
    for k in range(length // 2):
        turned = times(odd[k], k, length)
        lower.append(jax.tree.map(lambda a, b: a + b, even[k], turned))
        upper.append(jax.tree.map(lambda a, b: a - b, even[k], turned))
    return lower + upper


def times_pair(value, k, length):
    real, imag = value
    if k == 0:
        return value
    if 4 * k == length:
        return (imag, -real)
    cos_k = math.cos(2.0 * math.pi * k / length)
    sin_k = math.sin(2.0 * math.pi * k / length)
    return (real * cos_k + imag * sin_k, imag * cos_k - real * sin_k)


def place_of(owner, count_gl):
    shift = count_gl.bit_length() - 1
    z = ((owner >> shift) & 1) * 2 + ((owner >> (shift + 1)) & 1)
    return (((owner >> (shift + 2)) << shift) + (owner & (count_gl - 1))) * 4 + z


def owner_order(devices, count_gl):
    order = [0] * devices
    for owner in range(devices):
        order[place_of(owner, count_gl)] = owner
    return order


def pack_kernel(
    devices, count_gl, per_owner, comps, with_slots, count, me, owner_row, slot_row, tiles, *refs
):
    out, held, made, lists, sems, out_sems = refs[-6:]
    listed = owner_row.shape[1]
    fetches = [
        pltpu.make_async_copy(owner_row, lists.at[0], sems.at[0]),
        pltpu.make_async_copy(slot_row, lists.at[1], sems.at[1]),
    ]
    fetches += [
        pltpu.make_async_copy(tiles.at[:, comp], held.at[i], sems.at[2 + i])
        for i, comp in enumerate(comps)
    ]
    for fetch in fetches:
        fetch.start()
    sender = lax.broadcasted_iota(jnp.int32, (listed, listed), 0)
    reader = lax.broadcasted_iota(jnp.int32, (listed, listed), 1)
    before = jnp.where(sender < reader, 1.0, 0.0).astype(jnp.bfloat16)
    live = lax.broadcasted_iota(jnp.int32, (1, listed), 1) < count[0]
    fetches[0].wait()
    place = jnp.where(live, place_of(lists[0], count_gl), -1)
    place_at = lax.broadcasted_iota(jnp.int32, (devices, listed), 0)
    named = jnp.where(place_at == place, 1.0, 0.0)
    counted = jnp.dot(named.astype(jnp.bfloat16), before, preferred_element_type=jnp.float32)
    rank = jnp.sum(counted * named, axis=0, keepdims=True).astype(jnp.int32)
    target = jnp.where(live, place * per_owner + rank, -1)
    target_at = lax.broadcasted_iota(jnp.int32, (devices * per_owner, listed), 0)
    chosen = jnp.where(target_at == target, 1.0, 0.0).astype(jnp.bfloat16)
    fetches[1].wait()
    sends = []

    def send(start, rows):
        part = pl.ds(start, rows)
        copy = pltpu.make_async_copy(
            made.at[:, part], out.at[:, part], out_sems.at[len(sends)]
        )
        copy.start()
        sends.append(copy)

    if with_slots:
        stated = lists[1] + 1
        lane = rank + (me[0] & (128 // per_owner - 1)) * per_owner
        lane_at = lax.broadcasted_iota(jnp.int32, (128, listed), 0)
        laned = jnp.where(lane_at == lane, 1.0, 0.0).astype(jnp.bfloat16)
        coarse = (named * (stated >> 5).astype(jnp.float32)).astype(jnp.bfloat16)
        fine = (named * (stated & 31).astype(jnp.float32)).astype(jnp.bfloat16)
        slots = 32.0 * dot_rows(coarse, laned) + dot_rows(fine, laned)
        start = 2 * len(comps) * per_owner
        made[:, start:, :] = jnp.broadcast_to(slots[:, None, :], (devices, 8, 128))
        send(start, 8)
    for i in range(len(comps)):
        fetches[2 + i].wait()
        parts = [part for r in range(2) for part in split_two(held[i, r])]
        got = jnp.dot(
            chosen, jnp.concatenate(parts, axis=1), preferred_element_type=jnp.float32
        )
        for r in range(2):
            whole = got[:, 256 * r : 256 * r + 128] + got[:, 256 * r + 128 : 256 * r + 256]
            start = (2 * i + r) * per_owner
            made[:, start : start + per_owner, :] = whole.reshape(devices, per_owner, 128)
            send(start, per_owner)
    for copy in sends:
        copy.wait()


def pack(tiles, comps, owner_row, slot_row, count, me, after, devices, count_gl, per_owner):
    listed = tiles.shape[2]
    with_slots = after is None
    rows = 2 * len(comps) * per_owner + (8 if with_slots else 0)
    extra = () if with_slots else (after,)
    return pl.pallas_call(
        functools.partial(pack_kernel, devices, count_gl, per_owner, comps, with_slots),
        out_shape=pltpu.HBM((devices, rows, 128), jnp.float32),
        in_specs=[pl.BlockSpec(memory_space=pltpu.SMEM)] * 2
        + [pl.BlockSpec(memory_space=pltpu.HBM)] * (3 + len(extra)),
        out_specs=pl.BlockSpec(memory_space=pltpu.HBM),
        scratch_shapes=[
            pltpu.VMEM((len(comps), 2, listed, 128), jnp.float32),
            pltpu.VMEM((devices, rows, 128), jnp.float32),
            pltpu.VMEM((2, 1, listed), jnp.int32),
            pltpu.SemaphoreType.DMA((2 + len(comps),)),
            pltpu.SemaphoreType.DMA((1 + 2 * len(comps),)),
        ],
        compiler_params=params(24),
        cost_estimate=cost(
            devices * per_owner * listed * 512 * 2 * len(comps), devices * rows * 1024
        ),
    )(count, me, *[in_hbm(a) for a in (owner_row, slot_row, tiles, *extra)])


def complex_table(cos_part, sin_part):
    return np.concatenate(
        [
            np.concatenate([cos_part, sin_part], axis=1),
            np.concatenate([-sin_part, cos_part], axis=1),
        ]
    ).astype(np.float32)


def slab_kernel(count, x_local, blocks, per_owner, first, table, twist, data, *refs):
    if first:
        out, landings, made, slab, turned, out_sems = refs
    else:
        landings, out, made, slab, turned, out_sems = refs
    devices = data.shape[0]
    entries = devices * per_owner
    group = 128 // x_local
    pairs = blocks // group
    shift = blocks.bit_length() - 1
    if first:
        every = 128 // per_owner
        stated = [
            sum([data[o, data.shape[1] - 8 :][:1] for o in range(start, start + every)])
            for start in range(0, devices, every)
        ]
        slot = jnp.concatenate(stated, axis=1).astype(jnp.int32) - 1
        landing = jnp.where(slot >= 0, (slot & (blocks - 1)) * x_local + (slot >> shift), -1)
        landings[...] = landing
    else:
        landing = landings[...]
    parts = []
    for i in range(2 * count):
        one = data[:, i * per_owner : (i + 1) * per_owner, :]
        parts.extend(split_two(one.reshape(entries, 128)))
    parts = jnp.concatenate(parts, axis=1)
    for start in range(0, blocks * x_local, 256):
        place = start + lax.broadcasted_iota(jnp.int32, (256, entries), 0)
        chosen = jnp.where(place == landing, 1.0, 0.0).astype(jnp.bfloat16)
        got = jnp.dot(chosen, parts, preferred_element_type=jnp.float32)
        for i in range(2 * count):
            slab[i // 2, i % 2, start : start + 256, :] = (
                got[:, 256 * i : 256 * i + 128] + got[:, 256 * i + 128 : 256 * i + 256]
            )
    sends = []
    for index in range(count):

        @pl.loop(0, x_local // 8)
        def _(step):
            at = pl.multiple_of(step * 8, 8)
            values = [
                tuple(slab[index, r, pl.ds(t * x_local + at, 8), :] for r in range(2))
                for t in range(blocks)
            ]
            waves = flat_fft(values, times_pair)
            for k in range(blocks):
                real, imag = waves[k]
                cos_k, sin_k = twist[0, k : k + 1, :], twist[1, k : k + 1, :]
                rows = pl.ds(((k % pairs) * group + k // pairs) * x_local + at, 8)
                turned[rows, :128] = real * cos_k + imag * sin_k
                turned[rows, 128:] = imag * cos_k - real * sin_k

        for start in range(0, pairs, 2):
            moved = dot_rows_split(table[...], turned[start * 128 : (start + 2) * 128, :])
            for k in range(2):
                for r in range(2):
                    rows = pl.ds(r * pairs + start + k, 128, stride=2 * pairs)
                    made[index, rows, :] = moved[
                        r * 128 : (r + 1) * 128, k * 128 : (k + 1) * 128
                    ]
        send = pltpu.make_async_copy(
            made.at[index].reshape(devices, made.shape[1] // devices, 128),
            out.at[:, index],
            out_sems.at[index],
        )
        send.start()
        sends.append(send)
    for send in sends:
        send.wait()


def slab_waves(data, landings, x_local, blocks, count_gl, per_owner):
    devices = data.shape[0]
    count = data.shape[1] // (2 * per_owner)
    first = landings is None
    fine = angles(128, 128, 128)
    order = owner_order(devices, count_gl)
    fine = fine.reshape(devices, 128 // devices, 128)[order].reshape(128, 128)
    table = complex_table(np.cos(fine), np.sin(fine))
    twist_angle = angles(blocks, 128, blocks * 128)
    twist = np.stack([np.cos(twist_angle), np.sin(twist_angle)]).astype(np.float32)
    entries = devices * per_owner
    rows = blocks * x_local * 2
    out = pltpu.HBM((devices, count, rows // devices, 128), jnp.float32)
    landing = jax.ShapeDtypeStruct((1, entries), jnp.int32)
    in_place = pl.BlockSpec(memory_space=pltpu.VMEM)
    return pl.pallas_call(
        functools.partial(slab_kernel, count, x_local, blocks, per_owner, first),
        out_shape=(out, landing) if first else out,
        in_specs=[in_place] * (3 if first else 4),
        out_specs=(
            (pl.BlockSpec(memory_space=pltpu.HBM), in_place)
            if first
            else pl.BlockSpec(memory_space=pltpu.HBM)
        ),
        scratch_shapes=[
            pltpu.VMEM((count, rows, 128), jnp.float32),
            pltpu.VMEM((count, 2, blocks * x_local, 128), jnp.float32),
            pltpu.VMEM((blocks * x_local, 256), jnp.float32),
            pltpu.SemaphoreType.DMA((count,)),
        ],
        compiler_params=params(24),
        cost_estimate=cost(
            count * blocks * x_local * (entries * 1024 + 512 * 1024),
            count * (entries * 1024 + rows * 512),
        ),
    )(jnp.asarray(table), jnp.asarray(twist), in_vmem(data), *(() if first else (landings,)))


def choose(options, mask_of):
    made = options[0]
    for i in range(1, len(options)):
        made = jnp.where(mask_of(i), options[i], made)
    return made


def x_steps(
    devices, x_local, y_local, blocks, order, index, twist, table, data, turned, columns, store
):
    group = 128 // x_local
    pairs = blocks // group
    kept = y_local // blocks
    narrow = kept * pairs
    banks = 2 * group

    @pl.loop(0, kept)
    def _(step):
        at = pl.multiple_of(step * 2 * pairs, 2 * pairs)
        values = [
            tuple(
                data[order.index(o), index, pl.ds(at + r * pairs, pairs), :] for r in range(2)
            )
            for o in range(devices)
        ]
        waves = flat_fft(values, times_pair)
        rows = pl.ds(pl.multiple_of(step * pairs, pairs), pairs)
        for k in range(devices):
            real, imag = waves[k]
            cos_k, sin_k = twist[0, k : k + 1, :], twist[1, k : k + 1, :]
            turned[k, rows, :128] = real * cos_k + imag * sin_k
            turned[k, rows, 128:] = imag * cos_k - real * sin_k

    lane = lax.broadcasted_iota(jnp.int32, (1, 128), 1)
    square = banks * narrow == 128 and 128 // narrow == banks
    together = min(devices, 256 // narrow)
    for start in range(0, devices, together):
        stacked = turned[start : start + together].reshape(together * narrow, 256)
        moved = dot_rows_split(table[...], stacked)
        if square:
            for base in range(0, together, banks):
                rolled = []
                for bank in range(banks):
                    one = moved[bank * x_local : (bank + 1) * x_local, base * narrow :][:, :128]
                    rolled.append(pltpu.roll(one, bank * narrow, 1) if bank else one)
                for k in range(banks):
                    options = [rolled[(place - k) % banks] for place in range(banks)]
                    rows = pl.ds(start + base + k, x_local, stride=devices)
                    columns[rows, :] = choose(options, lambda i: lane // narrow == i)
        else:
            for k in range(together):
                one = jnp.concatenate(
                    [
                        moved[bank * x_local : (bank + 1) * x_local, k * narrow : (k + 1) * narrow]
                        for bank in range(banks)
                    ],
                    axis=1,
                )
                columns[pl.ds(start + k, x_local, stride=devices), :] = one
    for start in range(0, devices * x_local, 128):
        block = columns[start : start + 128, :].T
        pieces = [block[bank * narrow : (bank + 1) * narrow] for bank in range(banks)]
        for bank in range(banks):
            one = pieces[bank]
            if square:
                options = [pieces[(bank + k) % banks] for k in range(banks)]
                one = choose(options, lambda i: lane % banks == i)
            for step in range(kept):
                row = step * blocks + (bank % group) * pairs
                store(bank // group, row, start, one[step * pairs : (step + 1) * pairs])


def mix_rows(rows, columns, tensor, waves, sums, terms):
    for row, entry, wave in terms:
        green_real, green_imag = tensor[entry, 0, rows, columns], tensor[entry, 1, rows, columns]
        real, imag = waves[wave][0, rows, columns], waves[wave][1, rows, columns]
        real_term = green_real * real - green_imag * imag
        imag_term = green_real * imag + green_imag * real
        old = sums[row]
        sums[row] = (
            (real_term, imag_term) if old is None else (old[0] + real_term, old[1] + imag_term)
        )
    return sums


def mix_pieces(y_local, width, made, out, out_sems, sums_of):
    sends = []
    for piece in range(made.shape[0]):
        columns = pl.ds(piece * width, width)

        @pl.loop(0, y_local // 8)
        def _(step):
            rows = pl.ds(pl.multiple_of(step * 8, 8), 8)
            for row, pair in enumerate(sums_of(rows, columns)):
                for r in range(2):
                    made[piece, r, row, rows, :] = pair[r]

        send = pltpu.make_async_copy(
            made.at[piece], out.at[:, :, :, columns], out_sems.at[piece]
        )
        send.start()
        sends.append(send)
    for send in sends:
        send.wait()


def fetch_entries(green, tensor, entries, sems):
    fetches = [
        pltpu.make_async_copy(green.at[:, entry], tensor.at[i], sems.at[i])
        for i, entry in enumerate(entries)
    ]
    for fetch in fetches:
        fetch.start()
    return fetches


early_entries, late_entries = (0, 1, 3, 4, 5), (4, 5, 2)


def early_kernel(sizes, twist, table, data, green, out, *scratch):
    y_local, x_cells = green.shape[2:]
    turned, columns, tensor, kept, made, in_sems, out_sems = scratch
    fetches = fetch_entries(green, tensor, early_entries, in_sems)
    for comp in range(2):

        def store(r, row, start, block):
            kept[comp, r, row : row + block.shape[0], start : start + 128] = block

        x_steps(*sizes, comp, twist, table, data, turned, columns, store)
    for fetch in fetches:
        fetch.wait()
    terms = [
        (row, early_entries.index(pair_index[row][comp]), comp)
        for row in range(3)
        for comp in range(2)
    ]
    waves = [kept.at[0], kept.at[1]]

    def sums_of(rows, columns):
        return mix_rows(rows, columns, tensor, waves, [None] * 3, terms)

    mix_pieces(y_local, x_cells // made.shape[0], made, out, out_sems, sums_of)


def last_kernel(sizes, twist, table, data, green, partial, out, *scratch):
    y_local, x_cells = green.shape[2:]
    turned, columns, tensor, kept, held, made, in_sems, out_sems = scratch
    fetches = fetch_entries(green, tensor, late_entries, in_sems)
    fetches.append(pltpu.make_async_copy(partial, held, in_sems.at[len(late_entries)]))
    fetches[-1].start()

    def store(r, row, start, block):
        kept[r, row : row + block.shape[0], start : start + 128] = block

    x_steps(*sizes, 0, twist, table, data, turned, columns, store)
    for fetch in fetches:
        fetch.wait()

    def sums_of(rows, columns):
        sums = [(held[0, row, rows, columns], held[1, row, rows, columns]) for row in range(3)]
        return mix_rows(rows, columns, tensor, [kept], sums, [(row, row, 0) for row in range(3)])

    mix_pieces(y_local, x_cells // made.shape[0], made, out, out_sems, sums_of)


def x_tables(devices, x_local, y_cells):
    x_cells = devices * x_local
    group = 128 // x_local
    fine = angles(x_local, x_local, x_local)
    scale = 1.0 / math.sqrt(x_cells * y_cells)
    apart = np.eye(group) * scale
    table = complex_table(np.kron(apart, np.cos(fine)), np.kron(apart, np.sin(fine)))
    angle = np.tile(angles(devices, x_local, x_cells), (1, group))
    twist = np.stack([np.cos(angle), np.sin(angle)]).astype(np.float32)
    return jnp.asarray(twist), jnp.asarray(table)


def x_scratch(devices, x_local, y_local):
    return [
        pltpu.VMEM((devices, y_local * x_local // 128, 256), jnp.float32),
        pltpu.VMEM((devices * x_local, 2 * y_local), jnp.float32),
    ]


def mixed_waves(data, green, partial, devices, x_local, y_local, y_cells, count_gl):
    x_cells = devices * x_local
    pieces = 8
    sizes = (devices, x_local, y_local, y_cells // 128, owner_order(devices, count_gl))
    first = partial is None
    comps, entries = (2, 5) if first else (1, 3)
    plane = (y_local, x_cells)
    held = [pltpu.VMEM((entries, 2) + plane, jnp.float32)]
    if first:
        held += [pltpu.VMEM((2, 2) + plane, jnp.float32)]
    else:
        held += [
            pltpu.VMEM((2,) + plane, jnp.float32),
            pltpu.VMEM((2, 3) + plane, jnp.float32),
        ]
    operands = (green,) if first else (green, partial)
    return pl.pallas_call(
        functools.partial(early_kernel if first else last_kernel, sizes),
        out_shape=pltpu.HBM((2, 3) + plane, jnp.float32),
        in_specs=[pl.BlockSpec(memory_space=pltpu.VMEM)] * 3
        + [pl.BlockSpec(memory_space=pltpu.HBM)] * len(operands),
        out_specs=pl.BlockSpec(memory_space=pltpu.HBM),
        scratch_shapes=x_scratch(devices, x_local, y_local)
        + held
        + [
            pltpu.VMEM((pieces, 2, 3, y_local, x_cells // pieces), jnp.float32),
            pltpu.SemaphoreType.DMA((5,)),
            pltpu.SemaphoreType.DMA((pieces,)),
        ],
        compiler_params=params(40),
        cost_estimate=cost(
            comps * x_cells * y_local * (x_local * 24 + 24), x_cells * y_local * 64
        ),
    )(
        *x_tables(devices, x_local, y_cells),
        in_vmem(data),
        *[in_hbm(a) for a in operands],
    )


def gate_kernel(data, after, out):
    del data, after, out


def once_after(data, after):
    return pl.pallas_call(
        gate_kernel,
        out_shape=pltpu.HBM(data.shape, data.dtype),
        in_specs=[pl.BlockSpec(memory_space=pltpu.HBM), pl.BlockSpec(memory_space=pl.ANY)],
        out_specs=pl.BlockSpec(memory_space=pltpu.HBM),
        input_output_aliases={0: 0},
        compiler_params=params(1),
        cost_estimate=cost(0, 0),
    )(in_hbm(data), after)


places = ("gx", "gl", "zl", "zh")


def exchange(data):
    return lax.all_to_all(data, places, split_axis=0, concat_axis=0, tiled=True)


def per_device(tiles, tile_owner, tile_slot, tile_count, green):
    count_gl = lax.axis_size("gl")
    devices = lax.axis_size("gx") * 4 * count_gl
    tile_total, tile_len = tiles.shape[2], tiles.shape[3]
    planes, y_local, x_cells = green.shape[2:]
    y_cells = y_local * devices
    x_local = x_cells // devices
    blocks = y_cells // tile_len
    per_owner = max(2, 2 * tile_total // devices)
    assert planes == 1 and tile_len == 128
    owner_row, slot_row = tile_owner.reshape(1, tile_total), tile_slot.reshape(1, tile_total)
    green = green.reshape(2, 6, y_local, x_cells)
    me = lax.axis_index(places).reshape(1).astype(jnp.int32)
    lists = (owner_row, slot_row, tile_count, me)
    early = pack(tiles, (0, 1), *lists, None, devices, count_gl, per_owner)
    late = pack(tiles, (2,), *lists, early, devices, count_gl, per_owner)
    early = exchange(early)
    late = exchange(once_after(late, early))
    grid = (x_local, blocks, count_gl, per_owner)
    early, landings = slab_waves(early, None, *grid)
    early = exchange(once_after(early, late))
    late = slab_waves(late, landings, *grid)
    late = exchange(once_after(late, early))
    sizes = (devices, x_local, y_local, y_cells, count_gl)
    mixed = mixed_waves(early, green, None, *sizes)
    mixed = mixed_waves(late, green, mixed, *sizes)
    return mixed.reshape(2, 3, planes, y_local, x_cells)


def solution(mesh):
    count_gx, count_gy = mesh.devices.shape
    fine_mesh = jax.sharding.Mesh(
        mesh.devices.reshape(count_gx, 2, 2, count_gy // 4), ("gx", "zh", "zl", "gl")
    )
    every = ("gx", "zh", "zl", "gl")
    in_specs = (
        P(None, None, every, None),
        P(every, None),
        P(every),
        P(every),
        P(None, None, None, every, None),
    )
    out_specs = P(None, None, None, every, None)
    return jax.shard_map(
        per_device, mesh=fine_mesh, in_specs=in_specs, out_specs=out_specs, check_vma=False
    )
```

```python
import functools
import math

import jax
import jax.numpy as jnp
import ml_dtypes
import numpy as np
from jax import lax
from jax.experimental import pallas as pl
from jax.experimental.pallas import tpu as pltpu
from jax.sharding import PartitionSpec as P

pair_index = ((0, 3, 4), (3, 1, 5), (4, 5, 2))
by_rows = (((1,), (1,)), ((), ()))


def params(mebibytes):
    return pltpu.CompilerParams(vmem_limit_bytes=mebibytes * 1024 * 1024)


def in_hbm(array):
    return pltpu.with_memory_space_constraint(array, pltpu.HBM)


def in_vmem(array):
    return pltpu.with_memory_space_constraint(array, pltpu.VMEM)


def cost(flops, moved):
    return pl.CostEstimate(flops=flops, bytes_accessed=moved, transcendentals=0)


def angles(rows, columns, length):
    products = np.outer(np.arange(rows), np.arange(columns)) % length
    return 2.0 * math.pi / length * products


def halves(table):
    wide = np.asarray(table, np.float32)
    high = wide.astype(ml_dtypes.bfloat16)
    low = (wide - high.astype(np.float32)).astype(ml_dtypes.bfloat16)
    return jnp.asarray(high), jnp.asarray(low)


def split_two(data):
    high = data.astype(jnp.bfloat16)
    return high, (data - high.astype(jnp.float32)).astype(jnp.bfloat16)


def split_three(data):
    high = data.astype(jnp.bfloat16)
    rest = data - high.astype(jnp.float32)
    middle = rest.astype(jnp.bfloat16)
    return high, middle, (rest - middle.astype(jnp.float32)).astype(jnp.bfloat16)


def dot_rows(left, right):
    return lax.dot_general(left, right, by_rows, preferred_element_type=jnp.float32)


def dot_rows_split(table, data):
    rows, depth = table.shape
    table_high, table_low = split_two(table)
    high, low = split_two(data)
    if depth > 128:
        both = dot_rows(jnp.concatenate([table_high, table_low]), high)
        return both[:rows] + both[rows:] + dot_rows(table_high, low)
    left = jnp.concatenate(
        [
            jnp.concatenate([table_high, table_high], axis=1),
            jnp.concatenate([table_low, jnp.zeros_like(table_low)], axis=1),
        ]
    )
    both = dot_rows(left, jnp.concatenate([high, low], axis=1))
    return both[:rows] + both[rows:]


def flat_fft(values, times):
    length = len(values)
    if length == 1:
        return values
    even = flat_fft(values[0::2], times)
    odd = flat_fft(values[1::2], times)
    lower, upper = [], []
    for k in range(length // 2):
        turned = times(odd[k], k, length)
        lower.append(jax.tree.map(lambda a, b: a + b, even[k], turned))
        upper.append(jax.tree.map(lambda a, b: a - b, even[k], turned))
    return lower + upper


def times_pair(value, k, length):
    real, imag = value
    if k == 0:
        return value
    if 4 * k == length:
        return (imag, -real)
    cos_k = math.cos(2.0 * math.pi * k / length)
    sin_k = math.sin(2.0 * math.pi * k / length)
    return (real * cos_k + imag * sin_k, imag * cos_k - real * sin_k)


def place_of(owner, count_gl):
    shift = count_gl.bit_length() - 1
    z = (owner >> shift) & 3
    return (((owner >> (shift + 2)) << shift) + (owner & (count_gl - 1))) * 4 + z


def owner_order(devices, count_gl):
    order = [0] * devices
    for owner in range(devices):
        order[place_of(owner, count_gl)] = owner
    return order


def pack_kernel(
    devices, count_gl, per_owner, count, me, owner_row, slot_row, tiles, out, *scratch
):
    held, made, lists, sems, out_sems = scratch
    comps = range(tiles.shape[1])
    listed = owner_row.shape[1]
    fetches = [
        pltpu.make_async_copy(owner_row, lists.at[0], sems.at[0]),
        pltpu.make_async_copy(slot_row, lists.at[1], sems.at[1]),
    ]
    fetches += [
        pltpu.make_async_copy(tiles.at[:, comp], held.at[i], sems.at[2 + i])
        for i, comp in enumerate(comps)
    ]
    for fetch in fetches:
        fetch.start()
    sender = lax.broadcasted_iota(jnp.int32, (listed, listed), 0)
    reader = lax.broadcasted_iota(jnp.int32, (listed, listed), 1)
    before = jnp.where(sender < reader, 1.0, 0.0).astype(jnp.bfloat16)
    live = lax.broadcasted_iota(jnp.int32, (1, listed), 1) < count[0]
    fetches[0].wait()
    place = jnp.where(live, place_of(lists[0], count_gl), -1)
    place_at = lax.broadcasted_iota(jnp.int32, (devices, listed), 0)
    named = jnp.where(place_at == place, 1.0, 0.0)
    counted = jnp.dot(named.astype(jnp.bfloat16), before, preferred_element_type=jnp.float32)
    rank = jnp.sum(counted * named, axis=0, keepdims=True).astype(jnp.int32)
    target = jnp.where(live, place * per_owner + rank, -1)
    target_at = lax.broadcasted_iota(jnp.int32, (devices * per_owner, listed), 0)
    chosen = jnp.where(target_at == target, 1.0, 0.0).astype(jnp.bfloat16)
    fetches[1].wait()
    sends = []

    def send(start, rows):
        part = pl.ds(start, rows)
        copy = pltpu.make_async_copy(
            made.at[:, part], out.at[:, part], out_sems.at[len(sends)]
        )
        copy.start()
        sends.append(copy)

    stated = lists[1] + 1
    lane = rank + (me[0] & (128 // per_owner - 1)) * per_owner
    lane_at = lax.broadcasted_iota(jnp.int32, (128, listed), 0)
    laned = jnp.where(lane_at == lane, 1.0, 0.0).astype(jnp.bfloat16)
    coarse = (named * (stated >> 5).astype(jnp.float32)).astype(jnp.bfloat16)
    fine = (named * (stated & 31).astype(jnp.float32)).astype(jnp.bfloat16)
    slots = 32.0 * dot_rows(coarse, laned) + dot_rows(fine, laned)
    start = 2 * len(comps) * per_owner
    made[:, start:, :] = jnp.broadcast_to(slots[:, None, :], (devices, 8, 128))
    send(start, 8)
    for i in range(len(comps)):
        fetches[2 + i].wait()
        parts = [part for r in range(2) for part in split_two(held[i, r])]
        got = jnp.dot(
            chosen, jnp.concatenate(parts, axis=1), preferred_element_type=jnp.float32
        )
        for r in range(2):
            whole = got[:, 256 * r : 256 * r + 128] + got[:, 256 * r + 128 : 256 * r + 256]
            start = (2 * i + r) * per_owner
            made[:, start : start + per_owner, :] = whole.reshape(devices, per_owner, 128)
            send(start, per_owner)
    for copy in sends:
        copy.wait()


def pack(tiles, owner_row, slot_row, count, me, devices, count_gl, per_owner):
    comps, listed = tiles.shape[1:3]
    rows = 2 * comps * per_owner + 8
    return pl.pallas_call(
        functools.partial(pack_kernel, devices, count_gl, per_owner),
        out_shape=pltpu.HBM((devices, rows, 128), jnp.float32),
        in_specs=[pl.BlockSpec(memory_space=pltpu.SMEM)] * 2
        + [pl.BlockSpec(memory_space=pltpu.HBM)] * 3,
        out_specs=pl.BlockSpec(memory_space=pltpu.HBM),
        scratch_shapes=[
            pltpu.VMEM((comps, 2, listed, 128), jnp.float32),
            pltpu.VMEM((devices, rows, 128), jnp.float32),
            pltpu.VMEM((2, 1, listed), jnp.int32),
            pltpu.SemaphoreType.DMA((2 + comps,)),
            pltpu.SemaphoreType.DMA((1 + 2 * comps,)),
        ],
        compiler_params=params(24),
        cost_estimate=cost(
            devices * per_owner * listed * 512 * 2 * comps, devices * rows * 1024
        ),
    )(count, me, *[in_hbm(a) for a in (owner_row, slot_row, tiles)])


def complex_table(cos_part, sin_part):
    return np.concatenate(
        [
            np.concatenate([cos_part, sin_part], axis=1),
            np.concatenate([-sin_part, cos_part], axis=1),
        ]
    ).astype(np.float32)


def slab_kernel(count, x_local, blocks, per_owner, table, twist, data, out, *scratch):
    made, slab, turned, out_sems = scratch
    devices = data.shape[0]
    entries = devices * per_owner
    group = 128 // x_local
    pairs = blocks // group
    shift = blocks.bit_length() - 1
    every = 128 // per_owner
    stated = [
        sum([data[o, data.shape[1] - 8 :][:1] for o in range(start, start + every)])
        for start in range(0, devices, every)
    ]
    slot = jnp.concatenate(stated, axis=1).astype(jnp.int32) - 1
    landing = jnp.where(slot >= 0, (slot & (blocks - 1)) * x_local + (slot >> shift), -1)
    parts = []
    for i in range(2 * count):
        one = data[:, i * per_owner : (i + 1) * per_owner, :]
        parts.extend(split_two(one.reshape(entries, 128)))
    parts = jnp.concatenate(parts, axis=1)
    step_rows = min(512, blocks * x_local)
    for start in range(0, blocks * x_local, step_rows):
        place = start + lax.broadcasted_iota(jnp.int32, (step_rows, entries), 0)
        chosen = jnp.where(place == landing, 1.0, 0.0).astype(jnp.bfloat16)
        got = jnp.dot(chosen, parts, preferred_element_type=jnp.float32)
        for i in range(2 * count):
            slab[i // 2, i % 2, start : start + step_rows, :] = (
                got[:, 256 * i : 256 * i + 128] + got[:, 256 * i + 128 : 256 * i + 256]
            )
    sends = []
    for index in range(count):

        @pl.loop(0, x_local // 8)
        def _(step):
            at = pl.multiple_of(step * 8, 8)
            values = [
                tuple(slab[index, r, pl.ds(t * x_local + at, 8), :] for r in range(2))
                for t in range(blocks)
            ]
            waves = flat_fft(values, times_pair)
            for k in range(blocks):
                real, imag = waves[k]
                cos_k, sin_k = twist[0, k : k + 1, :], twist[1, k : k + 1, :]
                rows = pl.ds(((k % pairs) * group + k // pairs) * x_local + at, 8)
                turned[rows, :128] = real * cos_k + imag * sin_k
                turned[rows, 128:] = imag * cos_k - real * sin_k

        for start in range(0, pairs, 2):
            moved = dot_rows_split(table[...], turned[start * 128 : (start + 2) * 128, :])
            for k in range(2):
                for r in range(2):
                    rows = pl.ds(r * pairs + start + k, 128, stride=2 * pairs)
                    made[index, rows, :] = moved[
                        r * 128 : (r + 1) * 128, k * 128 : (k + 1) * 128
                    ]
        send = pltpu.make_async_copy(
            made.at[index].reshape(devices, made.shape[1] // devices, 128),
            out.at[:, index],
            out_sems.at[index],
        )
        send.start()
        sends.append(send)
    for send in sends:
        send.wait()


def slab_waves(data, x_local, blocks, count_gl, per_owner):
    devices = data.shape[0]
    count = data.shape[1] // (2 * per_owner)
    fine = angles(128, 128, 128)
    order = owner_order(devices, count_gl)
    fine = fine.reshape(devices, 128 // devices, 128)[order].reshape(128, 128)
    table = complex_table(np.cos(fine), np.sin(fine))
    twist_angle = angles(blocks, 128, blocks * 128)
    twist = np.stack([np.cos(twist_angle), np.sin(twist_angle)]).astype(np.float32)
    entries = devices * per_owner
    rows = blocks * x_local * 2
    return pl.pallas_call(
        functools.partial(slab_kernel, count, x_local, blocks, per_owner),
        out_shape=pltpu.HBM((devices, count, rows // devices, 128), jnp.float32),
        in_specs=[pl.BlockSpec(memory_space=pltpu.VMEM)] * 3,
        out_specs=pl.BlockSpec(memory_space=pltpu.HBM),
        scratch_shapes=[
            pltpu.VMEM((count, rows, 128), jnp.float32),
            pltpu.VMEM((count, 2, blocks * x_local, 128), jnp.float32),
            pltpu.VMEM((blocks * x_local, 256), jnp.float32),
            pltpu.SemaphoreType.DMA((count,)),
        ],
        compiler_params=params(40),
        cost_estimate=cost(
            count * blocks * x_local * (entries * 1024 + 512 * 1024),
            count * (entries * 1024 + rows * 512),
        ),
    )(jnp.asarray(table), jnp.asarray(twist), in_vmem(data))


def choose(options, mask_of):
    made = options[0]
    for i in range(1, len(options)):
        made = jnp.where(mask_of(i), options[i], made)
    return made


def x_steps(
    devices, x_local, y_local, blocks, order, index, twist, table, data, turned, columns, store, whole
):
    group = 128 // x_local
    pairs = blocks // group
    kept = y_local // blocks
    narrow = kept * pairs
    banks = 2 * group

    @pl.loop(0, kept)
    def _(step):
        at = pl.multiple_of(step * 2 * pairs, 2 * pairs)
        values = [
            tuple(
                data[order.index(o), index, pl.ds(at + r * pairs, pairs), :] for r in range(2)
            )
            for o in range(devices)
        ]
        waves = flat_fft(values, times_pair)
        rows = pl.ds(pl.multiple_of(step * pairs, pairs), pairs)
        for k in range(devices):
            real, imag = waves[k]
            cos_k, sin_k = twist[0, k : k + 1, :], twist[1, k : k + 1, :]
            turned[k, rows, :128] = real * cos_k + imag * sin_k
            turned[k, rows, 128:] = imag * cos_k - real * sin_k

    lane = lax.broadcasted_iota(jnp.int32, (1, 128), 1)
    square = banks * narrow == 128 and 128 // narrow == banks
    together = min(devices, 256 // narrow)
    for start in range(0, devices, together):
        stacked = turned[start : start + together].reshape(together * narrow, 256)
        moved = dot_rows_split(table[...], stacked)
        if square:
            for base in range(0, together, banks):
                rolled = []
                for bank in range(banks):
                    one = moved[bank * x_local : (bank + 1) * x_local, base * narrow :][:, :128]
                    rolled.append(pltpu.roll(one, bank * narrow, 1) if bank else one)
                for k in range(banks):
                    options = [rolled[(place - k) % banks] for place in range(banks)]
                    rows = pl.ds(start + base + k, x_local, stride=devices)
                    columns[rows, :] = choose(options, lambda i: lane // narrow == i)
        else:
            for k in range(together):
                one = jnp.concatenate(
                    [
                        moved[bank * x_local : (bank + 1) * x_local, k * narrow : (k + 1) * narrow]
                        for bank in range(banks)
                    ],
                    axis=1,
                )
                columns[pl.ds(start + k, x_local, stride=devices), :] = one
    for start in range(0, devices * x_local, 128):
        block = columns[start : start + 128, :].T
        pieces = [block[bank * narrow : (bank + 1) * narrow] for bank in range(banks)]
        for bank in range(banks):
            one = pieces[bank]
            if square:
                options = [pieces[(bank + k) % banks] for k in range(banks)]
                one = choose(options, lambda i: lane % banks == i)
            for step in range(kept):
                row = step * blocks + (bank % group) * pairs
                store(bank // group, row, start, one[step * pairs : (step + 1) * pairs])
        whole(start)


def mix_rows(rows, columns, tensor, waves):
    sums = [None] * 3
    for row in range(3):
        for col in range(3):
            entry = pair_index[row][col]
            green_real, green_imag = tensor[0, entry, rows, columns], tensor[1, entry, rows, columns]
            real, imag = waves[col, 0, rows, columns], waves[col, 1, rows, columns]
            real_term = green_real * real - green_imag * imag
            imag_term = green_real * imag + green_imag * real
            old = sums[row]
            sums[row] = (
                (real_term, imag_term) if old is None else (old[0] + real_term, old[1] + imag_term)
            )
    return sums


def field_kernel(sizes, twist, table, data, green, out, *scratch):
    y_local, x_cells = green.shape[2:]
    turned, columns, tensor, kept, made, in_sem, out_sems = scratch
    width = x_cells // made.shape[0]
    fetch = pltpu.make_async_copy(green, tensor, in_sem)
    fetch.start()
    sends = []
    for comp in range(3):

        def store(r, row, start, block):
            kept[comp, r, row : row + block.shape[0], start : start + 128] = block

        def whole(start):
            if comp < 2 or (start + 128) % width:
                return
            piece = start // width
            part = pl.ds(piece * width, width)

            @pl.loop(0, y_local // 8)
            def _(step):
                rows = pl.ds(pl.multiple_of(step * 8, 8), 8)
                for row, pair in enumerate(mix_rows(rows, part, tensor, kept)):
                    for r in range(2):
                        made[piece, r, row, rows, :] = pair[r]

            send = pltpu.make_async_copy(
                made.at[piece], out.at[:, :, :, part], out_sems.at[piece]
            )
            send.start()
            sends.append(send)

        if comp == 2:
            fetch.wait()
        x_steps(*sizes, comp, twist, table, data, turned, columns, store, whole)
    for send in sends:
        send.wait()


def x_tables(devices, x_local, y_cells):
    x_cells = devices * x_local
    group = 128 // x_local
    fine = angles(x_local, x_local, x_local)
    scale = 1.0 / math.sqrt(x_cells * y_cells)
    apart = np.eye(group) * scale
    table = complex_table(np.kron(apart, np.cos(fine)), np.kron(apart, np.sin(fine)))
    angle = np.tile(angles(devices, x_local, x_cells), (1, group))
    twist = np.stack([np.cos(angle), np.sin(angle)]).astype(np.float32)
    return jnp.asarray(twist), jnp.asarray(table)


def x_scratch(devices, x_local, y_local):
    return [
        pltpu.VMEM((devices, y_local * x_local // 128, 256), jnp.float32),
        pltpu.VMEM((devices * x_local, 2 * y_local), jnp.float32),
    ]


def field(data, green, devices, x_local, y_local, y_cells, count_gl):
    x_cells = devices * x_local
    pieces = 8
    sizes = (devices, x_local, y_local, y_cells // 128, owner_order(devices, count_gl))
    plane = (y_local, x_cells)
    return pl.pallas_call(
        functools.partial(field_kernel, sizes),
        out_shape=pltpu.HBM((2, 3) + plane, jnp.float32),
        in_specs=[pl.BlockSpec(memory_space=pltpu.VMEM)] * 3
        + [pl.BlockSpec(memory_space=pltpu.HBM)],
        out_specs=pl.BlockSpec(memory_space=pltpu.HBM),
        scratch_shapes=x_scratch(devices, x_local, y_local)
        + [
            pltpu.VMEM((2, 6) + plane, jnp.float32),
            pltpu.VMEM((3, 2) + plane, jnp.float32),
            pltpu.VMEM((pieces, 2, 3, y_local, x_cells // pieces), jnp.float32),
            pltpu.SemaphoreType.DMA(()),
            pltpu.SemaphoreType.DMA((pieces,)),
        ],
        compiler_params=params(40),
        cost_estimate=cost(3 * x_cells * y_local * (x_local * 24 + 24), x_cells * y_local * 96),
    )(*x_tables(devices, x_local, y_cells), in_vmem(data), in_hbm(green))


places = ("gx", "gl", "gz")


def exchange(data):
    return lax.all_to_all(data, places, split_axis=0, concat_axis=0, tiled=True)


def per_device(tiles, tile_owner, tile_slot, tile_count, green):
    count_gl = lax.axis_size("gl")
    devices = lax.axis_size("gx") * 4 * count_gl
    tile_total, tile_len = tiles.shape[2], tiles.shape[3]
    planes, y_local, x_cells = green.shape[2:]
    y_cells = y_local * devices
    x_local = x_cells // devices
    blocks = y_cells // tile_len
    per_owner = max(2, 2 * tile_total // devices)
    assert planes == 1 and tile_len == 128
    owner_row, slot_row = tile_owner.reshape(1, tile_total), tile_slot.reshape(1, tile_total)
    green = green.reshape(2, 6, y_local, x_cells)
    me = lax.axis_index(places).reshape(1).astype(jnp.int32)
    lists = (owner_row, slot_row, tile_count, me)
    arrived = exchange(pack(tiles, *lists, devices, count_gl, per_owner))
    moved = exchange(slab_waves(arrived, x_local, blocks, count_gl, per_owner))
    mixed = field(moved, green, devices, x_local, y_local, y_cells, count_gl)
    return mixed.reshape(2, 3, planes, y_local, x_cells)


def solution(mesh):
    count_gx, count_gy = mesh.devices.shape
    fine_mesh = jax.sharding.Mesh(
        mesh.devices.reshape(count_gx, 4, count_gy // 4), ("gx", "gz", "gl")
    )
    every = ("gx", "gz", "gl")
    in_specs = (
        P(None, None, every, None),
        P(every, None),
        P(every),
        P(every),
        P(None, None, None, every, None),
    )
    out_specs = P(None, None, None, every, None)
    return jax.shard_map(
        per_device, mesh=fine_mesh, in_specs=in_specs, out_specs=out_specs, check_vma=False
    )
```

```python
import functools
import math

import jax
import jax.numpy as jnp
import numpy as np
from jax import lax
from jax.experimental import pallas as pl
from jax.experimental.pallas import tpu as pltpu
from jax.sharding import PartitionSpec as P

pair_index = ((0, 3, 4), (3, 1, 5), (4, 5, 2))
by_rows = (((1,), (1,)), ((), ()))


def params(mebibytes):
    return pltpu.CompilerParams(vmem_limit_bytes=mebibytes * 1024 * 1024)


def in_hbm(array):
    return pltpu.with_memory_space_constraint(array, pltpu.HBM)


def in_vmem(array):
    return pltpu.with_memory_space_constraint(array, pltpu.VMEM)


def cost(flops, moved):
    return pl.CostEstimate(flops=flops, bytes_accessed=moved, transcendentals=0)


def angles(rows, columns, length):
    products = np.outer(np.arange(rows), np.arange(columns)) % length
    return 2.0 * math.pi / length * products


def split_two(data):
    high = data.astype(jnp.bfloat16)
    return high, (data - high.astype(jnp.float32)).astype(jnp.bfloat16)


def dot_rows(left, right):
    return lax.dot_general(left, right, by_rows, preferred_element_type=jnp.float32)


def dot_rows_split(stacked, data):
    rows = stacked.shape[0] // 2
    high, low = split_two(data)
    both = dot_rows(stacked, high)
    return both[:rows] + both[rows:] + dot_rows(stacked[:rows], low)


def stacked_halves(table):
    return jnp.concatenate(split_two(table[...]))


def flat_fft(values, times):
    length = len(values)
    if length == 1:
        return values
    even = flat_fft(values[0::2], times)
    odd = flat_fft(values[1::2], times)
    lower, upper = [], []
    for k in range(length // 2):
        turned = times(odd[k], k, length)
        lower.append(jax.tree.map(lambda a, b: a + b, even[k], turned))
        upper.append(jax.tree.map(lambda a, b: a - b, even[k], turned))
    return lower + upper


def times_pair(value, k, length):
    real, imag = value
    if k == 0:
        return value
    if 4 * k == length:
        return (imag, -real)
    cos_k = math.cos(2.0 * math.pi * k / length)
    sin_k = math.sin(2.0 * math.pi * k / length)
    return (real * cos_k + imag * sin_k, imag * cos_k - real * sin_k)


def place_of(owner, count_gl):
    shift = count_gl.bit_length() - 1
    z = (owner >> shift) & 3
    return (((owner >> (shift + 2)) << shift) + (owner & (count_gl - 1))) * 4 + z


def owner_order(devices, count_gl):
    order = [0] * devices
    for owner in range(devices):
        order[place_of(owner, count_gl)] = owner
    return order


def pack_kernel(
    devices, count_gl, per_owner, count, me, owner_row, slot_row, tiles, out, *scratch
):
    held, lists, sems = scratch
    comps = range(tiles.shape[1])
    listed = owner_row.shape[1]
    fetches = [
        pltpu.make_async_copy(owner_row, lists.at[0], sems.at[0]),
        pltpu.make_async_copy(slot_row, lists.at[1], sems.at[1]),
    ]
    fetches += [
        pltpu.make_async_copy(tiles.at[:, comp], held.at[i], sems.at[2 + i])
        for i, comp in enumerate(comps)
    ]
    for fetch in fetches:
        fetch.start()
    sender = lax.broadcasted_iota(jnp.int32, (listed, listed), 0)
    reader = lax.broadcasted_iota(jnp.int32, (listed, listed), 1)
    before = jnp.where(sender < reader, 1.0, 0.0).astype(jnp.bfloat16)
    live = lax.broadcasted_iota(jnp.int32, (1, listed), 1) < count[0]
    fetches[0].wait()
    place = jnp.where(live, place_of(lists[0], count_gl), -1)
    place_at = lax.broadcasted_iota(jnp.int32, (devices, listed), 0)
    named = jnp.where(place_at == place, 1.0, 0.0)
    counted = jnp.dot(named.astype(jnp.bfloat16), before, preferred_element_type=jnp.float32)
    rank = jnp.sum(counted * named, axis=0, keepdims=True).astype(jnp.int32)
    target = jnp.where(live, place * per_owner + rank, -1)
    target_at = lax.broadcasted_iota(jnp.int32, (devices * per_owner, listed), 0)
    chosen = jnp.where(target_at == target, 1.0, 0.0).astype(jnp.bfloat16)
    fetches[1].wait()
    stated = lists[1] + 1
    lane = rank + (me[0] & (128 // per_owner - 1)) * per_owner
    lane_at = lax.broadcasted_iota(jnp.int32, (128, listed), 0)
    laned = jnp.where(lane_at == lane, 1.0, 0.0).astype(jnp.bfloat16)
    coarse = (named * (stated >> 5).astype(jnp.float32)).astype(jnp.bfloat16)
    fine = (named * (stated & 31).astype(jnp.float32)).astype(jnp.bfloat16)
    slots = 32.0 * dot_rows(coarse, laned) + dot_rows(fine, laned)
    start = 2 * len(comps) * per_owner
    out[:, start:, :] = jnp.broadcast_to(slots[:, None, :], (devices, 8, 128))
    for i in range(len(comps)):
        fetches[2 + i].wait()
        parts = [part for r in range(2) for part in split_two(held[i, r])]
        got = jnp.dot(
            chosen, jnp.concatenate(parts, axis=1), preferred_element_type=jnp.float32
        )
        for r in range(2):
            whole = got[:, 256 * r : 256 * r + 128] + got[:, 256 * r + 128 : 256 * r + 256]
            start = (2 * i + r) * per_owner
            out[:, start : start + per_owner, :] = whole.reshape(devices, per_owner, 128)


def pack(tiles, owner_row, slot_row, count, me, devices, count_gl, per_owner):
    comps, listed = tiles.shape[1:3]
    rows = 2 * comps * per_owner + 8
    return pl.pallas_call(
        functools.partial(pack_kernel, devices, count_gl, per_owner),
        out_shape=pltpu.VMEM((devices, rows, 128), jnp.float32),
        in_specs=[pl.BlockSpec(memory_space=pltpu.SMEM)] * 2
        + [pl.BlockSpec(memory_space=pltpu.HBM)] * 3,
        out_specs=pl.BlockSpec(memory_space=pltpu.VMEM),
        scratch_shapes=[
            pltpu.VMEM((comps, 2, listed, 128), jnp.float32),
            pltpu.VMEM((2, 1, listed), jnp.int32),
            pltpu.SemaphoreType.DMA((2 + comps,)),
        ],
        compiler_params=params(24),
        cost_estimate=cost(
            devices * per_owner * listed * 512 * 2 * comps, devices * rows * 1024
        ),
    )(count, me, *[in_hbm(a) for a in (owner_row, slot_row, tiles)])


def complex_table(cos_part, sin_part):
    return np.concatenate(
        [
            np.concatenate([cos_part, sin_part], axis=1),
            np.concatenate([-sin_part, cos_part], axis=1),
        ]
    ).astype(np.float32)


def slab_kernel(count, x_local, blocks, per_owner, table, twist, data, out, *scratch):
    slab, turned = scratch
    devices = data.shape[0]
    entries = devices * per_owner
    group = 128 // x_local
    pairs = blocks // group
    shift = blocks.bit_length() - 1
    every = 128 // per_owner
    stated = [
        sum([data[o, data.shape[1] - 8 :][:1] for o in range(start, start + every)])
        for start in range(0, devices, every)
    ]
    slot = jnp.concatenate(stated, axis=1).astype(jnp.int32) - 1
    landing = jnp.where(slot >= 0, (slot & (blocks - 1)) * x_local + (slot >> shift), -1)
    parts = []
    for i in range(2 * count):
        one = data[:, i * per_owner : (i + 1) * per_owner, :]
        parts.extend(split_two(one.reshape(entries, 128)))
    parts = jnp.concatenate(parts, axis=1)
    step_rows = min(512, blocks * x_local)
    for start in range(0, blocks * x_local, step_rows):
        place = start + lax.broadcasted_iota(jnp.int32, (step_rows, entries), 0)
        chosen = jnp.where(place == landing, 1.0, 0.0).astype(jnp.bfloat16)
        got = jnp.dot(chosen, parts, preferred_element_type=jnp.float32)
        for i in range(2 * count):
            slab[i // 2, i % 2, start : start + step_rows, :] = (
                got[:, 256 * i : 256 * i + 128] + got[:, 256 * i + 128 : 256 * i + 256]
            )
    stacked = stacked_halves(table)
    for index in range(count):

        @pl.loop(0, x_local // 8, unroll=2)
        def _(step):
            at = pl.multiple_of(step * 8, 8)
            values = [
                tuple(slab[index, r, pl.ds(t * x_local + at, 8), :] for r in range(2))
                for t in range(blocks)
            ]
            waves = flat_fft(values, times_pair)
            for k in range(blocks):
                real, imag = waves[k]
                cos_k, sin_k = twist[0, k : k + 1, :], twist[1, k : k + 1, :]
                rows = pl.ds(((k % pairs) * group + k // pairs) * x_local + at, 8)
                turned[rows, :128] = real * cos_k + imag * sin_k
                turned[rows, 128:] = imag * cos_k - real * sin_k

        for start in range(0, pairs, 2):
            moved = dot_rows_split(stacked, turned[start * 128 : (start + 2) * 128, :])
            for k in range(2):
                for r in range(2):
                    one = moved[r * 128 : (r + 1) * 128, k * 128 : (k + 1) * 128]
                    base = (index * 2 + r) * pairs + start + k
                    out[pl.ds(base, 128, stride=count * 2 * pairs), :] = one


def slab_waves(data, x_local, blocks, count_gl, per_owner):
    devices = data.shape[0]
    count = data.shape[1] // (2 * per_owner)
    fine = angles(128, 128, 128)
    order = owner_order(devices, count_gl)
    fine = fine.reshape(devices, 128 // devices, 128)[order].reshape(128, 128)
    table = complex_table(np.cos(fine), np.sin(fine))
    twist_angle = angles(blocks, 128, blocks * 128)
    twist = np.stack([np.cos(twist_angle), np.sin(twist_angle)]).astype(np.float32)
    entries = devices * per_owner
    rows = blocks * x_local * 2
    made = pl.pallas_call(
        functools.partial(slab_kernel, count, x_local, blocks, per_owner),
        out_shape=pltpu.VMEM((count * rows, 128), jnp.float32),
        in_specs=[pl.BlockSpec(memory_space=pltpu.VMEM)] * 3,
        out_specs=pl.BlockSpec(memory_space=pltpu.VMEM),
        scratch_shapes=[
            pltpu.VMEM((count, 2, blocks * x_local, 128), jnp.float32),
            pltpu.VMEM((blocks * x_local, 256), jnp.float32),
        ],
        compiler_params=params(40),
        cost_estimate=cost(
            count * blocks * x_local * (entries * 1024 + 512 * 1024),
            count * (entries * 1024 + rows * 512),
        ),
    )(jnp.asarray(table), jnp.asarray(twist), in_vmem(data))
    return made.reshape(devices, count * rows // devices, 128)


def choose(options, mask_of):
    made = options[0]
    for i in range(1, len(options)):
        made = jnp.where(mask_of(i), options[i], made)
    return made


def x_steps(
    devices, x_local, y_local, blocks, order, index, twist, stacked, data, turned, columns, store, whole
):
    group = 128 // x_local
    pairs = blocks // group
    kept = y_local // blocks
    narrow = kept * pairs
    banks = 2 * group

    @pl.loop(0, kept)
    def _(step):
        stride = data.shape[1] // kept
        at = pl.multiple_of(step * stride, 2 * pairs) + index * 2 * pairs
        values = [
            tuple(data[order.index(o), pl.ds(at + r * pairs, pairs), :] for r in range(2))
            for o in range(devices)
        ]
        waves = flat_fft(values, times_pair)
        rows = pl.ds(pl.multiple_of(step * pairs, pairs), pairs)
        for k in range(devices):
            real, imag = waves[k]
            cos_k, sin_k = twist[0, k : k + 1, :], twist[1, k : k + 1, :]
            turned[k, rows, :128] = real * cos_k + imag * sin_k
            turned[k, rows, 128:] = imag * cos_k - real * sin_k

    lane = lax.broadcasted_iota(jnp.int32, (1, 128), 1)
    square = banks * narrow == 128 and 128 // narrow == banks
    together = min(devices, 256 // narrow)
    for start in range(0, devices, together):
        rows = turned[start : start + together].reshape(together * narrow, 256)
        moved = dot_rows_split(stacked, rows)
        if square:
            for base in range(0, together, banks):
                rolled = []
                for bank in range(banks):
                    one = moved[bank * x_local : (bank + 1) * x_local, base * narrow :][:, :128]
                    rolled.append(pltpu.roll(one, bank * narrow, 1) if bank else one)
                for k in range(banks):
                    options = [rolled[(place - k) % banks] for place in range(banks)]
                    rows = pl.ds(start + base + k, x_local, stride=devices)
                    columns[rows, :] = choose(options, lambda i: lane // narrow == i)
        else:
            for k in range(together):
                one = jnp.concatenate(
                    [
                        moved[bank * x_local : (bank + 1) * x_local, k * narrow : (k + 1) * narrow]
                        for bank in range(banks)
                    ],
                    axis=1,
                )
                columns[pl.ds(start + k, x_local, stride=devices), :] = one
    for start in range(0, devices * x_local, 128):
        block = columns[start : start + 128, :].T
        pieces = [block[bank * narrow : (bank + 1) * narrow] for bank in range(banks)]
        for bank in range(banks):
            one = pieces[bank]
            if square:
                options = [pieces[(bank + k) % banks] for k in range(banks)]
                one = choose(options, lambda i: lane % banks == i)
            for step in range(kept):
                row = step * blocks + (bank % group) * pairs
                store(bank // group, row, start, one[step * pairs : (step + 1) * pairs])
        whole(start)


def mix_rows(rows, columns, tensor, waves):
    sums = [None] * 3
    for row in range(3):
        for col in range(3):
            entry = pair_index[row][col]
            green_real, green_imag = tensor[0, entry, rows, columns], tensor[1, entry, rows, columns]
            real, imag = waves[col, 0, rows, columns], waves[col, 1, rows, columns]
            real_term = green_real * real - green_imag * imag
            imag_term = green_real * imag + green_imag * real
            old = sums[row]
            sums[row] = (
                (real_term, imag_term) if old is None else (old[0] + real_term, old[1] + imag_term)
            )
    return sums


def field_kernel(sizes, twist, table, data, green, out, *scratch):
    y_local, x_cells = green.shape[2:]
    turned, columns, tensor, kept, made, in_sem, out_sems = scratch
    width = x_cells // made.shape[0]
    fetch = pltpu.make_async_copy(green, tensor, in_sem)
    fetch.start()
    stacked = stacked_halves(table)
    sends = []
    for comp in range(3):

        def store(r, row, start, block):
            kept[comp, r, row : row + block.shape[0], start : start + 128] = block

        def whole(start):
            if comp < 2 or (start + 128) % width:
                return
            piece = start // width
            part = pl.ds(piece * width, width)

            @pl.loop(0, y_local // 8, unroll=2)
            def _(step):
                rows = pl.ds(pl.multiple_of(step * 8, 8), 8)
                for row, pair in enumerate(mix_rows(rows, part, tensor, kept)):
                    for r in range(2):
                        made[piece, r, row, rows, :] = pair[r]

            send = pltpu.make_async_copy(
                made.at[piece], out.at[:, :, :, part], out_sems.at[piece]
            )
            send.start()
            sends.append(send)

        if comp == 2:
            fetch.wait()
        x_steps(*sizes, comp, twist, stacked, data, turned, columns, store, whole)
    for send in sends:
        send.wait()


def x_tables(devices, x_local, y_cells):
    x_cells = devices * x_local
    group = 128 // x_local
    fine = angles(x_local, x_local, x_local)
    scale = 1.0 / math.sqrt(x_cells * y_cells)
    apart = np.eye(group) * scale
    table = complex_table(np.kron(apart, np.cos(fine)), np.kron(apart, np.sin(fine)))
    angle = np.tile(angles(devices, x_local, x_cells), (1, group))
    twist = np.stack([np.cos(angle), np.sin(angle)]).astype(np.float32)
    return jnp.asarray(twist), jnp.asarray(table)


def x_scratch(devices, x_local, y_local):
    return [
        pltpu.VMEM((devices, y_local * x_local // 128, 256), jnp.float32),
        pltpu.VMEM((devices * x_local, 2 * y_local), jnp.float32),
    ]


def field(data, green, devices, x_local, y_local, y_cells, count_gl):
    x_cells = devices * x_local
    pieces = 8
    sizes = (devices, x_local, y_local, y_cells // 128, owner_order(devices, count_gl))
    plane = (y_local, x_cells)
    return pl.pallas_call(
        functools.partial(field_kernel, sizes),
        out_shape=pltpu.HBM((2, 3) + plane, jnp.float32),
        in_specs=[pl.BlockSpec(memory_space=pltpu.VMEM)] * 3
        + [pl.BlockSpec(memory_space=pltpu.HBM)],
        out_specs=pl.BlockSpec(memory_space=pltpu.HBM),
        scratch_shapes=x_scratch(devices, x_local, y_local)
        + [
            pltpu.VMEM((2, 6) + plane, jnp.float32),
            pltpu.VMEM((3, 2) + plane, jnp.float32),
            pltpu.VMEM((pieces, 2, 3, y_local, x_cells // pieces), jnp.float32),
            pltpu.SemaphoreType.DMA(()),
            pltpu.SemaphoreType.DMA((pieces,)),
        ],
        compiler_params=params(40),
        cost_estimate=cost(3 * x_cells * y_local * (x_local * 24 + 24), x_cells * y_local * 96),
    )(*x_tables(devices, x_local, y_cells), in_vmem(data), in_hbm(green))


places = ("gx", "gl", "gz")


def exchange(data):
    return lax.all_to_all(data, places, split_axis=0, concat_axis=0, tiled=True)


def per_device(tiles, tile_owner, tile_slot, tile_count, green):
    count_gl = lax.axis_size("gl")
    devices = lax.axis_size("gx") * 4 * count_gl
    tile_total, tile_len = tiles.shape[2], tiles.shape[3]
    planes, y_local, x_cells = green.shape[2:]
    y_cells = y_local * devices
    x_local = x_cells // devices
    blocks = y_cells // tile_len
    per_owner = max(2, 2 * tile_total // devices)
    assert planes == 1 and tile_len == 128
    owner_row, slot_row = tile_owner.reshape(1, tile_total), tile_slot.reshape(1, tile_total)
    green = green.reshape(2, 6, y_local, x_cells)
    me = lax.axis_index(places).reshape(1).astype(jnp.int32)
    lists = (owner_row, slot_row, tile_count, me)
    arrived = exchange(pack(tiles, *lists, devices, count_gl, per_owner))
    moved = exchange(slab_waves(arrived, x_local, blocks, count_gl, per_owner))
    mixed = field(moved, green, devices, x_local, y_local, y_cells, count_gl)
    return mixed.reshape(2, 3, planes, y_local, x_cells)


def solution(mesh):
    count_gx, count_gy = mesh.devices.shape
    fine_mesh = jax.sharding.Mesh(
        mesh.devices.reshape(count_gx, 4, count_gy // 4), ("gx", "gz", "gl")
    )
    every = ("gx", "gz", "gl")
    in_specs = (
        P(None, None, every, None),
        P(every, None),
        P(every),
        P(every),
        P(None, None, None, every, None),
    )
    out_specs = P(None, None, None, every, None)
    return jax.shard_map(
        per_device, mesh=fine_mesh, in_specs=in_specs, out_specs=out_specs, check_vma=False
    )
```

```python
import functools
import math

import jax
import jax.numpy as jnp
import numpy as np
from jax import lax
from jax.experimental import pallas as pl
from jax.experimental.pallas import tpu as pltpu
from jax.sharding import PartitionSpec as P

pair_index = ((0, 3, 4), (3, 1, 5), (4, 5, 2))
by_rows = (((1,), (1,)), ((), ()))


def params(mebibytes):
    return pltpu.CompilerParams(vmem_limit_bytes=mebibytes * 1024 * 1024)


def in_hbm(array):
    return pltpu.with_memory_space_constraint(array, pltpu.HBM)


def in_vmem(array):
    return pltpu.with_memory_space_constraint(array, pltpu.VMEM)


def cost(flops, moved):
    return pl.CostEstimate(flops=flops, bytes_accessed=moved, transcendentals=0)


def angles(rows, columns, length):
    products = np.outer(np.arange(rows), np.arange(columns)) % length
    return 2.0 * math.pi / length * products


def split_two(data):
    high = data.astype(jnp.bfloat16)
    return high, (data - high.astype(jnp.float32)).astype(jnp.bfloat16)


def dot_rows(left, right):
    return lax.dot_general(left, right, by_rows, preferred_element_type=jnp.float32)


def dot_rows_split(stacked, data):
    rows = stacked.shape[0] // 2
    high, low = split_two(data)
    both = dot_rows(stacked, high)
    return both[:rows] + both[rows:] + dot_rows(stacked[:rows], low)


def stacked_halves(table):
    return jnp.concatenate(split_two(table[...]))


def flat_fft(values, times):
    length = len(values)
    if length == 1:
        return values
    even = flat_fft(values[0::2], times)
    odd = flat_fft(values[1::2], times)
    lower, upper = [], []
    for k in range(length // 2):
        turned = times(odd[k], k, length)
        lower.append(jax.tree.map(lambda a, b: a + b, even[k], turned))
        upper.append(jax.tree.map(lambda a, b: a - b, even[k], turned))
    return lower + upper


def times_pair(value, k, length):
    real, imag = value
    if k == 0:
        return value
    if 4 * k == length:
        return (imag, -real)
    cos_k = math.cos(2.0 * math.pi * k / length)
    sin_k = math.sin(2.0 * math.pi * k / length)
    return (real * cos_k + imag * sin_k, imag * cos_k - real * sin_k)


def place_of(owner, count_gl):
    shift = count_gl.bit_length() - 1
    z = (owner >> shift) & 3
    return (((owner >> (shift + 2)) << shift) + (owner & (count_gl - 1))) * 4 + z


def owner_order(devices, count_gl):
    order = [0] * devices
    for owner in range(devices):
        order[place_of(owner, count_gl)] = owner
    return order


def pack_kernel(
    devices, count_gl, per_owner, count, me, owner_row, slot_row, tiles, out, *scratch
):
    held, lists, sems = scratch
    comps = range(tiles.shape[1])
    listed = owner_row.shape[1]
    fetches = [
        pltpu.make_async_copy(owner_row, lists.at[0], sems.at[0]),
        pltpu.make_async_copy(slot_row, lists.at[1], sems.at[1]),
    ]
    fetches += [
        pltpu.make_async_copy(tiles.at[:, comp], held.at[i], sems.at[2 + i])
        for i, comp in enumerate(comps)
    ]
    for fetch in fetches:
        fetch.start()
    sender = lax.broadcasted_iota(jnp.int32, (listed, listed), 0)
    reader = lax.broadcasted_iota(jnp.int32, (listed, listed), 1)
    before = jnp.where(sender < reader, 1.0, 0.0).astype(jnp.bfloat16)
    live = lax.broadcasted_iota(jnp.int32, (1, listed), 1) < count[0]
    fetches[0].wait()
    place = jnp.where(live, place_of(lists[0], count_gl), -1)
    place_at = lax.broadcasted_iota(jnp.int32, (devices, listed), 0)
    named = jnp.where(place_at == place, 1.0, 0.0)
    counted = jnp.dot(named.astype(jnp.bfloat16), before, preferred_element_type=jnp.float32)
    rank = jnp.sum(counted * named, axis=0, keepdims=True).astype(jnp.int32)
    target = jnp.where(live, place * per_owner + rank, -1)
    target_at = lax.broadcasted_iota(jnp.int32, (devices * per_owner, listed), 0)
    chosen = jnp.where(target_at == target, 1.0, 0.0).astype(jnp.bfloat16)
    fetches[1].wait()
    stated = lists[1] + 1
    lane = rank + (me[0] & (128 // per_owner - 1)) * per_owner
    lane_at = lax.broadcasted_iota(jnp.int32, (128, listed), 0)
    laned = jnp.where(lane_at == lane, 1.0, 0.0).astype(jnp.bfloat16)
    coarse = (named * (stated >> 5).astype(jnp.float32)).astype(jnp.bfloat16)
    fine = (named * (stated & 31).astype(jnp.float32)).astype(jnp.bfloat16)
    slots = 32.0 * dot_rows(coarse, laned) + dot_rows(fine, laned)
    start = 2 * len(comps) * per_owner
    out[:, start:, :] = jnp.broadcast_to(slots[:, None, :], (devices, 8, 128))
    for i in range(len(comps)):
        fetches[2 + i].wait()
        parts = [part for r in range(2) for part in split_two(held[i, r])]
        got = jnp.dot(
            chosen, jnp.concatenate(parts, axis=1), preferred_element_type=jnp.float32
        )
        for r in range(2):
            whole = got[:, 256 * r : 256 * r + 128] + got[:, 256 * r + 128 : 256 * r + 256]
            start = (2 * i + r) * per_owner
            out[:, start : start + per_owner, :] = whole.reshape(devices, per_owner, 128)


def pack(tiles, owner_row, slot_row, count, me, devices, count_gl, per_owner):
    comps, listed = tiles.shape[1:3]
    rows = 2 * comps * per_owner + 8
    return pl.pallas_call(
        functools.partial(pack_kernel, devices, count_gl, per_owner),
        out_shape=pltpu.VMEM((devices, rows, 128), jnp.float32),
        in_specs=[pl.BlockSpec(memory_space=pltpu.SMEM)] * 2
        + [pl.BlockSpec(memory_space=pltpu.HBM)] * 3,
        out_specs=pl.BlockSpec(memory_space=pltpu.VMEM),
        scratch_shapes=[
            pltpu.VMEM((comps, 2, listed, 128), jnp.float32),
            pltpu.VMEM((2, 1, listed), jnp.int32),
            pltpu.SemaphoreType.DMA((2 + comps,)),
        ],
        compiler_params=params(24),
        cost_estimate=cost(
            devices * per_owner * listed * 512 * 2 * comps, devices * rows * 1024
        ),
    )(count, me, *[in_hbm(a) for a in (owner_row, slot_row, tiles)])


def complex_table(cos_part, sin_part):
    return np.concatenate(
        [
            np.concatenate([cos_part, sin_part], axis=1),
            np.concatenate([-sin_part, cos_part], axis=1),
        ]
    ).astype(np.float32)


def slab_kernel(count, x_local, blocks, per_owner, table, twist, data, out, *scratch):
    chosen, slab, turned = scratch
    devices = data.shape[0]
    entries = devices * per_owner
    group = 128 // x_local
    pairs = blocks // group
    shift = blocks.bit_length() - 1
    every = 128 // per_owner
    stated = [
        sum([data[o, data.shape[1] - 8 :][:1] for o in range(start, start + every)])
        for start in range(0, devices, every)
    ]
    slot = jnp.concatenate(stated, axis=1).astype(jnp.int32) - 1
    landing = jnp.where(slot >= 0, (slot & (blocks - 1)) * x_local + (slot >> shift), -1)
    slab_rows = blocks * x_local
    place = lax.broadcasted_iota(jnp.int32, (slab_rows, entries), 0)
    chosen[...] = jnp.where(place == landing, 1.0, 0.0).astype(jnp.bfloat16)
    stacked = stacked_halves(table)
    step_rows = slab_rows // 2

    def scatter(index, half):
        parts = []
        for r in range(2):
            start = (2 * index + r) * per_owner
            parts.extend(split_two(data[:, start : start + per_owner, :].reshape(entries, 128)))
        rows = pl.ds(half * step_rows, step_rows)
        got = jnp.dot(
            chosen[rows, :], jnp.concatenate(parts, axis=1), preferred_element_type=jnp.float32
        )
        for r in range(2):
            slab[index, r, rows, :] = (
                got[:, 256 * r : 256 * r + 128] + got[:, 256 * r + 128 : 256 * r + 256]
            )

    def transform(index, step):
        at = step * 8
        values = [
            tuple(slab[index, r, pl.ds(t * x_local + at, 8), :] for r in range(2))
            for t in range(blocks)
        ]
        waves = flat_fft(values, times_pair)
        for k in range(blocks):
            real, imag = waves[k]
            cos_k, sin_k = twist[0, k : k + 1, :], twist[1, k : k + 1, :]
            rows = pl.ds(((k % pairs) * group + k // pairs) * x_local + at, 8)
            turned[index % 2, rows, :128] = real * cos_k + imag * sin_k
            turned[index % 2, rows, 128:] = imag * cos_k - real * sin_k

    def along_y(index, start):
        moved = dot_rows_split(stacked, turned[index % 2, start * 128 : (start + 2) * 128, :])
        for k in range(2):
            for r in range(2):
                one = moved[r * 128 : (r + 1) * 128, k * 128 : (k + 1) * 128]
                base = (index * 2 + r) * pairs + start + k
                out[pl.ds(base, 128, stride=count * 2 * pairs), :] = one

    steps = x_local // 8
    scatter(0, 0)
    scatter(0, 1)
    for index in range(count):
        for half in range(2):
            if index + 1 < count:
                scatter(index + 1, half)
            for step in range(half * steps // 2, (half + 1) * steps // 2):
                transform(index, step)
        for start in range(0, pairs, 2):
            along_y(index, start)


def slab_waves(data, x_local, blocks, count_gl, per_owner):
    devices = data.shape[0]
    count = data.shape[1] // (2 * per_owner)
    fine = angles(128, 128, 128)
    order = owner_order(devices, count_gl)
    fine = fine.reshape(devices, 128 // devices, 128)[order].reshape(128, 128)
    table = complex_table(np.cos(fine), np.sin(fine))
    twist_angle = angles(blocks, 128, blocks * 128)
    twist = np.stack([np.cos(twist_angle), np.sin(twist_angle)]).astype(np.float32)
    entries = devices * per_owner
    rows = blocks * x_local * 2
    made = pl.pallas_call(
        functools.partial(slab_kernel, count, x_local, blocks, per_owner),
        out_shape=pltpu.VMEM((count * rows, 128), jnp.float32),
        in_specs=[pl.BlockSpec(memory_space=pltpu.VMEM)] * 3,
        out_specs=pl.BlockSpec(memory_space=pltpu.VMEM),
        scratch_shapes=[
            pltpu.VMEM((blocks * x_local, entries), jnp.bfloat16),
            pltpu.VMEM((count, 2, blocks * x_local, 128), jnp.float32),
            pltpu.VMEM((2, blocks * x_local, 256), jnp.float32),
        ],
        compiler_params=params(40),
        cost_estimate=cost(
            count * blocks * x_local * (entries * 1024 + 512 * 1024),
            count * (entries * 1024 + rows * 512),
        ),
    )(jnp.asarray(table), jnp.asarray(twist), in_vmem(data))
    return made.reshape(devices, count * rows // devices, 128)


def choose(options, mask_of):
    made = options[0]
    for i in range(1, len(options)):
        made = jnp.where(mask_of(i), options[i], made)
    return made


def x_first(sizes, comp, step, twist, data, turned):
    devices, x_local, y_local, blocks, order = sizes
    pairs = blocks * x_local // 128
    kept = y_local // blocks
    at = step * (data.shape[1] // kept) + comp * 2 * pairs
    values = [
        tuple(data[order.index(o), pl.ds(at + r * pairs, pairs), :] for r in range(2))
        for o in range(devices)
    ]
    waves = flat_fft(values, times_pair)
    rows = pl.ds(step * pairs, pairs)
    for k in range(devices):
        real, imag = waves[k]
        cos_k, sin_k = twist[0, k : k + 1, :], twist[1, k : k + 1, :]
        turned[comp % 2, k, rows, :128] = real * cos_k + imag * sin_k
        turned[comp % 2, k, rows, 128:] = imag * cos_k - real * sin_k


def x_second(sizes, comp, start, together, stacked, turned, columns):
    devices, x_local, y_local, blocks, _ = sizes
    group = 128 // x_local
    narrow = (y_local // blocks) * (blocks // group)
    banks = 2 * group
    lane = lax.broadcasted_iota(jnp.int32, (1, 128), 1)
    rows = turned[comp % 2, start : start + together].reshape(together * narrow, 256)
    moved = dot_rows_split(stacked, rows)
    if square(sizes):
        for base in range(0, together, banks):
            rolled = []
            for bank in range(banks):
                one = moved[bank * x_local : (bank + 1) * x_local, base * narrow :][:, :128]
                rolled.append(pltpu.roll(one, bank * narrow, 1) if bank else one)
            for k in range(banks):
                options = [rolled[(place - k) % banks] for place in range(banks)]
                rows = pl.ds(start + base + k, x_local, stride=devices)
                columns[rows, :] = choose(options, lambda i: lane // narrow == i)
        return
    for k in range(together):
        one = jnp.concatenate(
            [
                moved[bank * x_local : (bank + 1) * x_local, k * narrow : (k + 1) * narrow]
                for bank in range(banks)
            ],
            axis=1,
        )
        columns[pl.ds(start + k, x_local, stride=devices), :] = one


def square(sizes):
    _, x_local, y_local, blocks, _ = sizes
    group = 128 // x_local
    narrow = (y_local // blocks) * (blocks // group)
    return 2 * group * narrow == 128 and 128 // narrow == 2 * group


def x_third(sizes, comp, start, columns, kept):
    _, x_local, y_local, blocks, _ = sizes
    group = 128 // x_local
    pairs = blocks // group
    steps = y_local // blocks
    narrow = steps * pairs
    banks = 2 * group
    lane = lax.broadcasted_iota(jnp.int32, (1, 128), 1)
    block = columns[start : start + 128, :].T
    pieces = [block[bank * narrow : (bank + 1) * narrow] for bank in range(banks)]
    for bank in range(banks):
        one = pieces[bank]
        if square(sizes):
            options = [pieces[(bank + k) % banks] for k in range(banks)]
            one = choose(options, lambda i: lane % banks == i)
        for step in range(steps):
            row = step * blocks + (bank % group) * pairs
            kept[comp, bank // group, row : row + pairs, start : start + 128] = one[
                step * pairs : (step + 1) * pairs
            ]


def mix_rows(rows, columns, tensor, waves):
    sums = [None] * 3
    for row in range(3):
        for col in range(3):
            entry = pair_index[row][col]
            green_real, green_imag = tensor[0, entry, rows, columns], tensor[1, entry, rows, columns]
            real, imag = waves[col, 0, rows, columns], waves[col, 1, rows, columns]
            real_term = green_real * real - green_imag * imag
            imag_term = green_real * imag + green_imag * real
            old = sums[row]
            sums[row] = (
                (real_term, imag_term) if old is None else (old[0] + real_term, old[1] + imag_term)
            )
    return sums


def field_kernel(sizes, twist, table, data, green, out, *scratch):
    y_local, x_cells = green.shape[2:]
    turned, columns, tensor, kept, made, in_sem, out_sems = scratch
    width = x_cells // made.shape[0]
    fetch = pltpu.make_async_copy(green, tensor, in_sem)
    fetch.start()
    stacked = stacked_halves(table)
    devices, x_local, _, blocks, _ = sizes
    steps = y_local // blocks
    narrow = y_local * x_local // 128
    together = min(devices, 256 // narrow)
    groups = devices // together
    for step in range(steps):
        x_first(sizes, 0, step, twist, data, turned)
    for comp in range(3):
        for i in range(max(steps, groups)):
            if comp < 2 and i < steps:
                x_first(sizes, comp + 1, i, twist, data, turned)
            if i < groups:
                x_second(sizes, comp, i * together, together, stacked, turned, columns)
        if comp < 2:
            for start in range(0, x_cells, 128):
                x_third(sizes, comp, start, columns, kept)
    fetch.wait()
    sends = []
    for piece in range(made.shape[0]):
        for start in range(piece * width, (piece + 1) * width, 128):
            x_third(sizes, 2, start, columns, kept)
        part = pl.ds(piece * width, width)

        @pl.loop(0, y_local // 8, unroll=2)
        def _(step):
            rows = pl.ds(pl.multiple_of(step * 8, 8), 8)
            for row, pair in enumerate(mix_rows(rows, part, tensor, kept)):
                for r in range(2):
                    made[piece, r, row, rows, :] = pair[r]

        send = pltpu.make_async_copy(made.at[piece], out.at[:, :, :, part], out_sems.at[piece])
        send.start()
        sends.append(send)
    for send in sends:
        send.wait()


def x_tables(devices, x_local, y_cells):
    x_cells = devices * x_local
    group = 128 // x_local
    fine = angles(x_local, x_local, x_local)
    scale = 1.0 / math.sqrt(x_cells * y_cells)
    apart = np.eye(group) * scale
    table = complex_table(np.kron(apart, np.cos(fine)), np.kron(apart, np.sin(fine)))
    angle = np.tile(angles(devices, x_local, x_cells), (1, group))
    twist = np.stack([np.cos(angle), np.sin(angle)]).astype(np.float32)
    return jnp.asarray(twist), jnp.asarray(table)


def x_scratch(devices, x_local, y_local):
    return [
        pltpu.VMEM((2, devices, y_local * x_local // 128, 256), jnp.float32),
        pltpu.VMEM((devices * x_local, 2 * y_local), jnp.float32),
    ]


def field(data, green, devices, x_local, y_local, y_cells, count_gl):
    x_cells = devices * x_local
    pieces = 8
    sizes = (devices, x_local, y_local, y_cells // 128, owner_order(devices, count_gl))
    plane = (y_local, x_cells)
    return pl.pallas_call(
        functools.partial(field_kernel, sizes),
        out_shape=pltpu.HBM((2, 3) + plane, jnp.float32),
        in_specs=[pl.BlockSpec(memory_space=pltpu.VMEM)] * 3
        + [pl.BlockSpec(memory_space=pltpu.HBM)],
        out_specs=pl.BlockSpec(memory_space=pltpu.HBM),
        scratch_shapes=x_scratch(devices, x_local, y_local)
        + [
            pltpu.VMEM((2, 6) + plane, jnp.float32),
            pltpu.VMEM((3, 2) + plane, jnp.float32),
            pltpu.VMEM((pieces, 2, 3, y_local, x_cells // pieces), jnp.float32),
            pltpu.SemaphoreType.DMA(()),
            pltpu.SemaphoreType.DMA((pieces,)),
        ],
        compiler_params=params(40),
        cost_estimate=cost(3 * x_cells * y_local * (x_local * 24 + 24), x_cells * y_local * 96),
    )(*x_tables(devices, x_local, y_cells), in_vmem(data), in_hbm(green))


places = ("gx", "gl", "gz")


def exchange(data):
    return lax.all_to_all(data, places, split_axis=0, concat_axis=0, tiled=True)


def per_device(tiles, tile_owner, tile_slot, tile_count, green):
    count_gl = lax.axis_size("gl")
    devices = lax.axis_size("gx") * 4 * count_gl
    tile_total, tile_len = tiles.shape[2], tiles.shape[3]
    planes, y_local, x_cells = green.shape[2:]
    y_cells = y_local * devices
    x_local = x_cells // devices
    blocks = y_cells // tile_len
    per_owner = max(2, 2 * tile_total // devices)
    assert planes == 1 and tile_len == 128
    owner_row, slot_row = tile_owner.reshape(1, tile_total), tile_slot.reshape(1, tile_total)
    green = green.reshape(2, 6, y_local, x_cells)
    me = lax.axis_index(places).reshape(1).astype(jnp.int32)
    lists = (owner_row, slot_row, tile_count, me)
    arrived = exchange(pack(tiles, *lists, devices, count_gl, per_owner))
    moved = exchange(slab_waves(arrived, x_local, blocks, count_gl, per_owner))
    mixed = field(moved, green, devices, x_local, y_local, y_cells, count_gl)
    return mixed.reshape(2, 3, planes, y_local, x_cells)


def solution(mesh):
    count_gx, count_gy = mesh.devices.shape
    fine_mesh = jax.sharding.Mesh(
        mesh.devices.reshape(count_gx, 4, count_gy // 4), ("gx", "gz", "gl")
    )
    every = ("gx", "gz", "gl")
    in_specs = (
        P(None, None, every, None),
        P(every, None),
        P(every),
        P(every),
        P(None, None, None, every, None),
    )
    out_specs = P(None, None, None, every, None)
    return jax.shard_map(
        per_device, mesh=fine_mesh, in_specs=in_specs, out_specs=out_specs, check_vma=False
    )
```

```python
import functools
import math

import jax
import jax.numpy as jnp
import numpy as np
from jax import lax
from jax.experimental import pallas as pl
from jax.experimental.pallas import tpu as pltpu
from jax.sharding import PartitionSpec as P

pair_index = ((0, 3, 4), (3, 1, 5), (4, 5, 2))
by_rows = (((1,), (1,)), ((), ()))


def params(mebibytes):
    return pltpu.CompilerParams(vmem_limit_bytes=mebibytes * 1024 * 1024)


def in_hbm(array):
    return pltpu.with_memory_space_constraint(array, pltpu.HBM)


def in_vmem(array):
    return pltpu.with_memory_space_constraint(array, pltpu.VMEM)


def cost(flops, moved):
    return pl.CostEstimate(flops=flops, bytes_accessed=moved, transcendentals=0)


def angles(rows, columns, length):
    products = np.outer(np.arange(rows), np.arange(columns)) % length
    return 2.0 * math.pi / length * products


def split_two(data):
    high = data.astype(jnp.bfloat16)
    return high, (data - high.astype(jnp.float32)).astype(jnp.bfloat16)


def dot_rows(left, right):
    return lax.dot_general(left, right, by_rows, preferred_element_type=jnp.float32)


def dot_rows_split(stacked, data):
    rows = stacked.shape[0] // 2
    high, low = split_two(data)
    both = dot_rows(stacked, high)
    return both[:rows] + both[rows:] + dot_rows(stacked[:rows], low)


def stacked_halves(table):
    return jnp.concatenate(split_two(table[...]))


def flat_fft(values, times):
    length = len(values)
    if length == 1:
        return values
    even = flat_fft(values[0::2], times)
    odd = flat_fft(values[1::2], times)
    lower, upper = [], []
    for k in range(length // 2):
        turned = times(odd[k], k, length)
        lower.append(jax.tree.map(lambda a, b: a + b, even[k], turned))
        upper.append(jax.tree.map(lambda a, b: a - b, even[k], turned))
    return lower + upper


def times_pair(value, k, length):
    real, imag = value
    if k == 0:
        return value
    if 4 * k == length:
        return (imag, -real)
    cos_k = math.cos(2.0 * math.pi * k / length)
    sin_k = math.sin(2.0 * math.pi * k / length)
    return (real * cos_k + imag * sin_k, imag * cos_k - real * sin_k)


def place_of(owner, count_gl):
    shift = count_gl.bit_length() - 1
    z = (owner >> shift) & 3
    return (((owner >> (shift + 2)) << shift) + (owner & (count_gl - 1))) * 4 + z


def owner_order(devices, count_gl):
    order = [0] * devices
    for owner in range(devices):
        order[place_of(owner, count_gl)] = owner
    return order


def pack_kernel(
    devices, count_gl, per_owner, count, me, owner_row, slot_row, tiles, out, *scratch
):
    held, lists, sems = scratch
    comps = range(tiles.shape[1])
    listed = owner_row.shape[1]
    fetches = [
        pltpu.make_async_copy(owner_row, lists.at[0], sems.at[0]),
        pltpu.make_async_copy(slot_row, lists.at[1], sems.at[1]),
    ]
    fetches += [
        pltpu.make_async_copy(tiles.at[:, comp], held.at[i], sems.at[2 + i])
        for i, comp in enumerate(comps)
    ]
    for fetch in fetches:
        fetch.start()
    sender = lax.broadcasted_iota(jnp.int32, (listed, listed), 0)
    reader = lax.broadcasted_iota(jnp.int32, (listed, listed), 1)
    before = jnp.where(sender < reader, 1.0, 0.0).astype(jnp.bfloat16)
    live = lax.broadcasted_iota(jnp.int32, (1, listed), 1) < count[0]
    fetches[0].wait()
    place = jnp.where(live, place_of(lists[0], count_gl), -1)
    place_at = lax.broadcasted_iota(jnp.int32, (devices, listed), 0)
    named = jnp.where(place_at == place, 1.0, 0.0)
    counted = jnp.dot(named.astype(jnp.bfloat16), before, preferred_element_type=jnp.float32)
    rank = jnp.sum(counted * named, axis=0, keepdims=True).astype(jnp.int32)
    target = jnp.where(live, place * per_owner + rank, -1)
    target_at = lax.broadcasted_iota(jnp.int32, (devices * per_owner, listed), 0)
    chosen = jnp.where(target_at == target, 1.0, 0.0).astype(jnp.bfloat16)
    fetches[1].wait()
    stated = lists[1] + 1
    lane = rank + (me[0] & (128 // per_owner - 1)) * per_owner
    lane_at = lax.broadcasted_iota(jnp.int32, (128, listed), 0)
    laned = jnp.where(lane_at == lane, 1.0, 0.0).astype(jnp.bfloat16)
    coarse = (named * (stated >> 5).astype(jnp.float32)).astype(jnp.bfloat16)
    fine = (named * (stated & 31).astype(jnp.float32)).astype(jnp.bfloat16)
    slots = 32.0 * dot_rows(coarse, laned) + dot_rows(fine, laned)
    start = 2 * len(comps) * per_owner
    out[:, start:, :] = jnp.broadcast_to(slots[:, None, :], (devices, 8, 128))
    for i in range(len(comps)):
        fetches[2 + i].wait()
        parts = [part for r in range(2) for part in split_two(held[i, r])]
        got = jnp.dot(
            chosen, jnp.concatenate(parts, axis=1), preferred_element_type=jnp.float32
        )
        for r in range(2):
            whole = got[:, 256 * r : 256 * r + 128] + got[:, 256 * r + 128 : 256 * r + 256]
            start = (2 * i + r) * per_owner
            out[:, start : start + per_owner, :] = whole.reshape(devices, per_owner, 128)


def pack(tiles, owner_row, slot_row, count, me, devices, count_gl, per_owner):
    comps, listed = tiles.shape[1:3]
    rows = 2 * comps * per_owner + 8
    return pl.pallas_call(
        functools.partial(pack_kernel, devices, count_gl, per_owner),
        out_shape=pltpu.VMEM((devices, rows, 128), jnp.float32),
        in_specs=[pl.BlockSpec(memory_space=pltpu.SMEM)] * 2
        + [pl.BlockSpec(memory_space=pltpu.HBM)] * 3,
        out_specs=pl.BlockSpec(memory_space=pltpu.VMEM),
        scratch_shapes=[
            pltpu.VMEM((comps, 2, listed, 128), jnp.float32),
            pltpu.VMEM((2, 1, listed), jnp.int32),
            pltpu.SemaphoreType.DMA((2 + comps,)),
        ],
        compiler_params=params(24),
        cost_estimate=cost(
            devices * per_owner * listed * 512 * 2 * comps, devices * rows * 1024
        ),
    )(count, me, *[in_hbm(a) for a in (owner_row, slot_row, tiles)])


def complex_table(cos_part, sin_part):
    return np.concatenate(
        [
            np.concatenate([cos_part, sin_part], axis=1),
            np.concatenate([-sin_part, cos_part], axis=1),
        ]
    ).astype(np.float32)


def slab_kernel(count, x_local, blocks, per_owner, table, twist, data, out, *scratch):
    chosen, slab, turned = scratch
    devices = data.shape[0]
    entries = devices * per_owner
    group = 128 // x_local
    pairs = blocks // group
    shift = blocks.bit_length() - 1
    every = 128 // per_owner
    stated = [
        sum([data[o, data.shape[1] - 8 :][:1] for o in range(start, start + every)])
        for start in range(0, devices, every)
    ]
    slot = jnp.concatenate(stated, axis=1).astype(jnp.int32) - 1
    landing = jnp.where(slot >= 0, (slot & (blocks - 1)) * x_local + (slot >> shift), -1)
    slab_rows = blocks * x_local
    place = lax.broadcasted_iota(jnp.int32, (slab_rows, entries), 0)
    chosen[...] = jnp.where(place == landing, 1.0, 0.0).astype(jnp.bfloat16)
    stacked = stacked_halves(table)
    step_rows = slab_rows // 2

    def scatter(index, half):
        parts = []
        for r in range(2):
            start = (2 * index + r) * per_owner
            parts.extend(split_two(data[:, start : start + per_owner, :].reshape(entries, 128)))
        rows = pl.ds(half * step_rows, step_rows)
        got = jnp.dot(
            chosen[rows, :], jnp.concatenate(parts, axis=1), preferred_element_type=jnp.float32
        )
        for r in range(2):
            slab[index, r, rows, :] = (
                got[:, 256 * r : 256 * r + 128] + got[:, 256 * r + 128 : 256 * r + 256]
            )

    def transform(index, step):
        at = step * 8
        values = [
            tuple(slab[index, r, pl.ds(t * x_local + at, 8), :] for r in range(2))
            for t in range(blocks)
        ]
        waves = flat_fft(values, times_pair)
        for k in range(blocks):
            real, imag = waves[k]
            cos_k, sin_k = twist[0, k : k + 1, :], twist[1, k : k + 1, :]
            rows = pl.ds(((k % pairs) * group + k // pairs) * x_local + at, 8)
            turned[index % 2, rows, :128] = real * cos_k + imag * sin_k
            turned[index % 2, rows, 128:] = imag * cos_k - real * sin_k

    def along_y(index, start):
        moved = dot_rows_split(stacked, turned[index % 2, start * 128 : (start + 2) * 128, :])
        for k in range(2):
            for r in range(2):
                one = moved[r * 128 : (r + 1) * 128, k * 128 : (k + 1) * 128]
                base = (index * 2 + r) * pairs + start + k
                out[pl.ds(base, 128, stride=count * 2 * pairs), :] = one

    steps = x_local // 8
    scatter(0, 0)
    scatter(0, 1)
    for index in range(count):
        for half in range(2):
            if index + 1 < count:
                scatter(index + 1, half)
            for step in range(half * steps // 2, (half + 1) * steps // 2):
                transform(index, step)
        for start in range(0, pairs, 2):
            along_y(index, start)


def slab_waves(data, x_local, blocks, count_gl, per_owner):
    devices = data.shape[0]
    count = data.shape[1] // (2 * per_owner)
    fine = angles(128, 128, 128)
    order = owner_order(devices, count_gl)
    fine = fine.reshape(devices, 128 // devices, 128)[order].reshape(128, 128)
    table = complex_table(np.cos(fine), np.sin(fine))
    twist_angle = angles(blocks, 128, blocks * 128)
    twist = np.stack([np.cos(twist_angle), np.sin(twist_angle)]).astype(np.float32)
    entries = devices * per_owner
    rows = blocks * x_local * 2
    made = pl.pallas_call(
        functools.partial(slab_kernel, count, x_local, blocks, per_owner),
        out_shape=pltpu.VMEM((count * rows, 128), jnp.float32),
        in_specs=[pl.BlockSpec(memory_space=pltpu.VMEM)] * 3,
        out_specs=pl.BlockSpec(memory_space=pltpu.VMEM),
        scratch_shapes=[
            pltpu.VMEM((blocks * x_local, entries), jnp.bfloat16),
            pltpu.VMEM((count, 2, blocks * x_local, 128), jnp.float32),
            pltpu.VMEM((2, blocks * x_local, 256), jnp.float32),
        ],
        compiler_params=params(40),
        cost_estimate=cost(
            count * blocks * x_local * (entries * 1024 + 512 * 1024),
            count * (entries * 1024 + rows * 512),
        ),
    )(jnp.asarray(table), jnp.asarray(twist), in_vmem(data))
    return made.reshape(devices, count * rows // devices, 128)


def choose(options, mask_of):
    made = options[0]
    for i in range(1, len(options)):
        made = jnp.where(mask_of(i), options[i], made)
    return made


def x_first(sizes, comp, step, twist, data, turned):
    devices, x_local, y_local, blocks, order = sizes
    pairs = blocks * x_local // 128
    kept = y_local // blocks
    at = pl.multiple_of(step * (data.shape[1] // kept), 2 * pairs) + comp * 2 * pairs
    values = [
        tuple(data[order.index(o), pl.ds(at + r * pairs, pairs), :] for r in range(2))
        for o in range(devices)
    ]
    waves = flat_fft(values, times_pair)
    rows = pl.ds(pl.multiple_of(step * pairs, pairs), pairs)
    for k in range(devices):
        real, imag = waves[k]
        cos_k, sin_k = twist[0, k : k + 1, :], twist[1, k : k + 1, :]
        turned[comp % 2, k, rows, :128] = real * cos_k + imag * sin_k
        turned[comp % 2, k, rows, 128:] = imag * cos_k - real * sin_k


def x_second(sizes, comp, step, together, stacked, turned, columns):
    devices, x_local, y_local, blocks, _ = sizes
    group = 128 // x_local
    narrow = (y_local // blocks) * (blocks // group)
    banks = 2 * group
    lane = lax.broadcasted_iota(jnp.int32, (1, 128), 1)
    start = step * together
    rows = turned[comp % 2, pl.ds(start, together)].reshape(together * narrow, 256)
    moved = dot_rows_split(stacked, rows)
    if square(sizes):
        for base in range(0, together, banks):
            rolled = []
            for bank in range(banks):
                one = moved[bank * x_local : (bank + 1) * x_local, base * narrow :][:, :128]
                rolled.append(pltpu.roll(one, bank * narrow, 1) if bank else one)
            for k in range(banks):
                options = [rolled[(place - k) % banks] for place in range(banks)]
                rows = pl.ds(start + base + k, x_local, stride=devices)
                columns[comp, rows, :] = choose(options, lambda i: lane // narrow == i)
        return
    for k in range(together):
        one = jnp.concatenate(
            [
                moved[bank * x_local : (bank + 1) * x_local, k * narrow : (k + 1) * narrow]
                for bank in range(banks)
            ],
            axis=1,
        )
        columns[comp, pl.ds(start + k, x_local, stride=devices), :] = one


def square(sizes):
    _, x_local, y_local, blocks, _ = sizes
    group = 128 // x_local
    narrow = (y_local // blocks) * (blocks // group)
    return 2 * group * narrow == 128 and 128 // narrow == 2 * group


def x_third(sizes, comp, start, columns, kept):
    _, x_local, y_local, blocks, _ = sizes
    group = 128 // x_local
    pairs = blocks // group
    steps = y_local // blocks
    narrow = steps * pairs
    banks = 2 * group
    lane = lax.broadcasted_iota(jnp.int32, (1, 128), 1)
    block = columns[comp, start : start + 128, :].T
    pieces = [block[bank * narrow : (bank + 1) * narrow] for bank in range(banks)]
    for bank in range(banks):
        one = pieces[bank]
        if square(sizes):
            options = [pieces[(bank + k) % banks] for k in range(banks)]
            one = choose(options, lambda i: lane % banks == i)
        for step in range(steps):
            row = step * blocks + (bank % group) * pairs
            kept[comp, bank // group, row : row + pairs, start : start + 128] = one[
                step * pairs : (step + 1) * pairs
            ]


def mix_rows(rows, columns, tensor, waves):
    sums = [None] * 3
    for row in range(3):
        for col in range(3):
            entry = pair_index[row][col]
            green_real, green_imag = tensor[0, entry, rows, columns], tensor[1, entry, rows, columns]
            real, imag = waves[col, 0, rows, columns], waves[col, 1, rows, columns]
            real_term = green_real * real - green_imag * imag
            imag_term = green_real * imag + green_imag * real
            old = sums[row]
            sums[row] = (
                (real_term, imag_term) if old is None else (old[0] + real_term, old[1] + imag_term)
            )
    return sums


def field_kernel(sizes, twist, table, data, green, out, *scratch):
    y_local, x_cells = green.shape[2:]
    turned, columns, tensor, kept, made, in_sem, out_sems = scratch
    width = x_cells // made.shape[0]
    fetch = pltpu.make_async_copy(green, tensor, in_sem)
    fetch.start()
    stacked = stacked_halves(table)
    devices, x_local, _, blocks, _ = sizes
    steps = y_local // blocks
    narrow = y_local * x_local // 128
    together = min(devices, 256 // narrow)
    groups = devices // together
    pl.loop(0, steps)(lambda i: x_first(sizes, 0, i, twist, data, turned))
    for comp in range(3):

        @pl.loop(0, groups)
        def _(i):
            if comp < 2 and steps == groups:
                x_first(sizes, comp + 1, i, twist, data, turned)
            x_second(sizes, comp, i, together, stacked, turned, columns)

        if comp < 2 and steps != groups:
            pl.loop(0, steps)(lambda i: x_first(sizes, comp + 1, i, twist, data, turned))
    fetch.wait()
    pieces = made.shape[0]

    def turn(piece):
        for start in range(piece * width, (piece + 1) * width, 128):
            for comp in range(3):
                x_third(sizes, comp, start, columns, kept)

    sends = []
    turn(0)
    for piece in range(pieces):
        if piece + 1 < pieces:
            turn(piece + 1)
        part = pl.ds(piece * width, width)
        for step in range(y_local // 8):
            rows = pl.ds(step * 8, 8)
            for row, pair in enumerate(mix_rows(rows, part, tensor, kept)):
                for r in range(2):
                    made[piece, r, row, rows, :] = pair[r]
        send = pltpu.make_async_copy(made.at[piece], out.at[:, :, :, part], out_sems.at[piece])
        send.start()
        sends.append(send)
    for send in sends:
        send.wait()


def x_tables(devices, x_local, y_cells):
    x_cells = devices * x_local
    group = 128 // x_local
    fine = angles(x_local, x_local, x_local)
    scale = 1.0 / math.sqrt(x_cells * y_cells)
    apart = np.eye(group) * scale
    table = complex_table(np.kron(apart, np.cos(fine)), np.kron(apart, np.sin(fine)))
    angle = np.tile(angles(devices, x_local, x_cells), (1, group))
    twist = np.stack([np.cos(angle), np.sin(angle)]).astype(np.float32)
    return jnp.asarray(twist), jnp.asarray(table)


def x_scratch(devices, x_local, y_local):
    return [
        pltpu.VMEM((2, devices, y_local * x_local // 128, 256), jnp.float32),
        pltpu.VMEM((3, devices * x_local, 2 * y_local), jnp.float32),
    ]


def field(data, green, devices, x_local, y_local, y_cells, count_gl):
    x_cells = devices * x_local
    pieces = 8
    sizes = (devices, x_local, y_local, y_cells // 128, owner_order(devices, count_gl))
    plane = (y_local, x_cells)
    return pl.pallas_call(
        functools.partial(field_kernel, sizes),
        out_shape=pltpu.HBM((2, 3) + plane, jnp.float32),
        in_specs=[pl.BlockSpec(memory_space=pltpu.VMEM)] * 3
        + [pl.BlockSpec(memory_space=pltpu.HBM)],
        out_specs=pl.BlockSpec(memory_space=pltpu.HBM),
        scratch_shapes=x_scratch(devices, x_local, y_local)
        + [
            pltpu.VMEM((2, 6) + plane, jnp.float32),
            pltpu.VMEM((3, 2) + plane, jnp.float32),
            pltpu.VMEM((pieces, 2, 3, y_local, x_cells // pieces), jnp.float32),
            pltpu.SemaphoreType.DMA(()),
            pltpu.SemaphoreType.DMA((pieces,)),
        ],
        compiler_params=params(40),
        cost_estimate=cost(3 * x_cells * y_local * (x_local * 24 + 24), x_cells * y_local * 96),
    )(*x_tables(devices, x_local, y_cells), in_vmem(data), in_hbm(green))


places = ("gx", "gl", "gz")


def exchange(data):
    return lax.all_to_all(data, places, split_axis=0, concat_axis=0, tiled=True)


def per_device(tiles, tile_owner, tile_slot, tile_count, green):
    count_gl = lax.axis_size("gl")
    devices = lax.axis_size("gx") * 4 * count_gl
    tile_total, tile_len = tiles.shape[2], tiles.shape[3]
    planes, y_local, x_cells = green.shape[2:]
    y_cells = y_local * devices
    x_local = x_cells // devices
    blocks = y_cells // tile_len
    per_owner = max(2, 2 * tile_total // devices)
    assert planes == 1 and tile_len == 128
    owner_row, slot_row = tile_owner.reshape(1, tile_total), tile_slot.reshape(1, tile_total)
    green = green.reshape(2, 6, y_local, x_cells)
    me = lax.axis_index(places).reshape(1).astype(jnp.int32)
    lists = (owner_row, slot_row, tile_count, me)
    arrived = exchange(pack(tiles, *lists, devices, count_gl, per_owner))
    moved = exchange(slab_waves(arrived, x_local, blocks, count_gl, per_owner))
    mixed = field(moved, green, devices, x_local, y_local, y_cells, count_gl)
    return mixed.reshape(2, 3, planes, y_local, x_cells)


def solution(mesh):
    count_gx, count_gy = mesh.devices.shape
    fine_mesh = jax.sharding.Mesh(
        mesh.devices.reshape(count_gx, 4, count_gy // 4), ("gx", "gz", "gl")
    )
    every = ("gx", "gz", "gl")
    in_specs = (
        P(None, None, every, None),
        P(every, None),
        P(every),
        P(every),
        P(None, None, None, every, None),
    )
    out_specs = P(None, None, None, every, None)
    return jax.shard_map(
        per_device, mesh=fine_mesh, in_specs=in_specs, out_specs=out_specs, check_vma=False
    )
```

```python
import functools
import math

import jax
import jax.numpy as jnp
import numpy as np
from jax import lax
from jax.experimental import pallas as pl
from jax.experimental.pallas import tpu as pltpu
from jax.sharding import PartitionSpec as P

pair_index = ((0, 3, 4), (3, 1, 5), (4, 5, 2))
by_rows = (((1,), (1,)), ((), ()))


def params(mebibytes):
    return pltpu.CompilerParams(vmem_limit_bytes=mebibytes * 1024 * 1024)


def in_hbm(array):
    return pltpu.with_memory_space_constraint(array, pltpu.HBM)


def in_vmem(array):
    return pltpu.with_memory_space_constraint(array, pltpu.VMEM)


def cost(flops, moved):
    return pl.CostEstimate(flops=flops, bytes_accessed=moved, transcendentals=0)


def angles(rows, columns, length):
    products = np.outer(np.arange(rows), np.arange(columns)) % length
    return 2.0 * math.pi / length * products


def split_two(data):
    high = data.astype(jnp.bfloat16)
    return high, (data - high.astype(jnp.float32)).astype(jnp.bfloat16)


def dot_rows(left, right):
    return lax.dot_general(left, right, by_rows, preferred_element_type=jnp.float32)


def dot_rows_split(stacked, data):
    rows = stacked.shape[0] // 2
    high, low = split_two(data)
    both = dot_rows(stacked, high)
    return both[:rows] + both[rows:] + dot_rows(stacked[:rows], low)


def stacked_halves(table):
    return jnp.concatenate(split_two(table[...]))


def flat_fft(values, times):
    length = len(values)
    if length == 1:
        return values
    even = flat_fft(values[0::2], times)
    odd = flat_fft(values[1::2], times)
    lower, upper = [], []
    for k in range(length // 2):
        turned = times(odd[k], k, length)
        lower.append(jax.tree.map(lambda a, b: a + b, even[k], turned))
        upper.append(jax.tree.map(lambda a, b: a - b, even[k], turned))
    return lower + upper


def times_pair(value, k, length):
    real, imag = value
    if k == 0:
        return value
    if 4 * k == length:
        return (imag, -real)
    cos_k = math.cos(2.0 * math.pi * k / length)
    sin_k = math.sin(2.0 * math.pi * k / length)
    return (real * cos_k + imag * sin_k, imag * cos_k - real * sin_k)


def place_of(owner, count_gl):
    shift = count_gl.bit_length() - 1
    z = (owner >> shift) & 3
    return (((owner >> (shift + 2)) << shift) + (owner & (count_gl - 1))) * 4 + z


def owner_order(devices, count_gl):
    order = [0] * devices
    for owner in range(devices):
        order[place_of(owner, count_gl)] = owner
    return order


def pack_kernel(
    devices, count_gl, per_owner, count, me, owner_row, slot_row, tiles, out, *scratch
):
    held, lists, sems = scratch
    comps = range(tiles.shape[1])
    listed = owner_row.shape[1]
    fetches = [
        pltpu.make_async_copy(owner_row, lists.at[0], sems.at[0]),
        pltpu.make_async_copy(slot_row, lists.at[1], sems.at[1]),
    ]
    fetches += [
        pltpu.make_async_copy(tiles.at[:, comp], held.at[i], sems.at[2 + i])
        for i, comp in enumerate(comps)
    ]
    for fetch in fetches:
        fetch.start()
    sender = lax.broadcasted_iota(jnp.int32, (listed, listed), 0)
    reader = lax.broadcasted_iota(jnp.int32, (listed, listed), 1)
    before = jnp.where(sender < reader, 1.0, 0.0).astype(jnp.bfloat16)
    live = lax.broadcasted_iota(jnp.int32, (1, listed), 1) < count[0]
    fetches[0].wait()
    place = jnp.where(live, place_of(lists[0], count_gl), -1)
    place_at = lax.broadcasted_iota(jnp.int32, (devices, listed), 0)
    named = jnp.where(place_at == place, 1.0, 0.0)
    counted = jnp.dot(named.astype(jnp.bfloat16), before, preferred_element_type=jnp.float32)
    rank = jnp.sum(counted * named, axis=0, keepdims=True).astype(jnp.int32)
    target = jnp.where(live, place * per_owner + rank, -1)
    target_at = lax.broadcasted_iota(jnp.int32, (devices * per_owner, listed), 0)
    chosen = jnp.where(target_at == target, 1.0, 0.0).astype(jnp.bfloat16)
    fetches[1].wait()
    stated = lists[1] + 1
    lane = rank + (me[0] & (128 // per_owner - 1)) * per_owner
    lane_at = lax.broadcasted_iota(jnp.int32, (128, listed), 0)
    laned = jnp.where(lane_at == lane, 1.0, 0.0).astype(jnp.bfloat16)
    coarse = (named * (stated >> 5).astype(jnp.float32)).astype(jnp.bfloat16)
    fine = (named * (stated & 31).astype(jnp.float32)).astype(jnp.bfloat16)
    slots = 32.0 * dot_rows(coarse, laned) + dot_rows(fine, laned)
    start = 2 * len(comps) * per_owner
    out[:, start:, :] = jnp.broadcast_to(slots[:, None, :], (devices, 8, 128))
    for i in range(len(comps)):
        fetches[2 + i].wait()
        parts = [part for r in range(2) for part in split_two(held[i, r])]
        got = jnp.dot(
            chosen, jnp.concatenate(parts, axis=1), preferred_element_type=jnp.float32
        )
        for r in range(2):
            whole = got[:, 256 * r : 256 * r + 128] + got[:, 256 * r + 128 : 256 * r + 256]
            start = (2 * i + r) * per_owner
            out[:, start : start + per_owner, :] = whole.reshape(devices, per_owner, 128)


def pack(tiles, owner_row, slot_row, count, me, devices, count_gl, per_owner):
    comps, listed = tiles.shape[1:3]
    rows = 2 * comps * per_owner + 8
    return pl.pallas_call(
        functools.partial(pack_kernel, devices, count_gl, per_owner),
        out_shape=pltpu.VMEM((devices, rows, 128), jnp.float32),
        in_specs=[pl.BlockSpec(memory_space=pltpu.SMEM)] * 2
        + [pl.BlockSpec(memory_space=pltpu.HBM)] * 3,
        out_specs=pl.BlockSpec(memory_space=pltpu.VMEM),
        scratch_shapes=[
            pltpu.VMEM((comps, 2, listed, 128), jnp.float32),
            pltpu.VMEM((2, 1, listed), jnp.int32),
            pltpu.SemaphoreType.DMA((2 + comps,)),
        ],
        compiler_params=params(24),
        cost_estimate=cost(
            devices * per_owner * listed * 512 * 2 * comps, devices * rows * 1024
        ),
    )(count, me, *[in_hbm(a) for a in (owner_row, slot_row, tiles)])


def complex_table(cos_part, sin_part):
    return np.concatenate(
        [
            np.concatenate([cos_part, sin_part], axis=1),
            np.concatenate([-sin_part, cos_part], axis=1),
        ]
    ).astype(np.float32)


def slab_kernel(count, x_local, blocks, per_owner, table, twist, data, out, *scratch):
    chosen, slab, turned = scratch
    devices = data.shape[0]
    entries = devices * per_owner
    group = 128 // x_local
    pairs = blocks // group
    shift = blocks.bit_length() - 1
    every = 128 // per_owner
    stated = [
        sum([data[o, data.shape[1] - 8 :][:1] for o in range(start, start + every)])
        for start in range(0, devices, every)
    ]
    slot = jnp.concatenate(stated, axis=1).astype(jnp.int32) - 1
    landing = jnp.where(slot >= 0, (slot & (blocks - 1)) * x_local + (slot >> shift), -1)
    slab_rows = blocks * x_local
    place = lax.broadcasted_iota(jnp.int32, (slab_rows, entries), 0)
    chosen[...] = jnp.where(place == landing, 1.0, 0.0).astype(jnp.bfloat16)
    stacked = stacked_halves(table)
    step_rows = slab_rows // 2

    def scatter(index, half):
        parts = []
        for r in range(2):
            start = (2 * index + r) * per_owner
            parts.extend(split_two(data[:, start : start + per_owner, :].reshape(entries, 128)))
        rows = pl.ds(half * step_rows, step_rows)
        got = jnp.dot(
            chosen[rows, :], jnp.concatenate(parts, axis=1), preferred_element_type=jnp.float32
        )
        for r in range(2):
            slab[index, r, rows, :] = (
                got[:, 256 * r : 256 * r + 128] + got[:, 256 * r + 128 : 256 * r + 256]
            )

    def transform(index, step):
        at = step * 8
        values = [
            tuple(slab[index, r, pl.ds(t * x_local + at, 8), :] for r in range(2))
            for t in range(blocks)
        ]
        waves = flat_fft(values, times_pair)
        for k in range(blocks):
            real, imag = waves[k]
            cos_k, sin_k = twist[0, k : k + 1, :], twist[1, k : k + 1, :]
            rows = pl.ds(((k % pairs) * group + k // pairs) * x_local + at, 8)
            turned[index % 2, rows, :128] = real * cos_k + imag * sin_k
            turned[index % 2, rows, 128:] = imag * cos_k - real * sin_k

    def along_y(index, start):
        moved = dot_rows_split(stacked, turned[index % 2, start * 128 : (start + 2) * 128, :])
        for k in range(2):
            for r in range(2):
                one = moved[r * 128 : (r + 1) * 128, k * 128 : (k + 1) * 128]
                base = (index * 2 + r) * pairs + start + k
                out[pl.ds(base, 128, stride=count * 2 * pairs), :] = one

    steps = x_local // 8
    scatter(0, 0)
    scatter(0, 1)
    for index in range(count):
        for half in range(2):
            if index + 1 < count:
                scatter(index + 1, half)
            for step in range(half * steps // 2, (half + 1) * steps // 2):
                transform(index, step)
        for start in range(0, pairs, 2):
            along_y(index, start)


def slab_waves(data, x_local, blocks, count_gl, per_owner):
    devices = data.shape[0]
    count = data.shape[1] // (2 * per_owner)
    fine = angles(128, 128, 128)
    order = owner_order(devices, count_gl)
    fine = fine.reshape(devices, 128 // devices, 128)[order].reshape(128, 128)
    table = complex_table(np.cos(fine), np.sin(fine))
    twist_angle = angles(blocks, 128, blocks * 128)
    twist = np.stack([np.cos(twist_angle), np.sin(twist_angle)]).astype(np.float32)
    entries = devices * per_owner
    rows = blocks * x_local * 2
    made = pl.pallas_call(
        functools.partial(slab_kernel, count, x_local, blocks, per_owner),
        out_shape=pltpu.VMEM((count * rows, 128), jnp.float32),
        in_specs=[pl.BlockSpec(memory_space=pltpu.VMEM)] * 3,
        out_specs=pl.BlockSpec(memory_space=pltpu.VMEM),
        scratch_shapes=[
            pltpu.VMEM((blocks * x_local, entries), jnp.bfloat16),
            pltpu.VMEM((count, 2, blocks * x_local, 128), jnp.float32),
            pltpu.VMEM((2, blocks * x_local, 256), jnp.float32),
        ],
        compiler_params=params(40),
        cost_estimate=cost(
            count * blocks * x_local * (entries * 1024 + 512 * 1024),
            count * (entries * 1024 + rows * 512),
        ),
    )(jnp.asarray(table), jnp.asarray(twist), in_vmem(data))
    return made.reshape(devices, count * rows // devices, 128)


def choose(options, mask_of):
    made = options[0]
    for i in range(1, len(options)):
        made = jnp.where(mask_of(i), options[i], made)
    return made


def x_first(sizes, comp, step, twist, data, turned):
    devices, x_local, y_local, blocks, order = sizes
    pairs = blocks * x_local // 128
    kept = y_local // blocks
    at = pl.multiple_of(step * (data.shape[1] // kept), 2 * pairs) + comp * 2 * pairs
    values = [
        tuple(data[order.index(o), pl.ds(at + r * pairs, pairs), :] for r in range(2))
        for o in range(devices)
    ]
    waves = flat_fft(values, times_pair)
    rows = pl.ds(pl.multiple_of(step * pairs, pairs), pairs)
    for k in range(devices):
        real, imag = waves[k]
        cos_k, sin_k = twist[0, k : k + 1, :], twist[1, k : k + 1, :]
        turned[comp % 2, k, rows, :128] = real * cos_k + imag * sin_k
        turned[comp % 2, k, rows, 128:] = imag * cos_k - real * sin_k


def x_second(sizes, comp, step, together, stacked, turned, columns):
    devices, x_local, y_local, blocks, _ = sizes
    group = 128 // x_local
    narrow = (y_local // blocks) * (blocks // group)
    banks = 2 * group
    lane = lax.broadcasted_iota(jnp.int32, (1, 128), 1)
    start = step * together
    rows = turned[comp % 2, pl.ds(start, together)].reshape(together * narrow, 256)
    moved = dot_rows_split(stacked, rows)
    if square(sizes):
        for base in range(0, together, banks):
            rolled = []
            for bank in range(banks):
                one = moved[bank * x_local : (bank + 1) * x_local, base * narrow :][:, :128]
                rolled.append(pltpu.roll(one, bank * narrow, 1) if bank else one)
            for k in range(banks):
                options = [rolled[(place - k) % banks] for place in range(banks)]
                rows = pl.ds(start + base + k, x_local, stride=devices)
                columns[comp, rows, :] = choose(options, lambda i: lane // narrow == i)
        return
    for k in range(together):
        one = jnp.concatenate(
            [
                moved[bank * x_local : (bank + 1) * x_local, k * narrow : (k + 1) * narrow]
                for bank in range(banks)
            ],
            axis=1,
        )
        columns[comp, pl.ds(start + k, x_local, stride=devices), :] = one


def square(sizes):
    _, x_local, y_local, blocks, _ = sizes
    group = 128 // x_local
    narrow = (y_local // blocks) * (blocks // group)
    return 2 * group * narrow == 128 and 128 // narrow == 2 * group


def x_third(sizes, comp, start, columns, kept):
    _, x_local, y_local, blocks, _ = sizes
    group = 128 // x_local
    pairs = blocks // group
    steps = y_local // blocks
    narrow = steps * pairs
    banks = 2 * group
    lane = lax.broadcasted_iota(jnp.int32, (1, 128), 1)
    block = columns[comp, start : start + 128, :].T
    pieces = [block[bank * narrow : (bank + 1) * narrow] for bank in range(banks)]
    for bank in range(banks):
        one = pieces[bank]
        if square(sizes):
            options = [pieces[(bank + k) % banks] for k in range(banks)]
            one = choose(options, lambda i: lane % banks == i)
        for step in range(steps):
            row = step * blocks + (bank % group) * pairs
            kept[comp, bank // group, row : row + pairs, start : start + 128] = one[
                step * pairs : (step + 1) * pairs
            ]


def mix_rows(rows, columns, tensor, waves):
    sums = [None] * 3
    for row in range(3):
        for col in range(3):
            entry = pair_index[row][col]
            green_real, green_imag = tensor[0, entry, rows, columns], tensor[1, entry, rows, columns]
            real, imag = waves[col, 0, rows, columns], waves[col, 1, rows, columns]
            real_term = green_real * real - green_imag * imag
            imag_term = green_real * imag + green_imag * real
            old = sums[row]
            sums[row] = (
                (real_term, imag_term) if old is None else (old[0] + real_term, old[1] + imag_term)
            )
    return sums


def field_kernel(sizes, twist, table, data, green, out, *scratch):
    y_local, x_cells = green.shape[2:]
    turned, columns, tensor, kept, made, in_sem, out_sems = scratch
    width = x_cells // made.shape[0]
    fetch = pltpu.make_async_copy(green, tensor, in_sem)
    fetch.start()
    stacked = stacked_halves(table)
    devices, x_local, _, blocks, _ = sizes
    steps = y_local // blocks
    narrow = y_local * x_local // 128
    together = min(devices, 256 // narrow)
    groups = devices // together
    blocks_each = x_cells // 128 // groups
    for comp in range(3):
        pl.loop(0, steps)(lambda i: x_first(sizes, comp, i, twist, data, turned))
        for i in range(groups):
            x_second(sizes, comp, i, together, stacked, turned, columns)
            for block in range(i * blocks_each, (i + 1) * blocks_each):
                if comp > 0:
                    x_third(sizes, comp - 1, block * 128, columns, kept)
    fetch.wait()
    sends = []
    for piece in range(made.shape[0]):
        for start in range(piece * width, (piece + 1) * width, 128):
            x_third(sizes, 2, start, columns, kept)
        part = pl.ds(piece * width, width)

        @pl.loop(0, y_local // 8, unroll=2)
        def _(step):
            rows = pl.ds(pl.multiple_of(step * 8, 8), 8)
            for row, pair in enumerate(mix_rows(rows, part, tensor, kept)):
                for r in range(2):
                    made[piece, r, row, rows, :] = pair[r]

        send = pltpu.make_async_copy(made.at[piece], out.at[:, :, :, part], out_sems.at[piece])
        send.start()
        sends.append(send)
    for send in sends:
        send.wait()


def x_tables(devices, x_local, y_cells):
    x_cells = devices * x_local
    group = 128 // x_local
    fine = angles(x_local, x_local, x_local)
    scale = 1.0 / math.sqrt(x_cells * y_cells)
    apart = np.eye(group) * scale
    table = complex_table(np.kron(apart, np.cos(fine)), np.kron(apart, np.sin(fine)))
    angle = np.tile(angles(devices, x_local, x_cells), (1, group))
    twist = np.stack([np.cos(angle), np.sin(angle)]).astype(np.float32)
    return jnp.asarray(twist), jnp.asarray(table)


def x_scratch(devices, x_local, y_local):
    return [
        pltpu.VMEM((2, devices, y_local * x_local // 128, 256), jnp.float32),
        pltpu.VMEM((3, devices * x_local, 2 * y_local), jnp.float32),
    ]


def field(data, green, devices, x_local, y_local, y_cells, count_gl):
    x_cells = devices * x_local
    pieces = 8
    sizes = (devices, x_local, y_local, y_cells // 128, owner_order(devices, count_gl))
    plane = (y_local, x_cells)
    return pl.pallas_call(
        functools.partial(field_kernel, sizes),
        out_shape=pltpu.HBM((2, 3) + plane, jnp.float32),
        in_specs=[pl.BlockSpec(memory_space=pltpu.VMEM)] * 3
        + [pl.BlockSpec(memory_space=pltpu.HBM)],
        out_specs=pl.BlockSpec(memory_space=pltpu.HBM),
        scratch_shapes=x_scratch(devices, x_local, y_local)
        + [
            pltpu.VMEM((2, 6) + plane, jnp.float32),
            pltpu.VMEM((3, 2) + plane, jnp.float32),
            pltpu.VMEM((pieces, 2, 3, y_local, x_cells // pieces), jnp.float32),
            pltpu.SemaphoreType.DMA(()),
            pltpu.SemaphoreType.DMA((pieces,)),
        ],
        compiler_params=params(40),
        cost_estimate=cost(3 * x_cells * y_local * (x_local * 24 + 24), x_cells * y_local * 96),
    )(*x_tables(devices, x_local, y_cells), in_vmem(data), in_hbm(green))


places = ("gx", "gl", "gz")


def exchange(data):
    return lax.all_to_all(data, places, split_axis=0, concat_axis=0, tiled=True)


def per_device(tiles, tile_owner, tile_slot, tile_count, green):
    count_gl = lax.axis_size("gl")
    devices = lax.axis_size("gx") * 4 * count_gl
    tile_total, tile_len = tiles.shape[2], tiles.shape[3]
    planes, y_local, x_cells = green.shape[2:]
    y_cells = y_local * devices
    x_local = x_cells // devices
    blocks = y_cells // tile_len
    per_owner = max(2, 2 * tile_total // devices)
    assert planes == 1 and tile_len == 128
    owner_row, slot_row = tile_owner.reshape(1, tile_total), tile_slot.reshape(1, tile_total)
    green = green.reshape(2, 6, y_local, x_cells)
    me = lax.axis_index(places).reshape(1).astype(jnp.int32)
    lists = (owner_row, slot_row, tile_count, me)
    arrived = exchange(pack(tiles, *lists, devices, count_gl, per_owner))
    moved = exchange(slab_waves(arrived, x_local, blocks, count_gl, per_owner))
    mixed = field(moved, green, devices, x_local, y_local, y_cells, count_gl)
    return mixed.reshape(2, 3, planes, y_local, x_cells)


def solution(mesh):
    count_gx, count_gy = mesh.devices.shape
    fine_mesh = jax.sharding.Mesh(
        mesh.devices.reshape(count_gx, 4, count_gy // 4), ("gx", "gz", "gl")
    )
    every = ("gx", "gz", "gl")
    in_specs = (
        P(None, None, every, None),
        P(every, None),
        P(every),
        P(every),
        P(None, None, None, every, None),
    )
    out_specs = P(None, None, None, every, None)
    return jax.shard_map(
        per_device, mesh=fine_mesh, in_specs=in_specs, out_specs=out_specs, check_vma=False
    )
```

```python
import functools
import math

import jax
import jax.numpy as jnp
import numpy as np
from jax import lax
from jax.experimental import pallas as pl
from jax.experimental.pallas import tpu as pltpu
from jax.sharding import PartitionSpec as P

pair_index = ((0, 3, 4), (3, 1, 5), (4, 5, 2))
by_rows = (((1,), (1,)), ((), ()))


def params(mebibytes):
    return pltpu.CompilerParams(vmem_limit_bytes=mebibytes * 1024 * 1024)


def in_hbm(array):
    return pltpu.with_memory_space_constraint(array, pltpu.HBM)


def in_vmem(array):
    return pltpu.with_memory_space_constraint(array, pltpu.VMEM)


def cost(flops, moved):
    return pl.CostEstimate(flops=flops, bytes_accessed=moved, transcendentals=0)


def angles(rows, columns, length):
    products = np.outer(np.arange(rows), np.arange(columns)) % length
    return 2.0 * math.pi / length * products


def split_two(data):
    high = data.astype(jnp.bfloat16)
    return high, (data - high.astype(jnp.float32)).astype(jnp.bfloat16)


def dot_rows(left, right):
    return lax.dot_general(left, right, by_rows, preferred_element_type=jnp.float32)


def dot_rows_split(stacked, data):
    rows = stacked.shape[0] // 2
    high, low = split_two(data)
    both = dot_rows(stacked, high)
    return both[:rows] + both[rows:] + dot_rows(stacked[:rows], low)


def stacked_halves(table):
    return jnp.concatenate(split_two(table[...]))


def flat_fft(values, times):
    length = len(values)
    if length == 1:
        return values
    even = flat_fft(values[0::2], times)
    odd = flat_fft(values[1::2], times)
    lower, upper = [], []
    for k in range(length // 2):
        turned = times(odd[k], k, length)
        lower.append(jax.tree.map(lambda a, b: a + b, even[k], turned))
        upper.append(jax.tree.map(lambda a, b: a - b, even[k], turned))
    return lower + upper


def times_pair(value, k, length):
    real, imag = value
    if k == 0:
        return value
    if 4 * k == length:
        return (imag, -real)
    cos_k = math.cos(2.0 * math.pi * k / length)
    sin_k = math.sin(2.0 * math.pi * k / length)
    return (real * cos_k + imag * sin_k, imag * cos_k - real * sin_k)


def place_of(owner, sizes):
    count_gx, count_gl = sizes
    shift = count_gl.bit_length() - 1
    z = (owner >> shift) & 3
    return ((owner & (count_gl - 1)) * count_gx + (owner >> (shift + 2))) * 4 + z


def owner_order(sizes):
    devices = 4 * sizes[0] * sizes[1]
    order = [0] * devices
    for owner in range(devices):
        order[place_of(owner, sizes)] = owner
    return order


def pack_kernel(
    devices, mesh_sizes, per_owner, count, me, owner_row, slot_row, tiles, out, *scratch
):
    held, lists, sems = scratch
    comps = range(tiles.shape[1])
    listed = owner_row.shape[1]
    fetches = [
        pltpu.make_async_copy(owner_row, lists.at[0], sems.at[0]),
        pltpu.make_async_copy(slot_row, lists.at[1], sems.at[1]),
    ]
    fetches += [
        pltpu.make_async_copy(tiles.at[:, comp], held.at[i], sems.at[2 + i])
        for i, comp in enumerate(comps)
    ]
    for fetch in fetches:
        fetch.start()
    sender = lax.broadcasted_iota(jnp.int32, (listed, listed), 0)
    reader = lax.broadcasted_iota(jnp.int32, (listed, listed), 1)
    before = jnp.where(sender < reader, 1.0, 0.0).astype(jnp.bfloat16)
    live = lax.broadcasted_iota(jnp.int32, (1, listed), 1) < count[0]
    fetches[0].wait()
    place = jnp.where(live, place_of(lists[0], mesh_sizes), -1)
    place_at = lax.broadcasted_iota(jnp.int32, (devices, listed), 0)
    named = jnp.where(place_at == place, 1.0, 0.0)
    counted = jnp.dot(named.astype(jnp.bfloat16), before, preferred_element_type=jnp.float32)
    rank = jnp.sum(counted * named, axis=0, keepdims=True).astype(jnp.int32)
    target = jnp.where(live, place * per_owner + rank, -1)
    target_at = lax.broadcasted_iota(jnp.int32, (devices * per_owner, listed), 0)
    chosen = jnp.where(target_at == target, 1.0, 0.0).astype(jnp.bfloat16)
    fetches[1].wait()
    stated = lists[1] + 1
    lane = rank + (me[0] & (128 // per_owner - 1)) * per_owner
    lane_at = lax.broadcasted_iota(jnp.int32, (128, listed), 0)
    laned = jnp.where(lane_at == lane, 1.0, 0.0).astype(jnp.bfloat16)
    coarse = (named * (stated >> 5).astype(jnp.float32)).astype(jnp.bfloat16)
    fine = (named * (stated & 31).astype(jnp.float32)).astype(jnp.bfloat16)
    slots = 32.0 * dot_rows(coarse, laned) + dot_rows(fine, laned)
    start = 2 * len(comps) * per_owner
    out[:, start:, :] = jnp.broadcast_to(slots[:, None, :], (devices, 8, 128))
    for i in range(len(comps)):
        fetches[2 + i].wait()
        parts = [part for r in range(2) for part in split_two(held[i, r])]
        got = jnp.dot(
            chosen, jnp.concatenate(parts, axis=1), preferred_element_type=jnp.float32
        )
        for r in range(2):
            whole = got[:, 256 * r : 256 * r + 128] + got[:, 256 * r + 128 : 256 * r + 256]
            start = (2 * i + r) * per_owner
            out[:, start : start + per_owner, :] = whole.reshape(devices, per_owner, 128)


def pack(tiles, owner_row, slot_row, count, me, devices, mesh_sizes, per_owner):
    comps, listed = tiles.shape[1:3]
    rows = 2 * comps * per_owner + 8
    return pl.pallas_call(
        functools.partial(pack_kernel, devices, mesh_sizes, per_owner),
        out_shape=pltpu.VMEM((devices, rows, 128), jnp.float32),
        in_specs=[pl.BlockSpec(memory_space=pltpu.SMEM)] * 2
        + [pl.BlockSpec(memory_space=pltpu.HBM)] * 3,
        out_specs=pl.BlockSpec(memory_space=pltpu.VMEM),
        scratch_shapes=[
            pltpu.VMEM((comps, 2, listed, 128), jnp.float32),
            pltpu.VMEM((2, 1, listed), jnp.int32),
            pltpu.SemaphoreType.DMA((2 + comps,)),
        ],
        compiler_params=params(24),
        cost_estimate=cost(
            devices * per_owner * listed * 512 * 2 * comps, devices * rows * 1024
        ),
    )(count, me, *[in_hbm(a) for a in (owner_row, slot_row, tiles)])


def complex_table(cos_part, sin_part):
    return np.concatenate(
        [
            np.concatenate([cos_part, sin_part], axis=1),
            np.concatenate([-sin_part, cos_part], axis=1),
        ]
    ).astype(np.float32)


def slab_kernel(count, x_local, blocks, per_owner, table, twist, data, out, *scratch):
    chosen, slab, turned = scratch
    devices = data.shape[0]
    entries = devices * per_owner
    group = 128 // x_local
    pairs = blocks // group
    shift = blocks.bit_length() - 1
    every = 128 // per_owner
    stated = [
        sum([data[o, data.shape[1] - 8 :][:1] for o in range(start, start + every)])
        for start in range(0, devices, every)
    ]
    slot = jnp.concatenate(stated, axis=1).astype(jnp.int32) - 1
    landing = jnp.where(slot >= 0, (slot & (blocks - 1)) * x_local + (slot >> shift), -1)
    slab_rows = blocks * x_local
    place = lax.broadcasted_iota(jnp.int32, (slab_rows, entries), 0)
    chosen[...] = jnp.where(place == landing, 1.0, 0.0).astype(jnp.bfloat16)
    stacked = stacked_halves(table)
    step_rows = slab_rows // 2

    def scatter(index, half):
        parts = []
        for r in range(2):
            start = (2 * index + r) * per_owner
            parts.extend(split_two(data[:, start : start + per_owner, :].reshape(entries, 128)))
        rows = pl.ds(half * step_rows, step_rows)
        got = jnp.dot(
            chosen[rows, :], jnp.concatenate(parts, axis=1), preferred_element_type=jnp.float32
        )
        for r in range(2):
            slab[index, r, rows, :] = (
                got[:, 256 * r : 256 * r + 128] + got[:, 256 * r + 128 : 256 * r + 256]
            )

    def transform(index, step):
        at = step * 8
        values = [
            tuple(slab[index, r, pl.ds(t * x_local + at, 8), :] for r in range(2))
            for t in range(blocks)
        ]
        waves = flat_fft(values, times_pair)
        for k in range(blocks):
            real, imag = waves[k]
            cos_k, sin_k = twist[0, k : k + 1, :], twist[1, k : k + 1, :]
            rows = pl.ds(((k % pairs) * group + k // pairs) * x_local + at, 8)
            turned[index % 2, rows, :128] = real * cos_k + imag * sin_k
            turned[index % 2, rows, 128:] = imag * cos_k - real * sin_k

    def along_y(index, start):
        moved = dot_rows_split(stacked, turned[index % 2, start * 128 : (start + 2) * 128, :])
        for k in range(2):
            for r in range(2):
                one = moved[r * 128 : (r + 1) * 128, k * 128 : (k + 1) * 128]
                base = (index * 2 + r) * pairs + start + k
                out[pl.ds(base, 128, stride=count * 2 * pairs), :] = one

    steps = x_local // 8
    scatter(0, 0)
    scatter(0, 1)
    for index in range(count):
        for half in range(2):
            if index + 1 < count:
                scatter(index + 1, half)
            for step in range(half * steps // 2, (half + 1) * steps // 2):
                transform(index, step)
        for start in range(0, pairs, 2):
            along_y(index, start)


def slab_waves(data, x_local, blocks, mesh_sizes, per_owner):
    devices = data.shape[0]
    count = data.shape[1] // (2 * per_owner)
    fine = angles(128, 128, 128)
    order = owner_order(mesh_sizes)
    fine = fine.reshape(devices, 128 // devices, 128)[order].reshape(128, 128)
    table = complex_table(np.cos(fine), np.sin(fine))
    twist_angle = angles(blocks, 128, blocks * 128)
    twist = np.stack([np.cos(twist_angle), np.sin(twist_angle)]).astype(np.float32)
    entries = devices * per_owner
    rows = blocks * x_local * 2
    made = pl.pallas_call(
        functools.partial(slab_kernel, count, x_local, blocks, per_owner),
        out_shape=pltpu.VMEM((count * rows, 128), jnp.float32),
        in_specs=[pl.BlockSpec(memory_space=pltpu.VMEM)] * 3,
        out_specs=pl.BlockSpec(memory_space=pltpu.VMEM),
        scratch_shapes=[
            pltpu.VMEM((blocks * x_local, entries), jnp.bfloat16),
            pltpu.VMEM((count, 2, blocks * x_local, 128), jnp.float32),
            pltpu.VMEM((2, blocks * x_local, 256), jnp.float32),
        ],
        compiler_params=params(40),
        cost_estimate=cost(
            count * blocks * x_local * (entries * 1024 + 512 * 1024),
            count * (entries * 1024 + rows * 512),
        ),
    )(jnp.asarray(table), jnp.asarray(twist), in_vmem(data))
    return made.reshape(devices, count * rows // devices, 128)


def choose(options, mask_of):
    made = options[0]
    for i in range(1, len(options)):
        made = jnp.where(mask_of(i), options[i], made)
    return made


def x_first(sizes, comp, step, twist, data, turned):
    devices, x_local, y_local, blocks, order = sizes
    pairs = blocks * x_local // 128
    kept = y_local // blocks
    at = pl.multiple_of(step * (data.shape[1] // kept), 2 * pairs) + comp * 2 * pairs
    values = [
        tuple(data[order.index(o), pl.ds(at + r * pairs, pairs), :] for r in range(2))
        for o in range(devices)
    ]
    waves = flat_fft(values, times_pair)
    rows = pl.ds(pl.multiple_of(step * pairs, pairs), pairs)
    for k in range(devices):
        real, imag = waves[k]
        cos_k, sin_k = twist[0, k : k + 1, :], twist[1, k : k + 1, :]
        turned[comp % 2, k, rows, :128] = real * cos_k + imag * sin_k
        turned[comp % 2, k, rows, 128:] = imag * cos_k - real * sin_k


def x_second(sizes, comp, step, together, stacked, turned, columns):
    devices, x_local, y_local, blocks, _ = sizes
    group = 128 // x_local
    narrow = (y_local // blocks) * (blocks // group)
    banks = 2 * group
    lane = lax.broadcasted_iota(jnp.int32, (1, 128), 1)
    start = step * together
    rows = turned[comp % 2, pl.ds(start, together)].reshape(together * narrow, 256)
    moved = dot_rows_split(stacked, rows)
    if square(sizes):
        for base in range(0, together, banks):
            rolled = []
            for bank in range(banks):
                one = moved[bank * x_local : (bank + 1) * x_local, base * narrow :][:, :128]
                rolled.append(pltpu.roll(one, bank * narrow, 1) if bank else one)
            for k in range(banks):
                options = [rolled[(place - k) % banks] for place in range(banks)]
                rows = pl.ds(start + base + k, x_local, stride=devices)
                columns[comp, rows, :] = choose(options, lambda i: lane // narrow == i)
        return
    for k in range(together):
        one = jnp.concatenate(
            [
                moved[bank * x_local : (bank + 1) * x_local, k * narrow : (k + 1) * narrow]
                for bank in range(banks)
            ],
            axis=1,
        )
        columns[comp, pl.ds(start + k, x_local, stride=devices), :] = one


def square(sizes):
    _, x_local, y_local, blocks, _ = sizes
    group = 128 // x_local
    narrow = (y_local // blocks) * (blocks // group)
    return 2 * group * narrow == 128 and 128 // narrow == 2 * group


def x_third(sizes, comp, start, columns, kept):
    _, x_local, y_local, blocks, _ = sizes
    group = 128 // x_local
    pairs = blocks // group
    steps = y_local // blocks
    narrow = steps * pairs
    banks = 2 * group
    lane = lax.broadcasted_iota(jnp.int32, (1, 128), 1)
    block = columns[comp, start : start + 128, :].T
    pieces = [block[bank * narrow : (bank + 1) * narrow] for bank in range(banks)]
    for bank in range(banks):
        one = pieces[bank]
        if square(sizes):
            options = [pieces[(bank + k) % banks] for k in range(banks)]
            one = choose(options, lambda i: lane % banks == i)
        for step in range(steps):
            row = step * blocks + (bank % group) * pairs
            kept[comp, bank // group, row : row + pairs, start : start + 128] = one[
                step * pairs : (step + 1) * pairs
            ]


def mix_rows(rows, columns, tensor, waves):
    sums = [None] * 3
    for row in range(3):
        for col in range(3):
            entry = pair_index[row][col]
            green_real, green_imag = tensor[0, entry, rows, columns], tensor[1, entry, rows, columns]
            real, imag = waves[col, 0, rows, columns], waves[col, 1, rows, columns]
            real_term = green_real * real - green_imag * imag
            imag_term = green_real * imag + green_imag * real
            old = sums[row]
            sums[row] = (
                (real_term, imag_term) if old is None else (old[0] + real_term, old[1] + imag_term)
            )
    return sums


def field_kernel(sizes, twist, table, data, green, out, *scratch):
    y_local, x_cells = green.shape[2:]
    turned, columns, tensor, kept, made, in_sem, out_sems = scratch
    width = x_cells // made.shape[0]
    fetch = pltpu.make_async_copy(green, tensor, in_sem)
    fetch.start()
    stacked = stacked_halves(table)
    devices, x_local, _, blocks, _ = sizes
    steps = y_local // blocks
    narrow = y_local * x_local // 128
    together = min(devices, 256 // narrow)
    groups = devices // together
    blocks_each = x_cells // 128 // groups
    for comp in range(3):
        pl.loop(0, steps)(lambda i: x_first(sizes, comp, i, twist, data, turned))
        for i in range(groups):
            x_second(sizes, comp, i, together, stacked, turned, columns)
            for block in range(i * blocks_each, (i + 1) * blocks_each):
                if comp > 0:
                    x_third(sizes, comp - 1, block * 128, columns, kept)
    fetch.wait()
    pieces = made.shape[0]

    def turn(piece):
        for start in range(piece * width, (piece + 1) * width, 128):
            x_third(sizes, 2, start, columns, kept)

    sends = []
    turn(0)
    for piece in range(pieces):
        if piece + 1 < pieces:
            turn(piece + 1)
        part = pl.ds(piece * width, width)
        for step in range(y_local // 8):
            rows = pl.ds(step * 8, 8)
            for row, pair in enumerate(mix_rows(rows, part, tensor, kept)):
                for r in range(2):
                    made[piece, r, row, rows, :] = pair[r]
        send = pltpu.make_async_copy(made.at[piece], out.at[:, :, :, part], out_sems.at[piece])
        send.start()
        sends.append(send)
    for send in sends:
        send.wait()


def x_tables(devices, x_local, y_cells):
    x_cells = devices * x_local
    group = 128 // x_local
    fine = angles(x_local, x_local, x_local)
    scale = 1.0 / math.sqrt(x_cells * y_cells)
    apart = np.eye(group) * scale
    table = complex_table(np.kron(apart, np.cos(fine)), np.kron(apart, np.sin(fine)))
    angle = np.tile(angles(devices, x_local, x_cells), (1, group))
    twist = np.stack([np.cos(angle), np.sin(angle)]).astype(np.float32)
    return jnp.asarray(twist), jnp.asarray(table)


def x_scratch(devices, x_local, y_local):
    return [
        pltpu.VMEM((2, devices, y_local * x_local // 128, 256), jnp.float32),
        pltpu.VMEM((3, devices * x_local, 2 * y_local), jnp.float32),
    ]


def field(data, green, devices, x_local, y_local, y_cells, mesh_sizes):
    x_cells = devices * x_local
    pieces = 8
    sizes = (devices, x_local, y_local, y_cells // 128, owner_order(mesh_sizes))
    plane = (y_local, x_cells)
    return pl.pallas_call(
        functools.partial(field_kernel, sizes),
        out_shape=pltpu.HBM((2, 3) + plane, jnp.float32),
        in_specs=[pl.BlockSpec(memory_space=pltpu.VMEM)] * 3
        + [pl.BlockSpec(memory_space=pltpu.HBM)],
        out_specs=pl.BlockSpec(memory_space=pltpu.HBM),
        scratch_shapes=x_scratch(devices, x_local, y_local)
        + [
            pltpu.VMEM((2, 6) + plane, jnp.float32),
            pltpu.VMEM((3, 2) + plane, jnp.float32),
            pltpu.VMEM((pieces, 2, 3, y_local, x_cells // pieces), jnp.float32),
            pltpu.SemaphoreType.DMA(()),
            pltpu.SemaphoreType.DMA((pieces,)),
        ],
        compiler_params=params(40),
        cost_estimate=cost(3 * x_cells * y_local * (x_local * 24 + 24), x_cells * y_local * 96),
    )(*x_tables(devices, x_local, y_cells), in_vmem(data), in_hbm(green))


places = ("gl", "gx", "gz")


def exchange(data):
    return lax.all_to_all(data, places, split_axis=0, concat_axis=0, tiled=True)


def per_device(tiles, tile_owner, tile_slot, tile_count, green):
    count_gl = lax.axis_size("gl")
    mesh_sizes = (lax.axis_size("gx"), count_gl)
    devices = 4 * mesh_sizes[0] * count_gl
    tile_total, tile_len = tiles.shape[2], tiles.shape[3]
    planes, y_local, x_cells = green.shape[2:]
    y_cells = y_local * devices
    x_local = x_cells // devices
    blocks = y_cells // tile_len
    per_owner = max(2, 2 * tile_total // devices)
    assert planes == 1 and tile_len == 128
    owner_row, slot_row = tile_owner.reshape(1, tile_total), tile_slot.reshape(1, tile_total)
    green = green.reshape(2, 6, y_local, x_cells)
    me = lax.axis_index(places).reshape(1).astype(jnp.int32)
    lists = (owner_row, slot_row, tile_count, me)
    arrived = exchange(pack(tiles, *lists, devices, mesh_sizes, per_owner))
    moved = exchange(slab_waves(arrived, x_local, blocks, mesh_sizes, per_owner))
    mixed = field(moved, green, devices, x_local, y_local, y_cells, mesh_sizes)
    return mixed.reshape(2, 3, planes, y_local, x_cells)


def solution(mesh):
    count_gx, count_gy = mesh.devices.shape
    fine_mesh = jax.sharding.Mesh(
        mesh.devices.reshape(count_gx, 4, count_gy // 4), ("gx", "gz", "gl")
    )
    every = ("gx", "gz", "gl")
    in_specs = (
        P(None, None, every, None),
        P(every, None),
        P(every),
        P(every),
        P(None, None, None, every, None),
    )
    out_specs = P(None, None, None, every, None)
    return jax.shard_map(
        per_device, mesh=fine_mesh, in_specs=in_specs, out_specs=out_specs, check_vma=False
    )
```

```python
import functools
import math

import jax
import jax.numpy as jnp
import numpy as np
from jax import lax
from jax.experimental import pallas as pl
from jax.experimental.pallas import tpu as pltpu
from jax.sharding import PartitionSpec as P

pair_index = ((0, 3, 4), (3, 1, 5), (4, 5, 2))
by_rows = (((1,), (1,)), ((), ()))


def params(mebibytes):
    return pltpu.CompilerParams(vmem_limit_bytes=mebibytes * 1024 * 1024)


def in_hbm(array):
    return pltpu.with_memory_space_constraint(array, pltpu.HBM)


def in_vmem(array):
    return pltpu.with_memory_space_constraint(array, pltpu.VMEM)


def cost(flops, moved):
    return pl.CostEstimate(flops=flops, bytes_accessed=moved, transcendentals=0)


def angles(rows, columns, length):
    products = np.outer(np.arange(rows), np.arange(columns)) % length
    return 2.0 * math.pi / length * products


def split_two(data):
    high = data.astype(jnp.bfloat16)
    return high, (data - high.astype(jnp.float32)).astype(jnp.bfloat16)


def dot_rows(left, right):
    return lax.dot_general(left, right, by_rows, preferred_element_type=jnp.float32)


def dot_rows_split(stacked, data):
    rows = stacked.shape[0] // 2
    high, low = split_two(data)
    both = dot_rows(stacked, high)
    return both[:rows] + both[rows:] + dot_rows(stacked[:rows], low)


def stacked_halves(table):
    return jnp.concatenate(split_two(table[...]))


def flat_fft(values, times):
    length = len(values)
    if length == 1:
        return values
    even = flat_fft(values[0::2], times)
    odd = flat_fft(values[1::2], times)
    lower, upper = [], []
    for k in range(length // 2):
        turned = times(odd[k], k, length)
        lower.append(jax.tree.map(lambda a, b: a + b, even[k], turned))
        upper.append(jax.tree.map(lambda a, b: a - b, even[k], turned))
    return lower + upper


def times_pair(value, k, length):
    real, imag = value
    if k == 0:
        return value
    if 4 * k == length:
        return (imag, -real)
    cos_k = math.cos(2.0 * math.pi * k / length)
    sin_k = math.sin(2.0 * math.pi * k / length)
    return (real * cos_k + imag * sin_k, imag * cos_k - real * sin_k)


def place_of(owner, sizes):
    count_gx, count_gl = sizes
    shift = count_gl.bit_length() - 1
    z, gx = (owner >> shift) & 3, owner >> (shift + 2)
    return ((owner & (count_gl - 1)) * (count_gx // 2) + (gx >> 1)) * 8 + z * 2 + (gx & 1)


def owner_order(sizes):
    devices = 4 * sizes[0] * sizes[1]
    order = [0] * devices
    for owner in range(devices):
        order[place_of(owner, sizes)] = owner
    return order


def pack_kernel(
    devices, mesh_sizes, per_owner, count, me, owner_row, slot_row, tiles, out, *scratch
):
    held, lists, sems = scratch
    comps = range(tiles.shape[1])
    listed = owner_row.shape[1]
    fetches = [
        pltpu.make_async_copy(owner_row, lists.at[0], sems.at[0]),
        pltpu.make_async_copy(slot_row, lists.at[1], sems.at[1]),
    ]
    fetches += [
        pltpu.make_async_copy(tiles.at[:, comp], held.at[i], sems.at[2 + i])
        for i, comp in enumerate(comps)
    ]
    for fetch in fetches:
        fetch.start()
    sender = lax.broadcasted_iota(jnp.int32, (listed, listed), 0)
    reader = lax.broadcasted_iota(jnp.int32, (listed, listed), 1)
    before = jnp.where(sender < reader, 1.0, 0.0).astype(jnp.bfloat16)
    live = lax.broadcasted_iota(jnp.int32, (1, listed), 1) < count[0]
    fetches[0].wait()
    place = jnp.where(live, place_of(lists[0], mesh_sizes), -1)
    place_at = lax.broadcasted_iota(jnp.int32, (devices, listed), 0)
    named = jnp.where(place_at == place, 1.0, 0.0)
    counted = jnp.dot(named.astype(jnp.bfloat16), before, preferred_element_type=jnp.float32)
    rank = jnp.sum(counted * named, axis=0, keepdims=True).astype(jnp.int32)
    target = jnp.where(live, place * per_owner + rank, -1)
    target_at = lax.broadcasted_iota(jnp.int32, (devices * per_owner, listed), 0)
    chosen = jnp.where(target_at == target, 1.0, 0.0).astype(jnp.bfloat16)
    fetches[1].wait()
    stated = lists[1] + 1
    lane = rank + (me[0] & (128 // per_owner - 1)) * per_owner
    lane_at = lax.broadcasted_iota(jnp.int32, (128, listed), 0)
    laned = jnp.where(lane_at == lane, 1.0, 0.0).astype(jnp.bfloat16)
    coarse = (named * (stated >> 5).astype(jnp.float32)).astype(jnp.bfloat16)
    fine = (named * (stated & 31).astype(jnp.float32)).astype(jnp.bfloat16)
    slots = 32.0 * dot_rows(coarse, laned) + dot_rows(fine, laned)
    start = 2 * len(comps) * per_owner
    out[:, start:, :] = jnp.broadcast_to(slots[:, None, :], (devices, 8, 128))
    for i in range(len(comps)):
        fetches[2 + i].wait()
        parts = [part for r in range(2) for part in split_two(held[i, r])]
        got = jnp.dot(
            chosen, jnp.concatenate(parts, axis=1), preferred_element_type=jnp.float32
        )
        for r in range(2):
            whole = got[:, 256 * r : 256 * r + 128] + got[:, 256 * r + 128 : 256 * r + 256]
            start = (2 * i + r) * per_owner
            out[:, start : start + per_owner, :] = whole.reshape(devices, per_owner, 128)


def pack(tiles, owner_row, slot_row, count, me, devices, mesh_sizes, per_owner):
    comps, listed = tiles.shape[1:3]
    rows = 2 * comps * per_owner + 8
    return pl.pallas_call(
        functools.partial(pack_kernel, devices, mesh_sizes, per_owner),
        out_shape=pltpu.VMEM((devices, rows, 128), jnp.float32),
        in_specs=[pl.BlockSpec(memory_space=pltpu.SMEM)] * 2
        + [pl.BlockSpec(memory_space=pltpu.HBM)] * 3,
        out_specs=pl.BlockSpec(memory_space=pltpu.VMEM),
        scratch_shapes=[
            pltpu.VMEM((comps, 2, listed, 128), jnp.float32),
            pltpu.VMEM((2, 1, listed), jnp.int32),
            pltpu.SemaphoreType.DMA((2 + comps,)),
        ],
        compiler_params=params(24),
        cost_estimate=cost(
            devices * per_owner * listed * 512 * 2 * comps, devices * rows * 1024
        ),
    )(count, me, *[in_hbm(a) for a in (owner_row, slot_row, tiles)])


def complex_table(cos_part, sin_part):
    return np.concatenate(
        [
            np.concatenate([cos_part, sin_part], axis=1),
            np.concatenate([-sin_part, cos_part], axis=1),
        ]
    ).astype(np.float32)


def slab_kernel(count, x_local, blocks, per_owner, table, twist, data, out, *scratch):
    chosen, slab, turned = scratch
    devices = data.shape[0]
    entries = devices * per_owner
    group = 128 // x_local
    pairs = blocks // group
    shift = blocks.bit_length() - 1
    every = 128 // per_owner
    stated = [
        sum([data[o, data.shape[1] - 8 :][:1] for o in range(start, start + every)])
        for start in range(0, devices, every)
    ]
    slot = jnp.concatenate(stated, axis=1).astype(jnp.int32) - 1
    landing = jnp.where(slot >= 0, (slot & (blocks - 1)) * x_local + (slot >> shift), -1)
    slab_rows = blocks * x_local
    place = lax.broadcasted_iota(jnp.int32, (slab_rows, entries), 0)
    chosen[...] = jnp.where(place == landing, 1.0, 0.0).astype(jnp.bfloat16)
    stacked = stacked_halves(table)
    step_rows = slab_rows // 2

    def scatter(index, half):
        parts = []
        for r in range(2):
            start = (2 * index + r) * per_owner
            parts.extend(split_two(data[:, start : start + per_owner, :].reshape(entries, 128)))
        rows = pl.ds(half * step_rows, step_rows)
        got = jnp.dot(
            chosen[rows, :], jnp.concatenate(parts, axis=1), preferred_element_type=jnp.float32
        )
        for r in range(2):
            slab[index, r, rows, :] = (
                got[:, 256 * r : 256 * r + 128] + got[:, 256 * r + 128 : 256 * r + 256]
            )

    def transform(index, step):
        at = step * 8
        values = [
            tuple(slab[index, r, pl.ds(t * x_local + at, 8), :] for r in range(2))
            for t in range(blocks)
        ]
        waves = flat_fft(values, times_pair)
        for k in range(blocks):
            real, imag = waves[k]
            cos_k, sin_k = twist[0, k : k + 1, :], twist[1, k : k + 1, :]
            rows = pl.ds(((k % pairs) * group + k // pairs) * x_local + at, 8)
            turned[index % 2, rows, :128] = real * cos_k + imag * sin_k
            turned[index % 2, rows, 128:] = imag * cos_k - real * sin_k

    def along_y(index, start):
        moved = dot_rows_split(stacked, turned[index % 2, start * 128 : (start + 2) * 128, :])
        for k in range(2):
            for r in range(2):
                one = moved[r * 128 : (r + 1) * 128, k * 128 : (k + 1) * 128]
                base = (index * 2 + r) * pairs + start + k
                out[pl.ds(base, 128, stride=count * 2 * pairs), :] = one

    steps = x_local // 8
    scatter(0, 0)
    scatter(0, 1)
    for index in range(count):
        for half in range(2):
            if index + 1 < count:
                scatter(index + 1, half)
            for step in range(half * steps // 2, (half + 1) * steps // 2):
                transform(index, step)
        for start in range(0, pairs, 2):
            along_y(index, start)


def slab_waves(data, x_local, blocks, mesh_sizes, per_owner):
    devices = data.shape[0]
    count = data.shape[1] // (2 * per_owner)
    fine = angles(128, 128, 128)
    order = owner_order(mesh_sizes)
    fine = fine.reshape(devices, 128 // devices, 128)[order].reshape(128, 128)
    table = complex_table(np.cos(fine), np.sin(fine))
    twist_angle = angles(blocks, 128, blocks * 128)
    twist = np.stack([np.cos(twist_angle), np.sin(twist_angle)]).astype(np.float32)
    entries = devices * per_owner
    rows = blocks * x_local * 2
    made = pl.pallas_call(
        functools.partial(slab_kernel, count, x_local, blocks, per_owner),
        out_shape=pltpu.VMEM((count * rows, 128), jnp.float32),
        in_specs=[pl.BlockSpec(memory_space=pltpu.VMEM)] * 3,
        out_specs=pl.BlockSpec(memory_space=pltpu.VMEM),
        scratch_shapes=[
            pltpu.VMEM((blocks * x_local, entries), jnp.bfloat16),
            pltpu.VMEM((count, 2, blocks * x_local, 128), jnp.float32),
            pltpu.VMEM((2, blocks * x_local, 256), jnp.float32),
        ],
        compiler_params=params(40),
        cost_estimate=cost(
            count * blocks * x_local * (entries * 1024 + 512 * 1024),
            count * (entries * 1024 + rows * 512),
        ),
    )(jnp.asarray(table), jnp.asarray(twist), in_vmem(data))
    return made.reshape(devices, count * rows // devices, 128)


def rotated(pieces, selector):
    count = len(pieces)
    step = 1
    while step < count:
        taken = (selector & step) != 0
        pieces = [
            jnp.where(taken, pieces[(j + step) % count], pieces[j]) for j in range(count)
        ]
        step *= 2
    return pieces


def x_first(sizes, comp, step, twist, data, turned):
    devices, x_local, y_local, blocks, order = sizes
    pairs = blocks * x_local // 128
    kept = y_local // blocks
    at = pl.multiple_of(step * (data.shape[1] // kept), 2 * pairs) + comp * 2 * pairs
    values = [
        tuple(data[order.index(o), pl.ds(at + r * pairs, pairs), :] for r in range(2))
        for o in range(devices)
    ]
    waves = flat_fft(values, times_pair)
    rows = pl.ds(pl.multiple_of(step * pairs, pairs), pairs)
    for k in range(devices):
        real, imag = waves[k]
        cos_k, sin_k = twist[0, k : k + 1, :], twist[1, k : k + 1, :]
        turned[comp % 2, k, rows, :128] = real * cos_k + imag * sin_k
        turned[comp % 2, k, rows, 128:] = imag * cos_k - real * sin_k


def x_second(sizes, comp, step, together, stacked, turned, columns):
    devices, x_local, y_local, blocks, _ = sizes
    group = 128 // x_local
    narrow = (y_local // blocks) * (blocks // group)
    banks = 2 * group
    lane = lax.broadcasted_iota(jnp.int32, (1, 128), 1)
    start = step * together
    rows = turned[comp % 2, pl.ds(start, together)].reshape(together * narrow, 256)
    moved = dot_rows_split(stacked, rows)
    if square(sizes):
        for base in range(0, together, banks):
            rolled = []
            for bank in range(banks):
                one = moved[bank * x_local : (bank + 1) * x_local, base * narrow :][:, :128]
                rolled.append(pltpu.roll(one, bank * narrow, 1) if bank else one)
            made = rotated(rolled, lane >> (narrow.bit_length() - 1))
            for k in range(banks):
                rows = pl.ds(start + base + k, x_local, stride=devices)
                columns[comp, rows, :] = made[-k % banks]
        return
    for k in range(together):
        one = jnp.concatenate(
            [
                moved[bank * x_local : (bank + 1) * x_local, k * narrow : (k + 1) * narrow]
                for bank in range(banks)
            ],
            axis=1,
        )
        columns[comp, pl.ds(start + k, x_local, stride=devices), :] = one


def square(sizes):
    _, x_local, y_local, blocks, _ = sizes
    group = 128 // x_local
    narrow = (y_local // blocks) * (blocks // group)
    return 2 * group * narrow == 128 and 128 // narrow == 2 * group


def x_third(sizes, comp, start, columns, kept):
    _, x_local, y_local, blocks, _ = sizes
    group = 128 // x_local
    pairs = blocks // group
    steps = y_local // blocks
    narrow = steps * pairs
    banks = 2 * group
    lane = lax.broadcasted_iota(jnp.int32, (1, 128), 1)
    block = columns[comp, start : start + 128, :].T
    pieces = [block[bank * narrow : (bank + 1) * narrow] for bank in range(banks)]
    if square(sizes):
        pieces = rotated(pieces, lane & (banks - 1))
    for bank, one in enumerate(pieces):
        for step in range(steps):
            row = step * blocks + (bank % group) * pairs
            kept[comp, bank // group, row : row + pairs, start : start + 128] = one[
                step * pairs : (step + 1) * pairs
            ]


def mix_rows(rows, columns, tensor, waves):
    sums = [None] * 3
    for row in range(3):
        for col in range(3):
            entry = pair_index[row][col]
            green_real, green_imag = tensor[0, entry, rows, columns], tensor[1, entry, rows, columns]
            real, imag = waves[col, 0, rows, columns], waves[col, 1, rows, columns]
            real_term = green_real * real - green_imag * imag
            imag_term = green_real * imag + green_imag * real
            old = sums[row]
            sums[row] = (
                (real_term, imag_term) if old is None else (old[0] + real_term, old[1] + imag_term)
            )
    return sums


def field_kernel(sizes, twist, table, data, green, out, *scratch):
    y_local, x_cells = green.shape[2:]
    turned, columns, tensor, kept, made, in_sem, out_sems = scratch
    width = x_cells // made.shape[0]
    fetch = pltpu.make_async_copy(green, tensor, in_sem)
    fetch.start()
    stacked = stacked_halves(table)
    devices, x_local, _, blocks, _ = sizes
    steps = y_local // blocks
    narrow = y_local * x_local // 128
    together = min(devices, 256 // narrow)
    groups = devices // together
    blocks_each = x_cells // 128 // groups
    for comp in range(3):
        pl.loop(0, steps)(lambda i: x_first(sizes, comp, i, twist, data, turned))
        for i in range(groups):
            x_second(sizes, comp, i, together, stacked, turned, columns)
            for block in range(i * blocks_each, (i + 1) * blocks_each):
                if comp > 0:
                    x_third(sizes, comp - 1, block * 128, columns, kept)
    fetch.wait()
    pieces = made.shape[0]

    def turn(piece):
        for start in range(piece * width, (piece + 1) * width, 128):
            x_third(sizes, 2, start, columns, kept)

    sends = []
    turn(0)
    for piece in range(pieces):
        if piece + 1 < pieces:
            turn(piece + 1)
        part = pl.ds(piece * width, width)
        for step in range(y_local // 8):
            rows = pl.ds(step * 8, 8)
            for row, pair in enumerate(mix_rows(rows, part, tensor, kept)):
                for r in range(2):
                    made[piece, r, row, rows, :] = pair[r]
        send = pltpu.make_async_copy(made.at[piece], out.at[:, :, :, part], out_sems.at[piece])
        send.start()
        sends.append(send)
    for send in sends:
        send.wait()


def x_tables(devices, x_local, y_cells):
    x_cells = devices * x_local
    group = 128 // x_local
    fine = angles(x_local, x_local, x_local)
    scale = 1.0 / math.sqrt(x_cells * y_cells)
    apart = np.eye(group) * scale
    table = complex_table(np.kron(apart, np.cos(fine)), np.kron(apart, np.sin(fine)))
    angle = np.tile(angles(devices, x_local, x_cells), (1, group))
    twist = np.stack([np.cos(angle), np.sin(angle)]).astype(np.float32)
    return jnp.asarray(twist), jnp.asarray(table)


def x_scratch(devices, x_local, y_local):
    return [
        pltpu.VMEM((2, devices, y_local * x_local // 128, 256), jnp.float32),
        pltpu.VMEM((3, devices * x_local, 2 * y_local), jnp.float32),
    ]


def field(data, green, devices, x_local, y_local, y_cells, mesh_sizes):
    x_cells = devices * x_local
    pieces = 16
    sizes = (devices, x_local, y_local, y_cells // 128, owner_order(mesh_sizes))
    plane = (y_local, x_cells)
    return pl.pallas_call(
        functools.partial(field_kernel, sizes),
        out_shape=pltpu.HBM((2, 3) + plane, jnp.float32),
        in_specs=[pl.BlockSpec(memory_space=pltpu.VMEM)] * 3
        + [pl.BlockSpec(memory_space=pltpu.HBM)],
        out_specs=pl.BlockSpec(memory_space=pltpu.HBM),
        scratch_shapes=x_scratch(devices, x_local, y_local)
        + [
            pltpu.VMEM((2, 6) + plane, jnp.float32),
            pltpu.VMEM((3, 2) + plane, jnp.float32),
            pltpu.VMEM((pieces, 2, 3, y_local, x_cells // pieces), jnp.float32),
            pltpu.SemaphoreType.DMA(()),
            pltpu.SemaphoreType.DMA((pieces,)),
        ],
        compiler_params=params(40),
        cost_estimate=cost(3 * x_cells * y_local * (x_local * 24 + 24), x_cells * y_local * 96),
    )(*x_tables(devices, x_local, y_cells), in_vmem(data), in_hbm(green))


places = ("gl", "gy", "gz", "core")


def exchange(data):
    return lax.all_to_all(data, places, split_axis=0, concat_axis=0, tiled=True)


def per_device(tiles, tile_owner, tile_slot, tile_count, green):
    count_gl = lax.axis_size("gl")
    mesh_sizes = (lax.axis_size("gy") * 2, count_gl)
    devices = 4 * mesh_sizes[0] * count_gl
    tile_total, tile_len = tiles.shape[2], tiles.shape[3]
    planes, y_local, x_cells = green.shape[2:]
    y_cells = y_local * devices
    x_local = x_cells // devices
    blocks = y_cells // tile_len
    per_owner = max(2, 2 * tile_total // devices)
    assert planes == 1 and tile_len == 128
    owner_row, slot_row = tile_owner.reshape(1, tile_total), tile_slot.reshape(1, tile_total)
    green = green.reshape(2, 6, y_local, x_cells)
    me = lax.axis_index(places).reshape(1).astype(jnp.int32)
    lists = (owner_row, slot_row, tile_count, me)
    arrived = exchange(pack(tiles, *lists, devices, mesh_sizes, per_owner))
    moved = exchange(slab_waves(arrived, x_local, blocks, mesh_sizes, per_owner))
    mixed = field(moved, green, devices, x_local, y_local, y_cells, mesh_sizes)
    return mixed.reshape(2, 3, planes, y_local, x_cells)


def solution(mesh):
    count_gx, count_gy = mesh.devices.shape
    fine_mesh = jax.sharding.Mesh(
        mesh.devices.reshape(count_gx // 2, 2, 4, count_gy // 4), ("gy", "core", "gz", "gl")
    )
    every = ("gy", "core", "gz", "gl")
    in_specs = (
        P(None, None, every, None),
        P(every, None),
        P(every),
        P(every),
        P(None, None, None, every, None),
    )
    out_specs = P(None, None, None, every, None)
    return jax.shard_map(
        per_device, mesh=fine_mesh, in_specs=in_specs, out_specs=out_specs, check_vma=False
    )
```

```python
import functools
import math

import jax
import jax.numpy as jnp
import numpy as np
from jax import lax
from jax.experimental import pallas as pl
from jax.experimental.pallas import tpu as pltpu
from jax.sharding import PartitionSpec as P

pair_index = ((0, 3, 4), (3, 1, 5), (4, 5, 2))
by_rows = (((1,), (1,)), ((), ()))


def params(mebibytes):
    return pltpu.CompilerParams(vmem_limit_bytes=mebibytes * 1024 * 1024)


def in_hbm(array):
    return pltpu.with_memory_space_constraint(array, pltpu.HBM)


def in_vmem(array):
    return pltpu.with_memory_space_constraint(array, pltpu.VMEM)


def cost(flops, moved):
    return pl.CostEstimate(flops=flops, bytes_accessed=moved, transcendentals=0)


def angles(rows, columns, length):
    products = np.outer(np.arange(rows), np.arange(columns)) % length
    return 2.0 * math.pi / length * products


def split_two(data):
    high = data.astype(jnp.bfloat16)
    return high, (data - high.astype(jnp.float32)).astype(jnp.bfloat16)


def dot_rows(left, right):
    return lax.dot_general(left, right, by_rows, preferred_element_type=jnp.float32)


def dot_rows_split(stacked, data):
    rows = stacked.shape[0] // 2
    high, low = split_two(data)
    both = dot_rows(stacked, high)
    return both[:rows] + both[rows:] + dot_rows(stacked[:rows], low)


def stacked_halves(table):
    return jnp.concatenate(split_two(table[...]))


def flat_fft(values, times):
    length = len(values)
    if length == 1:
        return values
    even = flat_fft(values[0::2], times)
    odd = flat_fft(values[1::2], times)
    lower, upper = [], []
    for k in range(length // 2):
        turned = times(odd[k], k, length)
        lower.append(jax.tree.map(lambda a, b: a + b, even[k], turned))
        upper.append(jax.tree.map(lambda a, b: a - b, even[k], turned))
    return lower + upper


def times_pair(value, k, length):
    real, imag = value
    if k == 0:
        return value
    if 4 * k == length:
        return (imag, -real)
    cos_k = math.cos(2.0 * math.pi * k / length)
    sin_k = math.sin(2.0 * math.pi * k / length)
    return (real * cos_k + imag * sin_k, imag * cos_k - real * sin_k)


def place_of(owner, sizes):
    count_gx, count_gl = sizes
    shift = count_gl.bit_length() - 1
    z = (owner >> shift) & 3
    return ((owner & (count_gl - 1)) * count_gx + (owner >> (shift + 2))) * 4 + z


def owner_order(sizes):
    devices = 4 * sizes[0] * sizes[1]
    order = [0] * devices
    for owner in range(devices):
        order[place_of(owner, sizes)] = owner
    return order


def pack_kernel(
    devices, mesh_sizes, per_owner, count, owner_row, slot_row, tiles, out, table, *scratch
):
    held, lists, sems = scratch
    comps = range(tiles.shape[1])
    listed = owner_row.shape[1]
    fetches = [
        pltpu.make_async_copy(owner_row, lists.at[0], sems.at[0]),
        pltpu.make_async_copy(slot_row, lists.at[1], sems.at[1]),
    ]
    fetches += [
        pltpu.make_async_copy(tiles.at[:, comp], held.at[i], sems.at[2 + i])
        for i, comp in enumerate(comps)
    ]
    for fetch in fetches:
        fetch.start()
    sender = lax.broadcasted_iota(jnp.int32, (listed, listed), 0)
    reader = lax.broadcasted_iota(jnp.int32, (listed, listed), 1)
    before = jnp.where(sender < reader, 1.0, 0.0).astype(jnp.bfloat16)
    live = lax.broadcasted_iota(jnp.int32, (1, listed), 1) < count[0]
    fetches[0].wait()
    place = jnp.where(live, place_of(lists[0], mesh_sizes), -1)
    place_at = lax.broadcasted_iota(jnp.int32, (devices, listed), 0)
    named = jnp.where(place_at == place, 1.0, 0.0)
    counted = jnp.dot(named.astype(jnp.bfloat16), before, preferred_element_type=jnp.float32)
    rank = jnp.sum(counted * named, axis=0, keepdims=True).astype(jnp.int32)
    target = jnp.where(live, place * per_owner + rank, -1)
    target_at = lax.broadcasted_iota(jnp.int32, (devices * per_owner, listed), 0)
    chosen = jnp.where(target_at == target, 1.0, 0.0).astype(jnp.bfloat16)
    fetches[1].wait()
    stated = lists[1] + 1
    every = 128 // per_owner
    lane = jnp.where(live, rank + (place & (every - 1)) * per_owner, -1)
    lane_at = lax.broadcasted_iota(jnp.int32, (128, listed), 0)
    laned = jnp.where(lane_at == lane, 1.0, 0.0).astype(jnp.bfloat16)
    row_at = lax.broadcasted_iota(jnp.int32, (8, listed), 0)
    rowed = jnp.where(row_at == place >> (every.bit_length() - 1), 1.0, 0.0)
    coarse = (rowed * (stated >> 5).astype(jnp.float32)).astype(jnp.bfloat16)
    fine = (rowed * (stated & 31).astype(jnp.float32)).astype(jnp.bfloat16)
    table[...] = 32.0 * dot_rows(coarse, laned) + dot_rows(fine, laned)
    for i in range(len(comps)):
        fetches[2 + i].wait()
        parts = [part for r in range(2) for part in split_two(held[i, r])]
        got = jnp.dot(
            chosen, jnp.concatenate(parts, axis=1), preferred_element_type=jnp.float32
        )
        for r in range(2):
            whole = got[:, 256 * r : 256 * r + 128] + got[:, 256 * r + 128 : 256 * r + 256]
            start = (2 * i + r) * per_owner
            out[:, start : start + per_owner, :] = whole.reshape(devices, per_owner, 128)


def pack(tiles, owner_row, slot_row, count, devices, mesh_sizes, per_owner):
    comps, listed = tiles.shape[1:3]
    rows = 2 * comps * per_owner
    assert devices * per_owner == 1024
    return pl.pallas_call(
        functools.partial(pack_kernel, devices, mesh_sizes, per_owner),
        out_shape=(
            pltpu.VMEM((devices, rows, 128), jnp.float32),
            jax.ShapeDtypeStruct((8, 128), jnp.float32),
        ),
        in_specs=[pl.BlockSpec(memory_space=pltpu.SMEM)]
        + [pl.BlockSpec(memory_space=pltpu.HBM)] * 3,
        out_specs=(pl.BlockSpec(memory_space=pltpu.VMEM),) * 2,
        scratch_shapes=[
            pltpu.VMEM((comps, 2, listed, 128), jnp.float32),
            pltpu.VMEM((2, 1, listed), jnp.int32),
            pltpu.SemaphoreType.DMA((2 + comps,)),
        ],
        compiler_params=params(24),
        cost_estimate=cost(
            devices * per_owner * listed * 512 * 2 * comps, devices * rows * 1024
        ),
    )(count, *[in_hbm(a) for a in (owner_row, slot_row, tiles)])


def complex_table(cos_part, sin_part):
    return np.concatenate(
        [
            np.concatenate([cos_part, sin_part], axis=1),
            np.concatenate([-sin_part, cos_part], axis=1),
        ]
    ).astype(np.float32)


def slab_kernel(
    count, x_local, blocks, per_owner, order, me, slots, table, twist, data, out, *scratch
):
    chosen, slab, turned = scratch
    devices = data.shape[0]
    entries = devices * per_owner
    group = 128 // x_local
    pairs = blocks // group
    shift = blocks.bit_length() - 1
    every = 128 // per_owner
    lane = lax.broadcasted_iota(jnp.int32, (1, 128), 1)
    mine = me[0] & (every - 1)
    row = me[0] >> (every.bit_length() - 1)
    stated = []
    for start in range(0, devices, every):
        whole = None
        for i in range(every):
            one = slots[order[start + i] ^ me[1], pl.ds(row, 1), :]
            one = pltpu.roll(one, ((i + every - mine) & (every - 1)) * per_owner, 1)
            whole = one if i == 0 else jnp.where(lane // per_owner == i, one, whole)
        stated.append(whole)
    slot = jnp.concatenate(stated, axis=1).astype(jnp.int32) - 1
    landing = jnp.where(slot >= 0, (slot & (blocks - 1)) * x_local + (slot >> shift), -1)
    slab_rows = blocks * x_local
    place = lax.broadcasted_iota(jnp.int32, (slab_rows, entries), 0)
    chosen[...] = jnp.where(place == landing, 1.0, 0.0).astype(jnp.bfloat16)
    stacked = stacked_halves(table)
    step_rows = slab_rows // 2

    def scatter(index, half):
        parts = []
        for r in range(2):
            start = (2 * index + r) * per_owner
            parts.extend(split_two(data[:, start : start + per_owner, :].reshape(entries, 128)))
        rows = pl.ds(half * step_rows, step_rows)
        got = jnp.dot(
            chosen[rows, :], jnp.concatenate(parts, axis=1), preferred_element_type=jnp.float32
        )
        for r in range(2):
            slab[index, r, rows, :] = (
                got[:, 256 * r : 256 * r + 128] + got[:, 256 * r + 128 : 256 * r + 256]
            )

    def transform(index, step):
        at = step * 8
        values = [
            tuple(slab[index, r, pl.ds(t * x_local + at, 8), :] for r in range(2))
            for t in range(blocks)
        ]
        waves = flat_fft(values, times_pair)
        for k in range(blocks):
            real, imag = waves[k]
            cos_k, sin_k = twist[0, k : k + 1, :], twist[1, k : k + 1, :]
            rows = pl.ds(((k % pairs) * group + k // pairs) * x_local + at, 8)
            turned[index % 2, rows, :128] = real * cos_k + imag * sin_k
            turned[index % 2, rows, 128:] = imag * cos_k - real * sin_k

    def along_y(index, start):
        moved = dot_rows_split(stacked, turned[index % 2, start * 128 : (start + 2) * 128, :])
        for k in range(2):
            for r in range(2):
                one = moved[r * 128 : (r + 1) * 128, k * 128 : (k + 1) * 128]
                base = (index * 2 + r) * pairs + start + k
                out[pl.ds(base, 128, stride=count * 2 * pairs), :] = one

    steps = x_local // 8
    scatter(0, 0)
    scatter(0, 1)
    for index in range(count):
        for half in range(2):
            if index + 1 < count:
                scatter(index + 1, half)
            for step in range(half * steps // 2, (half + 1) * steps // 2):
                transform(index, step)
        for start in range(0, pairs, 2):
            along_y(index, start)


def slab_waves(data, me, slots, x_local, blocks, mesh_sizes, per_owner):
    devices = data.shape[0]
    count = data.shape[1] // (2 * per_owner)
    fine = angles(128, 128, 128)
    order = owner_order(mesh_sizes)
    fine = fine.reshape(devices, 128 // devices, 128)[order].reshape(128, 128)
    table = complex_table(np.cos(fine), np.sin(fine))
    twist_angle = angles(blocks, 128, blocks * 128)
    twist = np.stack([np.cos(twist_angle), np.sin(twist_angle)]).astype(np.float32)
    entries = devices * per_owner
    rows = blocks * x_local * 2
    made = pl.pallas_call(
        functools.partial(slab_kernel, count, x_local, blocks, per_owner, order),
        out_shape=pltpu.VMEM((count * rows, 128), jnp.float32),
        in_specs=[pl.BlockSpec(memory_space=pltpu.SMEM)]
        + [pl.BlockSpec(memory_space=pltpu.VMEM)] * 4,
        out_specs=pl.BlockSpec(memory_space=pltpu.VMEM),
        scratch_shapes=[
            pltpu.VMEM((blocks * x_local, entries), jnp.bfloat16),
            pltpu.VMEM((count, 2, blocks * x_local, 128), jnp.float32),
            pltpu.VMEM((2, blocks * x_local, 256), jnp.float32),
        ],
        compiler_params=params(40),
        cost_estimate=cost(
            count * blocks * x_local * (entries * 1024 + 512 * 1024),
            count * (entries * 1024 + rows * 512),
        ),
    )(me, slots, jnp.asarray(table), jnp.asarray(twist), in_vmem(data))
    return made.reshape(devices, count * rows // devices, 128)


def rotated(pieces, selector):
    count = len(pieces)
    step = 1
    while step < count:
        taken = (selector & step) != 0
        pieces = [
            jnp.where(taken, pieces[(j + step) % count], pieces[j]) for j in range(count)
        ]
        step *= 2
    return pieces


def x_first(sizes, comp, step, twist, data, turned):
    devices, x_local, y_local, blocks, order = sizes
    pairs = blocks * x_local // 128
    kept = y_local // blocks
    at = pl.multiple_of(step * (data.shape[1] // kept), 2 * pairs) + comp * 2 * pairs
    values = [
        tuple(data[order.index(o), pl.ds(at + r * pairs, pairs), :] for r in range(2))
        for o in range(devices)
    ]
    waves = flat_fft(values, times_pair)
    rows = pl.ds(pl.multiple_of(step * pairs, pairs), pairs)
    for k in range(devices):
        real, imag = waves[k]
        cos_k, sin_k = twist[0, k : k + 1, :], twist[1, k : k + 1, :]
        turned[comp % 2, k, rows, :128] = real * cos_k + imag * sin_k
        turned[comp % 2, k, rows, 128:] = imag * cos_k - real * sin_k


def x_second(sizes, comp, step, together, stacked, turned, columns):
    devices, x_local, y_local, blocks, _ = sizes
    group = 128 // x_local
    narrow = (y_local // blocks) * (blocks // group)
    banks = 2 * group
    lane = lax.broadcasted_iota(jnp.int32, (1, 128), 1)
    start = step * together
    rows = turned[comp % 2, pl.ds(start, together)].reshape(together * narrow, 256)
    moved = dot_rows_split(stacked, rows)
    if square(sizes):
        for base in range(0, together, banks):
            rolled = []
            for bank in range(banks):
                one = moved[bank * x_local : (bank + 1) * x_local, base * narrow :][:, :128]
                rolled.append(pltpu.roll(one, bank * narrow, 1) if bank else one)
            made = rotated(rolled, lane >> (narrow.bit_length() - 1))
            for k in range(banks):
                rows = pl.ds(start + base + k, x_local, stride=devices)
                columns[comp, rows, :] = made[-k % banks]
        return
    for k in range(together):
        one = jnp.concatenate(
            [
                moved[bank * x_local : (bank + 1) * x_local, k * narrow : (k + 1) * narrow]
                for bank in range(banks)
            ],
            axis=1,
        )
        columns[comp, pl.ds(start + k, x_local, stride=devices), :] = one


def square(sizes):
    _, x_local, y_local, blocks, _ = sizes
    group = 128 // x_local
    narrow = (y_local // blocks) * (blocks // group)
    return 2 * group * narrow == 128 and 128 // narrow == 2 * group


def x_third(sizes, comp, start, columns, kept):
    _, x_local, y_local, blocks, _ = sizes
    group = 128 // x_local
    pairs = blocks // group
    steps = y_local // blocks
    narrow = steps * pairs
    banks = 2 * group
    lane = lax.broadcasted_iota(jnp.int32, (1, 128), 1)
    block = columns[comp, start : start + 128, :].T
    pieces = [block[bank * narrow : (bank + 1) * narrow] for bank in range(banks)]
    if square(sizes):
        pieces = rotated(pieces, lane & (banks - 1))
    for bank, one in enumerate(pieces):
        for step in range(steps):
            row = step * blocks + (bank % group) * pairs
            kept[comp, bank // group, row : row + pairs, start : start + 128] = one[
                step * pairs : (step + 1) * pairs
            ]


def mix_rows(rows, columns, tensor, waves):
    sums = [None] * 3
    for row in range(3):
        for col in range(3):
            entry = pair_index[row][col]
            green_real, green_imag = tensor[0, entry, rows, columns], tensor[1, entry, rows, columns]
            real, imag = waves[col, 0, rows, columns], waves[col, 1, rows, columns]
            real_term = green_real * real - green_imag * imag
            imag_term = green_real * imag + green_imag * real
            old = sums[row]
            sums[row] = (
                (real_term, imag_term) if old is None else (old[0] + real_term, old[1] + imag_term)
            )
    return sums


def field_kernel(sizes, twist, table, data, green, out, *scratch):
    y_local, x_cells = green.shape[2:]
    turned, columns, tensor, kept, made, in_sem, out_sems = scratch
    width = x_cells // made.shape[0]
    fetch = pltpu.make_async_copy(green, tensor, in_sem)
    fetch.start()
    stacked = stacked_halves(table)
    devices, x_local, _, blocks, _ = sizes
    steps = y_local // blocks
    narrow = y_local * x_local // 128
    together = min(devices, 256 // narrow)
    groups = devices // together
    blocks_each = x_cells // 128 // groups
    for comp in range(3):
        pl.loop(0, steps)(lambda i: x_first(sizes, comp, i, twist, data, turned))
        for i in range(groups):
            x_second(sizes, comp, i, together, stacked, turned, columns)
            for block in range(i * blocks_each, (i + 1) * blocks_each):
                if comp > 0:
                    x_third(sizes, comp - 1, block * 128, columns, kept)
    fetch.wait()
    pieces = made.shape[0]

    def turn(piece):
        for start in range(piece * width, (piece + 1) * width, 128):
            x_third(sizes, 2, start, columns, kept)

    sends = []
    turn(0)
    for piece in range(pieces):
        if piece + 1 < pieces:
            turn(piece + 1)
        part = pl.ds(piece * width, width)
        for step in range(y_local // 8):
            rows = pl.ds(step * 8, 8)
            for row, pair in enumerate(mix_rows(rows, part, tensor, kept)):
                for r in range(2):
                    made[piece, r, row, rows, :] = pair[r]
        send = pltpu.make_async_copy(made.at[piece], out.at[:, :, :, part], out_sems.at[piece])
        send.start()
        sends.append(send)
    for send in sends:
        send.wait()


def x_tables(devices, x_local, y_cells):
    x_cells = devices * x_local
    group = 128 // x_local
    fine = angles(x_local, x_local, x_local)
    scale = 1.0 / math.sqrt(x_cells * y_cells)
    apart = np.eye(group) * scale
    table = complex_table(np.kron(apart, np.cos(fine)), np.kron(apart, np.sin(fine)))
    angle = np.tile(angles(devices, x_local, x_cells), (1, group))
    twist = np.stack([np.cos(angle), np.sin(angle)]).astype(np.float32)
    return jnp.asarray(twist), jnp.asarray(table)


def x_scratch(devices, x_local, y_local):
    return [
        pltpu.VMEM((2, devices, y_local * x_local // 128, 256), jnp.float32),
        pltpu.VMEM((3, devices * x_local, 2 * y_local), jnp.float32),
    ]


def field(data, green, devices, x_local, y_local, y_cells, mesh_sizes):
    x_cells = devices * x_local
    pieces = 8
    sizes = (devices, x_local, y_local, y_cells // 128, owner_order(mesh_sizes))
    plane = (y_local, x_cells)
    return pl.pallas_call(
        functools.partial(field_kernel, sizes),
        out_shape=pltpu.HBM((2, 3) + plane, jnp.float32),
        in_specs=[pl.BlockSpec(memory_space=pltpu.VMEM)] * 3
        + [pl.BlockSpec(memory_space=pltpu.HBM)],
        out_specs=pl.BlockSpec(memory_space=pltpu.HBM),
        scratch_shapes=x_scratch(devices, x_local, y_local)
        + [
            pltpu.VMEM((2, 6) + plane, jnp.float32),
            pltpu.VMEM((3, 2) + plane, jnp.float32),
            pltpu.VMEM((pieces, 2, 3, y_local, x_cells // pieces), jnp.float32),
            pltpu.SemaphoreType.DMA(()),
            pltpu.SemaphoreType.DMA((pieces,)),
        ],
        compiler_params=params(40),
        cost_estimate=cost(3 * x_cells * y_local * (x_local * 24 + 24), x_cells * y_local * 96),
    )(*x_tables(devices, x_local, y_cells), in_vmem(data), in_hbm(green))


places = ("gl", "gx", "gz")


def gather_tables(table, axes, devices):
    tables, mask = table[None], 1
    while mask < devices:
        pairs = [(d, d ^ mask) for d in range(devices)]
        tables = jnp.concatenate([tables, lax.ppermute(tables, axes, pairs)])
        mask *= 2
    return tables


def exchange(data):
    return lax.all_to_all(data, places, split_axis=0, concat_axis=0, tiled=True)


def per_device(tiles, tile_owner, tile_slot, tile_count, green):
    count_gl = lax.axis_size("gl")
    mesh_sizes = (lax.axis_size("gx"), count_gl)
    devices = 4 * mesh_sizes[0] * count_gl
    tile_total, tile_len = tiles.shape[2], tiles.shape[3]
    planes, y_local, x_cells = green.shape[2:]
    y_cells = y_local * devices
    x_local = x_cells // devices
    blocks = y_cells // tile_len
    per_owner = max(2, 2 * tile_total // devices)
    assert planes == 1 and tile_len == 128
    owner_row, slot_row = tile_owner.reshape(1, tile_total), tile_slot.reshape(1, tile_total)
    green = green.reshape(2, 6, y_local, x_cells)
    owners = ("gx", "gz", "gl")
    me = jnp.stack([lax.axis_index(places), lax.axis_index(owners)]).astype(jnp.int32)
    lists = (owner_row, slot_row, tile_count)
    packed, slots = pack(tiles, *lists, devices, mesh_sizes, per_owner)
    arrived, slots = exchange(packed), gather_tables(slots, owners, devices)
    moved = exchange(slab_waves(arrived, me, slots, x_local, blocks, mesh_sizes, per_owner))
    mixed = field(moved, green, devices, x_local, y_local, y_cells, mesh_sizes)
    return mixed.reshape(2, 3, planes, y_local, x_cells)


def solution(mesh):
    count_gx, count_gy = mesh.devices.shape
    fine_mesh = jax.sharding.Mesh(
        mesh.devices.reshape(count_gx, 4, count_gy // 4), ("gx", "gz", "gl")
    )
    every = ("gx", "gz", "gl")
    in_specs = (
        P(None, None, every, None),
        P(every, None),
        P(every),
        P(every),
        P(None, None, None, every, None),
    )
    out_specs = P(None, None, None, every, None)
    return jax.shard_map(
        per_device, mesh=fine_mesh, in_specs=in_specs, out_specs=out_specs, check_vma=False
    )
```

```python
import functools
import math

import jax
import jax.numpy as jnp
import numpy as np
from jax import lax
from jax.experimental import pallas as pl
from jax.experimental.pallas import tpu as pltpu
from jax.sharding import PartitionSpec as P

pair_index = ((0, 3, 4), (3, 1, 5), (4, 5, 2))
by_rows = (((1,), (1,)), ((), ()))


def params(mebibytes):
    return pltpu.CompilerParams(vmem_limit_bytes=mebibytes * 1024 * 1024)


def in_hbm(array):
    return pltpu.with_memory_space_constraint(array, pltpu.HBM)


def in_vmem(array):
    return pltpu.with_memory_space_constraint(array, pltpu.VMEM)


def cost(flops, moved):
    return pl.CostEstimate(flops=flops, bytes_accessed=moved, transcendentals=0)


def angles(rows, columns, length):
    products = np.outer(np.arange(rows), np.arange(columns)) % length
    return 2.0 * math.pi / length * products


def split_two(data):
    high = data.astype(jnp.bfloat16)
    return high, (data - high.astype(jnp.float32)).astype(jnp.bfloat16)


def dot_rows(left, right):
    return lax.dot_general(left, right, by_rows, preferred_element_type=jnp.float32)


def dot_rows_split(stacked, data):
    rows = stacked.shape[0] // 2
    high, low = split_two(data)
    both = dot_rows(stacked, high)
    return both[:rows] + both[rows:] + dot_rows(stacked[:rows], low)


def stacked_halves(table):
    return jnp.concatenate(split_two(table[...]))


def flat_fft(values, times):
    length = len(values)
    if length == 1:
        return values
    even = flat_fft(values[0::2], times)
    odd = flat_fft(values[1::2], times)
    lower, upper = [], []
    for k in range(length // 2):
        turned = times(odd[k], k, length)
        lower.append(jax.tree.map(lambda a, b: a + b, even[k], turned))
        upper.append(jax.tree.map(lambda a, b: a - b, even[k], turned))
    return lower + upper


def times_pair(value, k, length):
    real, imag = value
    if k == 0:
        return value
    if 4 * k == length:
        return (imag, -real)
    cos_k = math.cos(2.0 * math.pi * k / length)
    sin_k = math.sin(2.0 * math.pi * k / length)
    return (real * cos_k + imag * sin_k, imag * cos_k - real * sin_k)


def place_of(owner, sizes):
    count_gx, count_gl = sizes
    shift = count_gl.bit_length() - 1
    z = (owner >> shift) & 3
    return ((owner & (count_gl - 1)) * count_gx + (owner >> (shift + 2))) * 4 + z


def owner_order(sizes):
    devices = 4 * sizes[0] * sizes[1]
    order = [0] * devices
    for owner in range(devices):
        order[place_of(owner, sizes)] = owner
    return order


def pack_kernel(
    devices, mesh_sizes, per_owner, count, me, owner_row, slot_row, tiles, out, *scratch
):
    held, lists, sems = scratch
    comps = range(tiles.shape[1])
    listed = owner_row.shape[1]
    fetches = [
        pltpu.make_async_copy(owner_row, lists.at[0], sems.at[0]),
        pltpu.make_async_copy(slot_row, lists.at[1], sems.at[1]),
    ]
    fetches += [
        pltpu.make_async_copy(tiles.at[:, comp], held.at[i], sems.at[2 + i])
        for i, comp in enumerate(comps)
    ]
    for fetch in fetches:
        fetch.start()
    sender = lax.broadcasted_iota(jnp.int32, (listed, listed), 0)
    reader = lax.broadcasted_iota(jnp.int32, (listed, listed), 1)
    before = jnp.where(sender < reader, 1.0, 0.0).astype(jnp.bfloat16)
    live = lax.broadcasted_iota(jnp.int32, (1, listed), 1) < count[0]
    fetches[0].wait()
    place = jnp.where(live, place_of(lists[0], mesh_sizes), -1)
    place_at = lax.broadcasted_iota(jnp.int32, (devices, listed), 0)
    named = jnp.where(place_at == place, 1.0, 0.0)
    counted = jnp.dot(named.astype(jnp.bfloat16), before, preferred_element_type=jnp.float32)
    rank = jnp.sum(counted * named, axis=0, keepdims=True).astype(jnp.int32)
    target = jnp.where(live, place * per_owner + rank, -1)
    target_at = lax.broadcasted_iota(jnp.int32, (devices * per_owner, listed), 0)
    chosen = jnp.where(target_at == target, 1.0, 0.0).astype(jnp.bfloat16)
    fetches[1].wait()
    stated = lists[1] + 1
    lane = rank + (me[0] & (128 // per_owner - 1)) * per_owner
    lane_at = lax.broadcasted_iota(jnp.int32, (128, listed), 0)
    laned = jnp.where(lane_at == lane, 1.0, 0.0).astype(jnp.bfloat16)
    coarse = (named * (stated >> 5).astype(jnp.float32)).astype(jnp.bfloat16)
    fine = (named * (stated & 31).astype(jnp.float32)).astype(jnp.bfloat16)
    slots = 32.0 * dot_rows(coarse, laned) + dot_rows(fine, laned)
    start = 2 * len(comps) * per_owner
    out[:, start:, :] = jnp.broadcast_to(slots[:, None, :], (devices, 8, 128))
    for i in range(len(comps)):
        fetches[2 + i].wait()
        parts = [part for r in range(2) for part in split_two(held[i, r])]
        got = jnp.dot(
            chosen, jnp.concatenate(parts, axis=1), preferred_element_type=jnp.float32
        )
        for r in range(2):
            whole = got[:, 256 * r : 256 * r + 128] + got[:, 256 * r + 128 : 256 * r + 256]
            start = (2 * i + r) * per_owner
            out[:, start : start + per_owner, :] = whole.reshape(devices, per_owner, 128)


def pack(tiles, owner_row, slot_row, count, me, devices, mesh_sizes, per_owner):
    comps, listed = tiles.shape[1:3]
    rows = 2 * comps * per_owner + 8
    return pl.pallas_call(
        functools.partial(pack_kernel, devices, mesh_sizes, per_owner),
        out_shape=pltpu.VMEM((devices, rows, 128), jnp.float32),
        in_specs=[pl.BlockSpec(memory_space=pltpu.SMEM)] * 2
        + [pl.BlockSpec(memory_space=pltpu.HBM)] * 3,
        out_specs=pl.BlockSpec(memory_space=pltpu.VMEM),
        scratch_shapes=[
            pltpu.VMEM((comps, 2, listed, 128), jnp.float32),
            pltpu.VMEM((2, 1, listed), jnp.int32),
            pltpu.SemaphoreType.DMA((2 + comps,)),
        ],
        compiler_params=params(24),
        cost_estimate=cost(
            devices * per_owner * listed * 512 * 2 * comps, devices * rows * 1024
        ),
    )(count, me, *[in_hbm(a) for a in (owner_row, slot_row, tiles)])


def complex_table(cos_part, sin_part):
    return np.concatenate(
        [
            np.concatenate([cos_part, sin_part], axis=1),
            np.concatenate([-sin_part, cos_part], axis=1),
        ]
    ).astype(np.float32)


def slab_kernel(count, x_local, blocks, per_owner, table, twist, data, out, *scratch):
    chosen, slab, turned = scratch
    devices = data.shape[0]
    entries = devices * per_owner
    group = 128 // x_local
    pairs = blocks // group
    shift = blocks.bit_length() - 1
    every = 128 // per_owner
    stated = [
        sum([data[o, data.shape[1] - 8 :][:1] for o in range(start, start + every)])
        for start in range(0, devices, every)
    ]
    slot = jnp.concatenate(stated, axis=1).astype(jnp.int32) - 1
    landing = jnp.where(slot >= 0, (slot & (blocks - 1)) * x_local + (slot >> shift), -1)
    slab_rows = blocks * x_local
    stacked = stacked_halves(table)
    step_rows = slab_rows // 2

    def scatter(index, half):
        parts = []
        for r in range(2):
            start = (2 * index + r) * per_owner
            parts.extend(split_two(data[:, start : start + per_owner, :].reshape(entries, 128)))
        rows = pl.ds(half * step_rows, step_rows)
        got = jnp.dot(
            chosen[rows, :], jnp.concatenate(parts, axis=1), preferred_element_type=jnp.float32
        )
        for r in range(2):
            slab[index, r, rows, :] = (
                got[:, 256 * r : 256 * r + 128] + got[:, 256 * r + 128 : 256 * r + 256]
            )

    def transform(index, step):
        at = step * 8
        values = [
            tuple(slab[index, r, pl.ds(t * x_local + at, 8), :] for r in range(2))
            for t in range(blocks)
        ]
        waves = flat_fft(values, times_pair)
        for k in range(blocks):
            real, imag = waves[k]
            cos_k, sin_k = twist[0, k : k + 1, :], twist[1, k : k + 1, :]
            rows = pl.ds(((k % pairs) * group + k // pairs) * x_local + at, 8)
            turned[index % 2, rows, :128] = real * cos_k + imag * sin_k
            turned[index % 2, rows, 128:] = imag * cos_k - real * sin_k

    def along_y(index, start):
        moved = dot_rows_split(stacked, turned[index % 2, start * 128 : (start + 2) * 128, :])
        for k in range(2):
            for r in range(2):
                one = moved[r * 128 : (r + 1) * 128, k * 128 : (k + 1) * 128]
                base = (index * 2 + r) * pairs + start + k
                out[pl.ds(base, 128, stride=count * 2 * pairs), :] = one

    def choose(half):
        start = half * step_rows
        place = start + lax.broadcasted_iota(jnp.int32, (step_rows, entries), 0)
        chosen[pl.ds(start, step_rows), :] = jnp.where(place == landing, 1.0, 0.0).astype(
            jnp.bfloat16
        )

    steps = x_local // 8
    choose(0)
    scatter(0, 0)
    choose(1)
    scatter(0, 1)
    for index in range(count):
        for half in range(2):
            if index + 1 < count:
                scatter(index + 1, half)
            for step in range(half * steps // 2, (half + 1) * steps // 2):
                transform(index, step)
        for start in range(0, pairs, 2):
            along_y(index, start)


def slab_waves(data, x_local, blocks, mesh_sizes, per_owner):
    devices = data.shape[0]
    count = data.shape[1] // (2 * per_owner)
    fine = angles(128, 128, 128)
    order = owner_order(mesh_sizes)
    fine = fine.reshape(devices, 128 // devices, 128)[order].reshape(128, 128)
    table = complex_table(np.cos(fine), np.sin(fine))
    twist_angle = angles(blocks, 128, blocks * 128)
    twist = np.stack([np.cos(twist_angle), np.sin(twist_angle)]).astype(np.float32)
    entries = devices * per_owner
    rows = blocks * x_local * 2
    made = pl.pallas_call(
        functools.partial(slab_kernel, count, x_local, blocks, per_owner),
        out_shape=pltpu.VMEM((count * rows, 128), jnp.float32),
        in_specs=[pl.BlockSpec(memory_space=pltpu.VMEM)] * 3,
        out_specs=pl.BlockSpec(memory_space=pltpu.VMEM),
        scratch_shapes=[
            pltpu.VMEM((blocks * x_local, entries), jnp.bfloat16),
            pltpu.VMEM((count, 2, blocks * x_local, 128), jnp.float32),
            pltpu.VMEM((2, blocks * x_local, 256), jnp.float32),
        ],
        compiler_params=params(40),
        cost_estimate=cost(
            count * blocks * x_local * (entries * 1024 + 512 * 1024),
            count * (entries * 1024 + rows * 512),
        ),
    )(jnp.asarray(table), jnp.asarray(twist), in_vmem(data))
    return made.reshape(devices, count * rows // devices, 128)


def rotated(pieces, selector):
    count = len(pieces)
    step = 1
    while step < count:
        taken = (selector & step) != 0
        pieces = [
            jnp.where(taken, pieces[(j + step) % count], pieces[j]) for j in range(count)
        ]
        step *= 2
    return pieces


def x_first(sizes, comp, step, twist, data, turned):
    devices, x_local, y_local, blocks, order = sizes
    pairs = blocks * x_local // 128
    kept = y_local // blocks
    at = pl.multiple_of(step * (data.shape[1] // kept), 2 * pairs) + comp * 2 * pairs
    values = [
        tuple(data[order.index(o), pl.ds(at + r * pairs, pairs), :] for r in range(2))
        for o in range(devices)
    ]
    waves = flat_fft(values, times_pair)
    rows = pl.ds(pl.multiple_of(step * pairs, pairs), pairs)
    for k in range(devices):
        real, imag = waves[k]
        cos_k, sin_k = twist[0, k : k + 1, :], twist[1, k : k + 1, :]
        turned[comp % 2, k, rows, :128] = real * cos_k + imag * sin_k
        turned[comp % 2, k, rows, 128:] = imag * cos_k - real * sin_k


def x_second(sizes, comp, step, together, stacked, turned, columns):
    devices, x_local, y_local, blocks, _ = sizes
    group = 128 // x_local
    narrow = (y_local // blocks) * (blocks // group)
    banks = 2 * group
    lane = lax.broadcasted_iota(jnp.int32, (1, 128), 1)
    start = step * together
    rows = turned[comp % 2, pl.ds(start, together)].reshape(together * narrow, 256)
    moved = dot_rows_split(stacked, rows)
    if square(sizes):
        for base in range(0, together, banks):
            rolled = []
            for bank in range(banks):
                one = moved[bank * x_local : (bank + 1) * x_local, base * narrow :][:, :128]
                rolled.append(pltpu.roll(one, bank * narrow, 1) if bank else one)
            made = rotated(rolled, lane >> (narrow.bit_length() - 1))
            for k in range(banks):
                rows = pl.ds(start + base + k, x_local, stride=devices)
                columns[comp, rows, :] = made[-k % banks]
        return
    for k in range(together):
        one = jnp.concatenate(
            [
                moved[bank * x_local : (bank + 1) * x_local, k * narrow : (k + 1) * narrow]
                for bank in range(banks)
            ],
            axis=1,
        )
        columns[comp, pl.ds(start + k, x_local, stride=devices), :] = one


def square(sizes):
    _, x_local, y_local, blocks, _ = sizes
    group = 128 // x_local
    narrow = (y_local // blocks) * (blocks // group)
    return 2 * group * narrow == 128 and 128 // narrow == 2 * group


def x_third(sizes, comp, start, columns, kept):
    _, x_local, y_local, blocks, _ = sizes
    group = 128 // x_local
    pairs = blocks // group
    steps = y_local // blocks
    narrow = steps * pairs
    banks = 2 * group
    lane = lax.broadcasted_iota(jnp.int32, (1, 128), 1)
    block = columns[comp, start : start + 128, :].T
    pieces = [block[bank * narrow : (bank + 1) * narrow] for bank in range(banks)]
    if square(sizes):
        pieces = rotated(pieces, lane & (banks - 1))
    for bank, one in enumerate(pieces):
        for step in range(steps):
            row = step * blocks + (bank % group) * pairs
            kept[comp, bank // group, row : row + pairs, start : start + 128] = one[
                step * pairs : (step + 1) * pairs
            ]


def mix_rows(rows, columns, tensor, waves):
    sums = [None] * 3
    for row in range(3):
        for col in range(3):
            entry = pair_index[row][col]
            green_real, green_imag = tensor[0, entry, rows, columns], tensor[1, entry, rows, columns]
            real, imag = waves[col, 0, rows, columns], waves[col, 1, rows, columns]
            real_term = green_real * real - green_imag * imag
            imag_term = green_real * imag + green_imag * real
            old = sums[row]
            sums[row] = (
                (real_term, imag_term) if old is None else (old[0] + real_term, old[1] + imag_term)
            )
    return sums


def field_kernel(sizes, twist, table, data, green, out, *scratch):
    y_local, x_cells = green.shape[2:]
    turned, columns, tensor, kept, made, in_sem, out_sems = scratch
    width = x_cells // made.shape[0]
    fetch = pltpu.make_async_copy(green, tensor, in_sem)
    fetch.start()
    stacked = stacked_halves(table)
    devices, x_local, _, blocks, _ = sizes
    steps = y_local // blocks
    narrow = y_local * x_local // 128
    together = min(devices, 256 // narrow)
    groups = devices // together
    blocks_each = x_cells // 128 // groups
    for comp in range(3):
        unroll = 2 if steps % 2 == 0 else 1
        pl.loop(0, steps, unroll=unroll)(lambda i: x_first(sizes, comp, i, twist, data, turned))
        for i in range(groups):
            x_second(sizes, comp, i, together, stacked, turned, columns)
            for block in range(i * blocks_each, (i + 1) * blocks_each):
                if comp > 0:
                    x_third(sizes, comp - 1, block * 128, columns, kept)
    fetch.wait()
    pieces = made.shape[0]

    def turn(piece):
        for start in range(piece * width, (piece + 1) * width, 128):
            x_third(sizes, 2, start, columns, kept)

    sends = []
    turn(0)
    for piece in range(pieces):
        if piece + 1 < pieces:
            turn(piece + 1)
        part = pl.ds(piece * width, width)
        for step in range(y_local // 8):
            rows = pl.ds(step * 8, 8)
            for row, pair in enumerate(mix_rows(rows, part, tensor, kept)):
                for r in range(2):
                    made[piece, r, row, rows, :] = pair[r]
        send = pltpu.make_async_copy(made.at[piece], out.at[:, :, :, part], out_sems.at[piece])
        send.start()
        sends.append(send)
    for send in sends:
        send.wait()


def x_tables(devices, x_local, y_cells):
    x_cells = devices * x_local
    group = 128 // x_local
    fine = angles(x_local, x_local, x_local)
    scale = 1.0 / math.sqrt(x_cells * y_cells)
    apart = np.eye(group) * scale
    table = complex_table(np.kron(apart, np.cos(fine)), np.kron(apart, np.sin(fine)))
    angle = np.tile(angles(devices, x_local, x_cells), (1, group))
    twist = np.stack([np.cos(angle), np.sin(angle)]).astype(np.float32)
    return jnp.asarray(twist), jnp.asarray(table)


def x_scratch(devices, x_local, y_local):
    return [
        pltpu.VMEM((2, devices, y_local * x_local // 128, 256), jnp.float32),
        pltpu.VMEM((3, devices * x_local, 2 * y_local), jnp.float32),
    ]


def field(data, green, devices, x_local, y_local, y_cells, mesh_sizes):
    x_cells = devices * x_local
    pieces = 8
    sizes = (devices, x_local, y_local, y_cells // 128, owner_order(mesh_sizes))
    plane = (y_local, x_cells)
    return pl.pallas_call(
        functools.partial(field_kernel, sizes),
        out_shape=pltpu.HBM((2, 3) + plane, jnp.float32),
        in_specs=[pl.BlockSpec(memory_space=pltpu.VMEM)] * 3
        + [pl.BlockSpec(memory_space=pltpu.HBM)],
        out_specs=pl.BlockSpec(memory_space=pltpu.HBM),
        scratch_shapes=x_scratch(devices, x_local, y_local)
        + [
            pltpu.VMEM((2, 6) + plane, jnp.float32),
            pltpu.VMEM((3, 2) + plane, jnp.float32),
            pltpu.VMEM((pieces, 2, 3, y_local, x_cells // pieces), jnp.float32),
            pltpu.SemaphoreType.DMA(()),
            pltpu.SemaphoreType.DMA((pieces,)),
        ],
        compiler_params=params(40),
        cost_estimate=cost(3 * x_cells * y_local * (x_local * 24 + 24), x_cells * y_local * 96),
    )(*x_tables(devices, x_local, y_cells), in_vmem(data), in_hbm(green))


places = ("gl", "gx", "gz")


def exchange(data):
    return lax.all_to_all(data, places, split_axis=0, concat_axis=0, tiled=True)


def per_device(tiles, tile_owner, tile_slot, tile_count, green):
    count_gl = lax.axis_size("gl")
    mesh_sizes = (lax.axis_size("gx"), count_gl)
    devices = 4 * mesh_sizes[0] * count_gl
    tile_total, tile_len = tiles.shape[2], tiles.shape[3]
    planes, y_local, x_cells = green.shape[2:]
    y_cells = y_local * devices
    x_local = x_cells // devices
    blocks = y_cells // tile_len
    per_owner = max(2, 2 * tile_total // devices)
    assert planes == 1 and tile_len == 128
    owner_row, slot_row = tile_owner.reshape(1, tile_total), tile_slot.reshape(1, tile_total)
    green = green.reshape(2, 6, y_local, x_cells)
    me = lax.axis_index(places).reshape(1).astype(jnp.int32)
    lists = (owner_row, slot_row, tile_count, me)
    arrived = exchange(pack(tiles, *lists, devices, mesh_sizes, per_owner))
    moved = exchange(slab_waves(arrived, x_local, blocks, mesh_sizes, per_owner))
    mixed = field(moved, green, devices, x_local, y_local, y_cells, mesh_sizes)
    return mixed.reshape(2, 3, planes, y_local, x_cells)


def solution(mesh):
    count_gx, count_gy = mesh.devices.shape
    fine_mesh = jax.sharding.Mesh(
        mesh.devices.reshape(count_gx, 4, count_gy // 4), ("gx", "gz", "gl")
    )
    every = ("gx", "gz", "gl")
    in_specs = (
        P(None, None, every, None),
        P(every, None),
        P(every),
        P(every),
        P(None, None, None, every, None),
    )
    out_specs = P(None, None, None, every, None)
    return jax.shard_map(
        per_device, mesh=fine_mesh, in_specs=in_specs, out_specs=out_specs, check_vma=False
    )
```

```python
import functools
import math

import jax
import jax.numpy as jnp
import numpy as np
from jax import lax
from jax.experimental import pallas as pl
from jax.experimental.pallas import tpu as pltpu
from jax.sharding import PartitionSpec as P

pair_index = ((0, 3, 4), (3, 1, 5), (4, 5, 2))
by_rows = (((1,), (1,)), ((), ()))


def params(mebibytes):
    return pltpu.CompilerParams(vmem_limit_bytes=mebibytes * 1024 * 1024)


def in_hbm(array):
    return pltpu.with_memory_space_constraint(array, pltpu.HBM)


def in_vmem(array):
    return pltpu.with_memory_space_constraint(array, pltpu.VMEM)


def cost(flops, moved):
    return pl.CostEstimate(flops=flops, bytes_accessed=moved, transcendentals=0)


def angles(rows, columns, length):
    products = np.outer(np.arange(rows), np.arange(columns)) % length
    return 2.0 * math.pi / length * products


def split_two(data):
    high = data.astype(jnp.bfloat16)
    return high, (data - high.astype(jnp.float32)).astype(jnp.bfloat16)


def dot_rows(left, right):
    return lax.dot_general(left, right, by_rows, preferred_element_type=jnp.float32)


def dot_rows_split(stacked, data):
    rows = stacked.shape[0] // 2
    high, low = split_two(data)
    both = dot_rows(stacked, high)
    return both[:rows] + both[rows:] + dot_rows(stacked[:rows], low)


def stacked_halves(table):
    return jnp.concatenate(split_two(table[...]))


def flat_fft(values, times):
    length = len(values)
    if length == 1:
        return values
    even = flat_fft(values[0::2], times)
    odd = flat_fft(values[1::2], times)
    lower, upper = [], []
    for k in range(length // 2):
        turned = times(odd[k], k, length)
        lower.append(jax.tree.map(lambda a, b: a + b, even[k], turned))
        upper.append(jax.tree.map(lambda a, b: a - b, even[k], turned))
    return lower + upper


def times_pair(value, k, length):
    real, imag = value
    if k == 0:
        return value
    if 4 * k == length:
        return (imag, -real)
    cos_k = math.cos(2.0 * math.pi * k / length)
    sin_k = math.sin(2.0 * math.pi * k / length)
    return (real * cos_k + imag * sin_k, imag * cos_k - real * sin_k)


def place_of(owner, sizes):
    count_gx, count_gl = sizes
    shift = count_gl.bit_length() - 1
    z = (owner >> shift) & 3
    return ((owner & (count_gl - 1)) * count_gx + (owner >> (shift + 2))) * 4 + z


def owner_order(sizes):
    devices = 4 * sizes[0] * sizes[1]
    order = [0] * devices
    for owner in range(devices):
        order[place_of(owner, sizes)] = owner
    return order


def pack_kernel(
    devices, mesh_sizes, per_owner, count, me, owner_row, slot_row, tiles, out, *scratch
):
    held, lists, sems = scratch
    comps = range(tiles.shape[1])
    listed = owner_row.shape[1]
    fetches = [
        pltpu.make_async_copy(owner_row, lists.at[0], sems.at[0]),
        pltpu.make_async_copy(slot_row, lists.at[1], sems.at[1]),
    ]
    fetches += [
        pltpu.make_async_copy(tiles.at[:, comp], held.at[i], sems.at[2 + i])
        for i, comp in enumerate(comps)
    ]
    for fetch in fetches:
        fetch.start()
    sender = lax.broadcasted_iota(jnp.int32, (listed, listed), 0)
    reader = lax.broadcasted_iota(jnp.int32, (listed, listed), 1)
    before = jnp.where(sender < reader, 1.0, 0.0).astype(jnp.bfloat16)
    live = lax.broadcasted_iota(jnp.int32, (1, listed), 1) < count[0]
    fetches[0].wait()
    place = jnp.where(live, place_of(lists[0], mesh_sizes), -1)
    place_at = lax.broadcasted_iota(jnp.int32, (devices, listed), 0)
    named = jnp.where(place_at == place, 1.0, 0.0)
    counted = jnp.dot(named.astype(jnp.bfloat16), before, preferred_element_type=jnp.float32)
    rank = jnp.sum(counted * named, axis=0, keepdims=True).astype(jnp.int32)
    target = jnp.where(live, place * per_owner + rank, -1)
    target_at = lax.broadcasted_iota(jnp.int32, (devices * per_owner, listed), 0)
    chosen = jnp.where(target_at == target, 1.0, 0.0).astype(jnp.bfloat16)
    fetches[1].wait()
    stated = lists[1] + 1
    lane = rank + (me[0] & (128 // per_owner - 1)) * per_owner
    lane_at = lax.broadcasted_iota(jnp.int32, (128, listed), 0)
    laned = jnp.where(lane_at == lane, 1.0, 0.0).astype(jnp.bfloat16)
    coarse = (named * (stated >> 5).astype(jnp.float32)).astype(jnp.bfloat16)
    fine = (named * (stated & 31).astype(jnp.float32)).astype(jnp.bfloat16)
    slots = 32.0 * dot_rows(coarse, laned) + dot_rows(fine, laned)
    start = 2 * len(comps) * per_owner
    out[:, start:, :] = jnp.broadcast_to(slots[:, None, :], (devices, 8, 128))
    for i in range(len(comps)):
        fetches[2 + i].wait()
        parts = [part for r in range(2) for part in split_two(held[i, r])]
        got = jnp.dot(
            chosen, jnp.concatenate(parts, axis=1), preferred_element_type=jnp.float32
        )
        for r in range(2):
            whole = got[:, 256 * r : 256 * r + 128] + got[:, 256 * r + 128 : 256 * r + 256]
            start = (2 * i + r) * per_owner
            out[:, start : start + per_owner, :] = whole.reshape(devices, per_owner, 128)


def pack(tiles, owner_row, slot_row, count, me, devices, mesh_sizes, per_owner):
    comps, listed = tiles.shape[1:3]
    rows = 2 * comps * per_owner + 8
    return pl.pallas_call(
        functools.partial(pack_kernel, devices, mesh_sizes, per_owner),
        out_shape=pltpu.VMEM((devices, rows, 128), jnp.float32),
        in_specs=[pl.BlockSpec(memory_space=pltpu.SMEM)] * 2
        + [pl.BlockSpec(memory_space=pltpu.HBM)] * 3,
        out_specs=pl.BlockSpec(memory_space=pltpu.VMEM),
        scratch_shapes=[
            pltpu.VMEM((comps, 2, listed, 128), jnp.float32),
            pltpu.VMEM((2, 1, listed), jnp.int32),
            pltpu.SemaphoreType.DMA((2 + comps,)),
        ],
        compiler_params=params(24),
        cost_estimate=cost(
            devices * per_owner * listed * 512 * 2 * comps, devices * rows * 1024
        ),
    )(count, me, *[in_hbm(a) for a in (owner_row, slot_row, tiles)])


def complex_table(cos_part, sin_part):
    return np.concatenate(
        [
            np.concatenate([cos_part, sin_part], axis=1),
            np.concatenate([-sin_part, cos_part], axis=1),
        ]
    ).astype(np.float32)


def slab_kernel(count, x_local, blocks, per_owner, table, twist, data, out, *scratch):
    chosen, slab, turned = scratch
    devices = data.shape[0]
    entries = devices * per_owner
    group = 128 // x_local
    pairs = blocks // group
    shift = blocks.bit_length() - 1
    every = 128 // per_owner
    stated = [
        sum([data[o, data.shape[1] - 8 :][:1] for o in range(start, start + every)])
        for start in range(0, devices, every)
    ]
    slot = jnp.concatenate(stated, axis=1).astype(jnp.int32) - 1
    landing = jnp.where(slot >= 0, (slot & (blocks - 1)) * x_local + (slot >> shift), -1)
    slab_rows = blocks * x_local
    stacked = stacked_halves(table)

    def scatter(index):
        parts = []
        for r in range(2):
            start = (2 * index + r) * per_owner
            parts.extend(split_two(data[:, start : start + per_owner, :].reshape(entries, 128)))
        got = jnp.dot(
            chosen[...], jnp.concatenate(parts, axis=1), preferred_element_type=jnp.float32
        )
        for r in range(2):
            slab[index, r] = (
                got[:, 256 * r : 256 * r + 128] + got[:, 256 * r + 128 : 256 * r + 256]
            )

    def transform(index, step):
        at = step * 8
        values = [
            tuple(slab[index, r, pl.ds(t * x_local + at, 8), :] for r in range(2))
            for t in range(blocks)
        ]
        waves = flat_fft(values, times_pair)
        for k in range(blocks):
            real, imag = waves[k]
            cos_k, sin_k = twist[0, k : k + 1, :], twist[1, k : k + 1, :]
            rows = pl.ds(((k % pairs) * group + k // pairs) * x_local + at, 8)
            turned[index % 2, rows, :128] = real * cos_k + imag * sin_k
            turned[index % 2, rows, 128:] = imag * cos_k - real * sin_k

    def along_y(index, start):
        moved = dot_rows_split(stacked, turned[index % 2, start * 128 : (start + 2) * 128, :])
        for k in range(2):
            for r in range(2):
                one = moved[r * 128 : (r + 1) * 128, k * 128 : (k + 1) * 128]
                base = (index * 2 + r) * pairs + start + k
                out[pl.ds(base, 128, stride=count * 2 * pairs), :] = one

    place = lax.broadcasted_iota(jnp.int32, (slab_rows, entries), 0)
    chosen[...] = jnp.where(place == landing, 1.0, 0.0).astype(jnp.bfloat16)
    scatter(0)
    for index in range(count):
        if index + 1 < count:
            scatter(index + 1)
        for step in range(x_local // 8):
            transform(index, step)
        for start in range(0, pairs, 2):
            along_y(index, start)


def slab_waves(data, x_local, blocks, mesh_sizes, per_owner):
    devices = data.shape[0]
    count = data.shape[1] // (2 * per_owner)
    fine = angles(128, 128, 128)
    order = owner_order(mesh_sizes)
    fine = fine.reshape(devices, 128 // devices, 128)[order].reshape(128, 128)
    table = complex_table(np.cos(fine), np.sin(fine))
    twist_angle = angles(blocks, 128, blocks * 128)
    twist = np.stack([np.cos(twist_angle), np.sin(twist_angle)]).astype(np.float32)
    entries = devices * per_owner
    rows = blocks * x_local * 2
    made = pl.pallas_call(
        functools.partial(slab_kernel, count, x_local, blocks, per_owner),
        out_shape=pltpu.VMEM((count * rows, 128), jnp.float32),
        in_specs=[pl.BlockSpec(memory_space=pltpu.VMEM)] * 3,
        out_specs=pl.BlockSpec(memory_space=pltpu.VMEM),
        scratch_shapes=[
            pltpu.VMEM((blocks * x_local, entries), jnp.bfloat16),
            pltpu.VMEM((count, 2, blocks * x_local, 128), jnp.float32),
            pltpu.VMEM((2, blocks * x_local, 256), jnp.float32),
        ],
        compiler_params=params(40),
        cost_estimate=cost(
            count * blocks * x_local * (entries * 1024 + 512 * 1024),
            count * (entries * 1024 + rows * 512),
        ),
    )(jnp.asarray(table), jnp.asarray(twist), in_vmem(data))
    return made.reshape(devices, count * rows // devices, 128)


def rotated(pieces, selector):
    count = len(pieces)
    step = 1
    while step < count:
        taken = (selector & step) != 0
        pieces = [
            jnp.where(taken, pieces[(j + step) % count], pieces[j]) for j in range(count)
        ]
        step *= 2
    return pieces


def x_first(sizes, comp, step, twist, data, turned):
    devices, x_local, y_local, blocks, order = sizes
    pairs = blocks * x_local // 128
    kept = y_local // blocks
    at = pl.multiple_of(step * (data.shape[1] // kept), 2 * pairs) + comp * 2 * pairs
    values = [
        tuple(data[order.index(o), pl.ds(at + r * pairs, pairs), :] for r in range(2))
        for o in range(devices)
    ]
    waves = flat_fft(values, times_pair)
    rows = pl.ds(pl.multiple_of(step * pairs, pairs), pairs)
    for k in range(devices):
        real, imag = waves[k]
        cos_k, sin_k = twist[0, k : k + 1, :], twist[1, k : k + 1, :]
        turned[comp % 2, k, rows, :128] = real * cos_k + imag * sin_k
        turned[comp % 2, k, rows, 128:] = imag * cos_k - real * sin_k


def x_second(sizes, comp, step, together, stacked, turned, columns):
    devices, x_local, y_local, blocks, _ = sizes
    group = 128 // x_local
    narrow = (y_local // blocks) * (blocks // group)
    banks = 2 * group
    lane = lax.broadcasted_iota(jnp.int32, (1, 128), 1)
    start = step * together
    rows = turned[comp % 2, pl.ds(start, together)].reshape(together * narrow, 256)
    moved = dot_rows_split(stacked, rows)
    if square(sizes):
        for base in range(0, together, banks):
            rolled = []
            for bank in range(banks):
                one = moved[bank * x_local : (bank + 1) * x_local, base * narrow :][:, :128]
                rolled.append(pltpu.roll(one, bank * narrow, 1) if bank else one)
            made = rotated(rolled, lane >> (narrow.bit_length() - 1))
            for k in range(banks):
                rows = pl.ds(start + base + k, x_local, stride=devices)
                columns[comp, rows, :] = made[-k % banks]
        return
    for k in range(together):
        one = jnp.concatenate(
            [
                moved[bank * x_local : (bank + 1) * x_local, k * narrow : (k + 1) * narrow]
                for bank in range(banks)
            ],
            axis=1,
        )
        columns[comp, pl.ds(start + k, x_local, stride=devices), :] = one


def square(sizes):
    _, x_local, y_local, blocks, _ = sizes
    group = 128 // x_local
    narrow = (y_local // blocks) * (blocks // group)
    return 2 * group * narrow == 128 and 128 // narrow == 2 * group


def x_third(sizes, comp, start, columns, kept):
    _, x_local, y_local, blocks, _ = sizes
    group = 128 // x_local
    pairs = blocks // group
    steps = y_local // blocks
    narrow = steps * pairs
    banks = 2 * group
    lane = lax.broadcasted_iota(jnp.int32, (1, 128), 1)
    block = columns[comp, start : start + 128, :].T
    pieces = [block[bank * narrow : (bank + 1) * narrow] for bank in range(banks)]
    if square(sizes):
        pieces = rotated(pieces, lane & (banks - 1))
    for bank, one in enumerate(pieces):
        for step in range(steps):
            row = step * blocks + (bank % group) * pairs
            kept[comp, bank // group, row : row + pairs, start : start + 128] = one[
                step * pairs : (step + 1) * pairs
            ]


def mix_rows(rows, columns, tensor, waves):
    sums = [None] * 3
    for row in range(3):
        for col in range(3):
            entry = pair_index[row][col]
            green_real, green_imag = tensor[0, entry, rows, columns], tensor[1, entry, rows, columns]
            real, imag = waves[col, 0, rows, columns], waves[col, 1, rows, columns]
            real_term = green_real * real - green_imag * imag
            imag_term = green_real * imag + green_imag * real
            old = sums[row]
            sums[row] = (
                (real_term, imag_term) if old is None else (old[0] + real_term, old[1] + imag_term)
            )
    return sums


def field_kernel(sizes, twist, table, data, green, out, *scratch):
    y_local, x_cells = green.shape[2:]
    turned, columns, tensor, kept, made, in_sem, out_sems = scratch
    width = x_cells // made.shape[0]
    fetch = pltpu.make_async_copy(green, tensor, in_sem)
    fetch.start()
    stacked = stacked_halves(table)
    devices, x_local, _, blocks, _ = sizes
    steps = y_local // blocks
    narrow = y_local * x_local // 128
    together = min(devices, 256 // narrow)
    groups = devices // together
    blocks_each = x_cells // 128 // groups
    for comp in range(3):
        unroll = 2 if steps % 2 == 0 else 1
        pl.loop(0, steps, unroll=unroll)(lambda i: x_first(sizes, comp, i, twist, data, turned))
        for i in range(groups):
            x_second(sizes, comp, i, together, stacked, turned, columns)
            for block in range(i * blocks_each, (i + 1) * blocks_each):
                if comp > 0:
                    x_third(sizes, comp - 1, block * 128, columns, kept)
    fetch.wait()
    pieces = made.shape[0]

    def turn(piece):
        for start in range(piece * width, (piece + 1) * width, 128):
            x_third(sizes, 2, start, columns, kept)

    sends = []
    turn(0)
    for piece in range(pieces):
        if piece + 1 < pieces:
            turn(piece + 1)
        part = pl.ds(piece * width, width)
        for step in range(y_local // 8):
            rows = pl.ds(step * 8, 8)
            for row, pair in enumerate(mix_rows(rows, part, tensor, kept)):
                for r in range(2):
                    made[piece, r, row, rows, :] = pair[r]
        send = pltpu.make_async_copy(made.at[piece], out.at[:, :, :, part], out_sems.at[piece])
        send.start()
        sends.append(send)
    for send in sends:
        send.wait()


def x_tables(devices, x_local, y_cells):
    x_cells = devices * x_local
    group = 128 // x_local
    fine = angles(x_local, x_local, x_local)
    scale = 1.0 / math.sqrt(x_cells * y_cells)
    apart = np.eye(group) * scale
    table = complex_table(np.kron(apart, np.cos(fine)), np.kron(apart, np.sin(fine)))
    angle = np.tile(angles(devices, x_local, x_cells), (1, group))
    twist = np.stack([np.cos(angle), np.sin(angle)]).astype(np.float32)
    return jnp.asarray(twist), jnp.asarray(table)


def x_scratch(devices, x_local, y_local):
    return [
        pltpu.VMEM((2, devices, y_local * x_local // 128, 256), jnp.float32),
        pltpu.VMEM((3, devices * x_local, 2 * y_local), jnp.float32),
    ]


def field(data, green, devices, x_local, y_local, y_cells, mesh_sizes):
    x_cells = devices * x_local
    pieces = 8
    sizes = (devices, x_local, y_local, y_cells // 128, owner_order(mesh_sizes))
    plane = (y_local, x_cells)
    return pl.pallas_call(
        functools.partial(field_kernel, sizes),
        out_shape=pltpu.HBM((2, 3) + plane, jnp.float32),
        in_specs=[pl.BlockSpec(memory_space=pltpu.VMEM)] * 3
        + [pl.BlockSpec(memory_space=pltpu.HBM)],
        out_specs=pl.BlockSpec(memory_space=pltpu.HBM),
        scratch_shapes=x_scratch(devices, x_local, y_local)
        + [
            pltpu.VMEM((2, 6) + plane, jnp.float32),
            pltpu.VMEM((3, 2) + plane, jnp.float32),
            pltpu.VMEM((pieces, 2, 3, y_local, x_cells // pieces), jnp.float32),
            pltpu.SemaphoreType.DMA(()),
            pltpu.SemaphoreType.DMA((pieces,)),
        ],
        compiler_params=params(40),
        cost_estimate=cost(3 * x_cells * y_local * (x_local * 24 + 24), x_cells * y_local * 96),
    )(*x_tables(devices, x_local, y_cells), in_vmem(data), in_hbm(green))


places = ("gl", "gx", "gz")


def exchange(data):
    return lax.all_to_all(data, places, split_axis=0, concat_axis=0, tiled=True)


def per_device(tiles, tile_owner, tile_slot, tile_count, green):
    count_gl = lax.axis_size("gl")
    mesh_sizes = (lax.axis_size("gx"), count_gl)
    devices = 4 * mesh_sizes[0] * count_gl
    tile_total, tile_len = tiles.shape[2], tiles.shape[3]
    planes, y_local, x_cells = green.shape[2:]
    y_cells = y_local * devices
    x_local = x_cells // devices
    blocks = y_cells // tile_len
    per_owner = max(2, 2 * tile_total // devices)
    assert planes == 1 and tile_len == 128
    owner_row, slot_row = tile_owner.reshape(1, tile_total), tile_slot.reshape(1, tile_total)
    green = green.reshape(2, 6, y_local, x_cells)
    me = lax.axis_index(places).reshape(1).astype(jnp.int32)
    lists = (owner_row, slot_row, tile_count, me)
    arrived = exchange(pack(tiles, *lists, devices, mesh_sizes, per_owner))
    moved = exchange(slab_waves(arrived, x_local, blocks, mesh_sizes, per_owner))
    mixed = field(moved, green, devices, x_local, y_local, y_cells, mesh_sizes)
    return mixed.reshape(2, 3, planes, y_local, x_cells)


def solution(mesh):
    count_gx, count_gy = mesh.devices.shape
    fine_mesh = jax.sharding.Mesh(
        mesh.devices.reshape(count_gx, 4, count_gy // 4), ("gx", "gz", "gl")
    )
    every = ("gx", "gz", "gl")
    in_specs = (
        P(None, None, every, None),
        P(every, None),
        P(every),
        P(every),
        P(None, None, None, every, None),
    )
    out_specs = P(None, None, None, every, None)
    return jax.shard_map(
        per_device, mesh=fine_mesh, in_specs=in_specs, out_specs=out_specs, check_vma=False
    )
```

```python
import functools
import math

import jax
import jax.numpy as jnp
import numpy as np
from jax import lax
from jax.experimental import pallas as pl
from jax.experimental.pallas import tpu as pltpu
from jax.sharding import PartitionSpec as P

pair_index = ((0, 3, 4), (3, 1, 5), (4, 5, 2))
by_rows = (((1,), (1,)), ((), ()))


def params(mebibytes):
    return pltpu.CompilerParams(vmem_limit_bytes=mebibytes * 1024 * 1024)


def in_hbm(array):
    return pltpu.with_memory_space_constraint(array, pltpu.HBM)


def in_vmem(array):
    return pltpu.with_memory_space_constraint(array, pltpu.VMEM)


def cost(flops, moved):
    return pl.CostEstimate(flops=flops, bytes_accessed=moved, transcendentals=0)


def angles(rows, columns, length):
    products = np.outer(np.arange(rows), np.arange(columns)) % length
    return 2.0 * math.pi / length * products


def split_two(data):
    high = data.astype(jnp.bfloat16)
    return high, (data - high.astype(jnp.float32)).astype(jnp.bfloat16)


def dot_rows(left, right):
    return lax.dot_general(left, right, by_rows, preferred_element_type=jnp.float32)


def dot_rows_split(stacked, data):
    rows = stacked.shape[0] // 2
    high, low = split_two(data)
    both = dot_rows(stacked, high)
    return both[:rows] + both[rows:] + dot_rows(stacked[:rows], low)


def stacked_halves(table):
    return jnp.concatenate(split_two(table[...]))


def flat_fft(values, times):
    length = len(values)
    if length == 1:
        return values
    even = flat_fft(values[0::2], times)
    odd = flat_fft(values[1::2], times)
    lower, upper = [], []
    for k in range(length // 2):
        turned = times(odd[k], k, length)
        lower.append(jax.tree.map(lambda a, b: a + b, even[k], turned))
        upper.append(jax.tree.map(lambda a, b: a - b, even[k], turned))
    return lower + upper


def times_pair(value, k, length):
    real, imag = value
    if k == 0:
        return value
    if 4 * k == length:
        return (imag, -real)
    cos_k = math.cos(2.0 * math.pi * k / length)
    sin_k = math.sin(2.0 * math.pi * k / length)
    return (real * cos_k + imag * sin_k, imag * cos_k - real * sin_k)


def place_of(owner, sizes):
    count_gx, count_gl = sizes
    shift = count_gl.bit_length() - 1
    z = (owner >> shift) & 3
    return ((owner & (count_gl - 1)) * count_gx + (owner >> (shift + 2))) * 4 + z


def owner_order(sizes):
    devices = 4 * sizes[0] * sizes[1]
    order = [0] * devices
    for owner in range(devices):
        order[place_of(owner, sizes)] = owner
    return order


def pack_kernel(
    devices, mesh_sizes, per_owner, count, me, owner_row, slot_row, tiles, out, *scratch
):
    held, lists, sems = scratch
    comps = range(tiles.shape[1])
    listed = owner_row.shape[1]
    fetches = [
        pltpu.make_async_copy(owner_row, lists.at[0], sems.at[0]),
        pltpu.make_async_copy(slot_row, lists.at[1], sems.at[1]),
    ]
    fetches += [
        pltpu.make_async_copy(tiles.at[:, comp], held.at[i], sems.at[2 + i])
        for i, comp in enumerate(comps)
    ]
    for fetch in fetches:
        fetch.start()
    sender = lax.broadcasted_iota(jnp.int32, (listed, listed), 0)
    reader = lax.broadcasted_iota(jnp.int32, (listed, listed), 1)
    before = jnp.where(sender < reader, 1.0, 0.0).astype(jnp.bfloat16)
    live = lax.broadcasted_iota(jnp.int32, (1, listed), 1) < count[0]
    fetches[0].wait()
    place = jnp.where(live, place_of(lists[0], mesh_sizes), -1)
    place_at = lax.broadcasted_iota(jnp.int32, (devices, listed), 0)
    named = jnp.where(place_at == place, 1.0, 0.0)
    counted = jnp.dot(named.astype(jnp.bfloat16), before, preferred_element_type=jnp.float32)
    rank = jnp.sum(counted * named, axis=0, keepdims=True).astype(jnp.int32)
    target = jnp.where(live, place * per_owner + rank, -1)
    target_at = lax.broadcasted_iota(jnp.int32, (devices * per_owner, listed), 0)
    chosen = jnp.where(target_at == target, 1.0, 0.0).astype(jnp.bfloat16)
    fetches[1].wait()
    stated = lists[1] + 1
    lane = rank + (me[0] & (128 // per_owner - 1)) * per_owner
    lane_at = lax.broadcasted_iota(jnp.int32, (128, listed), 0)
    laned = jnp.where(lane_at == lane, 1.0, 0.0).astype(jnp.bfloat16)
    coarse = (named * (stated >> 5).astype(jnp.float32)).astype(jnp.bfloat16)
    fine = (named * (stated & 31).astype(jnp.float32)).astype(jnp.bfloat16)
    slots = 32.0 * dot_rows(coarse, laned) + dot_rows(fine, laned)
    out[:, out.shape[1] - 1] = jnp.broadcast_to(slots[:, None, :], (devices, 4, 128))
    for i in range(len(comps)):
        fetches[2 + i].wait()
        parts = [part for r in range(2) for part in split_two(held[i, r])]
        got = jnp.dot(
            chosen, jnp.concatenate(parts, axis=1), preferred_element_type=jnp.float32
        )
        for r in range(2):
            whole = got[:, 256 * r : 256 * r + 128] + got[:, 256 * r + 128 : 256 * r + 256]
            start = (2 * i + r) * per_owner // 4
            out[:, start : start + per_owner // 4] = whole.reshape(
                devices, per_owner // 4, 4, 128
            )


def pack(tiles, owner_row, slot_row, count, me, devices, mesh_sizes, per_owner):
    comps, listed = tiles.shape[1:3]
    rows = 2 * comps * per_owner + 4
    return pl.pallas_call(
        functools.partial(pack_kernel, devices, mesh_sizes, per_owner),
        out_shape=pltpu.VMEM((devices, rows // 4, 4, 128), jnp.float32),
        in_specs=[pl.BlockSpec(memory_space=pltpu.SMEM)] * 2
        + [pl.BlockSpec(memory_space=pltpu.HBM)] * 3,
        out_specs=pl.BlockSpec(memory_space=pltpu.VMEM),
        scratch_shapes=[
            pltpu.VMEM((comps, 2, listed, 128), jnp.float32),
            pltpu.VMEM((2, 1, listed), jnp.int32),
            pltpu.SemaphoreType.DMA((2 + comps,)),
        ],
        compiler_params=params(24),
        cost_estimate=cost(
            devices * per_owner * listed * 512 * 2 * comps, devices * rows * 1024
        ),
    )(count, me, *[in_hbm(a) for a in (owner_row, slot_row, tiles)])


def complex_table(cos_part, sin_part):
    return np.concatenate(
        [
            np.concatenate([cos_part, sin_part], axis=1),
            np.concatenate([-sin_part, cos_part], axis=1),
        ]
    ).astype(np.float32)


def slab_kernel(count, x_local, blocks, per_owner, table, twist, data, out, *scratch):
    chosen, slab, turned = scratch
    devices = data.shape[0]
    entries = devices * per_owner
    group = 128 // x_local
    pairs = blocks // group
    shift = blocks.bit_length() - 1
    every = 128 // per_owner
    stated = [
        sum([data[o, data.shape[1] - 1, :1] for o in range(start, start + every)])
        for start in range(0, devices, every)
    ]
    slot = jnp.concatenate(stated, axis=1).astype(jnp.int32) - 1
    landing = jnp.where(slot >= 0, (slot & (blocks - 1)) * x_local + (slot >> shift), -1)
    slab_rows = blocks * x_local
    stacked = stacked_halves(table)

    def scatter(index):
        parts = []
        for r in range(2):
            start = (2 * index + r) * per_owner // 4
            one = data[:, start : start + per_owner // 4]
            parts.extend(split_two(one.reshape(entries, 128)))
        got = jnp.dot(
            chosen[...], jnp.concatenate(parts, axis=1), preferred_element_type=jnp.float32
        )
        for r in range(2):
            slab[index, r] = (
                got[:, 256 * r : 256 * r + 128] + got[:, 256 * r + 128 : 256 * r + 256]
            )

    def transform(index, step):
        at = step * 8
        values = [
            tuple(slab[index, r, pl.ds(t * x_local + at, 8), :] for r in range(2))
            for t in range(blocks)
        ]
        waves = flat_fft(values, times_pair)
        for k in range(blocks):
            real, imag = waves[k]
            cos_k, sin_k = twist[0, k : k + 1, :], twist[1, k : k + 1, :]
            rows = pl.ds(((k % pairs) * group + k // pairs) * x_local + at, 8)
            turned[index % 2, rows, :128] = real * cos_k + imag * sin_k
            turned[index % 2, rows, 128:] = imag * cos_k - real * sin_k

    def along_y(index, start):
        moved = dot_rows_split(stacked, turned[index % 2, start * 128 : (start + 2) * 128, :])
        for k in range(2):
            for r in range(2):
                one = moved[r * 128 : (r + 1) * 128, k * 128 : (k + 1) * 128]
                base = (index * 2 + r) * pairs + start + k
                out[pl.ds(base, 128, stride=count * 2 * pairs), :] = one

    place = lax.broadcasted_iota(jnp.int32, (slab_rows, entries), 0)
    chosen[...] = jnp.where(place == landing, 1.0, 0.0).astype(jnp.bfloat16)
    scatter(0)
    for index in range(count):
        if index + 1 < count:
            scatter(index + 1)
        for step in range(x_local // 8):
            transform(index, step)
        for start in range(0, pairs, 2):
            along_y(index, start)


def slab_waves(data, x_local, blocks, mesh_sizes, per_owner):
    devices = data.shape[0]
    count = data.shape[1] * 4 // (2 * per_owner)
    fine = angles(128, 128, 128)
    order = owner_order(mesh_sizes)
    fine = fine.reshape(devices, 128 // devices, 128)[order].reshape(128, 128)
    table = complex_table(np.cos(fine), np.sin(fine))
    twist_angle = angles(blocks, 128, blocks * 128)
    twist = np.stack([np.cos(twist_angle), np.sin(twist_angle)]).astype(np.float32)
    entries = devices * per_owner
    rows = blocks * x_local * 2
    made = pl.pallas_call(
        functools.partial(slab_kernel, count, x_local, blocks, per_owner),
        out_shape=pltpu.VMEM((count * rows, 128), jnp.float32),
        in_specs=[pl.BlockSpec(memory_space=pltpu.VMEM)] * 3,
        out_specs=pl.BlockSpec(memory_space=pltpu.VMEM),
        scratch_shapes=[
            pltpu.VMEM((blocks * x_local, entries), jnp.bfloat16),
            pltpu.VMEM((count, 2, blocks * x_local, 128), jnp.float32),
            pltpu.VMEM((2, blocks * x_local, 256), jnp.float32),
        ],
        compiler_params=params(40),
        cost_estimate=cost(
            count * blocks * x_local * (entries * 1024 + 512 * 1024),
            count * (entries * 1024 + rows * 512),
        ),
    )(jnp.asarray(table), jnp.asarray(twist), in_vmem(data))
    return made.reshape(devices, count * rows // devices, 128)


def rotated(pieces, selector):
    count = len(pieces)
    step = 1
    while step < count:
        taken = (selector & step) != 0
        pieces = [
            jnp.where(taken, pieces[(j + step) % count], pieces[j]) for j in range(count)
        ]
        step *= 2
    return pieces


def x_first(sizes, comp, step, twist, data, turned):
    devices, x_local, y_local, blocks, order = sizes
    pairs = blocks * x_local // 128
    kept = y_local // blocks
    at = pl.multiple_of(step * (data.shape[1] // kept), 2 * pairs) + comp * 2 * pairs
    values = [
        tuple(data[order.index(o), pl.ds(at + r * pairs, pairs), :] for r in range(2))
        for o in range(devices)
    ]
    waves = flat_fft(values, times_pair)
    rows = pl.ds(pl.multiple_of(step * pairs, pairs), pairs)
    for k in range(devices):
        real, imag = waves[k]
        cos_k, sin_k = twist[0, k : k + 1, :], twist[1, k : k + 1, :]
        turned[comp % 2, k, rows, :128] = real * cos_k + imag * sin_k
        turned[comp % 2, k, rows, 128:] = imag * cos_k - real * sin_k


def x_second(sizes, comp, step, together, stacked, turned, columns):
    devices, x_local, y_local, blocks, _ = sizes
    group = 128 // x_local
    narrow = (y_local // blocks) * (blocks // group)
    banks = 2 * group
    lane = lax.broadcasted_iota(jnp.int32, (1, 128), 1)
    start = step * together
    rows = turned[comp % 2, pl.ds(start, together)].reshape(together * narrow, 256)
    moved = dot_rows_split(stacked, rows)
    if square(sizes):
        for base in range(0, together, banks):
            rolled = []
            for bank in range(banks):
                one = moved[bank * x_local : (bank + 1) * x_local, base * narrow :][:, :128]
                rolled.append(pltpu.roll(one, bank * narrow, 1) if bank else one)
            made = rotated(rolled, lane >> (narrow.bit_length() - 1))
            for k in range(banks):
                rows = pl.ds(start + base + k, x_local, stride=devices)
                columns[comp, rows, :] = made[-k % banks]
        return
    for k in range(together):
        one = jnp.concatenate(
            [
                moved[bank * x_local : (bank + 1) * x_local, k * narrow : (k + 1) * narrow]
                for bank in range(banks)
            ],
            axis=1,
        )
        columns[comp, pl.ds(start + k, x_local, stride=devices), :] = one


def square(sizes):
    _, x_local, y_local, blocks, _ = sizes
    group = 128 // x_local
    narrow = (y_local // blocks) * (blocks // group)
    return 2 * group * narrow == 128 and 128 // narrow == 2 * group


def x_third(sizes, comp, start, columns, kept):
    _, x_local, y_local, blocks, _ = sizes
    group = 128 // x_local
    pairs = blocks // group
    steps = y_local // blocks
    narrow = steps * pairs
    banks = 2 * group
    lane = lax.broadcasted_iota(jnp.int32, (1, 128), 1)
    block = columns[comp, start : start + 128, :].T
    pieces = [block[bank * narrow : (bank + 1) * narrow] for bank in range(banks)]
    if square(sizes):
        pieces = rotated(pieces, lane & (banks - 1))
    for bank, one in enumerate(pieces):
        for step in range(steps):
            row = step * blocks + (bank % group) * pairs
            kept[comp, bank // group, row : row + pairs, start : start + 128] = one[
                step * pairs : (step + 1) * pairs
            ]


def mix_rows(rows, columns, tensor, waves):
    sums = [None] * 3
    for row in range(3):
        for col in range(3):
            entry = pair_index[row][col]
            green_real, green_imag = tensor[0, entry, rows, columns], tensor[1, entry, rows, columns]
            real, imag = waves[col, 0, rows, columns], waves[col, 1, rows, columns]
            real_term = green_real * real - green_imag * imag
            imag_term = green_real * imag + green_imag * real
            old = sums[row]
            sums[row] = (
                (real_term, imag_term) if old is None else (old[0] + real_term, old[1] + imag_term)
            )
    return sums


def field_kernel(sizes, twist, table, data, green, out, *scratch):
    y_local, x_cells = green.shape[2:]
    turned, columns, tensor, kept, made, in_sem, out_sems = scratch
    width = x_cells // made.shape[0]
    fetch = pltpu.make_async_copy(green, tensor, in_sem)
    fetch.start()
    stacked = stacked_halves(table)
    devices, x_local, _, blocks, _ = sizes
    steps = y_local // blocks
    narrow = y_local * x_local // 128
    together = min(devices, 256 // narrow)
    groups = devices // together
    blocks_each = x_cells // 128 // groups
    for comp in range(3):
        unroll = 2 if steps % 2 == 0 else 1
        pl.loop(0, steps, unroll=unroll)(lambda i: x_first(sizes, comp, i, twist, data, turned))
        for i in range(groups):
            x_second(sizes, comp, i, together, stacked, turned, columns)
            for block in range(i * blocks_each, (i + 1) * blocks_each):
                if comp > 0:
                    x_third(sizes, comp - 1, block * 128, columns, kept)
    fetch.wait()
    pieces = made.shape[0]

    def turn(piece):
        for start in range(piece * width, (piece + 1) * width, 128):
            x_third(sizes, 2, start, columns, kept)

    sends = []
    turn(0)
    for piece in range(pieces):
        if piece + 1 < pieces:
            turn(piece + 1)
        part = pl.ds(piece * width, width)
        for step in range(y_local // 8):
            rows = pl.ds(step * 8, 8)
            for row, pair in enumerate(mix_rows(rows, part, tensor, kept)):
                for r in range(2):
                    made[piece, r, row, rows, :] = pair[r]
        send = pltpu.make_async_copy(made.at[piece], out.at[:, :, :, part], out_sems.at[piece])
        send.start()
        sends.append(send)
    for send in sends:
        send.wait()


def x_tables(devices, x_local, y_cells):
    x_cells = devices * x_local
    group = 128 // x_local
    fine = angles(x_local, x_local, x_local)
    scale = 1.0 / math.sqrt(x_cells * y_cells)
    apart = np.eye(group) * scale
    table = complex_table(np.kron(apart, np.cos(fine)), np.kron(apart, np.sin(fine)))
    angle = np.tile(angles(devices, x_local, x_cells), (1, group))
    twist = np.stack([np.cos(angle), np.sin(angle)]).astype(np.float32)
    return jnp.asarray(twist), jnp.asarray(table)


def x_scratch(devices, x_local, y_local):
    return [
        pltpu.VMEM((2, devices, y_local * x_local // 128, 256), jnp.float32),
        pltpu.VMEM((3, devices * x_local, 2 * y_local), jnp.float32),
    ]


def field(data, green, devices, x_local, y_local, y_cells, mesh_sizes):
    x_cells = devices * x_local
    pieces = 8
    sizes = (devices, x_local, y_local, y_cells // 128, owner_order(mesh_sizes))
    plane = (y_local, x_cells)
    return pl.pallas_call(
        functools.partial(field_kernel, sizes),
        out_shape=pltpu.HBM((2, 3) + plane, jnp.float32),
        in_specs=[pl.BlockSpec(memory_space=pltpu.VMEM)] * 3
        + [pl.BlockSpec(memory_space=pltpu.HBM)],
        out_specs=pl.BlockSpec(memory_space=pltpu.HBM),
        scratch_shapes=x_scratch(devices, x_local, y_local)
        + [
            pltpu.VMEM((2, 6) + plane, jnp.float32),
            pltpu.VMEM((3, 2) + plane, jnp.float32),
            pltpu.VMEM((pieces, 2, 3, y_local, x_cells // pieces), jnp.float32),
            pltpu.SemaphoreType.DMA(()),
            pltpu.SemaphoreType.DMA((pieces,)),
        ],
        compiler_params=params(40),
        cost_estimate=cost(3 * x_cells * y_local * (x_local * 24 + 24), x_cells * y_local * 96),
    )(*x_tables(devices, x_local, y_cells), in_vmem(data), in_hbm(green))


places = ("gl", "gx", "gz")


def exchange(data):
    return lax.all_to_all(data, places, split_axis=0, concat_axis=0, tiled=True)


def per_device(tiles, tile_owner, tile_slot, tile_count, green):
    count_gl = lax.axis_size("gl")
    mesh_sizes = (lax.axis_size("gx"), count_gl)
    devices = 4 * mesh_sizes[0] * count_gl
    tile_total, tile_len = tiles.shape[2], tiles.shape[3]
    planes, y_local, x_cells = green.shape[2:]
    y_cells = y_local * devices
    x_local = x_cells // devices
    blocks = y_cells // tile_len
    per_owner = max(2, 2 * tile_total // devices)
    assert planes == 1 and tile_len == 128
    owner_row, slot_row = tile_owner.reshape(1, tile_total), tile_slot.reshape(1, tile_total)
    green = green.reshape(2, 6, y_local, x_cells)
    me = lax.axis_index(places).reshape(1).astype(jnp.int32)
    lists = (owner_row, slot_row, tile_count, me)
    arrived = exchange(pack(tiles, *lists, devices, mesh_sizes, per_owner))
    moved = exchange(slab_waves(arrived, x_local, blocks, mesh_sizes, per_owner))
    mixed = field(moved, green, devices, x_local, y_local, y_cells, mesh_sizes)
    return mixed.reshape(2, 3, planes, y_local, x_cells)


def solution(mesh):
    count_gx, count_gy = mesh.devices.shape
    fine_mesh = jax.sharding.Mesh(
        mesh.devices.reshape(count_gx, 4, count_gy // 4), ("gx", "gz", "gl")
    )
    every = ("gx", "gz", "gl")
    in_specs = (
        P(None, None, every, None),
        P(every, None),
        P(every),
        P(every),
        P(None, None, None, every, None),
    )
    out_specs = P(None, None, None, every, None)
    return jax.shard_map(
        per_device, mesh=fine_mesh, in_specs=in_specs, out_specs=out_specs, check_vma=False
    )
```

```python
import functools
import math

import jax
import jax.numpy as jnp
import numpy as np
from jax import lax
from jax.experimental import pallas as pl
from jax.experimental.pallas import tpu as pltpu
from jax.sharding import PartitionSpec as P

pair_index = ((0, 3, 4), (3, 1, 5), (4, 5, 2))
by_rows = (((1,), (1,)), ((), ()))


def params(mebibytes):
    return pltpu.CompilerParams(vmem_limit_bytes=mebibytes * 1024 * 1024)


def in_hbm(array):
    return pltpu.with_memory_space_constraint(array, pltpu.HBM)


def in_vmem(array):
    return pltpu.with_memory_space_constraint(array, pltpu.VMEM)


def cost(flops, moved):
    return pl.CostEstimate(flops=flops, bytes_accessed=moved, transcendentals=0)


def angles(rows, columns, length):
    products = np.outer(np.arange(rows), np.arange(columns)) % length
    return 2.0 * math.pi / length * products


def split_two(data):
    high = data.astype(jnp.bfloat16)
    return high, (data - high.astype(jnp.float32)).astype(jnp.bfloat16)


def dot_rows(left, right):
    return lax.dot_general(left, right, by_rows, preferred_element_type=jnp.float32)


def dot_rows_split(stacked, data):
    rows = stacked.shape[0] // 2
    high, low = split_two(data)
    both = dot_rows(stacked, high)
    return both[:rows] + both[rows:] + dot_rows(stacked[:rows], low)


def stacked_halves(table):
    return jnp.concatenate(split_two(table[...]))


def flat_fft(values, times):
    length = len(values)
    if length == 1:
        return values
    even = flat_fft(values[0::2], times)
    odd = flat_fft(values[1::2], times)
    lower, upper = [], []
    for k in range(length // 2):
        turned = times(odd[k], k, length)
        lower.append(jax.tree.map(lambda a, b: a + b, even[k], turned))
        upper.append(jax.tree.map(lambda a, b: a - b, even[k], turned))
    return lower + upper


def times_pair(value, k, length):
    real, imag = value
    if k == 0:
        return value
    if 4 * k == length:
        return (imag, -real)
    cos_k = math.cos(2.0 * math.pi * k / length)
    sin_k = math.sin(2.0 * math.pi * k / length)
    return (real * cos_k + imag * sin_k, imag * cos_k - real * sin_k)


def place_of(owner, sizes):
    count_gx, count_gl = sizes
    shift = count_gl.bit_length() - 1
    z = (owner >> shift) & 3
    return ((owner & (count_gl - 1)) * count_gx + (owner >> (shift + 2))) * 4 + z


def owner_order(sizes):
    devices = 4 * sizes[0] * sizes[1]
    order = [0] * devices
    for owner in range(devices):
        order[place_of(owner, sizes)] = owner
    return order


def pack_kernel(
    devices, mesh_sizes, per_owner, count, me, owner_row, slot_row, tiles, out, *scratch
):
    held, lists, sems = scratch
    comps = range(tiles.shape[1])
    listed = owner_row.shape[1]
    fetches = [
        pltpu.make_async_copy(owner_row, lists.at[0], sems.at[0]),
        pltpu.make_async_copy(slot_row, lists.at[1], sems.at[1]),
    ]
    fetches += [
        pltpu.make_async_copy(tiles.at[:, comp], held.at[i], sems.at[2 + i])
        for i, comp in enumerate(comps)
    ]
    for fetch in fetches:
        fetch.start()
    sender = lax.broadcasted_iota(jnp.int32, (listed, listed), 0)
    reader = lax.broadcasted_iota(jnp.int32, (listed, listed), 1)
    before = jnp.where(sender < reader, 1.0, 0.0).astype(jnp.bfloat16)
    live = lax.broadcasted_iota(jnp.int32, (1, listed), 1) < count[0]
    fetches[0].wait()
    place = jnp.where(live, place_of(lists[0], mesh_sizes), -1)
    place_at = lax.broadcasted_iota(jnp.int32, (devices, listed), 0)
    named = jnp.where(place_at == place, 1.0, 0.0)
    counted = jnp.dot(named.astype(jnp.bfloat16), before, preferred_element_type=jnp.float32)
    rank = jnp.sum(counted * named, axis=0, keepdims=True).astype(jnp.int32)
    target = jnp.where(live, place * per_owner + rank, -1)
    target_at = lax.broadcasted_iota(jnp.int32, (devices * per_owner, listed), 0)
    chosen = jnp.where(target_at == target, 1.0, 0.0).astype(jnp.bfloat16)
    fetches[1].wait()
    stated = lists[1] + 1
    lane = rank + (me[0] & (128 // per_owner - 1)) * per_owner
    lane_at = lax.broadcasted_iota(jnp.int32, (128, listed), 0)
    laned = jnp.where(lane_at == lane, 1.0, 0.0).astype(jnp.bfloat16)
    coarse = (named * (stated >> 5).astype(jnp.float32)).astype(jnp.bfloat16)
    fine = (named * (stated & 31).astype(jnp.float32)).astype(jnp.bfloat16)
    slots = 32.0 * dot_rows(coarse, laned) + dot_rows(fine, laned)
    out[:, out.shape[1] - 1] = jnp.broadcast_to(slots[:, None, :], (devices, 2, 128))
    for i in range(len(comps)):
        fetches[2 + i].wait()
        parts = [part for r in range(2) for part in split_two(held[i, r])]
        got = jnp.dot(
            chosen, jnp.concatenate(parts, axis=1), preferred_element_type=jnp.float32
        )
        for r in range(2):
            whole = got[:, 256 * r : 256 * r + 128] + got[:, 256 * r + 128 : 256 * r + 256]
            start = (2 * i + r) * per_owner // 2
            out[:, start : start + per_owner // 2] = whole.reshape(
                devices, per_owner // 2, 2, 128
            )


def pack(tiles, owner_row, slot_row, count, me, devices, mesh_sizes, per_owner):
    comps, listed = tiles.shape[1:3]
    rows = 2 * comps * per_owner + 2
    return pl.pallas_call(
        functools.partial(pack_kernel, devices, mesh_sizes, per_owner),
        out_shape=pltpu.VMEM((devices, rows // 2, 2, 128), jnp.float32),
        in_specs=[pl.BlockSpec(memory_space=pltpu.SMEM)] * 2
        + [pl.BlockSpec(memory_space=pltpu.HBM)] * 3,
        out_specs=pl.BlockSpec(memory_space=pltpu.VMEM),
        scratch_shapes=[
            pltpu.VMEM((comps, 2, listed, 128), jnp.float32),
            pltpu.VMEM((2, 1, listed), jnp.int32),
            pltpu.SemaphoreType.DMA((2 + comps,)),
        ],
        compiler_params=params(24),
        cost_estimate=cost(
            devices * per_owner * listed * 512 * 2 * comps, devices * rows * 1024
        ),
    )(count, me, *[in_hbm(a) for a in (owner_row, slot_row, tiles)])


def complex_table(cos_part, sin_part):
    return np.concatenate(
        [
            np.concatenate([cos_part, sin_part], axis=1),
            np.concatenate([-sin_part, cos_part], axis=1),
        ]
    ).astype(np.float32)


def slab_kernel(count, x_local, blocks, per_owner, table, twist, data, out, *scratch):
    chosen, slab, turned = scratch
    devices = data.shape[0]
    entries = devices * per_owner
    group = 128 // x_local
    pairs = blocks // group
    shift = blocks.bit_length() - 1
    every = 128 // per_owner
    stated = [
        sum([data[o, data.shape[1] - 1, :1] for o in range(start, start + every)])
        for start in range(0, devices, every)
    ]
    slot = jnp.concatenate(stated, axis=1).astype(jnp.int32) - 1
    landing = jnp.where(slot >= 0, (slot & (blocks - 1)) * x_local + (slot >> shift), -1)
    slab_rows = blocks * x_local
    stacked = stacked_halves(table)

    def scatter(index):
        parts = []
        for r in range(2):
            start = (2 * index + r) * per_owner // 2
            one = data[:, start : start + per_owner // 2]
            parts.extend(split_two(one.reshape(entries, 128)))
        got = jnp.dot(
            chosen[...], jnp.concatenate(parts, axis=1), preferred_element_type=jnp.float32
        )
        for r in range(2):
            slab[index, r] = (
                got[:, 256 * r : 256 * r + 128] + got[:, 256 * r + 128 : 256 * r + 256]
            )

    def transform(index, step):
        at = step * 8
        values = [
            tuple(slab[index, r, pl.ds(t * x_local + at, 8), :] for r in range(2))
            for t in range(blocks)
        ]
        waves = flat_fft(values, times_pair)
        for k in range(blocks):
            real, imag = waves[k]
            cos_k, sin_k = twist[0, k : k + 1, :], twist[1, k : k + 1, :]
            rows = pl.ds(((k % pairs) * group + k // pairs) * x_local + at, 8)
            turned[index % 2, rows, :128] = real * cos_k + imag * sin_k
            turned[index % 2, rows, 128:] = imag * cos_k - real * sin_k

    def along_y(index, start):
        moved = dot_rows_split(stacked, turned[index % 2, start * 128 : (start + 2) * 128, :])
        for k in range(2):
            for r in range(2):
                one = moved[r * 128 : (r + 1) * 128, k * 128 : (k + 1) * 128]
                base = (index * 2 + r) * pairs + start + k
                out[pl.ds(base, 128, stride=count * 2 * pairs), :] = one

    place = lax.broadcasted_iota(jnp.int32, (slab_rows, entries), 0)
    chosen[...] = jnp.where(place == landing, 1.0, 0.0).astype(jnp.bfloat16)
    scatter(0)
    for index in range(count):
        if index + 1 < count:
            scatter(index + 1)
        for step in range(x_local // 8):
            transform(index, step)
        for start in range(0, pairs, 2):
            along_y(index, start)


def slab_waves(data, x_local, blocks, mesh_sizes, per_owner):
    devices = data.shape[0]
    count = data.shape[1] * 2 // (2 * per_owner)
    fine = angles(128, 128, 128)
    order = owner_order(mesh_sizes)
    fine = fine.reshape(devices, 128 // devices, 128)[order].reshape(128, 128)
    table = complex_table(np.cos(fine), np.sin(fine))
    twist_angle = angles(blocks, 128, blocks * 128)
    twist = np.stack([np.cos(twist_angle), np.sin(twist_angle)]).astype(np.float32)
    entries = devices * per_owner
    rows = blocks * x_local * 2
    made = pl.pallas_call(
        functools.partial(slab_kernel, count, x_local, blocks, per_owner),
        out_shape=pltpu.VMEM((count * rows, 128), jnp.float32),
        in_specs=[pl.BlockSpec(memory_space=pltpu.VMEM)] * 3,
        out_specs=pl.BlockSpec(memory_space=pltpu.VMEM),
        scratch_shapes=[
            pltpu.VMEM((blocks * x_local, entries), jnp.bfloat16),
            pltpu.VMEM((count, 2, blocks * x_local, 128), jnp.float32),
            pltpu.VMEM((2, blocks * x_local, 256), jnp.float32),
        ],
        compiler_params=params(40),
        cost_estimate=cost(
            count * blocks * x_local * (entries * 1024 + 512 * 1024),
            count * (entries * 1024 + rows * 512),
        ),
    )(jnp.asarray(table), jnp.asarray(twist), in_vmem(data))
    return made.reshape(devices, count * rows // devices, 128)


def rotated(pieces, selector):
    count = len(pieces)
    step = 1
    while step < count:
        taken = (selector & step) != 0
        pieces = [
            jnp.where(taken, pieces[(j + step) % count], pieces[j]) for j in range(count)
        ]
        step *= 2
    return pieces


def x_first(sizes, comp, step, twist, data, turned):
    devices, x_local, y_local, blocks, order = sizes
    pairs = blocks * x_local // 128
    kept = y_local // blocks
    at = pl.multiple_of(step * (data.shape[1] // kept), 2 * pairs) + comp * 2 * pairs
    values = [
        tuple(data[order.index(o), pl.ds(at + r * pairs, pairs), :] for r in range(2))
        for o in range(devices)
    ]
    waves = flat_fft(values, times_pair)
    rows = pl.ds(pl.multiple_of(step * pairs, pairs), pairs)
    for k in range(devices):
        real, imag = waves[k]
        cos_k, sin_k = twist[0, k : k + 1, :], twist[1, k : k + 1, :]
        turned[comp % 2, k, rows, :128] = real * cos_k + imag * sin_k
        turned[comp % 2, k, rows, 128:] = imag * cos_k - real * sin_k


def x_second(sizes, comp, step, together, stacked, turned, columns):
    devices, x_local, y_local, blocks, _ = sizes
    group = 128 // x_local
    narrow = (y_local // blocks) * (blocks // group)
    banks = 2 * group
    lane = lax.broadcasted_iota(jnp.int32, (1, 128), 1)
    start = step * together
    rows = turned[comp % 2, pl.ds(start, together)].reshape(together * narrow, 256)
    moved = dot_rows_split(stacked, rows)
    if square(sizes):
        for base in range(0, together, banks):
            rolled = []
            for bank in range(banks):
                one = moved[bank * x_local : (bank + 1) * x_local, base * narrow :][:, :128]
                rolled.append(pltpu.roll(one, bank * narrow, 1) if bank else one)
            made = rotated(rolled, lane >> (narrow.bit_length() - 1))
            for k in range(banks):
                rows = pl.ds(start + base + k, x_local, stride=devices)
                columns[comp, rows, :] = made[-k % banks]
        return
    for k in range(together):
        one = jnp.concatenate(
            [
                moved[bank * x_local : (bank + 1) * x_local, k * narrow : (k + 1) * narrow]
                for bank in range(banks)
            ],
            axis=1,
        )
        columns[comp, pl.ds(start + k, x_local, stride=devices), :] = one


def square(sizes):
    _, x_local, y_local, blocks, _ = sizes
    group = 128 // x_local
    narrow = (y_local // blocks) * (blocks // group)
    return 2 * group * narrow == 128 and 128 // narrow == 2 * group


def x_third(sizes, comp, start, columns, kept):
    _, x_local, y_local, blocks, _ = sizes
    group = 128 // x_local
    pairs = blocks // group
    steps = y_local // blocks
    narrow = steps * pairs
    banks = 2 * group
    lane = lax.broadcasted_iota(jnp.int32, (1, 128), 1)
    block = columns[comp, start : start + 128, :].T
    pieces = [block[bank * narrow : (bank + 1) * narrow] for bank in range(banks)]
    if square(sizes):
        pieces = rotated(pieces, lane & (banks - 1))
    for bank, one in enumerate(pieces):
        for step in range(steps):
            row = step * blocks + (bank % group) * pairs
            kept[comp, bank // group, row : row + pairs, start : start + 128] = one[
                step * pairs : (step + 1) * pairs
            ]


def mix_rows(rows, columns, tensor, waves):
    sums = [None] * 3
    for row in range(3):
        for col in range(3):
            entry = pair_index[row][col]
            green_real, green_imag = tensor[0, entry, rows, columns], tensor[1, entry, rows, columns]
            real, imag = waves[col, 0, rows, columns], waves[col, 1, rows, columns]
            real_term = green_real * real - green_imag * imag
            imag_term = green_real * imag + green_imag * real
            old = sums[row]
            sums[row] = (
                (real_term, imag_term) if old is None else (old[0] + real_term, old[1] + imag_term)
            )
    return sums


def field_kernel(sizes, twist, table, data, green, out, *scratch):
    y_local, x_cells = green.shape[2:]
    turned, columns, tensor, kept, made, in_sem, out_sems = scratch
    width = x_cells // made.shape[0]
    fetch = pltpu.make_async_copy(green, tensor, in_sem)
    fetch.start()
    stacked = stacked_halves(table)
    devices, x_local, _, blocks, _ = sizes
    steps = y_local // blocks
    narrow = y_local * x_local // 128
    together = min(devices, 256 // narrow)
    groups = devices // together
    blocks_each = x_cells // 128 // groups
    for comp in range(3):
        unroll = 2 if steps % 2 == 0 else 1
        pl.loop(0, steps, unroll=unroll)(lambda i: x_first(sizes, comp, i, twist, data, turned))
        for i in range(groups):
            x_second(sizes, comp, i, together, stacked, turned, columns)
            for block in range(i * blocks_each, (i + 1) * blocks_each):
                if comp > 0:
                    x_third(sizes, comp - 1, block * 128, columns, kept)
    fetch.wait()
    pieces = made.shape[0]

    def turn(piece):
        for start in range(piece * width, (piece + 1) * width, 128):
            x_third(sizes, 2, start, columns, kept)

    sends = []
    turn(0)
    for piece in range(pieces):
        if piece + 1 < pieces:
            turn(piece + 1)
        part = pl.ds(piece * width, width)
        for step in range(y_local // 8):
            rows = pl.ds(step * 8, 8)
            for row, pair in enumerate(mix_rows(rows, part, tensor, kept)):
                for r in range(2):
                    made[piece, r, row, rows, :] = pair[r]
        send = pltpu.make_async_copy(made.at[piece], out.at[:, :, :, part], out_sems.at[piece])
        send.start()
        sends.append(send)
    for send in sends:
        send.wait()


def x_tables(devices, x_local, y_cells):
    x_cells = devices * x_local
    group = 128 // x_local
    fine = angles(x_local, x_local, x_local)
    scale = 1.0 / math.sqrt(x_cells * y_cells)
    apart = np.eye(group) * scale
    table = complex_table(np.kron(apart, np.cos(fine)), np.kron(apart, np.sin(fine)))
    angle = np.tile(angles(devices, x_local, x_cells), (1, group))
    twist = np.stack([np.cos(angle), np.sin(angle)]).astype(np.float32)
    return jnp.asarray(twist), jnp.asarray(table)


def x_scratch(devices, x_local, y_local):
    return [
        pltpu.VMEM((2, devices, y_local * x_local // 128, 256), jnp.float32),
        pltpu.VMEM((3, devices * x_local, 2 * y_local), jnp.float32),
    ]


def field(data, green, devices, x_local, y_local, y_cells, mesh_sizes):
    x_cells = devices * x_local
    pieces = 8
    sizes = (devices, x_local, y_local, y_cells // 128, owner_order(mesh_sizes))
    plane = (y_local, x_cells)
    return pl.pallas_call(
        functools.partial(field_kernel, sizes),
        out_shape=pltpu.HBM((2, 3) + plane, jnp.float32),
        in_specs=[pl.BlockSpec(memory_space=pltpu.VMEM)] * 3
        + [pl.BlockSpec(memory_space=pltpu.HBM)],
        out_specs=pl.BlockSpec(memory_space=pltpu.HBM),
        scratch_shapes=x_scratch(devices, x_local, y_local)
        + [
            pltpu.VMEM((2, 6) + plane, jnp.float32),
            pltpu.VMEM((3, 2) + plane, jnp.float32),
            pltpu.VMEM((pieces, 2, 3, y_local, x_cells // pieces), jnp.float32),
            pltpu.SemaphoreType.DMA(()),
            pltpu.SemaphoreType.DMA((pieces,)),
        ],
        compiler_params=params(40),
        cost_estimate=cost(3 * x_cells * y_local * (x_local * 24 + 24), x_cells * y_local * 96),
    )(*x_tables(devices, x_local, y_cells), in_vmem(data), in_hbm(green))


places = ("gl", "gx", "gz")


def exchange(data):
    return lax.all_to_all(data, places, split_axis=0, concat_axis=0, tiled=True)


def per_device(tiles, tile_owner, tile_slot, tile_count, green):
    count_gl = lax.axis_size("gl")
    mesh_sizes = (lax.axis_size("gx"), count_gl)
    devices = 4 * mesh_sizes[0] * count_gl
    tile_total, tile_len = tiles.shape[2], tiles.shape[3]
    planes, y_local, x_cells = green.shape[2:]
    y_cells = y_local * devices
    x_local = x_cells // devices
    blocks = y_cells // tile_len
    per_owner = max(2, 2 * tile_total // devices)
    assert planes == 1 and tile_len == 128
    owner_row, slot_row = tile_owner.reshape(1, tile_total), tile_slot.reshape(1, tile_total)
    green = green.reshape(2, 6, y_local, x_cells)
    me = lax.axis_index(places).reshape(1).astype(jnp.int32)
    lists = (owner_row, slot_row, tile_count, me)
    arrived = exchange(pack(tiles, *lists, devices, mesh_sizes, per_owner))
    moved = exchange(slab_waves(arrived, x_local, blocks, mesh_sizes, per_owner))
    mixed = field(moved, green, devices, x_local, y_local, y_cells, mesh_sizes)
    return mixed.reshape(2, 3, planes, y_local, x_cells)


def solution(mesh):
    count_gx, count_gy = mesh.devices.shape
    fine_mesh = jax.sharding.Mesh(
        mesh.devices.reshape(count_gx, 4, count_gy // 4), ("gx", "gz", "gl")
    )
    every = ("gx", "gz", "gl")
    in_specs = (
        P(None, None, every, None),
        P(every, None),
        P(every),
        P(every),
        P(None, None, None, every, None),
    )
    out_specs = P(None, None, None, every, None)
    return jax.shard_map(
        per_device, mesh=fine_mesh, in_specs=in_specs, out_specs=out_specs, check_vma=False
    )
```
